32 devices in a mesh: seq: 8 (over y, x, core), head: 4 (over z).
Axes of the slice: x: 2, y: 2, z: 4, core: 2. Of those that a mesh axis runs over, the one named last changes fastest.
Arguments:
- inputs: bfloat16 [4096, 4096], P('seq', 'head'), may hold values from -6 to 6
- gate: bfloat16 [4096, 4096], P('seq', 'head'), may hold values from -6 to 6
- input_map: bfloat16 [128, 4096], P('head', 'seq'), may hold values from -3 to 3
- output_map: bfloat16 [128, 4096], P('head', 'seq'), may hold values from -3 to 3
- step: float32 [64, 4096], P('head', 'seq'), may hold values from 0.25 to 2
- decay_rate: float32 [64], P('head'), may hold values from 3e-05 to 0.03
- level_mix: float32 [9, 64, 4096], P(None, 'head', 'seq'), may hold values from 0.1 to 1
- skip: float32 [64], P('head'), may hold values from 0.25 to 0.75
- norm_gain: float32 [4096], P('head'), may hold values from 0.5 to 1.5
Outputs:
- normed: bfloat16 [4096, 4096], P('seq', 'head')
The draws below stay inside these ranges and needn't reach their ends.
All inputs are finite; a program needn't handle non-finite values.
Results may differ from the reference program's by a relative error of at most 0.0075.
Values may be sent and summed in bfloat16 or wider, within the bound.
No kernel may reach another device: no remote copies, remote signals or barrier semaphores. Data moves between devices by JAX's collectives and lax.ppermute only.
A program may use at most 64 MiB of HBM per device.

```python
import math
import jax
import jax.numpy as jnp
from jax import lax

HEADS = 64
P_SIZE = 64
N = 128
GROUP = 256
LEVELS = 9
TOKENS = 4096


def block_levels(own_key, extent, cuts, smallest, largest):
    loudness = 1.0
    for dim, blocks in cuts:
        steps = jax.random.uniform(jax.random.fold_in(jax.random.fold_in(own_key, 6), dim), (blocks,), jnp.float32, smallest / len(cuts), largest / len(cuts))
        loudness = loudness * jnp.repeat(jnp.exp(steps), extent[dim] // blocks).reshape((-1,) + (1,) * (len(extent) - 1 - dim))
    return loudness


def gaussian(stream_key, shape, width, reach, cuts=(), kind=jnp.bfloat16):
    drawn = jax.random.normal(stream_key, shape, jnp.float32) * width
    if len(cuts) > 0:
        drawn = block_levels(stream_key, shape, cuts, -0.22, 0.18) * drawn
    return jnp.clip(drawn, min=-reach, max=reach).astype(kind)


def setup_inputs(seed: int = 0) -> dict:
    streams_of = jax.random.split(jax.random.key(seed), 10)
    inputs = gaussian(streams_of[0], (TOKENS, HEADS * P_SIZE), 1.0, 6.0, ((0, 8), (1, 4)))
    gate = gaussian(streams_of[1], (TOKENS, HEADS * P_SIZE), 1.0, 6.0, ((0, 8), (1, 4)))
    input_map = gaussian(streams_of[2], (N, TOKENS), 0.5, 3.0, ((0, 4), (1, 8)))
    output_map = gaussian(streams_of[3], (N, TOKENS), 0.5, 3.0, ((0, 4), (1, 8)))
    step = jnp.clip(jnp.exp(math.log(2.0) - 2.0794415 * jax.random.uniform(streams_of[4], (HEADS, TOKENS), jnp.float32) ** block_levels(streams_of[4], (HEADS, TOKENS), ((0, 4), (1, 8)), -0.2, 0.2)), 0.25, 2.0)
    decay_rate = jnp.clip(jnp.exp(math.log(0.03) - 6.9077553 * jax.random.uniform(streams_of[5], (HEADS,), jnp.float32) ** block_levels(streams_of[5], (HEADS,), ((0, 4),), -0.2, 0.2)), 2.9999999242136255e-05, 0.03)
    level_mix = jnp.clip(0.1 + 0.9 * jax.random.uniform(streams_of[6], (LEVELS, HEADS, TOKENS), jnp.float32) ** block_levels(streams_of[6], (LEVELS, HEADS, TOKENS), ((1, 4), (2, 8)), -0.2, 0.2), 0.1, 1.0)
    skip = jnp.clip(0.25 + 0.5 * jax.random.uniform(streams_of[7], (HEADS,), jnp.float32) ** block_levels(streams_of[7], (HEADS,), ((0, 4),), -0.2, 0.2), 0.25, 0.75)
    norm_gain = jnp.clip(1.0 + 0.1 * jax.random.normal(streams_of[8], (HEADS * P_SIZE,), jnp.float32), 0.5, 1.5)
    return dict(inputs=inputs, gate=gate, input_map=input_map, output_map=output_map, step=step, decay_rate=decay_rate, level_mix=level_mix, skip=skip, norm_gain=norm_gain)


def reference(inputs, gate, input_map, output_map, step, decay_rate, level_mix, skip, norm_gain):
    groups = TOKENS // GROUP
    spans = LEVELS - 1
    highest = lax.Precision.HIGHEST
    pieces = (inputs.reshape(groups, GROUP, HEADS, P_SIZE), gate.reshape(groups, GROUP, HEADS * P_SIZE), input_map.reshape(N, groups, GROUP).transpose(1, 0, 2), output_map.reshape(N, groups, GROUP).transpose(1, 0, 2), step.reshape(HEADS, groups, GROUP).transpose(1, 0, 2), level_mix.reshape(LEVELS, HEADS, groups, GROUP).transpose(2, 0, 1, 3), jnp.arange(groups, dtype=jnp.int32))
    powers = jnp.left_shift(jnp.int32(1), jnp.arange(spans, dtype=jnp.int32))
    rows = jnp.arange(GROUP, dtype=jnp.int32)
    causal = rows[:, None] >= rows[None, :]

    def advance(carry, piece):
        values, gates, in_c, out_c, step_c, mix_c, index = piece
        cum = jnp.cumsum(-step_c * decay_rate[:, None], axis=1)
        scores = jnp.dot(out_c.T, in_c, preferred_element_type=jnp.float32)
        spread = cum[:, :, None] - cum[:, None, :]
        within = jnp.where(causal[None], jnp.exp(jnp.where(causal[None], spread, 0.0)), 0.0)
        weights = (scores[None] * within * step_c[:, None, :]).astype(jnp.bfloat16)
        v32 = values.astype(jnp.float32)
        intra = jnp.einsum('hts,shp->thp', weights.astype(jnp.float32), v32, precision=highest)
        proj = jnp.einsum('nt,bhnp->bthp', out_c.astype(jnp.float32), carry, precision=highest)
        spanned = jnp.einsum('bht,bthp->thp', mix_c[1:], proj, precision=highest)
        spanned = spanned * jnp.exp(cum).T[:, :, None]
        y = mix_c[0].T[:, :, None] * intra + spanned + skip[None, :, None] * v32
        gated = y.reshape(GROUP, HEADS * P_SIZE) * jax.nn.silu(gates.astype(jnp.float32))
        scale = lax.rsqrt(lax.optimization_barrier(jnp.mean(gated * gated, axis=1, keepdims=True)) + 1e-05)
        out = (gated * scale * norm_gain[None, :]).astype(jnp.bfloat16)
        loads = (in_c[None] * (jnp.exp(cum[:, -1:] - cum) * step_c)[:, None, :]).astype(jnp.bfloat16)
        state = jnp.einsum('hns,shp->hnp', loads.astype(jnp.float32), v32, precision=highest)
        decay = jnp.exp(cum[:, -1])[None, :, None, None]
        flag = jnp.bitwise_and(index + 1, jnp.bitwise_not(index))
        hit = (powers == flag)[:, None, None, None]
        low = (powers < flag)[:, None, None, None]
        merged = decay[0] * lax.optimization_barrier(jnp.sum(jnp.where(low, carry, 0.0), axis=0)) + state
        fresh = jnp.where(hit, merged[None], jnp.where(low, 0.0, decay * carry))
        return (fresh, out)
    start = jnp.zeros((spans, HEADS, N, P_SIZE), jnp.float32)
    _, outs = lax.scan(advance, start, pieces)
    return outs.reshape(TOKENS, HEADS * P_SIZE)
```

```python
import functools

import jax
import jax.numpy as jnp
from jax import lax
from jax.experimental import pallas as pl
from jax.experimental.pallas import tpu as pltpu
from jax.sharding import PartitionSpec as P

P_SIZE = 64
GROUP = 256
DECAY_ROWS = 16
BLOCK = 256
VMEM_LIMIT = 40 * 1024 * 1024

f32, bf16 = jnp.float32, jnp.bfloat16
HIGHEST = lax.Precision.HIGHEST
TRANSPOSED = (((0,), (0,)), ((), ()))


def expander(heads, width, copies):
    row = lax.broadcasted_iota(jnp.int32, (copies * heads, width), 0)
    col = lax.broadcasted_iota(jnp.int32, (copies * heads, width), 1)
    return jnp.where(lax.rem(row, heads) == lax.div(col, P_SIZE), 1.0, 0.0)


def two_parts(factor):
    high = factor.astype(bf16).astype(f32)
    return jnp.concatenate([high, factor - high], axis=0).astype(bf16)


def transposed_dot(left, right):
    return lax.dot_general(left, right, TRANSPOSED, preferred_element_type=f32)


def head_row(heads, width, column):
    return jnp.sum(expander(heads, width, 1) * column, axis=0, keepdims=True)


def group_slice(group):
    return slice(group * GROUP, (group + 1) * GROUP)


def blocks_of(width):
    return [slice(at, at + BLOCK) for at in range(0, width, BLOCK)]


def local_spans(groups):
    spans = []
    for later in range(groups):
        for bit in range(groups.bit_length() - 1):
            if later >> bit & 1:
                start = later >> bit + 1 << bit + 1
                spans.append((later, bit, start, start + 2**bit))
    return spans


def prepare_kernel(inputs_ref, step_ref, rate_ref, scaled_ref, cum_ref):
    heads, tokens = step_ref.shape
    width = inputs_ref.shape[1]
    step = step_ref[...]
    log_decay = -step * rate_ref[...]
    row = lax.broadcasted_iota(jnp.int32, (GROUP, GROUP), 0)
    col = lax.broadcasted_iota(jnp.int32, (GROUP, GROUP), 1)
    until = jnp.where(row <= col, 1.0, 0.0)
    expand = expander(heads, width, 2).astype(bf16)
    for group in range(tokens // GROUP):
        at = group_slice(group)
        cum = jnp.dot(log_decay[:, at], until, precision=HIGHEST, preferred_element_type=f32)
        cum_ref[:, at] = cum
        factor = two_parts(jnp.exp(-cum) * step[:, at])
        for cols in blocks_of(width):
            scale = transposed_dot(factor, expand[:, cols])
            scaled_ref[at, cols] = (inputs_ref[at, cols].astype(f32) * scale).astype(bf16)


def states_kernel(parts, *refs):
    in_refs, (scaled_ref, cum_ref), out_refs = refs[:parts], refs[parts : parts + 2], refs[parts + 2 :]
    shard_ref = out_refs[0]
    heads, tokens = cum_ref.shape
    width = scaled_ref.shape[1]
    in_map = jnp.concatenate([ref[...] for ref in in_refs], axis=0)
    size = in_map.shape[0]
    cum = cum_ref[...]
    states, decays = [], []
    for group in range(tokens // GROUP):
        at = group_slice(group)
        decay = head_row(heads, width, jnp.exp(cum[:, at.stop - 1 : at.stop]))
        raw = jnp.dot(in_map[:, at], scaled_ref[at, :], preferred_element_type=f32)
        states.append(raw * decay)
        decays.append(decay)
    total, decay = states[0], decays[0]
    for group in range(1, len(states)):
        total = total * decays[group] + states[group]
        decay = decay * decays[group]
    shard_ref[:size, :] = total.astype(bf16)
    shard_ref[size:, :] = jnp.broadcast_to(decay, (DECAY_ROWS, width)).astype(bf16)
    for index, (later, _, start, stop) in enumerate(local_spans(len(states))):
        span = states[start]
        for group in range(start + 1, later):
            span = span * decays[group]
            if group < stop:
                span = span + states[group]
        out_refs[1][index * size : (index + 1) * size, :] = span.astype(bf16)


def near_kernel(parts, spans, *refs):
    in_refs, map_refs = refs[:parts], refs[parts : 2 * parts]
    scaled_ref, cum_ref, inputs_ref, gate_ref, mix_ref, skip_ref = refs[2 * parts : 2 * parts + 6]
    span_refs = refs[2 * parts + 6 : -2]
    near_ref, swish_ref = refs[-2:]
    heads, tokens = cum_ref.shape
    width = scaled_ref.shape[1]
    in_map = jnp.concatenate([ref[...] for ref in in_refs], axis=0)
    out_map = jnp.concatenate([ref[...] for ref in map_refs], axis=0)
    size = in_map.shape[0]
    expand = expander(heads, width, 2).astype(bf16)
    skip = head_row(heads, width, skip_ref[...])
    row = lax.broadcasted_iota(jnp.int32, (GROUP, GROUP), 0)
    col = lax.broadcasted_iota(jnp.int32, (GROUP, GROUP), 1)
    for group in range(tokens // GROUP):
        at = group_slice(group)
        scores = transposed_dot(out_map[:, at], in_map[:, at])
        scores = jnp.where(row >= col, scores, 0.0).astype(bf16)
        decay = jnp.exp(cum_ref[:, at])
        mixes = [two_parts(mix_ref[0, :, at] * decay)]
        states = []
        for index, (later, bit, _, _) in enumerate(spans):
            if later == group:
                mixes.append(two_parts(mix_ref[1 + bit, :, at] * decay))
                states.append(slice(index * size, (index + 1) * size))
        for cols in blocks_of(width):
            own = jnp.dot(scores, scaled_ref[at, cols], preferred_element_type=f32)
            total = transposed_dot(mixes[0], expand[:, cols]) * own
            for mix, rows in zip(mixes[1:], states):
                reach = transposed_dot(out_map[:, at], span_refs[0][rows, cols])
                total = total + transposed_dot(mix, expand[:, cols]) * reach
            near_ref[at, cols] = total + skip[:, cols] * inputs_ref[at, cols].astype(f32)
            gate = gate_ref[at, cols].astype(f32)
            swish_ref[at, cols] = gate / (1.0 + jnp.exp(-gate))


def far_body(out_map, cum_ref, mix_ref, near_ref, swish_ref, state_of, levels, gated_ref, squares_ref):
    heads, tokens = cum_ref.shape
    width = near_ref.shape[1]
    groups = tokens // GROUP
    first = groups.bit_length()
    expand = expander(heads, width, 2).astype(bf16)
    mixes = []
    before = jnp.zeros((heads, 1), f32)
    for group in range(groups):
        at = group_slice(group)
        cum = cum_ref[:, at]
        decay = jnp.exp(cum + before)
        before = before + cum[:, GROUP - 1 : GROUP]
        mixes.append([two_parts(mix_ref[first + level, :, at] * decay) for level in range(levels)])
    squares = [jnp.zeros((GROUP, 128), f32) for _ in range(groups)]
    for cols in blocks_of(width):
        states = [state_of(level, cols).astype(bf16) for level in range(levels)]
        for group in range(groups):
            at = group_slice(group)
            total = near_ref[at, cols]
            for level in range(levels):
                reach = transposed_dot(out_map[:, at], states[level])
                total = total + transposed_dot(mixes[group][level], expand[:, cols]) * reach
            gated = total * swish_ref[at, cols]
            gated_ref[at, cols] = gated
            gated = gated * gated
            for part in range(0, BLOCK, 128):
                squares[group] = squares[group] + gated[:, part : part + 128]
    ones = jnp.ones((8, 128), f32)
    for group in range(groups):
        sums = lax.dot_general(
            ones, squares[group], (((1,), (1,)), ((), ())), precision=HIGHEST, preferred_element_type=f32
        )
        squares_ref[:, group_slice(group)] = sums[:1]


def far_kernel(parts, levels, *refs):
    out_map = jnp.concatenate([ref[...] for ref in refs[:parts]], axis=0)
    cum_ref, mix_ref, near_ref, swish_ref = refs[parts : parts + 4]
    state_refs = refs[parts + 4 : -2]
    gated_ref, squares_ref = refs[-2:]

    def state_of(level, cols):
        return state_refs[level][:, cols]

    far_body(out_map, cum_ref, mix_ref, near_ref, swish_ref, state_of, levels, gated_ref, squares_ref)


def far_kernel_of_pairs(parts, *refs):
    out_map = jnp.concatenate([ref[...] for ref in refs[:parts]], axis=0)
    cum_ref, mix_ref, near_ref, swish_ref, core_ref = refs[parts : parts + 5]
    own_refs, other_refs = refs[parts + 5 : parts + 8], refs[parts + 8 : parts + 11]
    gated_ref, squares_ref = refs[-2:]
    size = out_map.shape[0]
    rank = lax.axis_index("seq")
    core = lax.rem(rank, 2)
    along_x = lax.rem(lax.div(rank, 2), 2)
    half = own_refs[0].shape[1]

    def pair_of(index, cols):
        side = cols.start // half
        at = slice(cols.start - side * half, cols.stop - side * half)
        whole = jnp.where(core == side, own_refs[index][:, at], other_refs[index][:, at]).astype(f32)
        return whole[:size], whole[size : size + 1]

    def state_of(level, cols):
        core_state = jnp.where(core == 1, core_ref[:size, cols].astype(f32), 0.0)
        if level == 0:
            return core_state
        running = jnp.where(core == 1, core_ref[size : size + 1, cols].astype(f32), 1.0)
        x_state, x_decay = pair_of(0, cols)
        if level == 1:
            return x_state * running
        running = running * jnp.where(along_x == 1, x_decay, 1.0)
        y_state, y_decay = pair_of(1, cols)
        d_state, d_decay = pair_of(2, cols)
        newer = jnp.where(along_x == 1, y_state, d_state)
        newer_decay = jnp.where(along_x == 1, y_decay, d_decay)
        older = jnp.where(along_x == 1, d_state, y_state)
        return (older * newer_decay + newer) * running

    far_body(out_map, cum_ref, mix_ref, near_ref, swish_ref, state_of, 3, gated_ref, squares_ref)


def norm_kernel(parts, columns, *refs):
    sum_refs = refs[:parts]
    gated_ref, gain_ref, out_ref = refs[parts:]
    total = sum_refs[0][...]
    for ref in sum_refs[1:]:
        total = total + ref[...]
    scale = lax.rsqrt(total / columns + 1e-05)
    scale = jnp.transpose(jnp.broadcast_to(scale, (8, scale.shape[1])))[:, :1]
    out_ref[...] = (gated_ref[...] * scale * gain_ref[...]).astype(bf16)


def call(kernel, out_shape, args, flops=0, bytes_accessed=0):
    return pl.pallas_call(
        kernel,
        out_shape=out_shape,
        in_specs=[pl.BlockSpec(memory_space=pltpu.VMEM)] * len(args),
        out_specs=jax.tree.map(lambda _: pl.BlockSpec(memory_space=pltpu.VMEM), out_shape),
        compiler_params=pltpu.CompilerParams(vmem_limit_bytes=VMEM_LIMIT),
        cost_estimate=pl.CostEstimate(flops=flops, bytes_accessed=bytes_accessed, transcendentals=0),
    )(*args)


def shaped(shape, dtype):
    return jax.ShapeDtypeStruct(shape, dtype)


def around(array, axis):
    size = lax.axis_size(axis)
    return [array] + [
        lax.ppermute(array, axis, [(i, (i + shift) % size) for i in range(size)]) for shift in range(1, size)
    ]


def flip(array, axis, distance):
    return lax.ppermute(array, axis, [(i, i ^ 1 << distance) for i in range(lax.axis_size(axis))])


def merged(older, newer, size):
    older, newer = older.astype(f32), newer.astype(f32)
    decay = newer[size : size + 1]
    return jnp.concatenate([older[:size] * decay + newer[:size], older[size:] * decay], axis=0).astype(bf16)


def far_states(shard, size):
    rank = lax.axis_index("seq")
    levels = lax.axis_size("seq").bit_length() - 1
    states = []
    running = jnp.ones((1, shard.shape[1]), f32)
    for level in range(levels):
        theirs = flip(shard, "seq", level)
        upper = jnp.right_shift(rank, level) % 2 == 1
        states.append(jnp.where(upper, theirs[:size].astype(f32) * running, 0.0).astype(bf16))
        running = jnp.where(upper, running * theirs[size : size + 1].astype(f32), running)
        shard = merged(jnp.where(upper, theirs, shard), jnp.where(upper, shard, theirs), size)
    return states


def pair_states(shard, size):
    rank = lax.axis_index("seq")
    core = rank % 2
    half = shard.shape[1] // 2
    theirs = flip(shard, "seq", 0)
    mine_half, their_half = (lax.dynamic_slice_in_dim(a, core * half, half, 1) for a in (shard, theirs))
    pair = merged(
        jnp.where(core == 1, their_half, mine_half), jnp.where(core == 1, mine_half, their_half), size
    )
    from_x = lax.ppermute(pair, "seq", [(0, 2), (1, 3), (4, 6), (5, 7)])
    from_y = lax.ppermute(pair, "seq", [(i, i + 4) for i in range(4)])
    from_diagonal = lax.ppermute(pair, "seq", [(0, 6), (1, 7), (2, 4), (3, 5)])
    own = [from_x, from_y, from_diagonal]
    return theirs, own, [flip(array, "seq", 0) for array in own]


def on_device(inputs, gate, input_map, output_map, step, decay_rate, level_mix, skip, norm_gain):
    tokens, width = inputs.shape
    heads = step.shape[0]
    parts = lax.axis_size("head")
    size = input_map.shape[0] * parts
    groups = tokens // GROUP
    spans = local_spans(groups)
    in_maps = around(input_map, "head")
    out_maps = around(output_map, "head")
    dense = 2 * tokens * GROUP * width
    scaled, cum = call(
        prepare_kernel,
        (shaped((tokens, width), bf16), shaped((heads, tokens), f32)),
        (inputs, step, decay_rate[:, None]),
        flops=dense,
        bytes_accessed=4 * tokens * width,
    )
    shard_shape = shaped((size + DECAY_ROWS, width), bf16)
    span_shape = [shaped((len(spans) * size, width), bf16)] if spans else []
    shard, *span_states = call(
        functools.partial(states_kernel, parts),
        (shard_shape, *span_shape),
        (*in_maps, scaled, cum),
        flops=dense,
        bytes_accessed=4 * tokens * width,
    )
    pairs = lax.axis_size("seq") == 8 and parts == 4
    if pairs:
        core_state, own, other = pair_states(shard, size)
        far_args, kernel = (core_state, *own, *other), functools.partial(far_kernel_of_pairs, parts)
    else:
        far_args = far_states(shard, size)
        kernel = functools.partial(far_kernel, parts, len(far_args))
    near, swish = call(
        functools.partial(near_kernel, parts, spans),
        (shaped((tokens, width), f32),) * 2,
        (*in_maps, *out_maps, scaled, cum, inputs, gate, level_mix, skip[:, None], *span_states),
        flops=4 * dense,
        bytes_accessed=14 * tokens * width,
    )
    gated, squares = call(
        kernel,
        (shaped((tokens, width), f32), shaped((1, tokens), f32)),
        (*out_maps, cum, level_mix, near, swish, *far_args),
        flops=4 * dense,
        bytes_accessed=14 * tokens * width,
    )
    return call(
        functools.partial(norm_kernel, parts, width * parts),
        shaped((tokens, width), bf16),
        (*around(squares, "head"), gated, norm_gain[None, :]),
        flops=dense,
        bytes_accessed=6 * tokens * width,
    )


def solution(mesh):
    return jax.shard_map(
        on_device,
        mesh=mesh,
        in_specs=(
            P("seq", "head"),
            P("seq", "head"),
            P("head", "seq"),
            P("head", "seq"),
            P("head", "seq"),
            P("head"),
            P(None, "head", "seq"),
            P("head"),
            P("head"),
        ),
        out_specs=P("seq", "head"),
        check_vma=False,
    )
```

```python
import functools

import jax
import jax.numpy as jnp
from jax import lax
from jax.experimental import pallas as pl
from jax.experimental.pallas import tpu as pltpu
from jax.sharding import PartitionSpec as P

P_SIZE = 64
GROUP = 256
DECAY_ROWS = 16
BLOCK = 256
VMEM_LIMIT = 40 * 1024 * 1024

f32, bf16 = jnp.float32, jnp.bfloat16
HIGHEST = lax.Precision.HIGHEST
TRANSPOSED = (((0,), (0,)), ((), ()))


def expander(heads, width, copies):
    row = lax.broadcasted_iota(jnp.int32, (copies * heads, width), 0)
    col = lax.broadcasted_iota(jnp.int32, (copies * heads, width), 1)
    return jnp.where(lax.rem(row, heads) == lax.div(col, P_SIZE), 1.0, 0.0)


def two_parts(factor):
    high = factor.astype(bf16).astype(f32)
    return jnp.concatenate([high, factor - high], axis=0).astype(bf16)


def transposed_dot(left, right):
    return lax.dot_general(left, right, TRANSPOSED, preferred_element_type=f32)


def head_row(heads, width, column):
    return jnp.sum(expander(heads, width, 1) * column, axis=0, keepdims=True)


def group_slice(group):
    return slice(group * GROUP, (group + 1) * GROUP)


def blocks_of(width):
    return [slice(at, at + BLOCK) for at in range(0, width, BLOCK)]


def local_spans(groups):
    spans = []
    for later in range(groups):
        for bit in range(groups.bit_length() - 1):
            if later >> bit & 1:
                start = later >> bit + 1 << bit + 1
                spans.append((later, bit, start, start + 2**bit))
    return spans


def column_of(row):
    size = row.shape[1]
    at = lax.broadcasted_iota(jnp.int32, (size, size), 0) == lax.broadcasted_iota(jnp.int32, (size, size), 1)
    return jnp.sum(jnp.where(at, row, 0.0), axis=1, keepdims=True)


def map_rows(maps_ref, parts, which):
    rows = maps_ref.shape[0] // (2 * parts)
    maps = maps_ref[...] if rows % 16 == 0 else maps_ref[...].astype(f32)
    picked = [maps[(2 * part + which) * rows : (2 * part + which + 1) * rows] for part in range(parts)]
    return jnp.concatenate(picked, axis=0).astype(bf16)


def fetch(sources, targets, semaphores):
    copies = [
        pltpu.make_async_copy(source, target, semaphores.at[index])
        for index, (source, target) in enumerate(zip(sources, targets))
    ]
    for copy in copies:
        copy.start()
    return copies


def prepare_kernel(inputs_hbm, step_hbm, rate_hbm, scaled_ref, cum_ref, inputs_ref, step_ref, rate_ref, semaphores):
    copies = fetch((step_hbm, rate_hbm, inputs_hbm), (step_ref, rate_ref, inputs_ref), semaphores)
    heads, tokens = step_ref.shape
    width = inputs_ref.shape[1]
    row = lax.broadcasted_iota(jnp.int32, (GROUP, GROUP), 0)
    col = lax.broadcasted_iota(jnp.int32, (GROUP, GROUP), 1)
    until = jnp.where(row <= col, 1.0, 0.0)
    expand = expander(heads, width, 2).astype(bf16)
    copies[0].wait()
    copies[1].wait()
    step = step_ref[...]
    log_decay = -step * column_of(rate_ref[...])
    factors = []
    for group in range(tokens // GROUP):
        at = group_slice(group)
        cum = jnp.dot(log_decay[:, at], until, precision=HIGHEST, preferred_element_type=f32)
        cum_ref[:, at] = cum
        factors.append(two_parts(jnp.exp(-cum) * step[:, at]))
    factor = jnp.concatenate(factors, axis=1)
    copies[2].wait()
    for cols in blocks_of(width):
        scale = transposed_dot(factor, expand[:, cols])
        scaled_ref[:, cols] = (inputs_ref[:, cols].astype(f32) * scale).astype(bf16)


def states_kernel(parts, maps_ref, scaled_ref, cum_ref, *out_refs):
    shard_ref = out_refs[0]
    heads, tokens = cum_ref.shape
    width = scaled_ref.shape[1]
    in_map = map_rows(maps_ref, parts, 0)
    size = in_map.shape[0]
    cum = cum_ref[...]
    states, decays = [], []
    for group in range(tokens // GROUP):
        at = group_slice(group)
        decay = head_row(heads, width, jnp.exp(cum[:, at.stop - 1 : at.stop]))
        raw = jnp.dot(in_map[:, at], scaled_ref[at, :], preferred_element_type=f32)
        states.append(raw * decay)
        decays.append(decay)
    total, decay = states[0], decays[0]
    for group in range(1, len(states)):
        total = total * decays[group] + states[group]
        decay = decay * decays[group]
    shard_ref[:size, :] = total.astype(bf16)
    shard_ref[size:, :] = jnp.broadcast_to(decay, (DECAY_ROWS, width)).astype(bf16)
    for index, (later, _, start, stop) in enumerate(local_spans(len(states))):
        span = states[start]
        for group in range(start + 1, later):
            span = span * decays[group]
            if group < stop:
                span = span + states[group]
        out_refs[1][index * size : (index + 1) * size, :] = span.astype(bf16)


def merge_kernel(size, mine_ref, theirs_ref, pair_ref):
    core = lax.rem(lax.axis_index("seq"), 2)
    half = pair_ref.shape[1]
    mine = jnp.where(core == 1, mine_ref[:, half:], mine_ref[:, :half])
    theirs = jnp.where(core == 1, theirs_ref[:, half:], theirs_ref[:, :half])
    older = jnp.where(core == 1, theirs, mine).astype(f32)
    newer = jnp.where(core == 1, mine, theirs).astype(f32)
    decay = newer[size : size + 1]
    pair_ref[:size, :] = (older[:size] * decay + newer[:size]).astype(bf16)
    pair_ref[size:, :] = (older[size:] * decay).astype(bf16)


def near_kernel(parts, spans, levels, *refs):
    inputs_hbm, gate_hbm, mix_hbm, skip_hbm = refs[:4]
    maps_ref, scaled_ref, cum_ref, _ = refs[4:8]
    count = 1 if spans else 0
    span_refs = refs[8 : 8 + count]
    near_ref, far_ref, inputs_ref, gate_ref, mix_ref, skip_ref, semaphores = refs[8 + count :]
    copies = fetch(refs[:4], (inputs_ref, gate_ref, mix_ref, skip_ref), semaphores)
    heads, tokens = cum_ref.shape
    width = scaled_ref.shape[1]
    groups = tokens // GROUP
    first = groups.bit_length()
    in_map = map_rows(maps_ref, parts, 0)
    out_map = map_rows(maps_ref, parts, 1)
    size = in_map.shape[0]
    expand = expander(heads, width, 2).astype(bf16)
    row = lax.broadcasted_iota(jnp.int32, (GROUP, GROUP), 0)
    col = lax.broadcasted_iota(jnp.int32, (GROUP, GROUP), 1)
    scores = []
    for group in range(groups):
        at = group_slice(group)
        all_scores = transposed_dot(out_map[:, at], in_map[:, at])
        scores.append(jnp.where(row >= col, all_scores, 0.0).astype(bf16))
    for copy in copies:
        copy.wait()
    skip = head_row(heads, width, column_of(skip_ref[...]))
    before = jnp.zeros((heads, 1), f32)
    for group in range(groups):
        at = group_slice(group)
        cum = cum_ref[:, at]
        decay = jnp.exp(cum)
        mixes = [two_parts(mix_ref[0, :, at] * decay)]
        states = []
        for index, (later, bit, _, _) in enumerate(spans):
            if later == group:
                mixes.append(two_parts(mix_ref[1 + bit, :, at] * decay))
                states.append(slice(index * size, (index + 1) * size))
        decay = jnp.exp(cum + before)
        before = before + cum[:, GROUP - 1 : GROUP]
        far_mixes = [two_parts(mix_ref[first + level, :, at] * decay) for level in range(levels)]
        for cols in blocks_of(width):
            own = jnp.dot(scores[group], scaled_ref[at, cols], preferred_element_type=f32)
            total = transposed_dot(mixes[0], expand[:, cols]) * own
            for mix, rows in zip(mixes[1:], states):
                reach = transposed_dot(out_map[:, at], span_refs[0][rows, cols])
                total = total + transposed_dot(mix, expand[:, cols]) * reach
            total = total + skip[:, cols] * inputs_ref[at, cols].astype(f32)
            gate = gate_ref[at, cols].astype(f32)
            swish = gate / (1.0 + jnp.exp(-gate))
            near_ref[at, cols] = total * swish
            for level in range(levels):
                far_ref[level, at, cols] = (transposed_dot(far_mixes[level], expand[:, cols]) * swish).astype(bf16)


def far_body(out_map, near_ref, far_ref, start, columns, state_of, gated_ref):
    levels, tokens, _ = far_ref.shape
    squares = jnp.zeros((tokens, 128), f32)
    for cols in blocks_of(columns):
        at = pl.ds(pl.multiple_of(start + cols.start, BLOCK), BLOCK)
        total = near_ref[:, at]
        for level in range(levels):
            reach = transposed_dot(out_map, state_of(level, cols, at).astype(bf16))
            total = total + far_ref[level, :, at].astype(f32) * reach
        gated_ref[:, cols] = total
        total = total * total
        for part in range(0, BLOCK, 128):
            squares = squares + total[:, part : part + 128]
    ones = jnp.ones((8, 128), f32)
    sums = lax.dot_general(
        ones, squares, (((1,), (1,)), ((), ())), precision=HIGHEST, preferred_element_type=f32
    )
    return sums[:1]


def far_kernel(parts, maps_ref, near_ref, far_ref, *refs):
    state_refs = refs[:-2]
    gated_ref, squares_ref = refs[-2:]

    def state_of(level, cols, _):
        return state_refs[level][:, cols]

    out_map = map_rows(maps_ref, parts, 1)
    sums = far_body(out_map, near_ref, far_ref, 0, near_ref.shape[1], state_of, gated_ref)
    for part in range(parts):
        squares_ref[part] = sums


def far_kernel_of_half(parts, own, *refs):
    maps_ref, near_ref, far_ref, core_ref, x_ref, y_ref, diagonal_ref = refs[:7]
    gated_ref, squares_ref = refs[-2:]
    out_map = map_rows(maps_ref, parts, 1)
    size = out_map.shape[0]
    rank = lax.axis_index("seq")
    core = lax.rem(rank, 2)
    along_x = lax.rem(lax.div(rank, 2), 2)
    along_y = lax.div(rank, 4)
    half = x_ref.shape[1]
    start = (core if own else 1 - core) * half

    def parts_of(ref, cols):
        whole = ref[:, cols].astype(f32)
        return whole[:size], whole[size : size + 1]

    def state_of(level, cols, at):
        core_state, core_decay = parts_of(core_ref, at)
        if level == 0:
            return jnp.where(core == 1, core_state, 0.0)
        running = jnp.where(core == 1, core_decay, 1.0)
        x_state, x_decay = parts_of(x_ref, cols)
        if level == 1:
            return x_state * jnp.where(along_x == 1, running, 0.0)
        running = running * jnp.where(along_x == 1, x_decay, 1.0)
        running = jnp.where(along_y == 1, running, 0.0)
        y_state, y_decay = parts_of(y_ref, cols)
        d_state, d_decay = parts_of(diagonal_ref, cols)
        newer = jnp.where(along_x == 1, y_state, d_state)
        newer_decay = jnp.where(along_x == 1, y_decay, d_decay)
        older = jnp.where(along_x == 1, d_state, y_state)
        return (older * newer_decay + newer) * running

    sums = far_body(out_map, near_ref, far_ref, start, half, state_of, gated_ref)
    if own:
        squares_ref[...] = sums
    else:
        sums = sums + refs[7][...]
        for part in range(parts):
            squares_ref[part] = sums


def norm_kernel(columns, squares_ref, gain_ref, *refs):
    gated_refs, out_ref = refs[:-1], refs[-1]
    total = jnp.sum(squares_ref[...], axis=0)
    scale = lax.rsqrt(total / columns + 1e-05)
    scale = jnp.transpose(jnp.broadcast_to(scale, (8, scale.shape[1])))[:, :1]
    if len(gated_refs) == 1:
        out_ref[...] = (gated_refs[0][...] * scale * gain_ref[...]).astype(bf16)
        return
    half = gated_refs[0].shape[1]
    core = lax.rem(lax.axis_index("seq"), 2)
    for ref, side in zip(gated_refs, (core, 1 - core)):
        at = pl.ds(pl.multiple_of(side * half, half), half)
        out_ref[:, at] = (ref[...] * scale * gain_ref[:, at]).astype(bf16)


def call(kernel, out_shape, args, flops=0, bytes_accessed=0, hbm=0, fetched=()):
    specs = [pl.BlockSpec(memory_space=pl.ANY)] * hbm + [pl.BlockSpec(memory_space=pltpu.VMEM)] * (len(args) - hbm)
    args = [pltpu.with_memory_space_constraint(arg, pltpu.HBM) for arg in args[:hbm]] + list(args[hbm:])
    scratch = [pltpu.VMEM(arg.shape, arg.dtype) for arg in args[:hbm]]
    return pl.pallas_call(
        kernel,
        out_shape=out_shape,
        in_specs=specs,
        out_specs=jax.tree.map(lambda _: pl.BlockSpec(memory_space=pltpu.VMEM), out_shape),
        scratch_shapes=scratch + ([pltpu.SemaphoreType.DMA((hbm,))] if hbm else []),
        compiler_params=pltpu.CompilerParams(vmem_limit_bytes=VMEM_LIMIT),
        cost_estimate=pl.CostEstimate(flops=flops, bytes_accessed=bytes_accessed, transcendentals=0),
    )(*args)


def shaped(shape, dtype):
    return jax.ShapeDtypeStruct(shape, dtype)


def flip(array, axis, mask):
    return lax.ppermute(array, axis, [(i, i ^ mask) for i in range(lax.axis_size(axis))])


def from_each(array, axis):
    return lax.all_to_all(array, axis, 0, 0)


def merged(older, newer, size):
    older, newer = older.astype(f32), newer.astype(f32)
    decay = newer[size : size + 1]
    return jnp.concatenate([older[:size] * decay + newer[:size], older[size:] * decay], axis=0).astype(bf16)


def far_states(shard, size):
    rank = lax.axis_index("seq")
    levels = lax.axis_size("seq").bit_length() - 1
    states = []
    running = jnp.ones((1, shard.shape[1]), f32)
    for level in range(levels):
        theirs = flip(shard, "seq", 1 << level)
        upper = jnp.right_shift(rank, level) % 2 == 1
        states.append(jnp.where(upper, theirs[:size].astype(f32) * running, 0.0).astype(bf16))
        running = jnp.where(upper, running * theirs[size : size + 1].astype(f32), running)
        shard = merged(jnp.where(upper, theirs, shard), jnp.where(upper, shard, theirs), size)
    return states


def on_device(inputs, gate, input_map, output_map, step, decay_rate, level_mix, skip, norm_gain):
    tokens, width = inputs.shape
    heads = step.shape[0]
    parts = lax.axis_size("head")
    levels = lax.axis_size("seq").bit_length() - 1
    size = input_map.shape[0] * parts
    groups = tokens // GROUP
    spans = local_spans(groups)
    dense = 2 * tokens * GROUP * width
    area = tokens * width
    maps = jnp.concatenate([input_map, output_map], axis=0)
    maps = from_each(jnp.broadcast_to(maps[None], (parts, *maps.shape)), "head")
    maps = maps.reshape(-1, tokens)
    scaled, cum = call(
        prepare_kernel,
        (shaped((tokens, width), bf16), shaped((heads, tokens), f32)),
        (inputs, step, decay_rate[None, :]),
        flops=dense,
        bytes_accessed=4 * area,
        hbm=3,
    )
    shard_shape = shaped((size + DECAY_ROWS, width), bf16)
    span_shape = [shaped((len(spans) * size, width), bf16)] if spans else []
    shard, *span_states = call(
        functools.partial(states_kernel, parts),
        (shard_shape, *span_shape),
        (maps, scaled, cum),
        flops=dense,
        bytes_accessed=4 * area,
    )
    pairs = lax.axis_size("seq") == 8 and parts == 4
    if pairs:
        theirs = flip(shard, "seq", 1)
        message = call(
            functools.partial(merge_kernel, size),
            shaped((size + DECAY_ROWS, width // 2), bf16),
            (shard, theirs),
            bytes_accessed=area,
        )
    else:
        message = shard
    near, far = call(
        functools.partial(near_kernel, parts, spans, levels),
        (shaped((tokens, width), f32), shaped((levels, tokens, width), bf16)),
        (inputs, gate, level_mix, skip[None, :], maps, scaled, cum, message, *span_states),
        flops=8 * dense,
        bytes_accessed=16 * area,
        hbm=4,
    )
    gain = norm_gain[None, :]
    all_squares = shaped((parts, 1, tokens), f32)
    if pairs:
        own = [flip(message, "seq", mask) for mask in (2, 4, 6)]
        other = [flip(array, "seq", 1) for array in own]
        gated_shape = shaped((tokens, width // 2), f32)
        own_gated, own_squares = call(
            functools.partial(far_kernel_of_half, parts, True),
            (gated_shape, shaped((1, tokens), f32)),
            (maps, near, far, theirs, *own),
            flops=2 * dense,
            bytes_accessed=6 * area,
        )
        other_gated, squares = call(
            functools.partial(far_kernel_of_half, parts, False),
            (gated_shape, all_squares),
            (maps, near, far, theirs, *other, own_squares),
            flops=2 * dense,
            bytes_accessed=6 * area,
        )
        gated = (own_gated, other_gated)
    else:
        *gated, squares = call(
            functools.partial(far_kernel, parts),
            (shaped((tokens, width), f32), all_squares),
            (maps, near, far, *far_states(shard, size)),
            flops=4 * dense,
            bytes_accessed=12 * area,
        )
    return call(
        functools.partial(norm_kernel, width * parts),
        shaped((tokens, width), bf16),
        (from_each(squares, "head"), gain, *gated),
        flops=dense,
        bytes_accessed=6 * area,
    )


def solution(mesh):
    return jax.shard_map(
        on_device,
        mesh=mesh,
        in_specs=(
            P("seq", "head"),
            P("seq", "head"),
            P("head", "seq"),
            P("head", "seq"),
            P("head", "seq"),
            P("head"),
            P(None, "head", "seq"),
            P("head"),
            P("head"),
        ),
        out_specs=P("seq", "head"),
        check_vma=False,
    )
```

```python
import functools

import jax
import jax.numpy as jnp
from jax import lax
from jax.experimental import pallas as pl
from jax.experimental.pallas import tpu as pltpu
from jax.sharding import PartitionSpec as P

P_SIZE = 64
GROUP = 256
DECAY_ROWS = 16
BLOCK = 256
NORM_CHUNKS = 4
VMEM_LIMIT = 40 * 1024 * 1024

f32, bf16 = jnp.float32, jnp.bfloat16
HIGHEST = lax.Precision.HIGHEST
TRANSPOSED = (((0,), (0,)), ((), ()))


def expander(heads, width, copies):
    row = lax.broadcasted_iota(jnp.int32, (copies * heads, width), 0)
    col = lax.broadcasted_iota(jnp.int32, (copies * heads, width), 1)
    return jnp.where(lax.rem(row, heads) == lax.div(col, P_SIZE), 1.0, 0.0)


def two_parts(factor):
    high = factor.astype(bf16).astype(f32)
    return jnp.concatenate([high, factor - high], axis=0).astype(bf16)


def transposed_dot(left, right):
    return lax.dot_general(left, right, TRANSPOSED, preferred_element_type=f32)


def head_row(heads, width, column):
    return jnp.sum(expander(heads, width, 1) * column, axis=0, keepdims=True)


def group_slice(group):
    return slice(group * GROUP, (group + 1) * GROUP)


def blocks_of(width):
    return [slice(at, at + BLOCK) for at in range(0, width, BLOCK)]


def local_spans(groups):
    spans = []
    for later in range(groups):
        for bit in range(groups.bit_length() - 1):
            if later >> bit & 1:
                start = later >> bit + 1 << bit + 1
                spans.append((later, bit, start, start + 2**bit))
    return spans


def column_of(row):
    size = row.shape[1]
    at = lax.broadcasted_iota(jnp.int32, (size, size), 0) == lax.broadcasted_iota(jnp.int32, (size, size), 1)
    return jnp.sum(jnp.where(at, row, 0.0), axis=1, keepdims=True)


def map_rows(map_refs, which):
    rows = map_refs[0].shape[0] // 2
    picked = []
    for ref in map_refs:
        maps = ref[...] if rows % 16 == 0 else ref[...].astype(f32)
        picked.append(maps[which * rows : (which + 1) * rows])
    return jnp.concatenate(picked, axis=0).astype(bf16)


def fetch(sources, targets, semaphores):
    copies = [
        pltpu.make_async_copy(source, target, semaphores.at[index])
        for index, (source, target) in enumerate(zip(sources, targets))
    ]
    for copy in copies:
        copy.start()
    return copies


def prepare_kernel(inputs_hbm, step_hbm, rate_hbm, scaled_ref, cum_ref, inputs_ref, step_ref, rate_ref, semaphores):
    copies = fetch((step_hbm, rate_hbm, inputs_hbm), (step_ref, rate_ref, inputs_ref), semaphores)
    heads, tokens = step_ref.shape
    width = inputs_ref.shape[1]
    row = lax.broadcasted_iota(jnp.int32, (GROUP, GROUP), 0)
    col = lax.broadcasted_iota(jnp.int32, (GROUP, GROUP), 1)
    until = jnp.where(row <= col, 1.0, 0.0)
    expand = expander(heads, width, 2).astype(bf16)
    copies[0].wait()
    copies[1].wait()
    step = step_ref[...]
    log_decay = -step * column_of(rate_ref[...])
    factors = []
    for group in range(tokens // GROUP):
        at = group_slice(group)
        cum = jnp.dot(log_decay[:, at], until, precision=HIGHEST, preferred_element_type=f32)
        cum_ref[:, at] = cum
        factors.append(two_parts(jnp.exp(-cum) * step[:, at]))
    factor = jnp.concatenate(factors, axis=1)
    copies[2].wait()
    for cols in blocks_of(width):
        scale = transposed_dot(factor, expand[:, cols])
        scaled_ref[:, cols] = (inputs_ref[:, cols].astype(f32) * scale).astype(bf16)


def pack_kernel(in_hbm, out_hbm, maps_ref, semaphores):
    rows = in_hbm.shape[0]
    for copy in fetch((in_hbm, out_hbm), (maps_ref.at[:rows], maps_ref.at[rows:]), semaphores):
        copy.wait()


def states_kernel(parts, *refs):
    map_refs, (scaled_ref, cum_ref), out_refs = refs[:parts], refs[parts : parts + 2], refs[parts + 2 :]
    shard_ref = out_refs[0]
    heads, tokens = cum_ref.shape
    width = scaled_ref.shape[1]
    in_map = map_rows(map_refs, 0)
    size = in_map.shape[0]
    cum = cum_ref[...]
    states, decays = [], []
    for group in range(tokens // GROUP):
        at = group_slice(group)
        decay = head_row(heads, width, jnp.exp(cum[:, at.stop - 1 : at.stop]))
        raw = jnp.dot(in_map[:, at], scaled_ref[at, :], preferred_element_type=f32)
        states.append(raw * decay)
        decays.append(decay)
    total, decay = states[0], decays[0]
    for group in range(1, len(states)):
        total = total * decays[group] + states[group]
        decay = decay * decays[group]
    shard_ref[:size, :] = total.astype(bf16)
    shard_ref[size:, :] = jnp.broadcast_to(decay, (DECAY_ROWS, width)).astype(bf16)
    for index, (later, _, start, stop) in enumerate(local_spans(len(states))):
        span = states[start]
        for group in range(start + 1, later):
            span = span * decays[group]
            if group < stop:
                span = span + states[group]
        out_refs[1][index * size : (index + 1) * size, :] = span.astype(bf16)


def merge_kernel(size, mine_ref, theirs_ref, pair_ref):
    core = lax.rem(lax.axis_index("seq"), 2)
    half = pair_ref.shape[1]
    mine = jnp.where(core == 1, mine_ref[:, half:], mine_ref[:, :half])
    theirs = jnp.where(core == 1, theirs_ref[:, half:], theirs_ref[:, :half])
    older = jnp.where(core == 1, theirs, mine).astype(f32)
    newer = jnp.where(core == 1, mine, theirs).astype(f32)
    decay = newer[size : size + 1]
    pair_ref[:size, :] = (older[:size] * decay + newer[:size]).astype(bf16)
    pair_ref[size:, :] = (older[size:] * decay).astype(bf16)


def near_kernel(parts, spans, levels, *refs):
    inputs_hbm, gate_hbm, mix_hbm, skip_hbm = refs[:4]
    scaled_ref, cum_ref, _ = refs[4:7]
    map_refs = refs[7 : 7 + parts]
    count = 7 + parts + (1 if spans else 0)
    span_refs = refs[7 + parts : count]
    near_ref, far_ref, inputs_ref, gate_ref, mix_ref, skip_ref, semaphores = refs[count:]
    copies = fetch(refs[:4], (inputs_ref, gate_ref, mix_ref, skip_ref), semaphores)
    heads, tokens = cum_ref.shape
    width = scaled_ref.shape[1]
    groups = tokens // GROUP
    first = groups.bit_length()
    in_map = map_rows(map_refs, 0)
    out_map = map_rows(map_refs, 1)
    size = in_map.shape[0]
    expand = expander(heads, width, 2).astype(bf16)
    row = lax.broadcasted_iota(jnp.int32, (GROUP, GROUP), 0)
    col = lax.broadcasted_iota(jnp.int32, (GROUP, GROUP), 1)
    scores = []
    for group in range(groups):
        at = group_slice(group)
        all_scores = transposed_dot(out_map[:, at], in_map[:, at])
        scores.append(jnp.where(row >= col, all_scores, 0.0).astype(bf16))
    for copy in copies:
        copy.wait()
    skip = head_row(heads, width, column_of(skip_ref[...]))
    before = jnp.zeros((heads, 1), f32)
    for group in range(groups):
        at = group_slice(group)
        cum = cum_ref[:, at]
        decay = jnp.exp(cum)
        mixes = [two_parts(mix_ref[0, :, at] * decay)]
        states = []
        for index, (later, bit, _, _) in enumerate(spans):
            if later == group:
                mixes.append(two_parts(mix_ref[1 + bit, :, at] * decay))
                states.append(slice(index * size, (index + 1) * size))
        decay = jnp.exp(cum + before)
        before = before + cum[:, GROUP - 1 : GROUP]
        far_mixes = [two_parts(mix_ref[first + level, :, at] * decay) for level in range(levels)]
        for cols in blocks_of(width):
            own = jnp.dot(scores[group], scaled_ref[at, cols], preferred_element_type=f32)
            total = transposed_dot(mixes[0], expand[:, cols]) * own
            for mix, rows in zip(mixes[1:], states):
                reach = transposed_dot(out_map[:, at], span_refs[0][rows, cols])
                total = total + transposed_dot(mix, expand[:, cols]) * reach
            total = total + skip[:, cols] * inputs_ref[at, cols].astype(f32)
            gate = gate_ref[at, cols].astype(f32)
            swish = gate / (1.0 + jnp.exp(-gate))
            near_ref[at, cols] = total * swish
            for level in range(levels):
                far_ref[level, at, cols] = (transposed_dot(far_mixes[level], expand[:, cols]) * swish).astype(bf16)


def far_body(out_map, near_ref, far_ref, start, columns, state_of, gated_ref):
    levels, tokens, _ = far_ref.shape
    squares = jnp.zeros((tokens, 128), f32)
    for cols in blocks_of(columns):
        at = pl.ds(pl.multiple_of(start + cols.start, BLOCK), BLOCK)
        total = near_ref[:, at]
        for level in range(levels):
            reach = transposed_dot(out_map, state_of(level, cols, at).astype(bf16))
            total = total + far_ref[level, :, at].astype(f32) * reach
        gated_ref[:, cols] = total
        total = total * total
        for part in range(0, BLOCK, 128):
            squares = squares + total[:, part : part + 128]
    ones = jnp.ones((8, 128), f32)
    sums = lax.dot_general(
        ones, squares, (((1,), (1,)), ((), ())), precision=HIGHEST, preferred_element_type=f32
    )
    return sums[:1]


def far_kernel(parts, *refs):
    map_refs, (near_ref, far_ref) = refs[:parts], refs[parts : parts + 2]
    state_refs = refs[parts + 2 : -2]
    gated_ref, squares_ref = refs[-2:]

    def state_of(level, cols, _):
        return state_refs[level][:, cols]

    out_map = map_rows(map_refs, 1)
    squares_ref[...] = far_body(out_map, near_ref, far_ref, 0, near_ref.shape[1], state_of, gated_ref)


def far_kernel_of_half(parts, own, *refs):
    map_refs = refs[:parts]
    near_ref, far_ref, core_ref, x_ref, y_ref, diagonal_ref = refs[parts : parts + 6]
    gated_ref, squares_ref = refs[-2:]
    out_map = map_rows(map_refs, 1)
    size = out_map.shape[0]
    rank = lax.axis_index("seq")
    core = lax.rem(rank, 2)
    along_x = lax.rem(lax.div(rank, 2), 2)
    along_y = lax.div(rank, 4)
    half = x_ref.shape[1]
    start = (core if own else 1 - core) * half

    def parts_of(ref, cols):
        whole = ref[:, cols].astype(f32)
        return whole[:size], whole[size : size + 1]

    def state_of(level, cols, at):
        core_state, core_decay = parts_of(core_ref, at)
        if level == 0:
            return jnp.where(core == 1, core_state, 0.0)
        running = jnp.where(core == 1, core_decay, 1.0)
        x_state, x_decay = parts_of(x_ref, cols)
        if level == 1:
            return x_state * jnp.where(along_x == 1, running, 0.0)
        running = running * jnp.where(along_x == 1, x_decay, 1.0)
        running = jnp.where(along_y == 1, running, 0.0)
        y_state, y_decay = parts_of(y_ref, cols)
        d_state, d_decay = parts_of(diagonal_ref, cols)
        newer = jnp.where(along_x == 1, y_state, d_state)
        newer_decay = jnp.where(along_x == 1, y_decay, d_decay)
        older = jnp.where(along_x == 1, d_state, y_state)
        return (older * newer_decay + newer) * running

    sums = far_body(out_map, near_ref, far_ref, start, half, state_of, gated_ref)
    squares_ref[...] = sums if own else sums + refs[parts + 6][...]


def norm_kernel(parts, columns, *refs):
    gain_ref = refs[parts]
    gated_refs, (out_hbm, out_ref, semaphores) = refs[parts + 1 : -3], refs[-3:]
    total = refs[0][...]
    for ref in refs[1:parts]:
        total = total + ref[...]
    scale = lax.rsqrt(total / columns + 1e-05)
    scale = jnp.transpose(jnp.broadcast_to(scale, (8, scale.shape[1])))[:, :1]
    tokens = scale.shape[0]
    width = gated_refs[0].shape[1]
    core = lax.rem(lax.axis_index("seq"), 2)
    sides = (core, 1 - core) if len(gated_refs) == 2 else (0,)
    chunk = tokens // NORM_CHUNKS
    copies = []
    for index in range(NORM_CHUNKS):
        rows = slice(index * chunk, (index + 1) * chunk)
        for ref, side in zip(gated_refs, sides):
            at = pl.ds(pl.multiple_of(side * width, width), width)
            out_ref[rows, at] = (ref[rows, :] * scale[rows] * gain_ref[:, at]).astype(bf16)
        copies.append(pltpu.make_async_copy(out_ref.at[rows], out_hbm.at[rows], semaphores.at[index]))
        copies[-1].start()
    for copy in copies:
        copy.wait()


def call(kernel, out_shape, args, flops=0, bytes_accessed=0, hbm=0, scratch=None, out_space=pltpu.VMEM):
    specs = [pl.BlockSpec(memory_space=pl.ANY)] * hbm + [pl.BlockSpec(memory_space=pltpu.VMEM)] * (len(args) - hbm)
    args = [pltpu.with_memory_space_constraint(arg, pltpu.HBM) for arg in args[:hbm]] + list(args[hbm:])
    if scratch is None:
        scratch = [pltpu.VMEM(arg.shape, arg.dtype) for arg in args[:hbm]]
        scratch += [pltpu.SemaphoreType.DMA((hbm,))] if hbm else []
    return pl.pallas_call(
        kernel,
        out_shape=out_shape,
        in_specs=specs,
        out_specs=jax.tree.map(lambda _: pl.BlockSpec(memory_space=out_space), out_shape),
        scratch_shapes=scratch,
        compiler_params=pltpu.CompilerParams(vmem_limit_bytes=VMEM_LIMIT),
        cost_estimate=pl.CostEstimate(flops=flops, bytes_accessed=bytes_accessed, transcendentals=0),
    )(*args)


def shaped(shape, dtype):
    return jax.ShapeDtypeStruct(shape, dtype)


def flip(array, axis, mask):
    return lax.ppermute(array, axis, [(i, i ^ mask) for i in range(lax.axis_size(axis))])


def from_each(array, axis):
    return [array] + [flip(array, axis, mask) for mask in range(1, lax.axis_size(axis))]


def merged(older, newer, size):
    older, newer = older.astype(f32), newer.astype(f32)
    decay = newer[size : size + 1]
    return jnp.concatenate([older[:size] * decay + newer[:size], older[size:] * decay], axis=0).astype(bf16)


def far_states(shard, size):
    rank = lax.axis_index("seq")
    levels = lax.axis_size("seq").bit_length() - 1
    states = []
    running = jnp.ones((1, shard.shape[1]), f32)
    for level in range(levels):
        theirs = flip(shard, "seq", 1 << level)
        upper = jnp.right_shift(rank, level) % 2 == 1
        states.append(jnp.where(upper, theirs[:size].astype(f32) * running, 0.0).astype(bf16))
        running = jnp.where(upper, running * theirs[size : size + 1].astype(f32), running)
        shard = merged(jnp.where(upper, theirs, shard), jnp.where(upper, shard, theirs), size)
    return states


def on_device(inputs, gate, input_map, output_map, step, decay_rate, level_mix, skip, norm_gain):
    tokens, width = inputs.shape
    heads = step.shape[0]
    parts = lax.axis_size("head")
    levels = lax.axis_size("seq").bit_length() - 1
    size = input_map.shape[0] * parts
    groups = tokens // GROUP
    spans = local_spans(groups)
    dense = 2 * tokens * GROUP * width
    area = tokens * width
    rows = input_map.shape[0]
    if rows % 16 == 0:
        maps = call(
            pack_kernel,
            shaped((2 * rows, tokens), bf16),
            (input_map, output_map),
            bytes_accessed=4 * rows * tokens,
            hbm=2,
            scratch=[pltpu.SemaphoreType.DMA((2,))],
        )
    else:
        maps = jnp.concatenate([input_map, output_map], axis=0)
    maps = from_each(maps, "head")
    scaled, cum = call(
        prepare_kernel,
        (shaped((tokens, width), bf16), shaped((heads, tokens), f32)),
        (inputs, step, decay_rate[None, :]),
        flops=dense,
        bytes_accessed=4 * area,
        hbm=3,
    )
    shard_shape = shaped((size + DECAY_ROWS, width), bf16)
    span_shape = [shaped((len(spans) * size, width), bf16)] if spans else []
    shard, *span_states = call(
        functools.partial(states_kernel, parts),
        (shard_shape, *span_shape),
        (*maps, scaled, cum),
        flops=dense,
        bytes_accessed=4 * area,
    )
    pairs = lax.axis_size("seq") == 8 and parts == 4
    if pairs:
        theirs = flip(shard, "seq", 1)
        message = call(
            functools.partial(merge_kernel, size),
            shaped((size + DECAY_ROWS, width // 2), bf16),
            (shard, theirs),
            bytes_accessed=area,
        )
    else:
        message = shard
    near, far = call(
        functools.partial(near_kernel, parts, spans, levels),
        (shaped((tokens, width), f32), shaped((levels, tokens, width), bf16)),
        (inputs, gate, level_mix, skip[None, :], scaled, cum, message, *maps, *span_states),
        flops=8 * dense,
        bytes_accessed=16 * area,
        hbm=4,
    )
    gain = norm_gain[None, :]
    sums_shape = shaped((1, tokens), f32)
    if pairs:
        own = [flip(message, "seq", mask) for mask in (2, 4, 6)]
        *own, near, far = lax.optimization_barrier((*own, near, far))
        other = [flip(array, "seq", 1) for array in own]
        gated_shape = shaped((tokens, width // 2), f32)
        own_gated, own_squares = call(
            functools.partial(far_kernel_of_half, parts, True),
            (gated_shape, sums_shape),
            (*maps, near, far, theirs, *own),
            flops=2 * dense,
            bytes_accessed=6 * area,
        )
        other_gated, squares = call(
            functools.partial(far_kernel_of_half, parts, False),
            (gated_shape, sums_shape),
            (*maps, near, far, theirs, *other, own_squares),
            flops=2 * dense,
            bytes_accessed=6 * area,
        )
        gated = (own_gated, other_gated)
    else:
        *gated, squares = call(
            functools.partial(far_kernel, parts),
            (shaped((tokens, width), f32), sums_shape),
            (*maps, near, far, *far_states(shard, size)),
            flops=4 * dense,
            bytes_accessed=12 * area,
        )
    return call(
        functools.partial(norm_kernel, parts, width * parts),
        shaped((tokens, width), bf16),
        (*from_each(squares, "head"), gain, *gated),
        flops=dense,
        bytes_accessed=6 * area,
        scratch=[pltpu.VMEM((tokens, width), bf16), pltpu.SemaphoreType.DMA((NORM_CHUNKS,))],
        out_space=pl.ANY,
    )


def solution(mesh):
    return jax.shard_map(
        on_device,
        mesh=mesh,
        in_specs=(
            P("seq", "head"),
            P("seq", "head"),
            P("head", "seq"),
            P("head", "seq"),
            P("head", "seq"),
            P("head"),
            P(None, "head", "seq"),
            P("head"),
            P("head"),
        ),
        out_specs=P("seq", "head"),
        check_vma=False,
    )
```

```python
import functools

import jax
import jax.numpy as jnp
from jax import lax
from jax.experimental import pallas as pl
from jax.experimental.pallas import tpu as pltpu
from jax.sharding import PartitionSpec as P

P_SIZE = 64
GROUP = 256
DECAY_ROWS = 16
BLOCK = 256
NORM_CHUNKS = 4
VMEM_LIMIT = 40 * 1024 * 1024

f32, bf16 = jnp.float32, jnp.bfloat16
HIGHEST = lax.Precision.HIGHEST
TRANSPOSED = (((0,), (0,)), ((), ()))


def expander(heads, width, copies):
    row = lax.broadcasted_iota(jnp.int32, (copies * heads, width), 0)
    col = lax.broadcasted_iota(jnp.int32, (copies * heads, width), 1)
    return jnp.where(lax.rem(row, heads) == lax.div(col, P_SIZE), 1.0, 0.0)


def two_parts(factor):
    high = factor.astype(bf16).astype(f32)
    return jnp.concatenate([high, factor - high], axis=0).astype(bf16)


def transposed_dot(left, right):
    return lax.dot_general(left, right, TRANSPOSED, preferred_element_type=f32)


def head_row(heads, width, column):
    return jnp.sum(expander(heads, width, 1) * column, axis=0, keepdims=True)


def group_slice(group):
    return slice(group * GROUP, (group + 1) * GROUP)


def blocks_of(width):
    return [slice(at, at + BLOCK) for at in range(0, width, BLOCK)]


def local_spans(groups):
    spans = []
    for later in range(groups):
        for bit in range(groups.bit_length() - 1):
            if later >> bit & 1:
                start = later >> bit + 1 << bit + 1
                spans.append((later, bit, start, start + 2**bit))
    return spans


def column_of(row):
    size = row.shape[1]
    at = lax.broadcasted_iota(jnp.int32, (size, size), 0) == lax.broadcasted_iota(jnp.int32, (size, size), 1)
    return jnp.sum(jnp.where(at, row, 0.0), axis=1, keepdims=True)


def map_rows(map_refs, which):
    rows = map_refs[0].shape[0] // 2
    picked = []
    for ref in map_refs:
        maps = ref[...] if rows % 16 == 0 else ref[...].astype(f32)
        picked.append(maps[which * rows : (which + 1) * rows])
    return jnp.concatenate(picked, axis=0).astype(bf16)


def fetch(sources, targets, semaphores):
    copies = [
        pltpu.make_async_copy(source, target, semaphores.at[index])
        for index, (source, target) in enumerate(zip(sources, targets))
    ]
    for copy in copies:
        copy.start()
    return copies


def prepare_kernel(inputs_hbm, step_hbm, rate_hbm, scaled_ref, cum_ref, inputs_ref, step_ref, rate_ref, semaphores):
    copies = fetch((step_hbm, rate_hbm, inputs_hbm), (step_ref, rate_ref, inputs_ref), semaphores)
    heads, tokens = step_ref.shape
    width = inputs_ref.shape[1]
    row = lax.broadcasted_iota(jnp.int32, (GROUP, GROUP), 0)
    col = lax.broadcasted_iota(jnp.int32, (GROUP, GROUP), 1)
    until = jnp.where(row <= col, 1.0, 0.0)
    expand = expander(heads, width, 2).astype(bf16)
    copies[0].wait()
    copies[1].wait()
    step = step_ref[...]
    log_decay = -step * column_of(rate_ref[...])
    factors = []
    for group in range(tokens // GROUP):
        at = group_slice(group)
        cum = jnp.dot(log_decay[:, at], until, precision=HIGHEST, preferred_element_type=f32)
        cum_ref[:, at] = cum
        factors.append(two_parts(jnp.exp(-cum) * step[:, at]))
    factor = jnp.concatenate(factors, axis=1)
    copies[2].wait()
    for cols in blocks_of(width):
        scale = transposed_dot(factor, expand[:, cols])
        scaled_ref[:, cols] = (inputs_ref[:, cols].astype(f32) * scale).astype(bf16)


def pack_kernel(in_hbm, out_hbm, maps_ref, semaphores):
    rows = in_hbm.shape[0]
    for copy in fetch((in_hbm, out_hbm), (maps_ref.at[:rows], maps_ref.at[rows:]), semaphores):
        copy.wait()


def states_kernel(parts, *refs):
    map_refs, (scaled_ref, cum_ref), out_refs = refs[:parts], refs[parts : parts + 2], refs[parts + 2 :]
    shard_ref = out_refs[0]
    heads, tokens = cum_ref.shape
    width = scaled_ref.shape[1]
    in_map = map_rows(map_refs, 0)
    size = in_map.shape[0]
    cum = cum_ref[...]
    states, decays = [], []
    for group in range(tokens // GROUP):
        at = group_slice(group)
        decay = head_row(heads, width, jnp.exp(cum[:, at.stop - 1 : at.stop]))
        raw = jnp.dot(in_map[:, at], scaled_ref[at, :], preferred_element_type=f32)
        states.append(raw * decay)
        decays.append(decay)
    total, decay = states[0], decays[0]
    for group in range(1, len(states)):
        total = total * decays[group] + states[group]
        decay = decay * decays[group]
    shard_ref[:size, :] = total.astype(bf16)
    shard_ref[size:, :] = jnp.broadcast_to(decay, (DECAY_ROWS, width)).astype(bf16)
    for index, (later, _, start, stop) in enumerate(local_spans(len(states))):
        span = states[start]
        for group in range(start + 1, later):
            span = span * decays[group]
            if group < stop:
                span = span + states[group]
        out_refs[1][index * size : (index + 1) * size, :] = span.astype(bf16)


def merge_kernel(size, mine_ref, theirs_ref, pair_ref):
    core = lax.rem(lax.axis_index("seq"), 2)
    half = pair_ref.shape[1]
    mine = jnp.where(core == 1, mine_ref[:, half:], mine_ref[:, :half])
    theirs = jnp.where(core == 1, theirs_ref[:, half:], theirs_ref[:, :half])
    older = jnp.where(core == 1, theirs, mine).astype(f32)
    newer = jnp.where(core == 1, mine, theirs).astype(f32)
    decay = newer[size : size + 1]
    pair_ref[:size, :] = (older[:size] * decay + newer[:size]).astype(bf16)
    pair_ref[size:, :] = (older[size:] * decay).astype(bf16)


def near_kernel(parts, spans, levels, paired, *refs):
    inputs_hbm, gate_hbm, mix_hbm, skip_hbm = refs[:4]
    scaled_ref, cum_ref, _, core_ref = refs[4:8]
    map_refs = refs[8 : 8 + parts]
    count = 8 + parts + (1 if spans else 0)
    span_refs = refs[8 + parts : count]
    near_ref, far_ref, turned_ref, inputs_ref, gate_ref, mix_ref, skip_ref, semaphores = refs[count:]
    copies = fetch(refs[:4], (inputs_ref, gate_ref, mix_ref, skip_ref), semaphores)
    heads, tokens = cum_ref.shape
    width = scaled_ref.shape[1]
    groups = tokens // GROUP
    first = groups.bit_length()
    in_map = map_rows(map_refs, 0)
    out_map = map_rows(map_refs, 1)
    size = in_map.shape[0]
    turned_ref[...] = jnp.transpose(out_map)
    expand = expander(heads, width, 2).astype(bf16)
    row = lax.broadcasted_iota(jnp.int32, (GROUP, GROUP), 0)
    col = lax.broadcasted_iota(jnp.int32, (GROUP, GROUP), 1)
    scores = []
    has_core = lax.rem(lax.axis_index("seq"), 2) == 1
    for group in range(groups):
        at = group_slice(group)
        all_scores = transposed_dot(out_map[:, at], in_map[:, at])
        scores.append(jnp.where(row >= col, all_scores, 0.0).astype(bf16))
    for copy in copies:
        copy.wait()
    skip = head_row(heads, width, column_of(skip_ref[...]))
    before = jnp.zeros((heads, 1), f32)
    for group in range(groups):
        at = group_slice(group)
        cum = cum_ref[:, at]
        decay = jnp.exp(cum)
        mixes = [two_parts(mix_ref[0, :, at] * decay)]
        states = []
        for index, (later, bit, _, _) in enumerate(spans):
            if later == group:
                mixes.append(two_parts(mix_ref[1 + bit, :, at] * decay))
                states.append(slice(index * size, (index + 1) * size))
        decay = jnp.exp(cum + before)
        before = before + cum[:, GROUP - 1 : GROUP]
        far_mixes = [two_parts(mix_ref[first + level, :, at] * decay) for level in range(levels)]
        if paired:
            core_mix, *far_mixes = far_mixes
        for cols in blocks_of(width):
            own = jnp.dot(scores[group], scaled_ref[at, cols], preferred_element_type=f32)
            total = transposed_dot(mixes[0], expand[:, cols]) * own
            for mix, rows in zip(mixes[1:], states):
                reach = jnp.dot(turned_ref[at, :], span_refs[0][rows, cols], preferred_element_type=f32)
                total = total + transposed_dot(mix, expand[:, cols]) * reach
            if paired:
                reach = jnp.dot(turned_ref[at, :], core_ref[:size, cols], preferred_element_type=f32)
                reach = jnp.where(has_core, reach, 0.0)
                total = total + transposed_dot(core_mix, expand[:, cols]) * reach
            total = total + skip[:, cols] * inputs_ref[at, cols].astype(f32)
            gate = gate_ref[at, cols].astype(f32)
            swish = gate / (1.0 + jnp.exp(-gate))
            near_ref[at, cols] = total * swish
            for level, mix in enumerate(far_mixes):
                far_ref[level, at, cols] = (transposed_dot(mix, expand[:, cols]) * swish).astype(bf16)


def far_body(turned_ref, near_ref, far_ref, gain_ref, start, columns, state_of, gated_ref):
    levels, tokens, _ = far_ref.shape
    squares = jnp.zeros((tokens, 128), f32)
    for cols in blocks_of(columns):
        at = pl.ds(pl.multiple_of(start + cols.start, BLOCK), BLOCK)
        total = near_ref[:, at]
        for level in range(levels):
            state = state_of(level, cols, at).astype(bf16)
            reach = jnp.dot(turned_ref[...], state, preferred_element_type=f32)
            total = total + far_ref[level, :, at].astype(f32) * reach
        gated_ref[:, cols] = total * gain_ref[:, at]
        total = total * total
        for part in range(0, BLOCK, 128):
            squares = squares + total[:, part : part + 128]
    return squares


def row_sums(squares):
    ones = jnp.ones((8, squares.shape[1]), f32)
    sums = lax.dot_general(
        ones, squares, (((1,), (1,)), ((), ())), precision=HIGHEST, preferred_element_type=f32
    )
    return sums[:1]


def far_kernel(turned_ref, near_ref, far_ref, gain_ref, *refs):
    state_refs = refs[:-2]
    gated_ref, sums_ref = refs[-2:]

    def state_of(level, cols, _):
        return state_refs[level][:, cols]

    width = near_ref.shape[1]
    sums_ref[...] = row_sums(far_body(turned_ref, near_ref, far_ref, gain_ref, 0, width, state_of, gated_ref))


def far_kernel_of_half(own, *refs):
    turned_ref, near_ref, far_ref, gain_ref, core_ref, x_ref, y_ref, diagonal_ref = refs[:8]
    gated_ref, sums_ref = refs[-2:]
    size = turned_ref.shape[1]
    rank = lax.axis_index("seq")
    core = lax.rem(rank, 2)
    along_x = lax.rem(lax.div(rank, 2), 2)
    along_y = lax.div(rank, 4)
    half = x_ref.shape[1]
    start = (core if own else 1 - core) * half

    def parts_of(ref, cols):
        whole = ref[:, cols].astype(f32)
        return whole[:size], whole[size : size + 1]

    def state_of(level, cols, at):
        core_decay = core_ref[size:, at].astype(f32)[:1]
        running = jnp.where(core == 1, core_decay, 1.0)
        x_state, x_decay = parts_of(x_ref, cols)
        if level == 0:
            return x_state * jnp.where(along_x == 1, running, 0.0)
        running = running * jnp.where(along_x == 1, x_decay, 1.0)
        running = jnp.where(along_y == 1, running, 0.0)
        y_state, y_decay = parts_of(y_ref, cols)
        d_state, d_decay = parts_of(diagonal_ref, cols)
        newer = jnp.where(along_x == 1, y_state, d_state)
        newer_decay = jnp.where(along_x == 1, y_decay, d_decay)
        older = jnp.where(along_x == 1, d_state, y_state)
        return (older * newer_decay + newer) * running

    squares = far_body(turned_ref, near_ref, far_ref, gain_ref, start, half, state_of, gated_ref)
    sums_ref[...] = squares if own else row_sums(squares + refs[8][...])


def norm_kernel(parts, columns, *refs):
    gated_refs, (out_hbm, out_ref, semaphores) = refs[parts:-3], refs[-3:]
    total = refs[0][...]
    for ref in refs[1:parts]:
        total = total + ref[...]
    scale = lax.rsqrt(total / columns + 1e-05)
    scale = jnp.transpose(jnp.broadcast_to(scale, (8, scale.shape[1])))[:, :1]
    tokens = scale.shape[0]
    width = gated_refs[0].shape[1]
    core = lax.rem(lax.axis_index("seq"), 2)
    sides = (core, 1 - core) if len(gated_refs) == 2 else (0,)
    chunk = tokens // NORM_CHUNKS
    copies = []
    for index in range(NORM_CHUNKS):
        rows = slice(index * chunk, (index + 1) * chunk)
        for ref, side in zip(gated_refs, sides):
            at = pl.ds(pl.multiple_of(side * width, width), width)
            out_ref[rows, at] = (ref[rows, :] * scale[rows]).astype(bf16)
        copies.append(pltpu.make_async_copy(out_ref.at[rows], out_hbm.at[rows], semaphores.at[index]))
        copies[-1].start()
    for copy in copies:
        copy.wait()


def call(kernel, out_shape, args, flops=0, bytes_accessed=0, hbm=0, scratch=None, out_space=pltpu.VMEM):
    specs = [pl.BlockSpec(memory_space=pl.ANY)] * hbm + [pl.BlockSpec(memory_space=pltpu.VMEM)] * (len(args) - hbm)
    args = [pltpu.with_memory_space_constraint(arg, pltpu.HBM) for arg in args[:hbm]] + list(args[hbm:])
    if scratch is None:
        scratch = [pltpu.VMEM(arg.shape, arg.dtype) for arg in args[:hbm]]
        scratch += [pltpu.SemaphoreType.DMA((hbm,))] if hbm else []
    return pl.pallas_call(
        kernel,
        out_shape=out_shape,
        in_specs=specs,
        out_specs=jax.tree.map(lambda _: pl.BlockSpec(memory_space=out_space), out_shape),
        scratch_shapes=scratch,
        compiler_params=pltpu.CompilerParams(vmem_limit_bytes=VMEM_LIMIT),
        cost_estimate=pl.CostEstimate(flops=flops, bytes_accessed=bytes_accessed, transcendentals=0),
    )(*args)


def shaped(shape, dtype):
    return jax.ShapeDtypeStruct(shape, dtype)


def flip(array, axis, mask):
    return lax.ppermute(array, axis, [(i, i ^ mask) for i in range(lax.axis_size(axis))])


def from_each(array, axis):
    return [array] + [flip(array, axis, mask) for mask in range(1, lax.axis_size(axis))]


def add_kernel(left_ref, right_ref, sum_ref):
    sum_ref[...] = left_ref[...] + right_ref[...]


def sum_to_last(array, axis):
    size = lax.axis_size(axis)
    mask = 1
    theirs = flip(array, axis, mask)
    while 2 * mask < size:
        mask = 2 * mask
        array = call(add_kernel, shaped(array.shape, array.dtype), (array, theirs))
        theirs = flip(array, axis, mask)
    return array, theirs


def merged(older, newer, size):
    older, newer = older.astype(f32), newer.astype(f32)
    decay = newer[size : size + 1]
    return jnp.concatenate([older[:size] * decay + newer[:size], older[size:] * decay], axis=0).astype(bf16)


def far_states(shard, size):
    rank = lax.axis_index("seq")
    levels = lax.axis_size("seq").bit_length() - 1
    states = []
    running = jnp.ones((1, shard.shape[1]), f32)
    for level in range(levels):
        theirs = flip(shard, "seq", 1 << level)
        upper = jnp.right_shift(rank, level) % 2 == 1
        states.append(jnp.where(upper, theirs[:size].astype(f32) * running, 0.0).astype(bf16))
        running = jnp.where(upper, running * theirs[size : size + 1].astype(f32), running)
        shard = merged(jnp.where(upper, theirs, shard), jnp.where(upper, shard, theirs), size)
    return states


def on_device(inputs, gate, input_map, output_map, step, decay_rate, level_mix, skip, norm_gain):
    tokens, width = inputs.shape
    heads = step.shape[0]
    parts = lax.axis_size("head")
    levels = lax.axis_size("seq").bit_length() - 1
    size = input_map.shape[0] * parts
    groups = tokens // GROUP
    spans = local_spans(groups)
    dense = 2 * tokens * GROUP * width
    area = tokens * width
    rows = input_map.shape[0]
    if rows % 16 == 0:
        maps = call(
            pack_kernel,
            shaped((2 * rows, tokens), bf16),
            (input_map, output_map),
            bytes_accessed=4 * rows * tokens,
            hbm=2,
            scratch=[pltpu.SemaphoreType.DMA((2,))],
        )
    else:
        maps = jnp.concatenate([input_map, output_map], axis=0)
    maps = from_each(maps, "head")
    scaled, cum = call(
        prepare_kernel,
        (shaped((tokens, width), bf16), shaped((heads, tokens), f32)),
        (inputs, step, decay_rate[None, :]),
        flops=dense,
        bytes_accessed=4 * area,
        hbm=3,
    )
    shard_shape = shaped((size + DECAY_ROWS, width), bf16)
    span_shape = [shaped((len(spans) * size, width), bf16)] if spans else []
    shard, *span_states = call(
        functools.partial(states_kernel, parts),
        (shard_shape, *span_shape),
        (*maps, scaled, cum),
        flops=dense,
        bytes_accessed=4 * area,
    )
    pairs = lax.axis_size("seq") == 8 and parts == 4
    if pairs:
        theirs = flip(shard, "seq", 1)
        message = call(
            functools.partial(merge_kernel, size),
            shaped((size + DECAY_ROWS, width // 2), bf16),
            (shard, theirs),
            bytes_accessed=area,
        )
    else:
        message = shard
    near_levels = levels - 1 if pairs else levels
    near, far, turned = call(
        functools.partial(near_kernel, parts, spans, levels, pairs),
        (
            shaped((tokens, width), f32),
            shaped((near_levels, tokens, width), bf16),
            shaped((tokens, size), bf16),
        ),
        (
            *(inputs, gate, level_mix, skip[None, :], scaled, cum, message, theirs if pairs else message),
            *(*maps, *span_states),
        ),
        flops=8 * dense,
        bytes_accessed=16 * area,
        hbm=4,
    )
    gain = norm_gain[None, :]
    sums_shape = shaped((1, tokens), f32)
    if pairs:
        own = [flip(message, "seq", mask) for mask in (6, 2, 4)]
        *own, near, far = lax.optimization_barrier((*own, near, far))
        own = own[1], own[2], own[0]
        other = [flip(array, "seq", 1) for array in own]
        gated_shape = shaped((tokens, width // 2), f32)
        own_gated, own_squares = call(
            functools.partial(far_kernel_of_half, True),
            (gated_shape, shaped((tokens, 128), f32)),
            (turned, near, far, gain, theirs, *own),
            flops=2 * dense,
            bytes_accessed=6 * area,
        )
        other_gated, sums = call(
            functools.partial(far_kernel_of_half, False),
            (gated_shape, sums_shape),
            (turned, near, far, gain, theirs, *other, own_squares),
            flops=2 * dense,
            bytes_accessed=6 * area,
        )
        gated = (own_gated, other_gated)
    else:
        *gated, sums = call(
            far_kernel,
            (shaped((tokens, width), f32), sums_shape),
            (turned, near, far, gain, *far_states(shard, size)),
            flops=4 * dense,
            bytes_accessed=12 * area,
        )
    last = sum_to_last(sums, "head")
    return call(
        functools.partial(norm_kernel, len(last), width * parts),
        shaped((tokens, width), bf16),
        (*last, *gated),
        flops=dense,
        bytes_accessed=6 * area,
        scratch=[pltpu.VMEM((tokens, width), bf16), pltpu.SemaphoreType.DMA((NORM_CHUNKS,))],
        out_space=pl.ANY,
    )


def solution(mesh):
    return jax.shard_map(
        on_device,
        mesh=mesh,
        in_specs=(
            P("seq", "head"),
            P("seq", "head"),
            P("head", "seq"),
            P("head", "seq"),
            P("head", "seq"),
            P("head"),
            P(None, "head", "seq"),
            P("head"),
            P("head"),
        ),
        out_specs=P("seq", "head"),
        check_vma=False,
    )
```

```python
import functools

import jax
import jax.numpy as jnp
from jax import lax
from jax.experimental import pallas as pl
from jax.experimental.pallas import tpu as pltpu
from jax.sharding import PartitionSpec as P

P_SIZE = 64
GROUP = 256
DECAY_ROWS = 16
BLOCK = 256
NORM_CHUNKS = 8
VMEM_LIMIT = 40 * 1024 * 1024

f32, bf16 = jnp.float32, jnp.bfloat16
HIGHEST = lax.Precision.HIGHEST
TRANSPOSED = (((0,), (0,)), ((), ()))


def expander(heads, width, copies):
    row = lax.broadcasted_iota(jnp.int32, (copies * heads, width), 0)
    col = lax.broadcasted_iota(jnp.int32, (copies * heads, width), 1)
    return jnp.where(lax.rem(row, heads) == lax.div(col, P_SIZE), 1.0, 0.0)


def two_parts(factor):
    high = factor.astype(bf16).astype(f32)
    return jnp.concatenate([high, factor - high], axis=0).astype(bf16)


def transposed_dot(left, right):
    return lax.dot_general(left, right, TRANSPOSED, preferred_element_type=f32)


def head_row(heads, width, column):
    return jnp.sum(expander(heads, width, 1) * column, axis=0, keepdims=True)


def group_slice(group):
    return slice(group * GROUP, (group + 1) * GROUP)


def blocks_of(width):
    return [slice(at, at + BLOCK) for at in range(0, width, BLOCK)]


def local_spans(groups):
    spans = []
    for later in range(groups):
        for bit in range(groups.bit_length() - 1):
            if later >> bit & 1:
                start = later >> bit + 1 << bit + 1
                spans.append((later, bit, start, start + 2**bit))
    return spans


def column_of(row):
    size = row.shape[1]
    at = lax.broadcasted_iota(jnp.int32, (size, size), 0) == lax.broadcasted_iota(jnp.int32, (size, size), 1)
    return jnp.sum(jnp.where(at, row, 0.0), axis=1, keepdims=True)


def map_rows(map_refs, which):
    rows = map_refs[0].shape[0] // 2
    picked = []
    for ref in map_refs:
        maps = ref[...] if rows % 16 == 0 else ref[...].astype(f32)
        picked.append(maps[which * rows : (which + 1) * rows])
    return jnp.concatenate(picked, axis=0).astype(bf16)


def fetch(sources, targets, semaphores):
    copies = [
        pltpu.make_async_copy(source, target, semaphores.at[index])
        for index, (source, target) in enumerate(zip(sources, targets))
    ]
    for copy in copies:
        copy.start()
    return copies


def prepare_kernel(inputs_hbm, step_hbm, rate_hbm, scaled_ref, cum_ref, inputs_ref, step_ref, rate_ref, semaphores):
    copies = fetch((step_hbm, rate_hbm, inputs_hbm), (step_ref, rate_ref, inputs_ref), semaphores)
    heads, tokens = step_ref.shape
    width = inputs_ref.shape[1]
    row = lax.broadcasted_iota(jnp.int32, (GROUP, GROUP), 0)
    col = lax.broadcasted_iota(jnp.int32, (GROUP, GROUP), 1)
    until = jnp.where(row <= col, 1.0, 0.0)
    expand = expander(heads, width, 2).astype(bf16)
    copies[0].wait()
    copies[1].wait()
    step = step_ref[...]
    log_decay = -step * column_of(rate_ref[...])
    factors = []
    for group in range(tokens // GROUP):
        at = group_slice(group)
        cum = jnp.dot(log_decay[:, at], until, precision=HIGHEST, preferred_element_type=f32)
        cum_ref[:, at] = cum
        factors.append(two_parts(jnp.exp(-cum) * step[:, at]))
    factor = jnp.concatenate(factors, axis=1)
    copies[2].wait()
    for cols in blocks_of(width):
        scale = transposed_dot(factor, expand[:, cols])
        scaled_ref[:, cols] = (inputs_ref[:, cols].astype(f32) * scale).astype(bf16)


def pack_kernel(in_hbm, out_hbm, maps_ref, semaphores):
    rows = in_hbm.shape[0]
    for copy in fetch((in_hbm, out_hbm), (maps_ref.at[:rows], maps_ref.at[rows:]), semaphores):
        copy.wait()


def states_kernel(parts, *refs):
    map_refs, (scaled_ref, cum_ref), out_refs = refs[:parts], refs[parts : parts + 2], refs[parts + 2 :]
    shard_ref = out_refs[0]
    heads, tokens = cum_ref.shape
    width = scaled_ref.shape[1]
    in_map = map_rows(map_refs, 0)
    size = in_map.shape[0]
    cum = cum_ref[...]
    states, decays = [], []
    for group in range(tokens // GROUP):
        at = group_slice(group)
        decay = head_row(heads, width, jnp.exp(cum[:, at.stop - 1 : at.stop]))
        raw = jnp.dot(in_map[:, at], scaled_ref[at, :], preferred_element_type=f32)
        states.append(raw * decay)
        decays.append(decay)
    total, decay = states[0], decays[0]
    for group in range(1, len(states)):
        total = total * decays[group] + states[group]
        decay = decay * decays[group]
    shard_ref[:size, :] = total.astype(bf16)
    shard_ref[size:, :] = jnp.broadcast_to(decay, (DECAY_ROWS, width)).astype(bf16)
    for index, (later, _, start, stop) in enumerate(local_spans(len(states))):
        span = states[start]
        for group in range(start + 1, later):
            span = span * decays[group]
            if group < stop:
                span = span + states[group]
        out_refs[1][index * size : (index + 1) * size, :] = span.astype(bf16)


def merge_kernel(size, mine_ref, theirs_ref, pair_ref):
    core = lax.rem(lax.axis_index("seq"), 2)
    half = pair_ref.shape[1]
    mine = jnp.where(core == 1, mine_ref[:, half:], mine_ref[:, :half])
    theirs = jnp.where(core == 1, theirs_ref[:, half:], theirs_ref[:, :half])
    older = jnp.where(core == 1, theirs, mine).astype(f32)
    newer = jnp.where(core == 1, mine, theirs).astype(f32)
    decay = newer[size : size + 1]
    pair_ref[:size, :] = (older[:size] * decay + newer[:size]).astype(bf16)
    pair_ref[size:, :] = (older[size:] * decay).astype(bf16)


def near_kernel(parts, spans, levels, paired, *refs):
    inputs_hbm, gate_hbm, mix_hbm, skip_hbm = refs[:4]
    scaled_ref, cum_ref, _, core_ref = refs[4:8]
    map_refs = refs[8 : 8 + parts]
    count = 8 + parts + (1 if spans else 0)
    span_refs = refs[8 + parts : count]
    near_ref, far_ref, turned_ref, inputs_ref, gate_ref, mix_ref, skip_ref, semaphores = refs[count:]
    copies = fetch(refs[:4], (inputs_ref, gate_ref, mix_ref, skip_ref), semaphores)
    heads, tokens = cum_ref.shape
    width = scaled_ref.shape[1]
    groups = tokens // GROUP
    first = groups.bit_length()
    in_map = map_rows(map_refs, 0)
    out_map = map_rows(map_refs, 1)
    size = in_map.shape[0]
    turned_ref[...] = jnp.transpose(out_map)
    expand = expander(heads, width, 2).astype(bf16)
    row = lax.broadcasted_iota(jnp.int32, (GROUP, GROUP), 0)
    col = lax.broadcasted_iota(jnp.int32, (GROUP, GROUP), 1)
    scores = []
    has_core = lax.rem(lax.axis_index("seq"), 2) == 1
    for group in range(groups):
        at = group_slice(group)
        all_scores = transposed_dot(out_map[:, at], in_map[:, at])
        scores.append(jnp.where(row >= col, all_scores, 0.0).astype(bf16))
    for copy in copies:
        copy.wait()
    skip = head_row(heads, width, column_of(skip_ref[...]))
    before = jnp.zeros((heads, 1), f32)
    for group in range(groups):
        at = group_slice(group)
        cum = cum_ref[:, at]
        decay = jnp.exp(cum)
        mixes = [two_parts(mix_ref[0, :, at] * decay)]
        states = []
        for index, (later, bit, _, _) in enumerate(spans):
            if later == group:
                mixes.append(two_parts(mix_ref[1 + bit, :, at] * decay))
                states.append(slice(index * size, (index + 1) * size))
        decay = jnp.exp(cum + before)
        before = before + cum[:, GROUP - 1 : GROUP]
        far_mixes = [two_parts(mix_ref[first + level, :, at] * decay) for level in range(levels)]
        if paired:
            core_mix, *far_mixes = far_mixes
        for cols in blocks_of(width):
            own = jnp.dot(scores[group], scaled_ref[at, cols], preferred_element_type=f32)
            total = transposed_dot(mixes[0], expand[:, cols]) * own
            for mix, rows in zip(mixes[1:], states):
                reach = jnp.dot(turned_ref[at, :], span_refs[0][rows, cols], preferred_element_type=f32)
                total = total + transposed_dot(mix, expand[:, cols]) * reach
            if paired:
                reach = jnp.dot(turned_ref[at, :], core_ref[:size, cols], preferred_element_type=f32)
                reach = jnp.where(has_core, reach, 0.0)
                total = total + transposed_dot(core_mix, expand[:, cols]) * reach
            total = total + skip[:, cols] * inputs_ref[at, cols].astype(f32)
            gate = gate_ref[at, cols].astype(f32)
            swish = gate / (1.0 + jnp.exp(-gate))
            near_ref[at, cols] = total * swish
            for level, mix in enumerate(far_mixes):
                far_ref[level, at, cols] = (transposed_dot(mix, expand[:, cols]) * swish).astype(bf16)


def far_body(turned_ref, near_ref, far_ref, gain_ref, start, columns, state_of, gated_ref):
    levels, tokens, _ = far_ref.shape
    squares = jnp.zeros((tokens, 128), f32)
    for cols in blocks_of(columns):
        at = pl.ds(pl.multiple_of(start + cols.start, BLOCK), BLOCK)
        total = near_ref[:, at]
        for level in range(levels):
            state = state_of(level, cols, at).astype(bf16)
            reach = jnp.dot(turned_ref[...], state, preferred_element_type=f32)
            total = total + far_ref[level, :, at].astype(f32) * reach
        gated_ref[:, cols] = total * gain_ref[:, at]
        total = total * total
        for part in range(0, BLOCK, 128):
            squares = squares + total[:, part : part + 128]
    return squares


def row_sums(squares):
    high = squares.astype(bf16)
    low = (squares - high.astype(f32)).astype(bf16)
    parts = jnp.concatenate([high, low], axis=1)
    ones = jnp.ones((16, parts.shape[1]), bf16)
    return lax.dot_general(ones, parts, (((1,), (1,)), ((), ())), preferred_element_type=f32)[:1]


def far_kernel(turned_ref, near_ref, far_ref, gain_ref, *refs):
    state_refs = refs[:-2]
    gated_ref, sums_ref = refs[-2:]

    def state_of(level, cols, _):
        return state_refs[level][:, cols]

    width = near_ref.shape[1]
    sums_ref[...] = row_sums(far_body(turned_ref, near_ref, far_ref, gain_ref, 0, width, state_of, gated_ref))


def combine_kernel(size, x_ref, y_ref, diagonal_ref, spans_ref):
    rank = lax.axis_index("seq")
    along_x = lax.rem(lax.div(rank, 2), 2)
    along_y = lax.div(rank, 4)

    def parts_of(ref):
        return ref[:size, :].astype(f32), ref[size:, :].astype(f32)[:1]

    x_state, x_decay = parts_of(x_ref)
    y_state, y_decay = parts_of(y_ref)
    d_state, d_decay = parts_of(diagonal_ref)
    newer = jnp.where(along_x == 1, y_state, d_state)
    newer_decay = jnp.where(along_x == 1, y_decay, d_decay)
    older = jnp.where(along_x == 1, d_state, y_state)
    running = jnp.where(along_x == 1, x_decay, 1.0)
    running = jnp.where(along_y == 1, running, 0.0)
    spans_ref[:size, :] = jnp.where(along_x == 1, x_state, 0.0).astype(bf16)
    spans_ref[size:, :] = ((older * newer_decay + newer) * running).astype(bf16)


def far_kernel_of_half(own, *refs):
    turned_ref, near_ref, far_ref, gain_ref, core_ref, spans_ref = refs[:6]
    gated_ref, sums_ref = refs[-2:]
    size = turned_ref.shape[1]
    core = lax.rem(lax.axis_index("seq"), 2)
    half = spans_ref.shape[1]
    start = (core if own else 1 - core) * half

    def state_of(level, cols, at):
        core_decay = core_ref[size:, at].astype(f32)[:1]
        running = jnp.where(core == 1, core_decay, 1.0)
        return spans_ref[level * size : (level + 1) * size, cols].astype(f32) * running

    squares = far_body(turned_ref, near_ref, far_ref, gain_ref, start, half, state_of, gated_ref)
    sums_ref[...] = squares if own else row_sums(squares + refs[6][...])


def norm_kernel(parts, columns, *refs):
    gated_refs, (out_hbm, out_ref, semaphores) = refs[parts:-3], refs[-3:]
    total = refs[0][...]
    for ref in refs[1:parts]:
        total = total + ref[...]
    scale = lax.rsqrt(total / columns + 1e-05)
    pieces, rest = [], scale
    for _ in range(3):
        pieces.append(rest.astype(bf16).astype(f32))
        rest = rest - pieces[-1]
    tokens = scale.shape[1]
    pieces.append(jnp.zeros((16 - len(pieces), tokens), f32))
    scale = transposed_dot(jnp.concatenate(pieces, axis=0).astype(bf16), jnp.ones((16, 128), bf16))
    width = gated_refs[0].shape[1]
    core = lax.rem(lax.axis_index("seq"), 2)
    sides = (core, 1 - core) if len(gated_refs) == 2 else (0,)
    chunk = tokens // NORM_CHUNKS
    copies = []
    for index in range(NORM_CHUNKS):
        rows = slice(index * chunk, (index + 1) * chunk)
        for ref, side in zip(gated_refs, sides):
            for col in range(0, width, 128):
                at = pl.ds(pl.multiple_of(side * width + col, 128), 128)
                out_ref[rows, at] = (ref[rows, col : col + 128] * scale[rows]).astype(bf16)
        copies.append(pltpu.make_async_copy(out_ref.at[rows], out_hbm.at[rows], semaphores.at[index]))
        copies[-1].start()
    for copy in copies:
        copy.wait()


def call(kernel, out_shape, args, flops=0, bytes_accessed=0, hbm=0, scratch=None, out_space=pltpu.VMEM):
    specs = [pl.BlockSpec(memory_space=pl.ANY)] * hbm + [pl.BlockSpec(memory_space=pltpu.VMEM)] * (len(args) - hbm)
    args = [pltpu.with_memory_space_constraint(arg, pltpu.HBM) for arg in args[:hbm]] + list(args[hbm:])
    if scratch is None:
        scratch = [pltpu.VMEM(arg.shape, arg.dtype) for arg in args[:hbm]]
        scratch += [pltpu.SemaphoreType.DMA((hbm,))] if hbm else []
    return pl.pallas_call(
        kernel,
        out_shape=out_shape,
        in_specs=specs,
        out_specs=jax.tree.map(lambda _: pl.BlockSpec(memory_space=out_space), out_shape),
        scratch_shapes=scratch,
        compiler_params=pltpu.CompilerParams(vmem_limit_bytes=VMEM_LIMIT),
        cost_estimate=pl.CostEstimate(flops=flops, bytes_accessed=bytes_accessed, transcendentals=0),
    )(*args)


def shaped(shape, dtype):
    return jax.ShapeDtypeStruct(shape, dtype)


def flip(array, axis, mask):
    return lax.ppermute(array, axis, [(i, i ^ mask) for i in range(lax.axis_size(axis))])


def from_each(array, axis):
    return [array] + [flip(array, axis, mask) for mask in range(1, lax.axis_size(axis))]


def merged(older, newer, size):
    older, newer = older.astype(f32), newer.astype(f32)
    decay = newer[size : size + 1]
    return jnp.concatenate([older[:size] * decay + newer[:size], older[size:] * decay], axis=0).astype(bf16)


def far_states(shard, size):
    rank = lax.axis_index("seq")
    levels = lax.axis_size("seq").bit_length() - 1
    states = []
    running = jnp.ones((1, shard.shape[1]), f32)
    for level in range(levels):
        theirs = flip(shard, "seq", 1 << level)
        upper = jnp.right_shift(rank, level) % 2 == 1
        states.append(jnp.where(upper, theirs[:size].astype(f32) * running, 0.0).astype(bf16))
        running = jnp.where(upper, running * theirs[size : size + 1].astype(f32), running)
        shard = merged(jnp.where(upper, theirs, shard), jnp.where(upper, shard, theirs), size)
    return states


def on_device(inputs, gate, input_map, output_map, step, decay_rate, level_mix, skip, norm_gain):
    tokens, width = inputs.shape
    heads = step.shape[0]
    parts = lax.axis_size("head")
    levels = lax.axis_size("seq").bit_length() - 1
    size = input_map.shape[0] * parts
    groups = tokens // GROUP
    spans = local_spans(groups)
    dense = 2 * tokens * GROUP * width
    area = tokens * width
    rows = input_map.shape[0]
    if rows % 16 == 0:
        maps = call(
            pack_kernel,
            shaped((2 * rows, tokens), bf16),
            (input_map, output_map),
            bytes_accessed=4 * rows * tokens,
            hbm=2,
            scratch=[pltpu.SemaphoreType.DMA((2,))],
        )
    else:
        maps = jnp.concatenate([input_map, output_map], axis=0)
    maps = from_each(maps, "head")
    scaled, cum = call(
        prepare_kernel,
        (shaped((tokens, width), bf16), shaped((heads, tokens), f32)),
        (inputs, step, decay_rate[None, :]),
        flops=dense,
        bytes_accessed=4 * area,
        hbm=3,
    )
    shard_shape = shaped((size + DECAY_ROWS, width), bf16)
    span_shape = [shaped((len(spans) * size, width), bf16)] if spans else []
    shard, *span_states = call(
        functools.partial(states_kernel, parts),
        (shard_shape, *span_shape),
        (*maps, scaled, cum),
        flops=dense,
        bytes_accessed=4 * area,
    )
    pairs = lax.axis_size("seq") == 8 and parts == 4
    if pairs:
        theirs = flip(shard, "seq", 1)
        message = call(
            functools.partial(merge_kernel, size),
            shaped((size + DECAY_ROWS, width // 2), bf16),
            (shard, theirs),
            bytes_accessed=area,
        )
    else:
        message = shard
    near_levels = levels - 1 if pairs else levels
    near, far, turned = call(
        functools.partial(near_kernel, parts, spans, levels, pairs),
        (
            shaped((tokens, width), f32),
            shaped((near_levels, tokens, width), bf16),
            shaped((tokens, size), bf16),
        ),
        (
            *(inputs, gate, level_mix, skip[None, :], scaled, cum, message, theirs if pairs else message),
            *(*maps, *span_states),
        ),
        flops=8 * dense,
        bytes_accessed=16 * area,
        hbm=4,
    )
    gain = norm_gain[None, :]
    sums_shape = shaped((1, tokens), f32)
    if pairs:
        received = [flip(message, "seq", mask) for mask in (2, 4, 6)]
        *received, near, far = lax.optimization_barrier((*received, near, far))
        own = call(
            functools.partial(combine_kernel, size),
            shaped((2 * size, width // 2), bf16),
            received,
            bytes_accessed=area,
        )
        other = flip(own, "seq", 1)
        gated_shape = shaped((tokens, width // 2), f32)
        own_gated, own_squares = call(
            functools.partial(far_kernel_of_half, True),
            (gated_shape, shaped((tokens, 128), f32)),
            (turned, near, far, gain, theirs, own),
            flops=2 * dense,
            bytes_accessed=6 * area,
        )
        other_gated, sums = call(
            functools.partial(far_kernel_of_half, False),
            (gated_shape, sums_shape),
            (turned, near, far, gain, theirs, other, own_squares),
            flops=2 * dense,
            bytes_accessed=6 * area,
        )
        gated = (own_gated, other_gated)
    else:
        *gated, sums = call(
            far_kernel,
            (shaped((tokens, width), f32), sums_shape),
            (turned, near, far, gain, *far_states(shard, size)),
            flops=4 * dense,
            bytes_accessed=12 * area,
        )
    last = from_each(sums, "head")
    return call(
        functools.partial(norm_kernel, len(last), width * parts),
        shaped((tokens, width), bf16),
        (*last, *gated),
        flops=dense,
        bytes_accessed=6 * area,
        scratch=[pltpu.VMEM((tokens, width), bf16), pltpu.SemaphoreType.DMA((NORM_CHUNKS,))],
        out_space=pl.ANY,
    )


def solution(mesh):
    return jax.shard_map(
        on_device,
        mesh=mesh,
        in_specs=(
            P("seq", "head"),
            P("seq", "head"),
            P("head", "seq"),
            P("head", "seq"),
            P("head", "seq"),
            P("head"),
            P(None, "head", "seq"),
            P("head"),
            P("head"),
        ),
        out_specs=P("seq", "head"),
        check_vma=False,
    )
```

```python
import functools

import jax
import jax.numpy as jnp
from jax import lax
from jax.experimental import pallas as pl
from jax.experimental.pallas import tpu as pltpu
from jax.sharding import PartitionSpec as P

P_SIZE = 64
GROUP = 256
DECAY_ROWS = 16
BLOCK = 256
NORM_CHUNKS = 8
VMEM_LIMIT = 40 * 1024 * 1024

f32, bf16 = jnp.float32, jnp.bfloat16
HIGHEST = lax.Precision.HIGHEST
TRANSPOSED = (((0,), (0,)), ((), ()))


def expander(heads, width, copies):
    row = lax.broadcasted_iota(jnp.int32, (copies * heads, width), 0)
    col = lax.broadcasted_iota(jnp.int32, (copies * heads, width), 1)
    return jnp.where(lax.rem(row, heads) == lax.div(col, P_SIZE), 1.0, 0.0)


def two_parts(factor):
    high = factor.astype(bf16).astype(f32)
    return jnp.concatenate([high, factor - high], axis=0).astype(bf16)


def transposed_dot(left, right):
    return lax.dot_general(left, right, TRANSPOSED, preferred_element_type=f32)


def head_row(heads, width, column):
    return jnp.sum(expander(heads, width, 1) * column, axis=0, keepdims=True)


def group_slice(group):
    return slice(group * GROUP, (group + 1) * GROUP)


def blocks_of(width):
    return [slice(at, at + BLOCK) for at in range(0, width, BLOCK)]


def local_spans(groups):
    spans = []
    for later in range(groups):
        for bit in range(groups.bit_length() - 1):
            if later >> bit & 1:
                start = later >> bit + 1 << bit + 1
                spans.append((later, bit, start, start + 2**bit))
    return spans


def column_of(row):
    size = row.shape[1]
    at = lax.broadcasted_iota(jnp.int32, (size, size), 0) == lax.broadcasted_iota(jnp.int32, (size, size), 1)
    return jnp.sum(jnp.where(at, row, 0.0), axis=1, keepdims=True)


def map_rows(maps):
    if all(rows.shape[0] % 16 == 0 for rows in maps):
        return jnp.concatenate([rows[...] for rows in maps], axis=0)
    return jnp.concatenate([rows[...].astype(f32) for rows in maps], axis=0).astype(bf16)


def in_map_rows(map_refs):
    rows = map_refs[0].shape[0] // 2
    others = map_refs[:1:-1]
    if rows % 16 == 0:
        return map_rows([map_refs[0].at[:rows], map_refs[1].at[:rows], *others])
    return map_rows([map_refs[0][...].astype(f32)[:rows], map_refs[1][...].astype(f32)[:rows], *others])


def fetch(sources, targets, semaphores):
    copies = [
        pltpu.make_async_copy(source, target, semaphores.at[index])
        for index, (source, target) in enumerate(zip(sources, targets))
    ]
    for copy in copies:
        copy.start()
    return copies


def prepare_kernel(inputs_hbm, step_hbm, rate_hbm, scaled_ref, cum_ref, inputs_ref, step_ref, rate_ref, semaphores):
    copies = fetch((step_hbm, rate_hbm, inputs_hbm), (step_ref, rate_ref, inputs_ref), semaphores)
    heads, tokens = step_ref.shape
    width = inputs_ref.shape[1]
    row = lax.broadcasted_iota(jnp.int32, (GROUP, GROUP), 0)
    col = lax.broadcasted_iota(jnp.int32, (GROUP, GROUP), 1)
    until = jnp.where(row <= col, 1.0, 0.0)
    expand = expander(heads, width, 2).astype(bf16)
    copies[0].wait()
    copies[1].wait()
    step = step_ref[...]
    log_decay = -step * column_of(rate_ref[...])
    factors = []
    for group in range(tokens // GROUP):
        at = group_slice(group)
        cum = jnp.dot(log_decay[:, at], until, precision=HIGHEST, preferred_element_type=f32)
        cum_ref[:, at] = cum
        factors.append(two_parts(jnp.exp(-cum) * step[:, at]))
    factor = jnp.concatenate(factors, axis=1)
    copies[2].wait()
    for cols in blocks_of(width):
        scale = transposed_dot(factor, expand[:, cols])
        scaled_ref[:, cols] = (inputs_ref[:, cols].astype(f32) * scale).astype(bf16)


def pack_kernel(in_hbm, out_hbm, maps_ref, semaphores):
    rows = in_hbm.shape[0]
    for copy in fetch((in_hbm, out_hbm), (maps_ref.at[:rows], maps_ref.at[rows:]), semaphores):
        copy.wait()


def join_kernel(mine_ref, theirs_ref, _, both_ref):
    rows = mine_ref.shape[0] // 2
    both_ref[:rows, :] = mine_ref[rows:, :]
    both_ref[rows:, :] = theirs_ref[rows:, :]


def states_kernel(parts, *refs):
    map_refs, (scaled_ref, cum_ref), out_refs = refs[:parts], refs[parts : parts + 2], refs[parts + 2 :]
    shard_ref = out_refs[0]
    heads, tokens = cum_ref.shape
    width = scaled_ref.shape[1]
    in_map = in_map_rows(map_refs)
    size = in_map.shape[0]
    cum = cum_ref[...]
    states, decays = [], []
    for group in range(tokens // GROUP):
        at = group_slice(group)
        decay = head_row(heads, width, jnp.exp(cum[:, at.stop - 1 : at.stop]))
        raw = jnp.dot(in_map[:, at], scaled_ref[at, :], preferred_element_type=f32)
        states.append(raw * decay)
        decays.append(decay)
    total, decay = states[0], decays[0]
    for group in range(1, len(states)):
        total = total * decays[group] + states[group]
        decay = decay * decays[group]
    shard_ref[:size, :] = total.astype(bf16)
    shard_ref[size:, :] = jnp.broadcast_to(decay, (DECAY_ROWS, width)).astype(bf16)
    for index, (later, _, start, stop) in enumerate(local_spans(len(states))):
        span = states[start]
        for group in range(start + 1, later):
            span = span * decays[group]
            if group < stop:
                span = span + states[group]
        out_refs[1][index * size : (index + 1) * size, :] = span.astype(bf16)


def merge_kernel(size, mine_ref, theirs_ref, pair_ref):
    core = lax.rem(lax.axis_index("seq"), 2)
    half = pair_ref.shape[1]
    mine = jnp.where(core == 1, mine_ref[:, half:], mine_ref[:, :half])
    theirs = jnp.where(core == 1, theirs_ref[:, half:], theirs_ref[:, :half])
    older = jnp.where(core == 1, theirs, mine).astype(f32)
    newer = jnp.where(core == 1, mine, theirs).astype(f32)
    decay = newer[size : size + 1]
    pair_ref[:size, :] = (older[:size] * decay + newer[:size]).astype(bf16)
    pair_ref[size:, :] = (older[size:] * decay).astype(bf16)


def factor_kernel(spans, levels, *refs):
    inputs_hbm, gate_hbm, mix_hbm, skip_hbm, cum_ref, _ = refs[:6]
    base_ref, own_ref, far_ref = refs[6:9]
    span_refs = refs[9:-5]
    inputs_ref, gate_ref, mix_ref, skip_ref, semaphores = refs[-5:]
    copies = fetch(refs[:4], (inputs_ref, gate_ref, mix_ref, skip_ref), semaphores)
    heads, tokens = cum_ref.shape
    width = inputs_ref.shape[1]
    groups = tokens // GROUP
    first = groups.bit_length()
    expand = expander(heads, width, 2).astype(bf16)
    for copy in copies:
        copy.wait()
    skip = head_row(heads, width, column_of(skip_ref[...]))
    before = jnp.zeros((heads, 1), f32)
    for group in range(groups):
        at = group_slice(group)
        cum = cum_ref[:, at]
        decay = jnp.exp(cum)
        own_mix = two_parts(mix_ref[0, :, at] * decay)
        span_mixes = [
            (index, two_parts(mix_ref[1 + bit, :, at] * decay))
            for index, (later, bit, _, _) in enumerate(spans)
            if later == group
        ]
        decay = jnp.exp(cum + before)
        before = before + cum[:, GROUP - 1 : GROUP]
        far_mixes = [two_parts(mix_ref[first + level, :, at] * decay) for level in range(levels)]
        for cols in blocks_of(width):
            gate = gate_ref[at, cols].astype(f32)
            swish = gate / (1.0 + jnp.exp(-gate))
            base_ref[at, cols] = skip[:, cols] * inputs_ref[at, cols].astype(f32) * swish
            own_ref[at, cols] = transposed_dot(own_mix, expand[:, cols]) * swish
            for level, mix in enumerate(far_mixes):
                far_ref[level, at, cols] = (transposed_dot(mix, expand[:, cols]) * swish).astype(bf16)
            for index, mix in span_mixes:
                span_refs[0][index, :, cols] = (transposed_dot(mix, expand[:, cols]) * swish).astype(bf16)


def near_kernel(parts, spans, paired, *refs):
    base_ref, own_ref, far_ref, core_ref, scaled_ref = refs[:5]
    count = 5 + parts + parts // 2
    in_refs, out_refs = refs[5 : 5 + parts], refs[5 + parts : count]
    span_refs = refs[count:-2]
    near_ref, turned_ref = refs[-2:]
    tokens, width = base_ref.shape
    in_map = in_map_rows(in_refs)
    turned = jnp.transpose(map_rows([out_refs[0], *out_refs[:0:-1]]))
    turned_ref[...] = turned
    size = in_map.shape[0]
    row = lax.broadcasted_iota(jnp.int32, (GROUP, GROUP), 0)
    col = lax.broadcasted_iota(jnp.int32, (GROUP, GROUP), 1)
    has_core = lax.rem(lax.axis_index("seq"), 2) == 1
    for group in range(tokens // GROUP):
        at = group_slice(group)
        scores = jnp.dot(turned[at], in_map[:, at], preferred_element_type=f32)
        scores = jnp.where(row >= col, scores, 0.0).astype(bf16)
        for cols in blocks_of(width):
            own = jnp.dot(scores, scaled_ref[at, cols], preferred_element_type=f32)
            total = base_ref[at, cols] + own_ref[at, cols] * own
            for index, (later, _, _, _) in enumerate(spans):
                if later == group:
                    rows = slice(index * size, (index + 1) * size)
                    reach = jnp.dot(turned[at], span_refs[0][rows, cols], preferred_element_type=f32)
                    total = total + span_refs[1][index, :, cols].astype(f32) * reach
            if paired:
                reach = jnp.dot(turned[at], core_ref[:size, cols], preferred_element_type=f32)
                reach = jnp.where(has_core, reach, 0.0)
                total = total + far_ref[0, at, cols].astype(f32) * reach
            near_ref[at, cols] = total


def far_body(turned_ref, near_ref, far_ref, gain_ref, start, columns, levels, state_of, gated_ref):
    tokens = far_ref.shape[1]
    squares = jnp.zeros((tokens, 128), f32)
    for cols in blocks_of(columns):
        at = pl.ds(pl.multiple_of(start + cols.start, BLOCK), BLOCK)
        total = near_ref[:, at]
        for level in levels:
            state = state_of(level, cols, at).astype(bf16)
            reach = jnp.dot(turned_ref[...], state, preferred_element_type=f32)
            total = total + far_ref[level, :, at].astype(f32) * reach
        gated_ref[:, cols] = total * gain_ref[:, at]
        total = total * total
        for part in range(0, BLOCK, 128):
            squares = squares + total[:, part : part + 128]
    return squares


def row_sums(squares):
    high = squares.astype(bf16)
    low = (squares - high.astype(f32)).astype(bf16)
    parts = jnp.concatenate([high, low], axis=1)
    ones = jnp.ones((16, parts.shape[1]), bf16)
    return lax.dot_general(ones, parts, (((1,), (1,)), ((), ())), preferred_element_type=f32)[:1]


def far_kernel(turned_ref, near_ref, far_ref, gain_ref, *refs):
    state_refs = refs[:-2]
    gated_ref, sums_ref = refs[-2:]

    def state_of(level, cols, _):
        return state_refs[level][:, cols]

    width = near_ref.shape[1]
    levels = range(far_ref.shape[0])
    squares = far_body(turned_ref, near_ref, far_ref, gain_ref, 0, width, levels, state_of, gated_ref)
    sums_ref[...] = row_sums(squares)


def combine_kernel(size, x_ref, y_ref, diagonal_ref, spans_ref):
    rank = lax.axis_index("seq")
    along_x = lax.rem(lax.div(rank, 2), 2)
    along_y = lax.div(rank, 4)

    def parts_of(ref):
        return ref[:size, :].astype(f32), ref[size:, :].astype(f32)[:1]

    x_state, x_decay = parts_of(x_ref)
    y_state, y_decay = parts_of(y_ref)
    d_state, d_decay = parts_of(diagonal_ref)
    newer = jnp.where(along_x == 1, y_state, d_state)
    newer_decay = jnp.where(along_x == 1, y_decay, d_decay)
    older = jnp.where(along_x == 1, d_state, y_state)
    running = jnp.where(along_x == 1, x_decay, 1.0)
    running = jnp.where(along_y == 1, running, 0.0)
    spans_ref[:size, :] = jnp.where(along_x == 1, x_state, 0.0).astype(bf16)
    spans_ref[size:, :] = ((older * newer_decay + newer) * running).astype(bf16)


def far_kernel_of_half(own, *refs):
    turned_ref, near_ref, far_ref, gain_ref, core_ref, spans_ref = refs[:6]
    gated_ref, sums_ref = refs[-2:]
    size = turned_ref.shape[1]
    core = lax.rem(lax.axis_index("seq"), 2)
    half = spans_ref.shape[1]
    start = (core if own else 1 - core) * half

    def state_of(level, cols, at):
        core_decay = core_ref[size:, at].astype(f32)[:1]
        running = jnp.where(core == 1, core_decay, 1.0)
        return spans_ref[(level - 1) * size : level * size, cols].astype(f32) * running

    squares = far_body(turned_ref, near_ref, far_ref, gain_ref, start, half, (1, 2), state_of, gated_ref)
    sums_ref[...] = squares if own else row_sums(squares + refs[6][...])


def norm_kernel(parts, columns, *refs):
    gated_refs, (out_hbm, out_ref, semaphores) = refs[parts:-3], refs[-3:]
    total = refs[0][...]
    for ref in refs[1:parts]:
        total = total + ref[...]
    scale = lax.rsqrt(total / columns + 1e-05)
    pieces, rest = [], scale
    for _ in range(3):
        pieces.append(rest.astype(bf16).astype(f32))
        rest = rest - pieces[-1]
    tokens = scale.shape[1]
    pieces.append(jnp.zeros((16 - len(pieces), tokens), f32))
    scale = transposed_dot(jnp.concatenate(pieces, axis=0).astype(bf16), jnp.ones((16, 128), bf16))
    width = gated_refs[0].shape[1]
    core = lax.rem(lax.axis_index("seq"), 2)
    sides = (core, 1 - core) if len(gated_refs) == 2 else (0,)
    chunk = tokens // NORM_CHUNKS
    copies = []
    for index in range(NORM_CHUNKS):
        rows = slice(index * chunk, (index + 1) * chunk)
        for ref, side in zip(gated_refs, sides):
            for col in range(0, width, 128):
                at = pl.ds(pl.multiple_of(side * width + col, 128), 128)
                out_ref[rows, at] = (ref[rows, col : col + 128] * scale[rows]).astype(bf16)
        copies.append(pltpu.make_async_copy(out_ref.at[rows], out_hbm.at[rows], semaphores.at[index]))
        copies[-1].start()
    for copy in copies:
        copy.wait()


def call(kernel, out_shape, args, flops=0, bytes_accessed=0, hbm=0, scratch=None, out_space=pltpu.VMEM):
    specs = [pl.BlockSpec(memory_space=pl.ANY)] * hbm + [pl.BlockSpec(memory_space=pltpu.VMEM)] * (len(args) - hbm)
    args = [pltpu.with_memory_space_constraint(arg, pltpu.HBM) for arg in args[:hbm]] + list(args[hbm:])
    if scratch is None:
        scratch = [pltpu.VMEM(arg.shape, arg.dtype) for arg in args[:hbm]]
        scratch += [pltpu.SemaphoreType.DMA((hbm,))] if hbm else []
    return pl.pallas_call(
        kernel,
        out_shape=out_shape,
        in_specs=specs,
        out_specs=jax.tree.map(lambda _: pl.BlockSpec(memory_space=out_space), out_shape),
        scratch_shapes=scratch,
        compiler_params=pltpu.CompilerParams(vmem_limit_bytes=VMEM_LIMIT),
        cost_estimate=pl.CostEstimate(flops=flops, bytes_accessed=bytes_accessed, transcendentals=0),
    )(*args)


def shaped(shape, dtype):
    return jax.ShapeDtypeStruct(shape, dtype)


def flip(array, axis, mask):
    return lax.ppermute(array, axis, [(i, i ^ mask) for i in range(lax.axis_size(axis))])


def from_each(array, axis, first=1, stride=1):
    masks = range(first, lax.axis_size(axis), stride)
    return [flip(array, axis, mask) for mask in reversed(masks)]


def merged(older, newer, size):
    older, newer = older.astype(f32), newer.astype(f32)
    decay = newer[size : size + 1]
    return jnp.concatenate([older[:size] * decay + newer[:size], older[size:] * decay], axis=0).astype(bf16)


def far_states(shard, size):
    rank = lax.axis_index("seq")
    levels = lax.axis_size("seq").bit_length() - 1
    states = []
    running = jnp.ones((1, shard.shape[1]), f32)
    for level in range(levels):
        theirs = flip(shard, "seq", 1 << level)
        upper = jnp.right_shift(rank, level) % 2 == 1
        states.append(jnp.where(upper, theirs[:size].astype(f32) * running, 0.0).astype(bf16))
        running = jnp.where(upper, running * theirs[size : size + 1].astype(f32), running)
        shard = merged(jnp.where(upper, theirs, shard), jnp.where(upper, shard, theirs), size)
    return states


def on_device(inputs, gate, input_map, output_map, step, decay_rate, level_mix, skip, norm_gain):
    tokens, width = inputs.shape
    heads = step.shape[0]
    parts = lax.axis_size("head")
    levels = lax.axis_size("seq").bit_length() - 1
    size = input_map.shape[0] * parts
    groups = tokens // GROUP
    spans = local_spans(groups)
    dense = 2 * tokens * GROUP * width
    area = tokens * width
    others = from_each(input_map, "head", first=2)
    rows = input_map.shape[0]
    if rows % 16 == 0:
        maps = call(
            pack_kernel,
            shaped((2 * rows, tokens), bf16),
            (input_map, output_map),
            bytes_accessed=4 * rows * tokens,
            hbm=2,
            scratch=[pltpu.SemaphoreType.DMA((2,))],
        )
    else:
        maps = jnp.concatenate([input_map, output_map], axis=0)
    near_maps = flip(maps, "head", 1)
    in_maps = [maps, near_maps, *others]
    scaled, cum = call(
        prepare_kernel,
        (shaped((tokens, width), bf16), shaped((heads, tokens), f32)),
        (inputs, step, decay_rate[None, :]),
        flops=16 * dense,
        bytes_accessed=4 * area,
        hbm=3,
    )
    shard_shape = shaped((size + DECAY_ROWS, width), bf16)
    span_shape = [shaped((len(spans) * size, width), bf16)] if spans else []
    shard, *span_states = call(
        functools.partial(states_kernel, parts),
        (shard_shape, *span_shape),
        (*in_maps, scaled, cum),
        flops=dense,
        bytes_accessed=4 * area,
    )
    pairs = lax.axis_size("seq") == 8 and parts == 4
    if pairs:
        theirs = flip(shard, "seq", 1)
        message = call(
            functools.partial(merge_kernel, size),
            shaped((size + DECAY_ROWS, width // 2), bf16),
            (shard, theirs),
            bytes_accessed=area,
        )
    else:
        message = shard
    if rows % 16 == 0:
        both = call(
            join_kernel, shaped((2 * rows, tokens), bf16), (maps, near_maps, shard), bytes_accessed=8 * rows * tokens
        )
    else:
        both = jnp.concatenate([maps[rows:], near_maps[rows:]], axis=0)
    out_maps = [both, *from_each(both, "head", first=2, stride=2)]
    factor_shape = [shaped((len(spans), GROUP, width), bf16)] if spans else []
    base, own_factor, far, *span_factors = call(
        functools.partial(factor_kernel, spans, levels),
        (
            *(shaped((tokens, width), f32), shaped((tokens, width), f32)),
            *(shaped((levels, tokens, width), bf16), *factor_shape),
        ),
        (inputs, gate, level_mix, skip[None, :], cum, message),
        flops=8 * dense,
        bytes_accessed=16 * area,
        hbm=4,
    )
    near, turned = call(
        functools.partial(near_kernel, parts, spans, pairs),
        (shaped((tokens, width), f32), shaped((tokens, size), bf16)),
        (
            *(base, own_factor, far, theirs if pairs else message, scaled),
            *(*in_maps, *out_maps, *span_states, *span_factors),
        ),
        flops=4 * dense,
        bytes_accessed=16 * area,
    )
    gain = norm_gain[None, :]
    sums_shape = shaped((1, tokens), f32)
    if pairs:
        received = [flip(message, "seq", mask) for mask in (6, 4, 2)]
        *received, near, far = lax.optimization_barrier((*received, near, far))
        own = call(
            functools.partial(combine_kernel, size),
            shaped((2 * size, width // 2), bf16),
            received[::-1],
            bytes_accessed=area,
        )
        other = flip(own, "seq", 1)
        gated_shape = shaped((tokens, width // 2), f32)
        own_gated, own_squares = call(
            functools.partial(far_kernel_of_half, True),
            (gated_shape, shaped((tokens, 128), f32)),
            (turned, near, far, gain, theirs, own),
            flops=2 * dense,
            bytes_accessed=6 * area,
        )
        other_gated, sums = call(
            functools.partial(far_kernel_of_half, False),
            (gated_shape, sums_shape),
            (turned, near, far, gain, theirs, other, own_squares),
            flops=2 * dense,
            bytes_accessed=6 * area,
        )
        gated = (own_gated, other_gated)
    else:
        *gated, sums = call(
            far_kernel,
            (shaped((tokens, width), f32), sums_shape),
            (turned, near, far, gain, *far_states(shard, size)),
            flops=4 * dense,
            bytes_accessed=12 * area,
        )
    *last, nearest = [sums, *from_each(sums, "head")]
    last = [nearest, *last]
    return call(
        functools.partial(norm_kernel, len(last), width * parts),
        shaped((tokens, width), bf16),
        (*last, *gated),
        flops=dense,
        bytes_accessed=6 * area,
        scratch=[pltpu.VMEM((tokens, width), bf16), pltpu.SemaphoreType.DMA((NORM_CHUNKS,))],
        out_space=pl.ANY,
    )


def solution(mesh):
    return jax.shard_map(
        on_device,
        mesh=mesh,
        in_specs=(
            P("seq", "head"),
            P("seq", "head"),
            P("head", "seq"),
            P("head", "seq"),
            P("head", "seq"),
            P("head"),
            P(None, "head", "seq"),
            P("head"),
            P("head"),
        ),
        out_specs=P("seq", "head"),
        check_vma=False,
    )
```

```python
import functools

import jax
import jax.numpy as jnp
from jax import lax
from jax.experimental import pallas as pl
from jax.experimental.pallas import tpu as pltpu
from jax.sharding import PartitionSpec as P

P_SIZE = 64
GROUP = 256
DECAY_ROWS = 16
BLOCK = 256
NORM_CHUNKS = 8
VMEM_LIMIT = 40 * 1024 * 1024

f32, bf16 = jnp.float32, jnp.bfloat16
HIGHEST = lax.Precision.HIGHEST
TRANSPOSED = (((0,), (0,)), ((), ()))


def expander(heads, width, copies):
    row = lax.broadcasted_iota(jnp.int32, (copies * heads, width), 0)
    col = lax.broadcasted_iota(jnp.int32, (copies * heads, width), 1)
    return jnp.where(lax.rem(row, heads) == lax.div(col, P_SIZE), 1.0, 0.0)


def two_parts(factor):
    high = factor.astype(bf16).astype(f32)
    return jnp.concatenate([high, factor - high], axis=0).astype(bf16)


def transposed_dot(left, right):
    return lax.dot_general(left, right, TRANSPOSED, preferred_element_type=f32)


def head_row(heads, width, column):
    return jnp.sum(expander(heads, width, 1) * column, axis=0, keepdims=True)


def group_slice(group):
    return slice(group * GROUP, (group + 1) * GROUP)


def blocks_of(width):
    return [slice(at, at + BLOCK) for at in range(0, width, BLOCK)]


def local_spans(groups):
    spans = []
    for later in range(groups):
        for bit in range(groups.bit_length() - 1):
            if later >> bit & 1:
                start = later >> bit + 1 << bit + 1
                spans.append((later, bit, start, start + 2**bit))
    return spans


def column_of(row):
    size = row.shape[1]
    at = lax.broadcasted_iota(jnp.int32, (size, size), 0) == lax.broadcasted_iota(jnp.int32, (size, size), 1)
    return jnp.sum(jnp.where(at, row, 0.0), axis=1, keepdims=True)


def map_rows(maps):
    if all(rows.shape[0] % 16 == 0 for rows in maps):
        return jnp.concatenate([rows[...] for rows in maps], axis=0)
    return jnp.concatenate([rows[...].astype(f32) for rows in maps], axis=0).astype(bf16)


def out_map_rows(map_refs):
    rows = map_refs[0].shape[0] // 2
    if rows % 16 == 0:
        return map_rows([map_refs[0].at[:rows], *map_refs[1:], map_refs[0].at[rows:]])
    pair = map_refs[0][...].astype(f32)
    return map_rows([pair[:rows], *map_refs[1:], pair[rows:]])


def fetch(sources, targets, semaphores):
    copies = [
        pltpu.make_async_copy(source, target, semaphores.at[index])
        for index, (source, target) in enumerate(zip(sources, targets))
    ]
    for copy in copies:
        copy.start()
    return copies


def prepare_kernel(*refs):
    sources, (scaled_ref, cum_ref), kept_refs = refs[:8], refs[8:10], refs[10:16]
    step_ref, rate_ref, semaphores = refs[16:]
    inputs_ref = kept_refs[0]
    copies = fetch(sources, (step_ref, rate_ref, *kept_refs), semaphores)
    heads, tokens = step_ref.shape
    width = inputs_ref.shape[1]
    row = lax.broadcasted_iota(jnp.int32, (GROUP, GROUP), 0)
    col = lax.broadcasted_iota(jnp.int32, (GROUP, GROUP), 1)
    until = jnp.where(row <= col, 1.0, 0.0)
    expand = expander(heads, width, 2).astype(bf16)
    copies[0].wait()
    copies[1].wait()
    step = step_ref[...]
    log_decay = -step * column_of(rate_ref[...])
    factors = []
    for group in range(tokens // GROUP):
        at = group_slice(group)
        cum = jnp.dot(log_decay[:, at], until, precision=HIGHEST, preferred_element_type=f32)
        cum_ref[:, at] = cum
        factors.append(two_parts(jnp.exp(-cum) * step[:, at]))
    factor = jnp.concatenate(factors, axis=1)
    copies[2].wait()
    for cols in blocks_of(width):
        scale = transposed_dot(factor, expand[:, cols])
        scaled_ref[:, cols] = (inputs_ref[:, cols].astype(f32) * scale).astype(bf16)
    for copy in copies[3:]:
        copy.wait()


def join_kernel(mine_ref, theirs_ref, _, both_ref):
    rows = mine_ref.shape[0]
    both_ref[:rows, :] = mine_ref[...]
    both_ref[rows:, :] = theirs_ref[...]


def states_kernel(parts, *refs):
    map_refs, (scaled_ref, cum_ref), out_refs = refs[:parts], refs[parts : parts + 2], refs[parts + 3 :]
    shard_ref = out_refs[0]
    heads, tokens = cum_ref.shape
    width = scaled_ref.shape[1]
    in_map = map_rows(map_refs)
    size = in_map.shape[0]
    cum = cum_ref[...]
    states, decays = [], []
    for group in range(tokens // GROUP):
        at = group_slice(group)
        decay = head_row(heads, width, jnp.exp(cum[:, at.stop - 1 : at.stop]))
        raw = jnp.dot(in_map[:, at], scaled_ref[at, :], preferred_element_type=f32)
        states.append(raw * decay)
        decays.append(decay)
    total, decay = states[0], decays[0]
    for group in range(1, len(states)):
        total = total * decays[group] + states[group]
        decay = decay * decays[group]
    shard_ref[:size, :] = total.astype(bf16)
    shard_ref[size:, :] = jnp.broadcast_to(decay, (DECAY_ROWS, width)).astype(bf16)
    for index, (later, _, start, stop) in enumerate(local_spans(len(states))):
        span = states[start]
        for group in range(start + 1, later):
            span = span * decays[group]
            if group < stop:
                span = span + states[group]
        out_refs[1][index * size : (index + 1) * size, :] = span.astype(bf16)


def merge_kernel(size, mine_ref, theirs_ref, pair_ref):
    core = lax.rem(lax.axis_index("seq"), 2)
    half = pair_ref.shape[1]
    mine = jnp.where(core == 1, mine_ref[:, half:], mine_ref[:, :half])
    theirs = jnp.where(core == 1, theirs_ref[:, half:], theirs_ref[:, :half])
    older = jnp.where(core == 1, theirs, mine).astype(f32)
    newer = jnp.where(core == 1, mine, theirs).astype(f32)
    decay = newer[size : size + 1]
    pair_ref[:size, :] = (older[:size] * decay + newer[:size]).astype(bf16)
    pair_ref[size:, :] = (older[size:] * decay).astype(bf16)


def factor_kernel(spans, levels, *refs):
    inputs_ref, gate_ref, mix_ref, skip_ref, cum_ref, _ = refs[:6]
    base_ref, own_ref, far_ref = refs[6:9]
    span_refs = refs[9:]
    heads, tokens = cum_ref.shape
    width = inputs_ref.shape[1]
    groups = tokens // GROUP
    first = groups.bit_length()
    expand = expander(heads, width, 2).astype(bf16)
    skip = head_row(heads, width, column_of(skip_ref[...]))
    before = jnp.zeros((heads, 1), f32)
    for group in range(groups):
        at = group_slice(group)
        cum = cum_ref[:, at]
        decay = jnp.exp(cum)
        own_mix = two_parts(mix_ref[0, :, at] * decay)
        span_mixes = [
            (index, two_parts(mix_ref[1 + bit, :, at] * decay))
            for index, (later, bit, _, _) in enumerate(spans)
            if later == group
        ]
        decay = jnp.exp(cum + before)
        before = before + cum[:, GROUP - 1 : GROUP]
        far_mixes = [two_parts(mix_ref[first + level, :, at] * decay) for level in range(levels)]
        for cols in blocks_of(width):
            gate = gate_ref[at, cols].astype(f32)
            swish = gate / (1.0 + jnp.exp(-gate))
            base_ref[at, cols] = skip[:, cols] * inputs_ref[at, cols].astype(f32) * swish
            own_ref[at, cols] = transposed_dot(own_mix, expand[:, cols]) * swish
            for level, mix in enumerate(far_mixes):
                far_ref[level, at, cols] = (transposed_dot(mix, expand[:, cols]) * swish).astype(bf16)
            for index, mix in span_mixes:
                span_refs[0][index, :, cols] = (transposed_dot(mix, expand[:, cols]) * swish).astype(bf16)


def near_kernel(parts, spans, paired, *refs):
    base_ref, own_ref, far_ref, core_ref, scaled_ref = refs[:5]
    count = 5 + parts + parts // 2
    in_refs, out_refs = refs[5 : 5 + parts], refs[5 + parts : count]
    span_refs = refs[count:-2]
    near_ref, turned_ref = refs[-2:]
    tokens, width = base_ref.shape
    in_map = map_rows(in_refs)
    turned = jnp.transpose(out_map_rows(out_refs))
    turned_ref[...] = turned
    size = in_map.shape[0]
    row = lax.broadcasted_iota(jnp.int32, (GROUP, GROUP), 0)
    col = lax.broadcasted_iota(jnp.int32, (GROUP, GROUP), 1)
    has_core = lax.rem(lax.axis_index("seq"), 2) == 1
    for group in range(tokens // GROUP):
        at = group_slice(group)
        scores = jnp.dot(turned[at], in_map[:, at], preferred_element_type=f32)
        scores = jnp.where(row >= col, scores, 0.0).astype(bf16)
        for cols in blocks_of(width):
            own = jnp.dot(scores, scaled_ref[at, cols], preferred_element_type=f32)
            total = base_ref[at, cols] + own_ref[at, cols] * own
            for index, (later, _, _, _) in enumerate(spans):
                if later == group:
                    rows = slice(index * size, (index + 1) * size)
                    reach = jnp.dot(turned[at], span_refs[0][rows, cols], preferred_element_type=f32)
                    total = total + span_refs[1][index, :, cols].astype(f32) * reach
            if paired:
                reach = jnp.dot(turned[at], core_ref[:size, cols], preferred_element_type=f32)
                reach = jnp.where(has_core, reach, 0.0)
                total = total + far_ref[0, at, cols].astype(f32) * reach
            near_ref[at, cols] = total


def far_body(turned_ref, near_ref, far_ref, gain_ref, start, columns, levels, state_of, gated_ref):
    tokens = far_ref.shape[1]
    squares = jnp.zeros((tokens, 128), f32)
    for cols in blocks_of(columns):
        at = pl.ds(pl.multiple_of(start + cols.start, BLOCK), BLOCK)
        total = near_ref[:, at]
        for level in levels:
            state = state_of(level, cols, at).astype(bf16)
            reach = jnp.dot(turned_ref[...], state, preferred_element_type=f32)
            total = total + far_ref[level, :, at].astype(f32) * reach
        gated_ref[:, cols] = total * gain_ref[:, at]
        total = total * total
        for part in range(0, BLOCK, 128):
            squares = squares + total[:, part : part + 128]
    return squares


def row_sums(squares):
    high = squares.astype(bf16)
    low = (squares - high.astype(f32)).astype(bf16)
    parts = jnp.concatenate([high, low], axis=1)
    ones = jnp.ones((16, parts.shape[1]), bf16)
    return lax.dot_general(ones, parts, (((1,), (1,)), ((), ())), preferred_element_type=f32)[:1]


def far_kernel(turned_ref, near_ref, far_ref, gain_ref, *refs):
    state_refs = refs[:-2]
    gated_ref, sums_ref = refs[-2:]

    def state_of(level, cols, _):
        return state_refs[level][:, cols]

    width = near_ref.shape[1]
    levels = range(far_ref.shape[0])
    squares = far_body(turned_ref, near_ref, far_ref, gain_ref, 0, width, levels, state_of, gated_ref)
    sums_ref[...] = row_sums(squares)


def combine_kernel(size, x_ref, y_ref, diagonal_ref, spans_ref):
    rank = lax.axis_index("seq")
    along_x = lax.rem(lax.div(rank, 2), 2)
    along_y = lax.div(rank, 4)

    def parts_of(ref):
        return ref[:size, :].astype(f32), ref[size:, :].astype(f32)[:1]

    x_state, x_decay = parts_of(x_ref)
    y_state, y_decay = parts_of(y_ref)
    d_state, d_decay = parts_of(diagonal_ref)
    newer = jnp.where(along_x == 1, y_state, d_state)
    newer_decay = jnp.where(along_x == 1, y_decay, d_decay)
    older = jnp.where(along_x == 1, d_state, y_state)
    running = jnp.where(along_x == 1, x_decay, 1.0)
    running = jnp.where(along_y == 1, running, 0.0)
    spans_ref[:size, :] = jnp.where(along_x == 1, x_state, 0.0).astype(bf16)
    spans_ref[size:, :] = ((older * newer_decay + newer) * running).astype(bf16)


def far_kernel_of_half(own, *refs):
    turned_ref, near_ref, far_ref, gain_ref, core_ref, spans_ref = refs[:6]
    gated_ref, sums_ref = refs[-2:]
    size = turned_ref.shape[1]
    core = lax.rem(lax.axis_index("seq"), 2)
    half = spans_ref.shape[1]
    start = (core if own else 1 - core) * half

    def state_of(level, cols, at):
        core_decay = core_ref[size:, at].astype(f32)[:1]
        running = jnp.where(core == 1, core_decay, 1.0)
        return spans_ref[(level - 1) * size : level * size, cols].astype(f32) * running

    squares = far_body(turned_ref, near_ref, far_ref, gain_ref, start, half, (1, 2), state_of, gated_ref)
    sums_ref[...] = squares if own else row_sums(squares + refs[6][...])


def norm_kernel(parts, columns, *refs):
    gated_refs, (out_hbm, out_ref, semaphores) = refs[parts:-3], refs[-3:]
    total = refs[0][...]
    for ref in refs[1:parts]:
        total = total + ref[...]
    scale = lax.rsqrt(total / columns + 1e-05)
    pieces, rest = [], scale
    for _ in range(3):
        pieces.append(rest.astype(bf16).astype(f32))
        rest = rest - pieces[-1]
    tokens = scale.shape[1]
    pieces.append(jnp.zeros((16 - len(pieces), tokens), f32))
    scale = transposed_dot(jnp.concatenate(pieces, axis=0).astype(bf16), jnp.ones((16, 128), bf16))
    width = gated_refs[0].shape[1]
    core = lax.rem(lax.axis_index("seq"), 2)
    sides = (core, 1 - core) if len(gated_refs) == 2 else (0,)
    chunk = tokens // NORM_CHUNKS
    copies = []
    for index in range(NORM_CHUNKS):
        rows = slice(index * chunk, (index + 1) * chunk)
        for ref, side in zip(gated_refs, sides):
            for col in range(0, width, 128):
                at = pl.ds(pl.multiple_of(side * width + col, 128), 128)
                out_ref[rows, at] = (ref[rows, col : col + 128] * scale[rows]).astype(bf16)
        copies.append(pltpu.make_async_copy(out_ref.at[rows], out_hbm.at[rows], semaphores.at[index]))
        copies[-1].start()
    for copy in copies:
        copy.wait()


def call(kernel, out_shape, args, flops=0, bytes_accessed=0, hbm=0, scratch=None, out_space=pltpu.VMEM):
    specs = [pl.BlockSpec(memory_space=pl.ANY)] * hbm + [pl.BlockSpec(memory_space=pltpu.VMEM)] * (len(args) - hbm)
    args = [pltpu.with_memory_space_constraint(arg, pltpu.HBM) for arg in args[:hbm]] + list(args[hbm:])
    if scratch is None:
        scratch = [pltpu.VMEM(arg.shape, arg.dtype) for arg in args[:hbm]]
        scratch += [pltpu.SemaphoreType.DMA((hbm,))] if hbm else []
    return pl.pallas_call(
        kernel,
        out_shape=out_shape,
        in_specs=specs,
        out_specs=jax.tree.map(lambda _: pl.BlockSpec(memory_space=out_space), out_shape),
        scratch_shapes=scratch,
        compiler_params=pltpu.CompilerParams(vmem_limit_bytes=VMEM_LIMIT),
        cost_estimate=pl.CostEstimate(flops=flops, bytes_accessed=bytes_accessed, transcendentals=0),
    )(*args)


def shaped(shape, dtype):
    return jax.ShapeDtypeStruct(shape, dtype)


def flip(array, axis, mask):
    return lax.ppermute(array, axis, [(i, i ^ mask) for i in range(lax.axis_size(axis))])


def from_each(array, axis, first=1, stride=1):
    masks = sorted(range(first, lax.axis_size(axis), stride), key=lambda mask: (mask == 1, mask))
    return [flip(array, axis, mask) for mask in masks]


def merged(older, newer, size):
    older, newer = older.astype(f32), newer.astype(f32)
    decay = newer[size : size + 1]
    return jnp.concatenate([older[:size] * decay + newer[:size], older[size:] * decay], axis=0).astype(bf16)


def far_states(shard, size):
    rank = lax.axis_index("seq")
    levels = lax.axis_size("seq").bit_length() - 1
    states = []
    running = jnp.ones((1, shard.shape[1]), f32)
    for level in range(levels):
        theirs = flip(shard, "seq", 1 << level)
        upper = jnp.right_shift(rank, level) % 2 == 1
        states.append(jnp.where(upper, theirs[:size].astype(f32) * running, 0.0).astype(bf16))
        running = jnp.where(upper, running * theirs[size : size + 1].astype(f32), running)
        shard = merged(jnp.where(upper, theirs, shard), jnp.where(upper, shard, theirs), size)
    return states


def on_device(inputs, gate, input_map, output_map, step, decay_rate, level_mix, skip, norm_gain):
    tokens, width = inputs.shape
    heads = step.shape[0]
    parts = lax.axis_size("head")
    levels = lax.axis_size("seq").bit_length() - 1
    size = input_map.shape[0] * parts
    groups = tokens // GROUP
    spans = local_spans(groups)
    dense = 2 * tokens * GROUP * width
    area = tokens * width
    others = from_each(input_map, "head")
    beside = flip(output_map, "head", 1)
    kept = inputs, gate, level_mix, skip[None, :], input_map, output_map
    scaled, cum, *kept = call(
        prepare_kernel,
        (
            *(shaped((tokens, width), bf16), shaped((heads, tokens), f32)),
            *(shaped(array.shape, array.dtype) for array in kept),
        ),
        (step, decay_rate[None, :], *kept),
        flops=16 * dense,
        bytes_accessed=4 * area,
        hbm=8,
        scratch=[pltpu.VMEM(step.shape, f32), pltpu.VMEM((1, heads), f32), pltpu.SemaphoreType.DMA((8,))],
    )
    inputs, gate, level_mix, skip, input_map, output_map = kept
    in_maps = [input_map, *others]
    shard_shape = shaped((size + DECAY_ROWS, width), bf16)
    span_shape = [shaped((len(spans) * size, width), bf16)] if spans else []
    shard, *span_states = call(
        functools.partial(states_kernel, parts),
        (shard_shape, *span_shape),
        (*in_maps, scaled, cum, beside),
        flops=dense,
        bytes_accessed=4 * area,
    )
    pairs = lax.axis_size("seq") == 8 and parts == 4
    if pairs:
        theirs = flip(shard, "seq", 1)
        message = call(
            functools.partial(merge_kernel, size),
            shaped((size + DECAY_ROWS, width // 2), bf16),
            (shard, theirs),
            bytes_accessed=area,
        )
    else:
        message = shard
    rows = output_map.shape[0]
    if rows % 16 == 0:
        both = call(
            join_kernel,
            shaped((2 * rows, tokens), bf16),
            (output_map, beside, shard),
            bytes_accessed=8 * rows * tokens,
        )
    else:
        both = jnp.concatenate([output_map, beside], axis=0)
    out_maps = [both, *from_each(both, "head", first=2, stride=2)]
    factor_shape = [shaped((len(spans), GROUP, width), bf16)] if spans else []
    base, own_factor, far, *span_factors = call(
        functools.partial(factor_kernel, spans, levels),
        (
            *(shaped((tokens, width), f32), shaped((tokens, width), f32)),
            *(shaped((levels, tokens, width), bf16), *factor_shape),
        ),
        (inputs, gate, level_mix, skip, cum, message),
        flops=8 * dense,
        bytes_accessed=16 * area,
    )
    near, turned = call(
        functools.partial(near_kernel, parts, spans, pairs),
        (shaped((tokens, width), f32), shaped((tokens, size), bf16)),
        (
            *(base, own_factor, far, theirs if pairs else message, scaled),
            *(*in_maps, *out_maps, *span_states, *span_factors),
        ),
        flops=4 * dense,
        bytes_accessed=16 * area,
    )
    gain = norm_gain[None, :]
    sums_shape = shaped((1, tokens), f32)
    if pairs:
        received = [flip(message, "seq", mask) for mask in (6, 4, 2)]
        *received, near, far = lax.optimization_barrier((*received, near, far))
        own = call(
            functools.partial(combine_kernel, size),
            shaped((2 * size, width // 2), bf16),
            received[::-1],
            bytes_accessed=area,
        )
        other = flip(own, "seq", 1)
        gated_shape = shaped((tokens, width // 2), f32)
        own_gated, own_squares = call(
            functools.partial(far_kernel_of_half, True),
            (gated_shape, shaped((tokens, 128), f32)),
            (turned, near, far, gain, theirs, own),
            flops=2 * dense,
            bytes_accessed=6 * area,
        )
        other_gated, sums = call(
            functools.partial(far_kernel_of_half, False),
            (gated_shape, sums_shape),
            (turned, near, far, gain, theirs, other, own_squares),
            flops=2 * dense,
            bytes_accessed=6 * area,
        )
        gated = (own_gated, other_gated)
    else:
        *gated, sums = call(
            far_kernel,
            (shaped((tokens, width), f32), sums_shape),
            (turned, near, far, gain, *far_states(shard, size)),
            flops=4 * dense,
            bytes_accessed=12 * area,
        )
    last = [sums, *from_each(sums, "head")]
    return call(
        functools.partial(norm_kernel, len(last), width * parts),
        shaped((tokens, width), bf16),
        (*last, *gated),
        flops=dense,
        bytes_accessed=6 * area,
        scratch=[pltpu.VMEM((tokens, width), bf16), pltpu.SemaphoreType.DMA((NORM_CHUNKS,))],
        out_space=pl.ANY,
    )


def solution(mesh):
    return jax.shard_map(
        on_device,
        mesh=mesh,
        in_specs=(
            P("seq", "head"),
            P("seq", "head"),
            P("head", "seq"),
            P("head", "seq"),
            P("head", "seq"),
            P("head"),
            P(None, "head", "seq"),
            P("head"),
            P("head"),
        ),
        out_specs=P("seq", "head"),
        check_vma=False,
    )
```

```python
import functools

import jax
import jax.numpy as jnp
from jax import lax
from jax.experimental import pallas as pl
from jax.experimental.pallas import tpu as pltpu
from jax.sharding import PartitionSpec as P

P_SIZE = 64
GROUP = 256
DECAY_ROWS = 16
BLOCK = 256
NORM_CHUNKS = 8
VMEM_LIMIT = 40 * 1024 * 1024

f32, bf16 = jnp.float32, jnp.bfloat16
HIGHEST = lax.Precision.HIGHEST
TRANSPOSED = (((0,), (0,)), ((), ()))


def expander(heads, width, copies):
    row = lax.broadcasted_iota(jnp.int32, (copies * heads, width), 0)
    col = lax.broadcasted_iota(jnp.int32, (copies * heads, width), 1)
    return jnp.where(lax.rem(row, heads) == lax.div(col, P_SIZE), 1.0, 0.0)


def two_parts(factor):
    high = factor.astype(bf16).astype(f32)
    return jnp.concatenate([high, factor - high], axis=0).astype(bf16)


def transposed_dot(left, right):
    return lax.dot_general(left, right, TRANSPOSED, preferred_element_type=f32)


def head_row(heads, width, column):
    return jnp.sum(expander(heads, width, 1) * column, axis=0, keepdims=True)


def group_slice(group):
    return slice(group * GROUP, (group + 1) * GROUP)


def blocks_of(width):
    return [slice(at, at + BLOCK) for at in range(0, width, BLOCK)]


def local_spans(groups):
    spans = []
    for later in range(groups):
        for bit in range(groups.bit_length() - 1):
            if later >> bit & 1:
                start = later >> bit + 1 << bit + 1
                spans.append((later, bit, start, start + 2**bit))
    return spans


def column_of(row):
    size = row.shape[1]
    at = lax.broadcasted_iota(jnp.int32, (size, size), 0) == lax.broadcasted_iota(jnp.int32, (size, size), 1)
    return jnp.sum(jnp.where(at, row, 0.0), axis=1, keepdims=True)


def map_rows(maps):
    if all(rows.shape[0] % 16 == 0 for rows in maps):
        return jnp.concatenate([rows[...] for rows in maps], axis=0)
    return jnp.concatenate([rows[...].astype(f32) for rows in maps], axis=0).astype(bf16)


def out_map_rows(map_refs):
    rows = map_refs[0].shape[0] // 2
    if rows % 16 == 0:
        return map_rows([map_refs[0].at[:rows], *map_refs[1:], map_refs[0].at[rows:]])
    pair = map_refs[0][...].astype(f32)
    return map_rows([pair[:rows], *map_refs[1:], pair[rows:]])


def fetch(sources, targets, semaphores):
    copies = [
        pltpu.make_async_copy(source, target, semaphores.at[index])
        for index, (source, target) in enumerate(zip(sources, targets))
    ]
    for copy in copies:
        copy.start()
    return copies


def prepare_kernel(*refs):
    sources, (scaled_ref, cum_ref), kept_refs = refs[:8], refs[8:10], refs[10:16]
    step_ref, rate_ref, semaphores = refs[16:]
    inputs_ref = kept_refs[0]
    copies = fetch(sources, (step_ref, rate_ref, *kept_refs), semaphores)
    heads, tokens = step_ref.shape
    width = inputs_ref.shape[1]
    row = lax.broadcasted_iota(jnp.int32, (GROUP, GROUP), 0)
    col = lax.broadcasted_iota(jnp.int32, (GROUP, GROUP), 1)
    until = jnp.where(row <= col, 1.0, 0.0)
    expand = expander(heads, width, 2).astype(bf16)
    copies[0].wait()
    copies[1].wait()
    step = step_ref[...]
    log_decay = -step * column_of(rate_ref[...])
    factors = []
    for group in range(tokens // GROUP):
        at = group_slice(group)
        cum = jnp.dot(log_decay[:, at], until, precision=HIGHEST, preferred_element_type=f32)
        cum_ref[:, at] = cum
        factors.append(two_parts(jnp.exp(-cum) * step[:, at]))
    factor = jnp.concatenate(factors, axis=1)
    copies[2].wait()
    for cols in blocks_of(width):
        scale = transposed_dot(factor, expand[:, cols])
        scaled_ref[:, cols] = (inputs_ref[:, cols].astype(f32) * scale).astype(bf16)
    for copy in copies[3:]:
        copy.wait()


def join_kernel(mine_ref, theirs_ref, both_ref):
    rows = mine_ref.shape[0]
    both_ref[:rows, :] = mine_ref[...]
    both_ref[rows:, :] = theirs_ref[...]


def states_kernel(parts, *refs):
    map_refs, (scaled_ref, cum_ref), out_refs = refs[:parts], refs[parts : parts + 2], refs[parts + 2 :]
    shard_ref = out_refs[0]
    heads, tokens = cum_ref.shape
    width = scaled_ref.shape[1]
    in_map = map_rows(map_refs)
    size = in_map.shape[0]
    cum = cum_ref[...]
    states, decays = [], []
    for group in range(tokens // GROUP):
        at = group_slice(group)
        decay = head_row(heads, width, jnp.exp(cum[:, at.stop - 1 : at.stop]))
        raw = jnp.dot(in_map[:, at], scaled_ref[at, :], preferred_element_type=f32)
        states.append(raw * decay)
        decays.append(decay)
    total, decay = states[0], decays[0]
    for group in range(1, len(states)):
        total = total * decays[group] + states[group]
        decay = decay * decays[group]
    shard_ref[:size, :] = total.astype(bf16)
    shard_ref[size:, :] = jnp.broadcast_to(decay, (DECAY_ROWS, width)).astype(bf16)
    for index, (later, _, start, stop) in enumerate(local_spans(len(states))):
        span = states[start]
        for group in range(start + 1, later):
            span = span * decays[group]
            if group < stop:
                span = span + states[group]
        out_refs[1][index * size : (index + 1) * size, :] = span.astype(bf16)


def merge_kernel(size, mine_ref, theirs_ref, pair_ref):
    core = lax.rem(lax.axis_index("seq"), 2)
    half = pair_ref.shape[1]
    mine = jnp.where(core == 1, mine_ref[:, half:], mine_ref[:, :half])
    theirs = jnp.where(core == 1, theirs_ref[:, half:], theirs_ref[:, :half])
    older = jnp.where(core == 1, theirs, mine).astype(f32)
    newer = jnp.where(core == 1, mine, theirs).astype(f32)
    decay = newer[size : size + 1]
    pair_ref[:size, :] = (older[:size] * decay + newer[:size]).astype(bf16)
    pair_ref[size:, :] = (older[size:] * decay).astype(bf16)


def factor_kernel(spans, levels, *refs):
    inputs_ref, gate_ref, mix_ref, skip_ref, cum_ref, _ = refs[:6]
    base_ref, own_ref, far_ref = refs[6:9]
    span_refs = refs[9:]
    heads, tokens = cum_ref.shape
    width = inputs_ref.shape[1]
    groups = tokens // GROUP
    first = groups.bit_length()
    expand = expander(heads, width, 2).astype(bf16)
    skip = head_row(heads, width, column_of(skip_ref[...]))
    before = jnp.zeros((heads, 1), f32)
    for group in range(groups):
        at = group_slice(group)
        cum = cum_ref[:, at]
        decay = jnp.exp(cum)
        own_mix = two_parts(mix_ref[0, :, at] * decay)
        span_mixes = [
            (index, two_parts(mix_ref[1 + bit, :, at] * decay))
            for index, (later, bit, _, _) in enumerate(spans)
            if later == group
        ]
        decay = jnp.exp(cum + before)
        before = before + cum[:, GROUP - 1 : GROUP]
        far_mixes = [two_parts(mix_ref[first + level, :, at] * decay) for level in range(levels)]
        for cols in blocks_of(width):
            gate = gate_ref[at, cols].astype(f32)
            swish = gate / (1.0 + jnp.exp(-gate))
            base_ref[at, cols] = skip[:, cols] * inputs_ref[at, cols].astype(f32) * swish
            own_ref[at, cols] = transposed_dot(own_mix, expand[:, cols]) * swish
            for level, mix in enumerate(far_mixes):
                far_ref[level, at, cols] = (transposed_dot(mix, expand[:, cols]) * swish).astype(bf16)
            for index, mix in span_mixes:
                span_refs[0][index, :, cols] = (transposed_dot(mix, expand[:, cols]) * swish).astype(bf16)


def near_kernel(parts, spans, paired, *refs):
    base_ref, own_ref, far_ref, core_ref, scaled_ref = refs[:5]
    count = 5 + parts + parts // 2
    in_refs, out_refs = refs[5 : 5 + parts], refs[5 + parts : count]
    span_refs = refs[count:-2]
    near_ref, turned_ref = refs[-2:]
    tokens, width = base_ref.shape
    in_map = map_rows(in_refs)
    turned = jnp.transpose(out_map_rows(out_refs))
    turned_ref[...] = turned
    size = in_map.shape[0]
    row = lax.broadcasted_iota(jnp.int32, (GROUP, GROUP), 0)
    col = lax.broadcasted_iota(jnp.int32, (GROUP, GROUP), 1)
    has_core = lax.rem(lax.axis_index("seq"), 2) == 1
    for group in range(tokens // GROUP):
        at = group_slice(group)
        scores = jnp.dot(turned[at], in_map[:, at], preferred_element_type=f32)
        scores = jnp.where(row >= col, scores, 0.0).astype(bf16)
        for cols in blocks_of(width):
            own = jnp.dot(scores, scaled_ref[at, cols], preferred_element_type=f32)
            total = base_ref[at, cols] + own_ref[at, cols] * own
            for index, (later, _, _, _) in enumerate(spans):
                if later == group:
                    rows = slice(index * size, (index + 1) * size)
                    reach = jnp.dot(turned[at], span_refs[0][rows, cols], preferred_element_type=f32)
                    total = total + span_refs[1][index, :, cols].astype(f32) * reach
            if paired:
                reach = jnp.dot(turned[at], core_ref[:size, cols], preferred_element_type=f32)
                reach = jnp.where(has_core, reach, 0.0)
                total = total + far_ref[0, at, cols].astype(f32) * reach
            near_ref[at, cols] = total


def far_body(turned_ref, near_ref, far_ref, gain_ref, start, columns, levels, state_of, gated_ref):
    tokens = far_ref.shape[1]
    squares = jnp.zeros((tokens, 128), f32)
    for cols in blocks_of(columns):
        at = pl.ds(pl.multiple_of(start + cols.start, BLOCK), BLOCK)
        total = near_ref[:, at]
        for level in levels:
            state = state_of(level, cols, at).astype(bf16)
            reach = jnp.dot(turned_ref[...], state, preferred_element_type=f32)
            total = total + far_ref[level, :, at].astype(f32) * reach
        gated_ref[:, cols] = total * gain_ref[:, at]
        total = total * total
        for part in range(0, BLOCK, 128):
            squares = squares + total[:, part : part + 128]
    return squares


def row_sums(squares):
    high = squares.astype(bf16)
    low = (squares - high.astype(f32)).astype(bf16)
    parts = jnp.concatenate([high, low], axis=1)
    ones = jnp.ones((16, parts.shape[1]), bf16)
    return lax.dot_general(ones, parts, (((1,), (1,)), ((), ())), preferred_element_type=f32)[:1]


def far_kernel(turned_ref, near_ref, far_ref, gain_ref, *refs):
    state_refs = refs[:-2]
    gated_ref, sums_ref = refs[-2:]

    def state_of(level, cols, _):
        return state_refs[level][:, cols]

    width = near_ref.shape[1]
    levels = range(far_ref.shape[0])
    squares = far_body(turned_ref, near_ref, far_ref, gain_ref, 0, width, levels, state_of, gated_ref)
    sums_ref[...] = row_sums(squares)


def combine_kernel(size, x_ref, y_ref, diagonal_ref, spans_ref):
    rank = lax.axis_index("seq")
    along_x = lax.rem(lax.div(rank, 2), 2)
    along_y = lax.div(rank, 4)

    def parts_of(ref):
        return ref[:size, :].astype(f32), ref[size:, :].astype(f32)[:1]

    x_state, x_decay = parts_of(x_ref)
    y_state, y_decay = parts_of(y_ref)
    d_state, d_decay = parts_of(diagonal_ref)
    newer = jnp.where(along_x == 1, y_state, d_state)
    newer_decay = jnp.where(along_x == 1, y_decay, d_decay)
    older = jnp.where(along_x == 1, d_state, y_state)
    running = jnp.where(along_x == 1, x_decay, 1.0)
    running = jnp.where(along_y == 1, running, 0.0)
    spans_ref[:size, :] = jnp.where(along_x == 1, x_state, 0.0).astype(bf16)
    spans_ref[size:, :] = ((older * newer_decay + newer) * running).astype(bf16)


def far_kernel_of_half(own, *refs):
    turned_ref, near_ref, far_ref, gain_ref, core_ref, spans_ref = refs[:6]
    gated_ref, sums_ref = refs[-2:]
    size = turned_ref.shape[1]
    core = lax.rem(lax.axis_index("seq"), 2)
    half = spans_ref.shape[1]
    start = (core if own else 1 - core) * half

    def state_of(level, cols, at):
        core_decay = core_ref[size:, at].astype(f32)[:1]
        running = jnp.where(core == 1, core_decay, 1.0)
        return spans_ref[(level - 1) * size : level * size, cols].astype(f32) * running

    squares = far_body(turned_ref, near_ref, far_ref, gain_ref, start, half, (1, 2), state_of, gated_ref)
    sums_ref[...] = squares if own else row_sums(squares + refs[6][...])


def norm_kernel(parts, columns, *refs):
    gated_refs, (out_hbm, out_ref, semaphores) = refs[parts:-3], refs[-3:]
    total = refs[0][...]
    for ref in refs[1:parts]:
        total = total + ref[...]
    scale = lax.rsqrt(total / columns + 1e-05)
    pieces, rest = [], scale
    for _ in range(3):
        pieces.append(rest.astype(bf16).astype(f32))
        rest = rest - pieces[-1]
    tokens = scale.shape[1]
    pieces.append(jnp.zeros((16 - len(pieces), tokens), f32))
    scale = transposed_dot(jnp.concatenate(pieces, axis=0).astype(bf16), jnp.ones((16, 128), bf16))
    width = gated_refs[0].shape[1]
    core = lax.rem(lax.axis_index("seq"), 2)
    sides = (core, 1 - core) if len(gated_refs) == 2 else (0,)
    chunk = tokens // NORM_CHUNKS
    copies = []
    for index in range(NORM_CHUNKS):
        rows = slice(index * chunk, (index + 1) * chunk)
        for ref, side in zip(gated_refs, sides):
            for col in range(0, width, 128):
                at = pl.ds(pl.multiple_of(side * width + col, 128), 128)
                out_ref[rows, at] = (ref[rows, col : col + 128] * scale[rows]).astype(bf16)
        copies.append(pltpu.make_async_copy(out_ref.at[rows], out_hbm.at[rows], semaphores.at[index]))
        copies[-1].start()
    for copy in copies:
        copy.wait()


def call(kernel, out_shape, args, flops=0, bytes_accessed=0, hbm=0, scratch=None, out_space=pltpu.VMEM):
    specs = [pl.BlockSpec(memory_space=pl.ANY)] * hbm + [pl.BlockSpec(memory_space=pltpu.VMEM)] * (len(args) - hbm)
    args = [pltpu.with_memory_space_constraint(arg, pltpu.HBM) for arg in args[:hbm]] + list(args[hbm:])
    if scratch is None:
        scratch = [pltpu.VMEM(arg.shape, arg.dtype) for arg in args[:hbm]]
        scratch += [pltpu.SemaphoreType.DMA((hbm,))] if hbm else []
    return pl.pallas_call(
        kernel,
        out_shape=out_shape,
        in_specs=specs,
        out_specs=jax.tree.map(lambda _: pl.BlockSpec(memory_space=out_space), out_shape),
        scratch_shapes=scratch,
        compiler_params=pltpu.CompilerParams(vmem_limit_bytes=VMEM_LIMIT),
        cost_estimate=pl.CostEstimate(flops=flops, bytes_accessed=bytes_accessed, transcendentals=0),
    )(*args)


def shaped(shape, dtype):
    return jax.ShapeDtypeStruct(shape, dtype)


def flip(array, axis, mask):
    return lax.ppermute(array, axis, [(i, i ^ mask) for i in range(lax.axis_size(axis))])


def from_each(array, axis, first=1, stride=1):
    masks = sorted(range(first, lax.axis_size(axis), stride), key=lambda mask: (mask == 1, mask))
    return [flip(array, axis, mask) for mask in masks]


def merged(older, newer, size):
    older, newer = older.astype(f32), newer.astype(f32)
    decay = newer[size : size + 1]
    return jnp.concatenate([older[:size] * decay + newer[:size], older[size:] * decay], axis=0).astype(bf16)


def far_states(shard, size):
    rank = lax.axis_index("seq")
    levels = lax.axis_size("seq").bit_length() - 1
    states = []
    running = jnp.ones((1, shard.shape[1]), f32)
    for level in range(levels):
        theirs = flip(shard, "seq", 1 << level)
        upper = jnp.right_shift(rank, level) % 2 == 1
        states.append(jnp.where(upper, theirs[:size].astype(f32) * running, 0.0).astype(bf16))
        running = jnp.where(upper, running * theirs[size : size + 1].astype(f32), running)
        shard = merged(jnp.where(upper, theirs, shard), jnp.where(upper, shard, theirs), size)
    return states


def on_device(inputs, gate, input_map, output_map, step, decay_rate, level_mix, skip, norm_gain):
    tokens, width = inputs.shape
    heads = step.shape[0]
    parts = lax.axis_size("head")
    levels = lax.axis_size("seq").bit_length() - 1
    size = input_map.shape[0] * parts
    groups = tokens // GROUP
    spans = local_spans(groups)
    dense = 2 * tokens * GROUP * width
    area = tokens * width
    others = from_each(input_map, "head")
    kept = inputs, gate, level_mix, skip[None, :], input_map, output_map
    scaled, cum, *kept = call(
        prepare_kernel,
        (
            *(shaped((tokens, width), bf16), shaped((heads, tokens), f32)),
            *(shaped(array.shape, array.dtype) for array in kept),
        ),
        (step, decay_rate[None, :], *kept),
        flops=16 * dense,
        bytes_accessed=4 * area,
        hbm=8,
        scratch=[pltpu.VMEM(step.shape, f32), pltpu.VMEM((1, heads), f32), pltpu.SemaphoreType.DMA((8,))],
    )
    inputs, gate, level_mix, skip, input_map, output_map = kept
    in_maps = [input_map, *others]
    shard_shape = shaped((size + DECAY_ROWS, width), bf16)
    span_shape = [shaped((len(spans) * size, width), bf16)] if spans else []
    shard, *span_states = call(
        functools.partial(states_kernel, parts),
        (shard_shape, *span_shape),
        (*in_maps, scaled, cum),
        flops=dense,
        bytes_accessed=4 * area,
    )
    pairs = lax.axis_size("seq") == 8 and parts == 4
    if pairs:
        theirs = flip(shard, "seq", 1)
        message = call(
            functools.partial(merge_kernel, size),
            shaped((size + DECAY_ROWS, width // 2), bf16),
            (shard, theirs),
            flops=0,
            bytes_accessed=area,
        )
    else:
        message = shard
    output_map, _ = lax.optimization_barrier((output_map, shard))
    beside = flip(output_map, "head", 1)
    rows = output_map.shape[0]
    if rows % 16 == 0:
        both = call(
            join_kernel,
            shaped((2 * rows, tokens), bf16),
            (output_map, beside),
            bytes_accessed=8 * rows * tokens,
        )
    else:
        both = jnp.concatenate([output_map, beside], axis=0)
    out_maps = [both, *from_each(both, "head", first=2, stride=2)]
    factor_shape = [shaped((len(spans), GROUP, width), bf16)] if spans else []
    base, own_factor, far, *span_factors = call(
        functools.partial(factor_kernel, spans, levels),
        (
            *(shaped((tokens, width), f32), shaped((tokens, width), f32)),
            *(shaped((levels, tokens, width), bf16), *factor_shape),
        ),
        (inputs, gate, level_mix, skip, cum, message),
        flops=21 * dense // 4,
        bytes_accessed=0,
    )
    near, turned = call(
        functools.partial(near_kernel, parts, spans, pairs),
        (shaped((tokens, width), f32), shaped((tokens, size), bf16)),
        (
            *(base, own_factor, far, theirs if pairs else message, scaled),
            *(*in_maps, *out_maps, *span_states, *span_factors),
        ),
        flops=0,
        bytes_accessed=0,
    )
    gain = norm_gain[None, :]
    sums_shape = shaped((1, tokens), f32)
    if pairs:
        received = [flip(message, "seq", mask) for mask in (6, 4, 2)]
        *received, near, far = lax.optimization_barrier((*received, near, far))
        own = call(
            functools.partial(combine_kernel, size),
            shaped((2 * size, width // 2), bf16),
            received[::-1],
            bytes_accessed=area,
        )
        other = flip(own, "seq", 1)
        gated_shape = shaped((tokens, width // 2), f32)
        own_gated, own_squares = call(
            functools.partial(far_kernel_of_half, True),
            (gated_shape, shaped((tokens, 128), f32)),
            (turned, near, far, gain, theirs, own),
            flops=2 * dense,
            bytes_accessed=6 * area,
        )
        other_gated, sums = call(
            functools.partial(far_kernel_of_half, False),
            (gated_shape, sums_shape),
            (turned, near, far, gain, theirs, other, own_squares),
            flops=2 * dense,
            bytes_accessed=6 * area,
        )
        gated = (own_gated, other_gated)
    else:
        *gated, sums = call(
            far_kernel,
            (shaped((tokens, width), f32), sums_shape),
            (turned, near, far, gain, *far_states(shard, size)),
            flops=4 * dense,
            bytes_accessed=12 * area,
        )
    last = [sums, *from_each(sums, "head")]
    return call(
        functools.partial(norm_kernel, len(last), width * parts),
        shaped((tokens, width), bf16),
        (*last, *gated),
        flops=dense,
        bytes_accessed=6 * area,
        scratch=[pltpu.VMEM((tokens, width), bf16), pltpu.SemaphoreType.DMA((NORM_CHUNKS,))],
        out_space=pl.ANY,
    )


def solution(mesh):
    return jax.shard_map(
        on_device,
        mesh=mesh,
        in_specs=(
            P("seq", "head"),
            P("seq", "head"),
            P("head", "seq"),
            P("head", "seq"),
            P("head", "seq"),
            P("head"),
            P(None, "head", "seq"),
            P("head"),
            P("head"),
        ),
        out_specs=P("seq", "head"),
        check_vma=False,
    )
```

```python
import functools

import jax
import jax.numpy as jnp
from jax import lax
from jax.experimental import pallas as pl
from jax.experimental.pallas import tpu as pltpu
from jax.sharding import PartitionSpec as P

P_SIZE = 64
GROUP = 256
DECAY_ROWS = 16
BLOCK = 256
NORM_CHUNKS = 8
VMEM_LIMIT = 40 * 1024 * 1024

f32, bf16 = jnp.float32, jnp.bfloat16
HIGHEST = lax.Precision.HIGHEST
TRANSPOSED = (((0,), (0,)), ((), ()))


def expander(heads, width, copies):
    row = lax.broadcasted_iota(jnp.int32, (copies * heads, width), 0)
    col = lax.broadcasted_iota(jnp.int32, (copies * heads, width), 1)
    return jnp.where(lax.rem(row, heads) == lax.div(col, P_SIZE), 1.0, 0.0)


def two_parts(factor):
    high = factor.astype(bf16).astype(f32)
    return jnp.concatenate([high, factor - high], axis=0).astype(bf16)


def transposed_dot(left, right):
    return lax.dot_general(left, right, TRANSPOSED, preferred_element_type=f32)


def head_row(heads, width, column):
    return jnp.sum(expander(heads, width, 1) * column, axis=0, keepdims=True)


def group_slice(group):
    return slice(group * GROUP, (group + 1) * GROUP)


def blocks_of(width):
    return [slice(at, at + BLOCK) for at in range(0, width, BLOCK)]


def local_spans(groups):
    spans = []
    for later in range(groups):
        for bit in range(groups.bit_length() - 1):
            if later >> bit & 1:
                start = later >> bit + 1 << bit + 1
                spans.append((later, bit, start, start + 2**bit))
    return spans


def column_of(row):
    size = row.shape[1]
    at = lax.broadcasted_iota(jnp.int32, (size, size), 0) == lax.broadcasted_iota(jnp.int32, (size, size), 1)
    return jnp.sum(jnp.where(at, row, 0.0), axis=1, keepdims=True)


def map_rows(maps):
    if all(rows.shape[0] % 16 == 0 for rows in maps):
        return jnp.concatenate([rows[...] for rows in maps], axis=0)
    return jnp.concatenate([rows[...].astype(f32) for rows in maps], axis=0).astype(bf16)


def out_map_rows(map_refs):
    rows = map_refs[0].shape[0] // 2
    if rows % 16 == 0:
        return map_rows([map_refs[0].at[:rows], *map_refs[1:], map_refs[0].at[rows:]])
    pair = map_refs[0][...].astype(f32)
    return map_rows([pair[:rows], *map_refs[1:], pair[rows:]])


def fetch(sources, targets, semaphores):
    copies = [
        pltpu.make_async_copy(source, target, semaphores.at[index])
        for index, (source, target) in enumerate(zip(sources, targets))
    ]
    for copy in copies:
        copy.start()
    return copies


def prepare_kernel(*refs):
    sources, (scaled_ref, cum_ref), kept_refs = refs[:8], refs[8:10], refs[10:16]
    step_ref, rate_ref, semaphores = refs[16:]
    inputs_ref = kept_refs[0]
    copies = fetch(sources, (step_ref, rate_ref, *kept_refs), semaphores)
    heads, tokens = step_ref.shape
    width = inputs_ref.shape[1]
    row = lax.broadcasted_iota(jnp.int32, (GROUP, GROUP), 0)
    col = lax.broadcasted_iota(jnp.int32, (GROUP, GROUP), 1)
    until = jnp.where(row <= col, 1.0, 0.0)
    expand = expander(heads, width, 2).astype(bf16)
    copies[0].wait()
    copies[1].wait()
    step = step_ref[...]
    log_decay = -step * column_of(rate_ref[...])
    factors = []
    for group in range(tokens // GROUP):
        at = group_slice(group)
        cum = jnp.dot(log_decay[:, at], until, precision=HIGHEST, preferred_element_type=f32)
        cum_ref[:, at] = cum
        factors.append(two_parts(jnp.exp(-cum) * step[:, at]))
    factor = jnp.concatenate(factors, axis=1)
    copies[2].wait()
    for cols in blocks_of(width):
        scale = transposed_dot(factor, expand[:, cols])
        scaled_ref[:, cols] = (inputs_ref[:, cols].astype(f32) * scale).astype(bf16)
    for copy in copies[3:]:
        copy.wait()


def join_kernel(mine_ref, theirs_ref, both_ref):
    rows = mine_ref.shape[0]
    both_ref[:rows, :] = mine_ref[...]
    both_ref[rows:, :] = theirs_ref[...]


def states_kernel(parts, *refs):
    map_refs, (scaled_ref, cum_ref), out_refs = refs[:parts], refs[parts : parts + 2], refs[parts + 2 :]
    shard_ref = out_refs[0]
    heads, tokens = cum_ref.shape
    width = scaled_ref.shape[1]
    in_map = map_rows(map_refs)
    size = in_map.shape[0]
    cum = cum_ref[...]
    states, decays = [], []
    for group in range(tokens // GROUP):
        at = group_slice(group)
        decay = head_row(heads, width, jnp.exp(cum[:, at.stop - 1 : at.stop]))
        raw = jnp.dot(in_map[:, at], scaled_ref[at, :], preferred_element_type=f32)
        states.append(raw * decay)
        decays.append(decay)
    total, decay = states[0], decays[0]
    for group in range(1, len(states)):
        total = total * decays[group] + states[group]
        decay = decay * decays[group]
    shard_ref[:size, :] = total.astype(bf16)
    shard_ref[size:, :] = jnp.broadcast_to(decay, (DECAY_ROWS, width)).astype(bf16)
    for index, (later, _, start, stop) in enumerate(local_spans(len(states))):
        span = states[start]
        for group in range(start + 1, later):
            span = span * decays[group]
            if group < stop:
                span = span + states[group]
        out_refs[1][index * size : (index + 1) * size, :] = span.astype(bf16)


def merge_kernel(size, mine_ref, theirs_ref, pair_ref):
    core = lax.rem(lax.axis_index("seq"), 2)
    half = pair_ref.shape[1]
    mine = jnp.where(core == 1, mine_ref[:, half:], mine_ref[:, :half])
    theirs = jnp.where(core == 1, theirs_ref[:, half:], theirs_ref[:, :half])
    older = jnp.where(core == 1, theirs, mine).astype(f32)
    newer = jnp.where(core == 1, mine, theirs).astype(f32)
    decay = newer[size : size + 1]
    pair_ref[:size, :] = (older[:size] * decay + newer[:size]).astype(bf16)
    pair_ref[size:, :] = (older[size:] * decay).astype(bf16)


def factor_kernel(spans, levels, *refs):
    inputs_ref, gate_ref, mix_ref, skip_ref, cum_ref, _ = refs[:6]
    base_ref, own_ref, far_ref = refs[6:9]
    span_refs = refs[9:]
    heads, tokens = cum_ref.shape
    width = inputs_ref.shape[1]
    groups = tokens // GROUP
    first = groups.bit_length()
    expand = expander(heads, width, 2).astype(bf16)
    skip = head_row(heads, width, column_of(skip_ref[...]))
    before = jnp.zeros((heads, 1), f32)
    for group in range(groups):
        at = group_slice(group)
        cum = cum_ref[:, at]
        decay = jnp.exp(cum)
        own_mix = two_parts(mix_ref[0, :, at] * decay)
        span_mixes = [
            (index, two_parts(mix_ref[1 + bit, :, at] * decay))
            for index, (later, bit, _, _) in enumerate(spans)
            if later == group
        ]
        decay = jnp.exp(cum + before)
        before = before + cum[:, GROUP - 1 : GROUP]
        far_mixes = [two_parts(mix_ref[first + level, :, at] * decay) for level in range(levels)]
        for cols in blocks_of(width):
            gate = gate_ref[at, cols].astype(f32)
            swish = gate / (1.0 + jnp.exp(-gate))
            base_ref[at, cols] = skip[:, cols] * inputs_ref[at, cols].astype(f32) * swish
            own_ref[at, cols] = transposed_dot(own_mix, expand[:, cols]) * swish
            for level, mix in enumerate(far_mixes):
                far_ref[level, at, cols] = (transposed_dot(mix, expand[:, cols]) * swish).astype(bf16)
            for index, mix in span_mixes:
                span_refs[0][index, :, cols] = (transposed_dot(mix, expand[:, cols]) * swish).astype(bf16)


def near_body(spans, paired, start, scores_ref, turned_ref, refs, near_ref):
    base_ref, own_ref, far_ref, core_ref, scaled_ref = refs[:5]
    span_refs = refs[5:]
    tokens, size = turned_ref.shape
    has_core = lax.rem(lax.axis_index("seq"), 2) == 1
    for group in range(tokens // GROUP):
        at = group_slice(group)
        for cols in blocks_of(near_ref.shape[1]):
            of = pl.ds(pl.multiple_of(start + cols.start, BLOCK), BLOCK)
            own = jnp.dot(scores_ref[at, :], scaled_ref[at, of], preferred_element_type=f32)
            total = base_ref[at, of] + own_ref[at, of] * own
            for index, (later, _, _, _) in enumerate(spans):
                if later == group:
                    rows = slice(index * size, (index + 1) * size)
                    reach = jnp.dot(turned_ref[at, :], span_refs[0][rows, of], preferred_element_type=f32)
                    total = total + span_refs[1][index, :, of].astype(f32) * reach
            if paired:
                reach = jnp.dot(turned_ref[at, :], core_ref[:size, of], preferred_element_type=f32)
                reach = jnp.where(has_core, reach, 0.0)
                total = total + far_ref[0, at, of].astype(f32) * reach
            near_ref[at, cols] = total


def near_kernel(parts, spans, paired, *refs):
    count = parts + parts // 2
    in_refs, out_refs, rest = refs[:parts], refs[parts:count], refs[count:-3]
    near_ref, turned_ref, scores_ref = refs[-3:]
    in_map = map_rows(in_refs)
    turned = jnp.transpose(out_map_rows(out_refs))
    turned_ref[...] = turned
    row = lax.broadcasted_iota(jnp.int32, (GROUP, GROUP), 0)
    col = lax.broadcasted_iota(jnp.int32, (GROUP, GROUP), 1)
    for group in range(turned.shape[0] // GROUP):
        at = group_slice(group)
        scores = jnp.dot(turned[at], in_map[:, at], preferred_element_type=f32)
        scores_ref[at, :] = jnp.where(row >= col, scores, 0.0).astype(bf16)
    start = lax.rem(lax.axis_index("seq"), 2) * near_ref.shape[1] if paired else 0
    near_body(spans, paired, start, scores_ref, turned_ref, rest, near_ref)


def other_near_kernel(spans, scores_ref, turned_ref, _, *refs):
    near_ref = refs[-1]
    start = (1 - lax.rem(lax.axis_index("seq"), 2)) * near_ref.shape[1]
    near_body(spans, True, start, scores_ref, turned_ref, refs[:-1], near_ref)


def far_body(turned_ref, near_ref, far_ref, gain_ref, start, columns, levels, state_of, gated_ref):
    tokens = far_ref.shape[1]
    squares = jnp.zeros((tokens, 128), f32)
    for cols in blocks_of(columns):
        at = pl.ds(pl.multiple_of(start + cols.start, BLOCK), BLOCK)
        total = near_ref[:, cols]
        for level in levels:
            state = state_of(level, cols, at).astype(bf16)
            reach = jnp.dot(turned_ref[...], state, preferred_element_type=f32)
            total = total + far_ref[level, :, at].astype(f32) * reach
        gated_ref[:, cols] = total * gain_ref[:, at]
        total = total * total
        for part in range(0, BLOCK, 128):
            squares = squares + total[:, part : part + 128]
    return squares


def row_sums(squares):
    high = squares.astype(bf16)
    low = (squares - high.astype(f32)).astype(bf16)
    parts = jnp.concatenate([high, low], axis=1)
    ones = jnp.ones((16, parts.shape[1]), bf16)
    return lax.dot_general(ones, parts, (((1,), (1,)), ((), ())), preferred_element_type=f32)[:1]


def far_kernel(turned_ref, near_ref, far_ref, gain_ref, *refs):
    state_refs = refs[:-2]
    gated_ref, sums_ref = refs[-2:]

    def state_of(level, cols, _):
        return state_refs[level][:, cols]

    width = near_ref.shape[1]
    levels = range(far_ref.shape[0])
    squares = far_body(turned_ref, near_ref, far_ref, gain_ref, 0, width, levels, state_of, gated_ref)
    sums_ref[...] = row_sums(squares)


def combine_kernel(size, x_ref, y_ref, diagonal_ref, spans_ref):
    rank = lax.axis_index("seq")
    along_x = lax.rem(lax.div(rank, 2), 2)
    along_y = lax.div(rank, 4)

    def parts_of(ref):
        return ref[:size, :].astype(f32), ref[size:, :].astype(f32)[:1]

    x_state, x_decay = parts_of(x_ref)
    y_state, y_decay = parts_of(y_ref)
    d_state, d_decay = parts_of(diagonal_ref)
    newer = jnp.where(along_x == 1, y_state, d_state)
    newer_decay = jnp.where(along_x == 1, y_decay, d_decay)
    older = jnp.where(along_x == 1, d_state, y_state)
    running = jnp.where(along_x == 1, x_decay, 1.0)
    running = jnp.where(along_y == 1, running, 0.0)
    spans_ref[:size, :] = jnp.where(along_x == 1, x_state, 0.0).astype(bf16)
    spans_ref[size:, :] = ((older * newer_decay + newer) * running).astype(bf16)


def far_kernel_of_half(own, *refs):
    turned_ref, near_ref, far_ref, gain_ref, core_ref, spans_ref = refs[:6]
    gated_ref, sums_ref = refs[-2:]
    size = turned_ref.shape[1]
    core = lax.rem(lax.axis_index("seq"), 2)
    half = spans_ref.shape[1]
    start = (core if own else 1 - core) * half

    def state_of(level, cols, at):
        core_decay = core_ref[size:, at].astype(f32)[:1]
        running = jnp.where(core == 1, core_decay, 1.0)
        return spans_ref[(level - 1) * size : level * size, cols].astype(f32) * running

    squares = far_body(turned_ref, near_ref, far_ref, gain_ref, start, half, (1, 2), state_of, gated_ref)
    sums_ref[...] = squares if own else row_sums(squares + refs[6][...])


def norm_kernel(parts, columns, *refs):
    gated_refs, (out_hbm, out_ref, semaphores) = refs[parts:-3], refs[-3:]
    total = refs[0][...]
    for ref in refs[1:parts]:
        total = total + ref[...]
    scale = lax.rsqrt(total / columns + 1e-05)
    pieces, rest = [], scale
    for _ in range(3):
        pieces.append(rest.astype(bf16).astype(f32))
        rest = rest - pieces[-1]
    tokens = scale.shape[1]
    pieces.append(jnp.zeros((16 - len(pieces), tokens), f32))
    scale = transposed_dot(jnp.concatenate(pieces, axis=0).astype(bf16), jnp.ones((16, 128), bf16))
    width = gated_refs[0].shape[1]
    core = lax.rem(lax.axis_index("seq"), 2)
    sides = (core, 1 - core) if len(gated_refs) == 2 else (0,)
    chunk = tokens // NORM_CHUNKS
    copies = []
    for index in range(NORM_CHUNKS):
        rows = slice(index * chunk, (index + 1) * chunk)
        for ref, side in zip(gated_refs, sides):
            for col in range(0, width, 128):
                at = pl.ds(pl.multiple_of(side * width + col, 128), 128)
                out_ref[rows, at] = (ref[rows, col : col + 128] * scale[rows]).astype(bf16)
        copies.append(pltpu.make_async_copy(out_ref.at[rows], out_hbm.at[rows], semaphores.at[index]))
        copies[-1].start()
    for copy in copies:
        copy.wait()


def call(kernel, out_shape, args, flops=0, bytes_accessed=0, hbm=0, scratch=None, out_space=pltpu.VMEM):
    specs = [pl.BlockSpec(memory_space=pl.ANY)] * hbm + [pl.BlockSpec(memory_space=pltpu.VMEM)] * (len(args) - hbm)
    args = [pltpu.with_memory_space_constraint(arg, pltpu.HBM) for arg in args[:hbm]] + list(args[hbm:])
    if scratch is None:
        scratch = [pltpu.VMEM(arg.shape, arg.dtype) for arg in args[:hbm]]
        scratch += [pltpu.SemaphoreType.DMA((hbm,))] if hbm else []
    return pl.pallas_call(
        kernel,
        out_shape=out_shape,
        in_specs=specs,
        out_specs=jax.tree.map(lambda _: pl.BlockSpec(memory_space=out_space), out_shape),
        scratch_shapes=scratch,
        compiler_params=pltpu.CompilerParams(vmem_limit_bytes=VMEM_LIMIT),
        cost_estimate=pl.CostEstimate(flops=flops, bytes_accessed=bytes_accessed, transcendentals=0),
    )(*args)


def shaped(shape, dtype):
    return jax.ShapeDtypeStruct(shape, dtype)


def flip(array, axis, mask):
    return lax.ppermute(array, axis, [(i, i ^ mask) for i in range(lax.axis_size(axis))])


def from_each(array, axis, first=1, stride=1):
    masks = sorted(range(first, lax.axis_size(axis), stride), key=lambda mask: (mask == 1, mask))
    return [flip(array, axis, mask) for mask in masks]


def merged(older, newer, size):
    older, newer = older.astype(f32), newer.astype(f32)
    decay = newer[size : size + 1]
    return jnp.concatenate([older[:size] * decay + newer[:size], older[size:] * decay], axis=0).astype(bf16)


def far_states(shard, size):
    rank = lax.axis_index("seq")
    levels = lax.axis_size("seq").bit_length() - 1
    states = []
    running = jnp.ones((1, shard.shape[1]), f32)
    for level in range(levels):
        theirs = flip(shard, "seq", 1 << level)
        upper = jnp.right_shift(rank, level) % 2 == 1
        states.append(jnp.where(upper, theirs[:size].astype(f32) * running, 0.0).astype(bf16))
        running = jnp.where(upper, running * theirs[size : size + 1].astype(f32), running)
        shard = merged(jnp.where(upper, theirs, shard), jnp.where(upper, shard, theirs), size)
    return states


def on_device(inputs, gate, input_map, output_map, step, decay_rate, level_mix, skip, norm_gain):
    tokens, width = inputs.shape
    heads = step.shape[0]
    parts = lax.axis_size("head")
    levels = lax.axis_size("seq").bit_length() - 1
    size = input_map.shape[0] * parts
    groups = tokens // GROUP
    spans = local_spans(groups)
    dense = 2 * tokens * GROUP * width
    area = tokens * width
    others = from_each(input_map, "head")
    kept = inputs, gate, level_mix, skip[None, :], input_map, output_map
    scaled, cum, *kept = call(
        prepare_kernel,
        (
            *(shaped((tokens, width), bf16), shaped((heads, tokens), f32)),
            *(shaped(array.shape, array.dtype) for array in kept),
        ),
        (step, decay_rate[None, :], *kept),
        flops=16 * dense,
        bytes_accessed=4 * area,
        hbm=8,
        scratch=[pltpu.VMEM(step.shape, f32), pltpu.VMEM((1, heads), f32), pltpu.SemaphoreType.DMA((8,))],
    )
    inputs, gate, level_mix, skip, input_map, output_map = kept
    in_maps = [input_map, *others]
    shard_shape = shaped((size + DECAY_ROWS, width), bf16)
    span_shape = [shaped((len(spans) * size, width), bf16)] if spans else []
    shard, *span_states = call(
        functools.partial(states_kernel, parts),
        (shard_shape, *span_shape),
        (*in_maps, scaled, cum),
        flops=dense,
        bytes_accessed=4 * area,
    )
    pairs = lax.axis_size("seq") == 8 and parts == 4
    if pairs:
        theirs = flip(shard, "seq", 1)
        message = call(
            functools.partial(merge_kernel, size),
            shaped((size + DECAY_ROWS, width // 2), bf16),
            (shard, theirs),
            flops=0,
            bytes_accessed=area,
        )
    else:
        message = shard
    output_map, _ = lax.optimization_barrier((output_map, shard))
    beside = flip(output_map, "head", 1)
    rows = output_map.shape[0]
    if rows % 16 == 0:
        both = call(
            join_kernel,
            shaped((2 * rows, tokens), bf16),
            (output_map, beside),
            bytes_accessed=8 * rows * tokens,
        )
    else:
        both = jnp.concatenate([output_map, beside], axis=0)
    out_maps = [both, *from_each(both, "head", first=2, stride=2)]
    factor_shape = [shaped((len(spans), GROUP, width), bf16)] if spans else []
    base, own_factor, far, *span_factors = call(
        functools.partial(factor_kernel, spans, levels),
        (
            *(shaped((tokens, width), f32), shaped((tokens, width), f32)),
            *(shaped((levels, tokens, width), bf16), *factor_shape),
        ),
        (inputs, gate, level_mix, skip, cum, message),
        flops=21 * dense // 4,
        bytes_accessed=0,
    )
    near_args = base, own_factor, far, theirs if pairs else message, scaled, *span_states, *span_factors
    near_shape = shaped((tokens, width // 2 if pairs else width), f32)
    near, turned, scores = call(
        functools.partial(near_kernel, parts, spans, pairs),
        (near_shape, shaped((tokens, size), bf16), shaped((tokens, GROUP), bf16)),
        (*in_maps, *out_maps, *near_args),
    )
    gain = norm_gain[None, :]
    sums_shape = shaped((1, tokens), f32)
    if pairs:
        received = [flip(message, "seq", mask) for mask in (6, 4, 2)]
        *received, near, far = lax.optimization_barrier((*received, near, far))
        own = call(
            functools.partial(combine_kernel, size),
            shaped((2 * size, width // 2), bf16),
            received[::-1],
            bytes_accessed=area,
        )
        other = flip(own, "seq", 1)
        other_near = call(
            functools.partial(other_near_kernel, spans), near_shape, (scores, turned, own, *near_args), flops=dense
        )
        gated_shape = shaped((tokens, width // 2), f32)
        own_gated, own_squares = call(
            functools.partial(far_kernel_of_half, True),
            (gated_shape, shaped((tokens, 128), f32)),
            (turned, near, far, gain, theirs, own),
            flops=2 * dense,
            bytes_accessed=6 * area,
        )
        other_gated, sums = call(
            functools.partial(far_kernel_of_half, False),
            (gated_shape, sums_shape),
            (turned, other_near, far, gain, theirs, other, own_squares),
            flops=2 * dense,
            bytes_accessed=6 * area,
        )
        gated = (own_gated, other_gated)
    else:
        *gated, sums = call(
            far_kernel,
            (shaped((tokens, width), f32), sums_shape),
            (turned, near, far, gain, *far_states(shard, size)),
            flops=4 * dense,
            bytes_accessed=12 * area,
        )
    last = [sums, *from_each(sums, "head")]
    return call(
        functools.partial(norm_kernel, len(last), width * parts),
        shaped((tokens, width), bf16),
        (*last, *gated),
        flops=dense,
        bytes_accessed=6 * area,
        scratch=[pltpu.VMEM((tokens, width), bf16), pltpu.SemaphoreType.DMA((NORM_CHUNKS,))],
        out_space=pl.ANY,
    )


def solution(mesh):
    return jax.shard_map(
        on_device,
        mesh=mesh,
        in_specs=(
            P("seq", "head"),
            P("seq", "head"),
            P("head", "seq"),
            P("head", "seq"),
            P("head", "seq"),
            P("head"),
            P(None, "head", "seq"),
            P("head"),
            P("head"),
        ),
        out_specs=P("seq", "head"),
        check_vma=False,
    )
```

```python
import functools

import jax
import jax.numpy as jnp
from jax import lax
from jax.experimental import pallas as pl
from jax.experimental.pallas import tpu as pltpu
from jax.sharding import PartitionSpec as P

P_SIZE = 64
GROUP = 256
DECAY_ROWS = 16
BLOCK = 256
NORM_CHUNKS = 8
VMEM_LIMIT = 40 * 1024 * 1024

f32, bf16 = jnp.float32, jnp.bfloat16
HIGHEST = lax.Precision.HIGHEST
TRANSPOSED = (((0,), (0,)), ((), ()))


def expander(heads, width, copies):
    row = lax.broadcasted_iota(jnp.int32, (copies * heads, width), 0)
    col = lax.broadcasted_iota(jnp.int32, (copies * heads, width), 1)
    return jnp.where(lax.rem(row, heads) == lax.div(col, P_SIZE), 1.0, 0.0)


def two_parts(factor):
    high = factor.astype(bf16).astype(f32)
    return jnp.concatenate([high, factor - high], axis=0).astype(bf16)


def transposed_dot(left, right):
    return lax.dot_general(left, right, TRANSPOSED, preferred_element_type=f32)


def head_row(heads, width, column):
    return jnp.sum(expander(heads, width, 1) * column, axis=0, keepdims=True)


def group_slice(group):
    return slice(group * GROUP, (group + 1) * GROUP)


def blocks_of(width):
    return [slice(at, at + BLOCK) for at in range(0, width, BLOCK)]


def local_spans(groups):
    spans = []
    for later in range(groups):
        for bit in range(groups.bit_length() - 1):
            if later >> bit & 1:
                start = later >> bit + 1 << bit + 1
                spans.append((later, bit, start, start + 2**bit))
    return spans


def column_of(row):
    size = row.shape[1]
    at = lax.broadcasted_iota(jnp.int32, (size, size), 0) == lax.broadcasted_iota(jnp.int32, (size, size), 1)
    return jnp.sum(jnp.where(at, row, 0.0), axis=1, keepdims=True)


def map_rows(maps):
    if all(rows.shape[0] % 16 == 0 for rows in maps):
        return jnp.concatenate([rows[...] for rows in maps], axis=0)
    return jnp.concatenate([rows[...].astype(f32) for rows in maps], axis=0).astype(bf16)


def out_map_rows(map_refs):
    rows = map_refs[0].shape[0] // 2
    if rows % 16 == 0:
        return map_rows([map_refs[0].at[:rows], *map_refs[1:], map_refs[0].at[rows:]])
    pair = map_refs[0][...].astype(f32)
    return map_rows([pair[:rows], *map_refs[1:], pair[rows:]])


def fetch(sources, targets, semaphores):
    copies = [
        pltpu.make_async_copy(source, target, semaphores.at[index])
        for index, (source, target) in enumerate(zip(sources, targets))
    ]
    for copy in copies:
        copy.start()
    return copies


def prepare_kernel(*refs):
    sources, (scaled_ref, cum_ref), kept_refs = refs[:8], refs[8:10], refs[10:16]
    step_ref, rate_ref, semaphores = refs[16:]
    inputs_ref = kept_refs[0]
    copies = fetch(sources, (step_ref, rate_ref, *kept_refs), semaphores)
    heads, tokens = step_ref.shape
    width = inputs_ref.shape[1]
    row = lax.broadcasted_iota(jnp.int32, (GROUP, GROUP), 0)
    col = lax.broadcasted_iota(jnp.int32, (GROUP, GROUP), 1)
    until = jnp.where(row <= col, 1.0, 0.0)
    expand = expander(heads, width, 2).astype(bf16)
    copies[0].wait()
    copies[1].wait()
    step = step_ref[...]
    log_decay = -step * column_of(rate_ref[...])
    factors = []
    for group in range(tokens // GROUP):
        at = group_slice(group)
        cum = jnp.dot(log_decay[:, at], until, precision=HIGHEST, preferred_element_type=f32)
        cum_ref[:, at] = cum
        factors.append(two_parts(jnp.exp(-cum) * step[:, at]))
    factor = jnp.concatenate(factors, axis=1)
    copies[2].wait()
    for cols in blocks_of(width):
        scale = transposed_dot(factor, expand[:, cols])
        scaled_ref[:, cols] = (inputs_ref[:, cols].astype(f32) * scale).astype(bf16)
    for copy in copies[3:]:
        copy.wait()


def join_kernel(mine_ref, theirs_ref, both_ref):
    rows = mine_ref.shape[0]
    both_ref[:rows, :] = mine_ref[...]
    both_ref[rows:, :] = theirs_ref[...]


def states_kernel(parts, *refs):
    map_refs, (scaled_ref, cum_ref), out_refs = refs[:parts], refs[parts : parts + 2], refs[parts + 2 :]
    shard_ref = out_refs[0]
    heads, tokens = cum_ref.shape
    width = scaled_ref.shape[1]
    in_map = map_rows(map_refs)
    size = in_map.shape[0]
    cum = cum_ref[...]
    states, decays = [], []
    for group in range(tokens // GROUP):
        at = group_slice(group)
        decay = head_row(heads, width, jnp.exp(cum[:, at.stop - 1 : at.stop]))
        raw = jnp.dot(in_map[:, at], scaled_ref[at, :], preferred_element_type=f32)
        states.append(raw * decay)
        decays.append(decay)
    total, decay = states[0], decays[0]
    for group in range(1, len(states)):
        total = total * decays[group] + states[group]
        decay = decay * decays[group]
    shard_ref[:size, :] = total.astype(bf16)
    shard_ref[size:, :] = jnp.broadcast_to(decay, (DECAY_ROWS, width)).astype(bf16)
    for index, (later, _, start, stop) in enumerate(local_spans(len(states))):
        span = states[start]
        for group in range(start + 1, later):
            span = span * decays[group]
            if group < stop:
                span = span + states[group]
        out_refs[1][index * size : (index + 1) * size, :] = span.astype(bf16)


def merge_kernel(size, mine_ref, theirs_ref, pair_ref):
    core = lax.rem(lax.axis_index("seq"), 2)
    half = pair_ref.shape[1]
    mine = jnp.where(core == 1, mine_ref[:, half:], mine_ref[:, :half])
    theirs = jnp.where(core == 1, theirs_ref[:, half:], theirs_ref[:, :half])
    older = jnp.where(core == 1, theirs, mine).astype(f32)
    newer = jnp.where(core == 1, mine, theirs).astype(f32)
    decay = newer[size : size + 1]
    pair_ref[:size, :] = (older[:size] * decay + newer[:size]).astype(bf16)
    pair_ref[size:, :] = (older[size:] * decay).astype(bf16)


def factor_kernel(spans, levels, *refs):
    inputs_ref, gate_ref, mix_ref, skip_ref, cum_ref, _ = refs[:6]
    base_ref, own_ref, far_ref = refs[6:9]
    span_refs = refs[9:]
    heads, tokens = cum_ref.shape
    width = inputs_ref.shape[1]
    groups = tokens // GROUP
    first = groups.bit_length()
    expand = expander(heads, width, 2).astype(bf16)
    skip = head_row(heads, width, column_of(skip_ref[...]))
    before = jnp.zeros((heads, 1), f32)
    for group in range(groups):
        at = group_slice(group)
        cum = cum_ref[:, at]
        decay = jnp.exp(cum)
        own_mix = two_parts(mix_ref[0, :, at] * decay)
        span_mixes = [
            (index, two_parts(mix_ref[1 + bit, :, at] * decay))
            for index, (later, bit, _, _) in enumerate(spans)
            if later == group
        ]
        decay = jnp.exp(cum + before)
        before = before + cum[:, GROUP - 1 : GROUP]
        far_mixes = [two_parts(mix_ref[first + level, :, at] * decay) for level in range(levels)]
        for cols in blocks_of(width):
            gate = gate_ref[at, cols].astype(f32)
            swish = gate / (1.0 + jnp.exp(-gate))
            base_ref[at, cols] = skip[:, cols] * inputs_ref[at, cols].astype(f32) * swish
            own_ref[at, cols] = transposed_dot(own_mix, expand[:, cols]) * swish
            for level, mix in enumerate(far_mixes):
                far_ref[level, at, cols] = (transposed_dot(mix, expand[:, cols]) * swish).astype(bf16)
            for index, mix in span_mixes:
                span_refs[0][index, :, cols] = (transposed_dot(mix, expand[:, cols]) * swish).astype(bf16)


def near_body(spans, paired, start, scores_ref, turned_ref, refs, near_ref):
    base_ref, own_ref, far_ref, core_ref, scaled_ref = refs[:5]
    span_refs = refs[5:]
    tokens, size = turned_ref.shape
    has_core = lax.rem(lax.axis_index("seq"), 2) == 1
    for group in range(tokens // GROUP):
        at = group_slice(group)
        for cols in blocks_of(near_ref.shape[1]):
            of = pl.ds(pl.multiple_of(start + cols.start, BLOCK), BLOCK)
            own = jnp.dot(scores_ref[at, :], scaled_ref[at, of], preferred_element_type=f32)
            total = base_ref[at, of] + own_ref[at, of] * own
            for index, (later, _, _, _) in enumerate(spans):
                if later == group:
                    rows = slice(index * size, (index + 1) * size)
                    reach = jnp.dot(turned_ref[at, :], span_refs[0][rows, of], preferred_element_type=f32)
                    total = total + span_refs[1][index, :, of].astype(f32) * reach
            if paired:
                reach = jnp.dot(turned_ref[at, :], core_ref[:size, of], preferred_element_type=f32)
                reach = jnp.where(has_core, reach, 0.0)
                total = total + far_ref[0, at, of].astype(f32) * reach
            near_ref[at, cols] = total


def near_kernel(parts, spans, paired, _, *refs):
    count = parts + parts // 2
    in_refs, out_refs, rest = refs[:parts], refs[parts:count], refs[count:-3]
    near_ref, turned_ref, scores_ref = refs[-3:]
    in_map = map_rows(in_refs)
    turned = jnp.transpose(out_map_rows(out_refs))
    turned_ref[...] = turned
    row = lax.broadcasted_iota(jnp.int32, (GROUP, GROUP), 0)
    col = lax.broadcasted_iota(jnp.int32, (GROUP, GROUP), 1)
    for group in range(turned.shape[0] // GROUP):
        at = group_slice(group)
        scores = jnp.dot(turned[at], in_map[:, at], preferred_element_type=f32)
        scores_ref[at, :] = jnp.where(row >= col, scores, 0.0).astype(bf16)
    start = lax.rem(lax.axis_index("seq"), 2) * near_ref.shape[1] if paired else 0
    near_body(spans, paired, start, scores_ref, turned_ref, rest, near_ref)


def other_near_kernel(spans, scores_ref, turned_ref, _, *refs):
    near_ref = refs[-1]
    start = (1 - lax.rem(lax.axis_index("seq"), 2)) * near_ref.shape[1]
    near_body(spans, True, start, scores_ref, turned_ref, refs[:-1], near_ref)


def far_body(turned_ref, near_ref, far_ref, gain_ref, start, columns, levels, state_of, gated_ref):
    tokens = far_ref.shape[1]
    squares = jnp.zeros((tokens, 128), f32)
    for cols in blocks_of(columns):
        at = pl.ds(pl.multiple_of(start + cols.start, BLOCK), BLOCK)
        total = near_ref[:, cols]
        for level in levels:
            state = state_of(level, cols, at).astype(bf16)
            reach = jnp.dot(turned_ref[...], state, preferred_element_type=f32)
            total = total + far_ref[level, :, at].astype(f32) * reach
        gated_ref[:, cols] = total * gain_ref[:, at]
        total = total * total
        for part in range(0, BLOCK, 128):
            squares = squares + total[:, part : part + 128]
    return squares


def row_sums(squares):
    high = squares.astype(bf16)
    low = (squares - high.astype(f32)).astype(bf16)
    parts = jnp.concatenate([high, low], axis=1)
    ones = jnp.ones((16, parts.shape[1]), bf16)
    return lax.dot_general(ones, parts, (((1,), (1,)), ((), ())), preferred_element_type=f32)[:1]


def far_kernel(turned_ref, near_ref, far_ref, gain_ref, *refs):
    state_refs = refs[:-2]
    gated_ref, sums_ref = refs[-2:]

    def state_of(level, cols, _):
        return state_refs[level][:, cols]

    width = near_ref.shape[1]
    levels = range(far_ref.shape[0])
    squares = far_body(turned_ref, near_ref, far_ref, gain_ref, 0, width, levels, state_of, gated_ref)
    sums_ref[...] = row_sums(squares)


def combine_kernel(size, x_ref, y_ref, diagonal_ref, spans_ref):
    rank = lax.axis_index("seq")
    along_x = lax.rem(lax.div(rank, 2), 2)
    along_y = lax.div(rank, 4)

    def parts_of(ref):
        return ref[:size, :].astype(f32), ref[size:, :].astype(f32)[:1]

    x_state, x_decay = parts_of(x_ref)
    y_state, y_decay = parts_of(y_ref)
    d_state, d_decay = parts_of(diagonal_ref)
    newer = jnp.where(along_x == 1, y_state, d_state)
    newer_decay = jnp.where(along_x == 1, y_decay, d_decay)
    older = jnp.where(along_x == 1, d_state, y_state)
    running = jnp.where(along_x == 1, x_decay, 1.0)
    running = jnp.where(along_y == 1, running, 0.0)
    spans_ref[:size, :] = jnp.where(along_x == 1, x_state, 0.0).astype(bf16)
    spans_ref[size:, :] = ((older * newer_decay + newer) * running).astype(bf16)


def far_kernel_of_half(own, *refs):
    turned_ref, near_ref, far_ref, gain_ref, core_ref, spans_ref = refs[:6]
    gated_ref, sums_ref = refs[-2:]
    size = turned_ref.shape[1]
    core = lax.rem(lax.axis_index("seq"), 2)
    half = spans_ref.shape[1]
    start = (core if own else 1 - core) * half

    def state_of(level, cols, at):
        core_decay = core_ref[size:, at].astype(f32)[:1]
        running = jnp.where(core == 1, core_decay, 1.0)
        return spans_ref[(level - 1) * size : level * size, cols].astype(f32) * running

    squares = far_body(turned_ref, near_ref, far_ref, gain_ref, start, half, (1, 2), state_of, gated_ref)
    sums_ref[...] = squares if own else row_sums(squares + refs[6][...])


def norm_kernel(parts, columns, *refs):
    gated_refs, (out_hbm, out_ref, semaphores) = refs[parts:-3], refs[-3:]
    total = refs[0][...]
    for ref in refs[1:parts]:
        total = total + ref[...]
    scale = lax.rsqrt(total / columns + 1e-05)
    pieces, rest = [], scale
    for _ in range(3):
        pieces.append(rest.astype(bf16).astype(f32))
        rest = rest - pieces[-1]
    tokens = scale.shape[1]
    pieces.append(jnp.zeros((16 - len(pieces), tokens), f32))
    scale = transposed_dot(jnp.concatenate(pieces, axis=0).astype(bf16), jnp.ones((16, 128), bf16))
    width = gated_refs[0].shape[1]
    core = lax.rem(lax.axis_index("seq"), 2)
    sides = (core, 1 - core) if len(gated_refs) == 2 else (0,)
    chunk = tokens // NORM_CHUNKS
    copies = []
    for index in range(NORM_CHUNKS):
        rows = slice(index * chunk, (index + 1) * chunk)
        for ref, side in zip(gated_refs, sides):
            for col in range(0, width, 128):
                at = pl.ds(pl.multiple_of(side * width + col, 128), 128)
                out_ref[rows, at] = (ref[rows, col : col + 128] * scale[rows]).astype(bf16)
        copies.append(pltpu.make_async_copy(out_ref.at[rows], out_hbm.at[rows], semaphores.at[index]))
        copies[-1].start()
    for copy in copies:
        copy.wait()


def call(kernel, out_shape, args, flops=0, bytes_accessed=0, hbm=0, scratch=None, out_space=pltpu.VMEM):
    specs = [pl.BlockSpec(memory_space=pl.ANY)] * hbm + [pl.BlockSpec(memory_space=pltpu.VMEM)] * (len(args) - hbm)
    args = [pltpu.with_memory_space_constraint(arg, pltpu.HBM) for arg in args[:hbm]] + list(args[hbm:])
    if scratch is None:
        scratch = [pltpu.VMEM(arg.shape, arg.dtype) for arg in args[:hbm]]
        scratch += [pltpu.SemaphoreType.DMA((hbm,))] if hbm else []
    return pl.pallas_call(
        kernel,
        out_shape=out_shape,
        in_specs=specs,
        out_specs=jax.tree.map(lambda _: pl.BlockSpec(memory_space=out_space), out_shape),
        scratch_shapes=scratch,
        compiler_params=pltpu.CompilerParams(vmem_limit_bytes=VMEM_LIMIT),
        cost_estimate=pl.CostEstimate(flops=flops, bytes_accessed=bytes_accessed, transcendentals=0),
    )(*args)


def shaped(shape, dtype):
    return jax.ShapeDtypeStruct(shape, dtype)


def flip(array, axis, mask):
    return lax.ppermute(array, axis, [(i, i ^ mask) for i in range(lax.axis_size(axis))])


def from_each(array, axis, first=1, stride=1):
    masks = sorted(range(first, lax.axis_size(axis), stride), key=lambda mask: (mask == 1, mask))
    return [flip(array, axis, mask) for mask in masks]


def merged(older, newer, size):
    older, newer = older.astype(f32), newer.astype(f32)
    decay = newer[size : size + 1]
    return jnp.concatenate([older[:size] * decay + newer[:size], older[size:] * decay], axis=0).astype(bf16)


def far_states(shard, size):
    rank = lax.axis_index("seq")
    levels = lax.axis_size("seq").bit_length() - 1
    states = []
    running = jnp.ones((1, shard.shape[1]), f32)
    for level in range(levels):
        theirs = flip(shard, "seq", 1 << level)
        upper = jnp.right_shift(rank, level) % 2 == 1
        states.append(jnp.where(upper, theirs[:size].astype(f32) * running, 0.0).astype(bf16))
        running = jnp.where(upper, running * theirs[size : size + 1].astype(f32), running)
        shard = merged(jnp.where(upper, theirs, shard), jnp.where(upper, shard, theirs), size)
    return states


def on_device(inputs, gate, input_map, output_map, step, decay_rate, level_mix, skip, norm_gain):
    tokens, width = inputs.shape
    heads = step.shape[0]
    parts = lax.axis_size("head")
    levels = lax.axis_size("seq").bit_length() - 1
    size = input_map.shape[0] * parts
    groups = tokens // GROUP
    spans = local_spans(groups)
    dense = 2 * tokens * GROUP * width
    area = tokens * width
    others = from_each(input_map, "head")
    kept = inputs, gate, level_mix, skip[None, :], input_map, output_map
    scaled, cum, *kept = call(
        prepare_kernel,
        (
            *(shaped((tokens, width), bf16), shaped((heads, tokens), f32)),
            *(shaped(array.shape, array.dtype) for array in kept),
        ),
        (step, decay_rate[None, :], *kept),
        flops=16 * dense,
        bytes_accessed=4 * area,
        hbm=8,
        scratch=[pltpu.VMEM(step.shape, f32), pltpu.VMEM((1, heads), f32), pltpu.SemaphoreType.DMA((8,))],
    )
    inputs, gate, level_mix, skip, input_map, output_map = kept
    in_maps = [input_map, *others]
    shard_shape = shaped((size + DECAY_ROWS, width), bf16)
    span_shape = [shaped((len(spans) * size, width), bf16)] if spans else []
    shard, *span_states = call(
        functools.partial(states_kernel, parts),
        (shard_shape, *span_shape),
        (*in_maps, scaled, cum),
        flops=dense,
        bytes_accessed=4 * area,
    )
    pairs = lax.axis_size("seq") == 8 and parts == 4
    if pairs:
        theirs = flip(shard, "seq", 1)
        message = call(
            functools.partial(merge_kernel, size),
            shaped((size + DECAY_ROWS, width // 2), bf16),
            (shard, theirs),
            flops=0,
            bytes_accessed=area,
        )
    else:
        message = shard
    output_map, _ = lax.optimization_barrier((output_map, shard))
    beside = flip(output_map, "head", 1)
    rows = output_map.shape[0]
    if rows % 16 == 0:
        both = call(
            join_kernel,
            shaped((2 * rows, tokens), bf16),
            (output_map, beside),
            bytes_accessed=8 * rows * tokens,
        )
    else:
        both = jnp.concatenate([output_map, beside], axis=0)
    out_maps = [both, *from_each(both, "head", first=2, stride=2)]
    factor_shape = [shaped((len(spans), GROUP, width), bf16)] if spans else []
    base, own_factor, far, *span_factors = call(
        functools.partial(factor_kernel, spans, levels),
        (
            *(shaped((tokens, width), f32), shaped((tokens, width), f32)),
            *(shaped((levels, tokens, width), bf16), *factor_shape),
        ),
        (inputs, gate, level_mix, skip, cum, message),
        flops=21 * dense // 4,
        bytes_accessed=0,
    )
    near_args = base, own_factor, far, theirs if pairs else message, scaled, *span_states, *span_factors
    near_shape = shaped((tokens, width // 2 if pairs else width), f32)
    received = [flip(message, "seq", mask) for mask in (6, 4, 2)] if pairs else [message]
    near, turned, scores = call(
        functools.partial(near_kernel, parts, spans, pairs),
        (near_shape, shaped((tokens, size), bf16), shaped((tokens, GROUP), bf16)),
        (received[0], *in_maps, *out_maps, *near_args),
        flops=4 * dense,
    )
    gain = norm_gain[None, :]
    sums_shape = shaped((1, tokens), f32)
    if pairs:
        *received, near, far = lax.optimization_barrier((*received, near, far))
        own = call(
            functools.partial(combine_kernel, size),
            shaped((2 * size, width // 2), bf16),
            received[::-1],
            bytes_accessed=area,
        )
        other = flip(own, "seq", 1)
        other_near = call(
            functools.partial(other_near_kernel, spans), near_shape, (scores, turned, own, *near_args), flops=dense
        )
        gated_shape = shaped((tokens, width // 2), f32)
        own_gated, own_squares = call(
            functools.partial(far_kernel_of_half, True),
            (gated_shape, shaped((tokens, 128), f32)),
            (turned, near, far, gain, theirs, own),
            flops=2 * dense,
            bytes_accessed=6 * area,
        )
        other_gated, sums = call(
            functools.partial(far_kernel_of_half, False),
            (gated_shape, sums_shape),
            (turned, other_near, far, gain, theirs, other, own_squares),
            flops=2 * dense,
            bytes_accessed=6 * area,
        )
        gated = (own_gated, other_gated)
    else:
        *gated, sums = call(
            far_kernel,
            (shaped((tokens, width), f32), sums_shape),
            (turned, near, far, gain, *far_states(shard, size)),
            flops=4 * dense,
            bytes_accessed=12 * area,
        )
    last = [sums, *from_each(sums, "head")]
    return call(
        functools.partial(norm_kernel, len(last), width * parts),
        shaped((tokens, width), bf16),
        (*last, *gated),
        flops=dense,
        bytes_accessed=6 * area,
        scratch=[pltpu.VMEM((tokens, width), bf16), pltpu.SemaphoreType.DMA((NORM_CHUNKS,))],
        out_space=pl.ANY,
    )


def solution(mesh):
    return jax.shard_map(
        on_device,
        mesh=mesh,
        in_specs=(
            P("seq", "head"),
            P("seq", "head"),
            P("head", "seq"),
            P("head", "seq"),
            P("head", "seq"),
            P("head"),
            P(None, "head", "seq"),
            P("head"),
            P("head"),
        ),
        out_specs=P("seq", "head"),
        check_vma=False,
    )
```

```python
import functools

import jax
import jax.numpy as jnp
from jax import lax
from jax.experimental import pallas as pl
from jax.experimental.pallas import tpu as pltpu
from jax.sharding import PartitionSpec as P

P_SIZE = 64
GROUP = 256
DECAY_ROWS = 16
BLOCK = 256
NORM_CHUNKS = 8
FIRST_HOP = 2
VMEM_LIMIT = 40 * 1024 * 1024

f32, bf16 = jnp.float32, jnp.bfloat16
HIGHEST = lax.Precision.HIGHEST
TRANSPOSED = (((0,), (0,)), ((), ()))


def expander(heads, width, copies):
    row = lax.broadcasted_iota(jnp.int32, (copies * heads, width), 0)
    col = lax.broadcasted_iota(jnp.int32, (copies * heads, width), 1)
    return jnp.where(lax.rem(row, heads) == lax.div(col, P_SIZE), 1.0, 0.0)


def far_first_masks(size):
    return (*range(2, size), 1)


def pair_masks(size):
    return tuple(mask for mask in range(1, size) if not mask & FIRST_HOP)


def two_parts(factor):
    high = factor.astype(bf16).astype(f32)
    return jnp.concatenate([high, factor - high], axis=0).astype(bf16)


def transposed_dot(left, right):
    return lax.dot_general(left, right, TRANSPOSED, preferred_element_type=f32)


def head_row(heads, width, column):
    return jnp.sum(expander(heads, width, 1) * column, axis=0, keepdims=True)


def group_slice(group):
    return slice(group * GROUP, (group + 1) * GROUP)


def blocks_of(width):
    return [slice(at, at + BLOCK) for at in range(0, width, BLOCK)]


def local_spans(groups):
    spans = []
    for later in range(groups):
        for bit in range(groups.bit_length() - 1):
            if later >> bit & 1:
                start = later >> bit + 1 << bit + 1
                spans.append((later, bit, start, start + 2**bit))
    return spans


def column_of(row):
    size = row.shape[1]
    at = lax.broadcasted_iota(jnp.int32, (size, size), 0) == lax.broadcasted_iota(jnp.int32, (size, size), 1)
    return jnp.sum(jnp.where(at, row, 0.0), axis=1, keepdims=True)


def map_rows(maps):
    if all(rows.shape[0] % 16 == 0 for rows in maps):
        return jnp.concatenate([rows[...] for rows in maps], axis=0)
    return jnp.concatenate([rows[...].astype(f32) for rows in maps], axis=0).astype(bf16)


def out_map_rows(map_refs, parts):
    rows = map_refs[0].shape[0] // 2
    pairs = [ref if rows % 16 == 0 else ref[...].astype(f32) for ref in map_refs]
    sent = (0, *pair_masks(parts))
    picked = []
    for mask in (0, *far_first_masks(parts)):
        pair = pairs[sent.index(mask & ~FIRST_HOP)]
        at = slice(rows, 2 * rows) if mask & FIRST_HOP else slice(0, rows)
        picked.append(pair.at[at] if rows % 16 == 0 else pair[at])
    return map_rows(picked)


def fetch(sources, targets, semaphores):
    copies = [
        pltpu.make_async_copy(source, target, semaphores.at[index])
        for index, (source, target) in enumerate(zip(sources, targets))
    ]
    for copy in copies:
        copy.start()
    return copies


def prepare_kernel(*refs):
    sources, (scaled_ref, cum_ref), kept_refs = refs[:8], refs[8:10], refs[10:16]
    step_ref, rate_ref, semaphores = refs[16:]
    inputs_ref = kept_refs[0]
    copies = fetch(sources, (step_ref, rate_ref, *kept_refs), semaphores)
    heads, tokens = step_ref.shape
    width = inputs_ref.shape[1]
    row = lax.broadcasted_iota(jnp.int32, (GROUP, GROUP), 0)
    col = lax.broadcasted_iota(jnp.int32, (GROUP, GROUP), 1)
    until = jnp.where(row <= col, 1.0, 0.0)
    expand = expander(heads, width, 2).astype(bf16)
    copies[0].wait()
    copies[1].wait()
    step = step_ref[...]
    log_decay = -step * column_of(rate_ref[...])
    factors = []
    for group in range(tokens // GROUP):
        at = group_slice(group)
        cum = jnp.dot(log_decay[:, at], until, precision=HIGHEST, preferred_element_type=f32)
        cum_ref[:, at] = cum
        factors.append(two_parts(jnp.exp(-cum) * step[:, at]))
    factor = jnp.concatenate(factors, axis=1)
    copies[2].wait()
    for cols in blocks_of(width):
        scale = transposed_dot(factor, expand[:, cols])
        scaled_ref[:, cols] = (inputs_ref[:, cols].astype(f32) * scale).astype(bf16)
    for copy in copies[3:]:
        copy.wait()


def join_kernel(mine_ref, theirs_ref, both_ref):
    rows = mine_ref.shape[0]
    both_ref[:rows, :] = mine_ref[...]
    both_ref[rows:, :] = theirs_ref[...]


def states_kernel(parts, *refs):
    map_refs, (scaled_ref, cum_ref), out_refs = refs[:parts], refs[parts : parts + 2], refs[parts + 2 :]
    shard_ref = out_refs[0]
    heads, tokens = cum_ref.shape
    width = scaled_ref.shape[1]
    in_map = map_rows(map_refs)
    size = in_map.shape[0]
    cum = cum_ref[...]
    states, decays = [], []
    for group in range(tokens // GROUP):
        at = group_slice(group)
        decay = head_row(heads, width, jnp.exp(cum[:, at.stop - 1 : at.stop]))
        raw = jnp.dot(in_map[:, at], scaled_ref[at, :], preferred_element_type=f32)
        states.append(raw * decay)
        decays.append(decay)
    total, decay = states[0], decays[0]
    for group in range(1, len(states)):
        total = total * decays[group] + states[group]
        decay = decay * decays[group]
    shard_ref[:size, :] = total.astype(bf16)
    shard_ref[size:, :] = jnp.broadcast_to(decay, (DECAY_ROWS, width)).astype(bf16)
    for index, (later, _, start, stop) in enumerate(local_spans(len(states))):
        span = states[start]
        for group in range(start + 1, later):
            span = span * decays[group]
            if group < stop:
                span = span + states[group]
        out_refs[1][index * size : (index + 1) * size, :] = span.astype(bf16)


def merge_kernel(size, mine_ref, theirs_ref, pair_ref):
    core = lax.rem(lax.axis_index("seq"), 2)
    half = pair_ref.shape[1]
    mine = jnp.where(core == 1, mine_ref[:, half:], mine_ref[:, :half])
    theirs = jnp.where(core == 1, theirs_ref[:, half:], theirs_ref[:, :half])
    older = jnp.where(core == 1, theirs, mine).astype(f32)
    newer = jnp.where(core == 1, mine, theirs).astype(f32)
    decay = newer[size : size + 1]
    pair_ref[:size, :] = (older[:size] * decay + newer[:size]).astype(bf16)
    pair_ref[size:, :] = (older[size:] * decay).astype(bf16)


def factor_kernel(spans, levels, *refs):
    inputs_ref, gate_ref, mix_ref, skip_ref, cum_ref, _ = refs[:6]
    base_ref, own_ref, far_ref = refs[6:9]
    span_refs = refs[9:]
    heads, tokens = cum_ref.shape
    width = inputs_ref.shape[1]
    groups = tokens // GROUP
    first = groups.bit_length()
    expand = expander(heads, width, 2).astype(bf16)
    skip = head_row(heads, width, column_of(skip_ref[...]))
    before = jnp.zeros((heads, 1), f32)
    for group in range(groups):
        at = group_slice(group)
        cum = cum_ref[:, at]
        decay = jnp.exp(cum)
        own_mix = two_parts(mix_ref[0, :, at] * decay)
        span_mixes = [
            (index, two_parts(mix_ref[1 + bit, :, at] * decay))
            for index, (later, bit, _, _) in enumerate(spans)
            if later == group
        ]
        decay = jnp.exp(cum + before)
        before = before + cum[:, GROUP - 1 : GROUP]
        far_mixes = [two_parts(mix_ref[first + level, :, at] * decay) for level in range(levels)]
        for cols in blocks_of(width):
            gate = gate_ref[at, cols].astype(f32)
            swish = gate / (1.0 + jnp.exp(-gate))
            base_ref[at, cols] = skip[:, cols] * inputs_ref[at, cols].astype(f32) * swish
            own_ref[at, cols] = transposed_dot(own_mix, expand[:, cols]) * swish
            for level, mix in enumerate(far_mixes):
                far_ref[level, at, cols] = (transposed_dot(mix, expand[:, cols]) * swish).astype(bf16)
            for index, mix in span_mixes:
                span_refs[0][index, :, cols] = (transposed_dot(mix, expand[:, cols]) * swish).astype(bf16)


def near_body(spans, paired, start, scores_ref, turned_ref, refs, near_ref):
    base_ref, own_ref, far_ref, core_ref, scaled_ref = refs[:5]
    span_refs = refs[5:]
    tokens, size = turned_ref.shape
    has_core = lax.rem(lax.axis_index("seq"), 2) == 1
    for group in range(tokens // GROUP):
        at = group_slice(group)
        for cols in blocks_of(near_ref.shape[1]):
            of = pl.ds(pl.multiple_of(start + cols.start, BLOCK), BLOCK)
            own = jnp.dot(scores_ref[at, :], scaled_ref[at, of], preferred_element_type=f32)
            total = base_ref[at, of] + own_ref[at, of] * own
            for index, (later, _, _, _) in enumerate(spans):
                if later == group:
                    rows = slice(index * size, (index + 1) * size)
                    reach = jnp.dot(turned_ref[at, :], span_refs[0][rows, of], preferred_element_type=f32)
                    total = total + span_refs[1][index, :, of].astype(f32) * reach
            if paired:
                reach = jnp.dot(turned_ref[at, :], core_ref[:size, of], preferred_element_type=f32)
                reach = jnp.where(has_core, reach, 0.0)
                total = total + far_ref[0, at, of].astype(f32) * reach
            near_ref[at, cols] = total


def near_kernel(parts, spans, paired, *refs):
    count = parts + parts // 2
    in_refs, out_refs, rest = refs[:parts], refs[parts:count], refs[count:-3]
    near_ref, turned_ref, scores_ref = refs[-3:]
    in_map = map_rows(in_refs)
    turned = jnp.transpose(out_map_rows(out_refs, parts))
    turned_ref[...] = turned
    row = lax.broadcasted_iota(jnp.int32, (GROUP, GROUP), 0)
    col = lax.broadcasted_iota(jnp.int32, (GROUP, GROUP), 1)
    for group in range(turned.shape[0] // GROUP):
        at = group_slice(group)
        scores = jnp.dot(turned[at], in_map[:, at], preferred_element_type=f32)
        scores_ref[at, :] = jnp.where(row >= col, scores, 0.0).astype(bf16)
    start = lax.rem(lax.axis_index("seq"), 2) * near_ref.shape[1] if paired else 0
    near_body(spans, paired, start, scores_ref, turned_ref, rest, near_ref)


def other_near_kernel(spans, scores_ref, turned_ref, _, *refs):
    near_ref = refs[-1]
    start = (1 - lax.rem(lax.axis_index("seq"), 2)) * near_ref.shape[1]
    near_body(spans, True, start, scores_ref, turned_ref, refs[:-1], near_ref)


def far_body(turned_ref, near_ref, far_ref, gain_ref, start, columns, levels, state_of, gated_ref):
    tokens = far_ref.shape[1]
    squares = jnp.zeros((tokens, 128), f32)
    for cols in blocks_of(columns):
        at = pl.ds(pl.multiple_of(start + cols.start, BLOCK), BLOCK)
        total = near_ref[:, cols]
        for level in levels:
            state = state_of(level, cols, at).astype(bf16)
            reach = jnp.dot(turned_ref[...], state, preferred_element_type=f32)
            total = total + far_ref[level, :, at].astype(f32) * reach
        gated_ref[:, cols] = total * gain_ref[:, at]
        total = total * total
        for part in range(0, BLOCK, 128):
            squares = squares + total[:, part : part + 128]
    return squares


def row_sums(squares):
    high = squares.astype(bf16)
    low = (squares - high.astype(f32)).astype(bf16)
    parts = jnp.concatenate([high, low], axis=1)
    ones = jnp.ones((16, parts.shape[1]), bf16)
    return lax.dot_general(ones, parts, (((1,), (1,)), ((), ())), preferred_element_type=f32)[:1]


def far_kernel(turned_ref, near_ref, far_ref, gain_ref, *refs):
    state_refs = refs[:-2]
    gated_ref, sums_ref = refs[-2:]

    def state_of(level, cols, _):
        return state_refs[level][:, cols]

    width = near_ref.shape[1]
    levels = range(far_ref.shape[0])
    squares = far_body(turned_ref, near_ref, far_ref, gain_ref, 0, width, levels, state_of, gated_ref)
    sums_ref[...] = row_sums(squares)


def combine_kernel(size, x_ref, y_ref, diagonal_ref, spans_ref):
    rank = lax.axis_index("seq")
    along_x = lax.rem(lax.div(rank, 2), 2)
    along_y = lax.div(rank, 4)

    def parts_of(ref):
        return ref[:size, :].astype(f32), ref[size:, :].astype(f32)[:1]

    x_state, x_decay = parts_of(x_ref)
    y_state, y_decay = parts_of(y_ref)
    d_state, d_decay = parts_of(diagonal_ref)
    newer = jnp.where(along_x == 1, y_state, d_state)
    newer_decay = jnp.where(along_x == 1, y_decay, d_decay)
    older = jnp.where(along_x == 1, d_state, y_state)
    running = jnp.where(along_x == 1, x_decay, 1.0)
    running = jnp.where(along_y == 1, running, 0.0)
    spans_ref[:size, :] = jnp.where(along_x == 1, x_state, 0.0).astype(bf16)
    spans_ref[size:, :] = ((older * newer_decay + newer) * running).astype(bf16)


def far_kernel_of_half(own, *refs):
    turned_ref, near_ref, far_ref, gain_ref, core_ref, spans_ref = refs[:6]
    gated_ref, sums_ref = refs[-2:]
    size = turned_ref.shape[1]
    core = lax.rem(lax.axis_index("seq"), 2)
    half = spans_ref.shape[1]
    start = (core if own else 1 - core) * half

    def state_of(level, cols, at):
        core_decay = core_ref[size:, at].astype(f32)[:1]
        running = jnp.where(core == 1, core_decay, 1.0)
        return spans_ref[(level - 1) * size : level * size, cols].astype(f32) * running

    squares = far_body(turned_ref, near_ref, far_ref, gain_ref, start, half, (1, 2), state_of, gated_ref)
    sums_ref[...] = squares if own else row_sums(squares + refs[6][...])


def norm_kernel(parts, columns, *refs):
    gated_refs, (out_hbm, out_ref, semaphores) = refs[parts:-3], refs[-3:]
    total = refs[0][...]
    for ref in refs[1:parts]:
        total = total + ref[...]
    scale = lax.rsqrt(total / columns + 1e-05)
    pieces, rest = [], scale
    for _ in range(3):
        pieces.append(rest.astype(bf16).astype(f32))
        rest = rest - pieces[-1]
    tokens = scale.shape[1]
    pieces.append(jnp.zeros((16 - len(pieces), tokens), f32))
    scale = transposed_dot(jnp.concatenate(pieces, axis=0).astype(bf16), jnp.ones((16, 128), bf16))
    width = gated_refs[0].shape[1]
    core = lax.rem(lax.axis_index("seq"), 2)
    sides = (core, 1 - core) if len(gated_refs) == 2 else (0,)
    chunk = tokens // NORM_CHUNKS
    copies = []
    for index in range(NORM_CHUNKS):
        rows = slice(index * chunk, (index + 1) * chunk)
        for ref, side in zip(gated_refs, sides):
            for col in range(0, width, 128):
                at = pl.ds(pl.multiple_of(side * width + col, 128), 128)
                out_ref[rows, at] = (ref[rows, col : col + 128] * scale[rows]).astype(bf16)
        copies.append(pltpu.make_async_copy(out_ref.at[rows], out_hbm.at[rows], semaphores.at[index]))
        copies[-1].start()
    for copy in copies:
        copy.wait()


def call(kernel, out_shape, args, flops=0, bytes_accessed=0, hbm=0, scratch=None, out_space=pltpu.VMEM):
    specs = [pl.BlockSpec(memory_space=pl.ANY)] * hbm + [pl.BlockSpec(memory_space=pltpu.VMEM)] * (len(args) - hbm)
    args = [pltpu.with_memory_space_constraint(arg, pltpu.HBM) for arg in args[:hbm]] + list(args[hbm:])
    if scratch is None:
        scratch = [pltpu.VMEM(arg.shape, arg.dtype) for arg in args[:hbm]]
        scratch += [pltpu.SemaphoreType.DMA((hbm,))] if hbm else []
    return pl.pallas_call(
        kernel,
        out_shape=out_shape,
        in_specs=specs,
        out_specs=jax.tree.map(lambda _: pl.BlockSpec(memory_space=out_space), out_shape),
        scratch_shapes=scratch,
        compiler_params=pltpu.CompilerParams(vmem_limit_bytes=VMEM_LIMIT),
        cost_estimate=pl.CostEstimate(flops=flops, bytes_accessed=bytes_accessed, transcendentals=0),
    )(*args)


def shaped(shape, dtype):
    return jax.ShapeDtypeStruct(shape, dtype)


def flip(array, axis, mask):
    return lax.ppermute(array, axis, [(i, i ^ mask) for i in range(lax.axis_size(axis))])


def from_each(array, axis, masks):
    return [flip(array, axis, mask) for mask in masks]


def merged(older, newer, size):
    older, newer = older.astype(f32), newer.astype(f32)
    decay = newer[size : size + 1]
    return jnp.concatenate([older[:size] * decay + newer[:size], older[size:] * decay], axis=0).astype(bf16)


def far_states(shard, size):
    rank = lax.axis_index("seq")
    levels = lax.axis_size("seq").bit_length() - 1
    states = []
    running = jnp.ones((1, shard.shape[1]), f32)
    for level in range(levels):
        theirs = flip(shard, "seq", 1 << level)
        upper = jnp.right_shift(rank, level) % 2 == 1
        states.append(jnp.where(upper, theirs[:size].astype(f32) * running, 0.0).astype(bf16))
        running = jnp.where(upper, running * theirs[size : size + 1].astype(f32), running)
        shard = merged(jnp.where(upper, theirs, shard), jnp.where(upper, shard, theirs), size)
    return states


def on_device(inputs, gate, input_map, output_map, step, decay_rate, level_mix, skip, norm_gain):
    tokens, width = inputs.shape
    heads = step.shape[0]
    parts = lax.axis_size("head")
    levels = lax.axis_size("seq").bit_length() - 1
    size = input_map.shape[0] * parts
    groups = tokens // GROUP
    spans = local_spans(groups)
    dense = 2 * tokens * GROUP * width
    area = tokens * width
    others = from_each(input_map, "head", far_first_masks(parts))
    kept = inputs, gate, level_mix, skip[None, :], input_map, output_map
    scaled, cum, *kept = call(
        prepare_kernel,
        (
            *(shaped((tokens, width), bf16), shaped((heads, tokens), f32)),
            *(shaped(array.shape, array.dtype) for array in kept),
        ),
        (step, decay_rate[None, :], *kept),
        flops=16 * dense,
        bytes_accessed=4 * area,
        hbm=8,
        scratch=[pltpu.VMEM(step.shape, f32), pltpu.VMEM((1, heads), f32), pltpu.SemaphoreType.DMA((8,))],
    )
    inputs, gate, level_mix, skip, input_map, output_map = kept
    in_maps = [input_map, *others]
    shard_shape = shaped((size + DECAY_ROWS, width), bf16)
    span_shape = [shaped((len(spans) * size, width), bf16)] if spans else []
    shard, *span_states = call(
        functools.partial(states_kernel, parts),
        (shard_shape, *span_shape),
        (*in_maps, scaled, cum),
        flops=dense,
        bytes_accessed=4 * area,
    )
    pairs = lax.axis_size("seq") == 8 and parts == 4
    if pairs:
        theirs = flip(shard, "seq", 1)
        message = call(
            functools.partial(merge_kernel, size),
            shaped((size + DECAY_ROWS, width // 2), bf16),
            (shard, theirs),
            flops=0,
            bytes_accessed=area,
        )
    else:
        message = shard
    output_map, _ = lax.optimization_barrier((output_map, shard))
    beside = flip(output_map, "head", FIRST_HOP)
    rows = output_map.shape[0]
    if rows % 16 == 0:
        both = call(
            join_kernel,
            shaped((2 * rows, tokens), bf16),
            (output_map, beside),
            bytes_accessed=8 * rows * tokens,
        )
    else:
        both = jnp.concatenate([output_map, beside], axis=0)
    out_maps = [both, *from_each(both, "head", pair_masks(parts))]
    factor_shape = [shaped((len(spans), GROUP, width), bf16)] if spans else []
    base, own_factor, far, *span_factors = call(
        functools.partial(factor_kernel, spans, levels),
        (
            *(shaped((tokens, width), f32), shaped((tokens, width), f32)),
            *(shaped((levels, tokens, width), bf16), *factor_shape),
        ),
        (inputs, gate, level_mix, skip, cum, message),
        flops=21 * dense // 4,
        bytes_accessed=0,
    )
    near_args = base, own_factor, far, theirs if pairs else message, scaled, *span_states, *span_factors
    near_shape = shaped((tokens, width // 2 if pairs else width), f32)
    near, turned, scores = call(
        functools.partial(near_kernel, parts, spans, pairs),
        (near_shape, shaped((tokens, size), bf16), shaped((tokens, GROUP), bf16)),
        (*in_maps, *out_maps, *near_args),
    )
    gain = norm_gain[None, :]
    sums_shape = shaped((1, tokens), f32)
    if pairs:
        received = [flip(message, "seq", mask) for mask in (6, 4, 2)]
        *received, near, far = lax.optimization_barrier((*received, near, far))
        own = call(
            functools.partial(combine_kernel, size),
            shaped((2 * size, width // 2), bf16),
            received[::-1],
            bytes_accessed=area,
        )
        other = flip(own, "seq", 1)
        other_near = call(
            functools.partial(other_near_kernel, spans), near_shape, (scores, turned, own, *near_args), flops=dense
        )
        gated_shape = shaped((tokens, width // 2), f32)
        own_gated, own_squares = call(
            functools.partial(far_kernel_of_half, True),
            (gated_shape, shaped((tokens, 128), f32)),
            (turned, near, far, gain, theirs, own),
            flops=2 * dense,
            bytes_accessed=6 * area,
        )
        other_gated, sums = call(
            functools.partial(far_kernel_of_half, False),
            (gated_shape, sums_shape),
            (turned, other_near, far, gain, theirs, other, own_squares),
            flops=2 * dense,
            bytes_accessed=6 * area,
        )
        gated = (own_gated, other_gated)
    else:
        *gated, sums = call(
            far_kernel,
            (shaped((tokens, width), f32), sums_shape),
            (turned, near, far, gain, *far_states(shard, size)),
            flops=4 * dense,
            bytes_accessed=12 * area,
        )
    last = [sums, *from_each(sums, "head", far_first_masks(parts))]
    return call(
        functools.partial(norm_kernel, len(last), width * parts),
        shaped((tokens, width), bf16),
        (*last, *gated),
        flops=dense,
        bytes_accessed=6 * area,
        scratch=[pltpu.VMEM((tokens, width), bf16), pltpu.SemaphoreType.DMA((NORM_CHUNKS,))],
        out_space=pl.ANY,
    )


def solution(mesh):
    return jax.shard_map(
        on_device,
        mesh=mesh,
        in_specs=(
            P("seq", "head"),
            P("seq", "head"),
            P("head", "seq"),
            P("head", "seq"),
            P("head", "seq"),
            P("head"),
            P(None, "head", "seq"),
            P("head"),
            P("head"),
        ),
        out_specs=P("seq", "head"),
        check_vma=False,
    )
```

```python
import functools

import jax
import jax.numpy as jnp
from jax import lax
from jax.experimental import pallas as pl
from jax.experimental.pallas import tpu as pltpu
from jax.sharding import PartitionSpec as P

P_SIZE = 64
GROUP = 256
DECAY_ROWS = 8
BLOCK = 256
NORM_CHUNKS = 4
FIRST_HOP = 2
VMEM_LIMIT = 40 * 1024 * 1024

f32, bf16 = jnp.float32, jnp.bfloat16
HIGHEST = lax.Precision.HIGHEST
TRANSPOSED = (((0,), (0,)), ((), ()))


def expander(heads, width, copies):
    row = lax.broadcasted_iota(jnp.int32, (copies * heads, width), 0)
    col = lax.broadcasted_iota(jnp.int32, (copies * heads, width), 1)
    return jnp.where(lax.rem(row, heads) == lax.div(col, P_SIZE), 1.0, 0.0)


def far_first_masks(size):
    return (*range(2, size), 1)


def pair_masks(size):
    return tuple(mask for mask in range(1, size) if not mask & FIRST_HOP)


def two_parts(factor):
    high = factor.astype(bf16).astype(f32)
    return jnp.concatenate([high, factor - high], axis=0).astype(bf16)


def transposed_dot(left, right):
    return lax.dot_general(left, right, TRANSPOSED, preferred_element_type=f32)


def head_row(heads, width, column):
    return jnp.sum(expander(heads, width, 1) * column, axis=0, keepdims=True)


def group_slice(group):
    return slice(group * GROUP, (group + 1) * GROUP)


def blocks_of(width):
    return [slice(at, at + BLOCK) for at in range(0, width, BLOCK)]


def local_spans(groups):
    spans = []
    for later in range(groups):
        for bit in range(groups.bit_length() - 1):
            if later >> bit & 1:
                start = later >> bit + 1 << bit + 1
                spans.append((later, bit, start, start + 2**bit))
    return spans


def column_of(row):
    size = row.shape[1]
    at = lax.broadcasted_iota(jnp.int32, (size, size), 0) == lax.broadcasted_iota(jnp.int32, (size, size), 1)
    return jnp.sum(jnp.where(at, row, 0.0), axis=1, keepdims=True)


def map_rows(maps):
    if all(rows.shape[0] % 16 == 0 for rows in maps):
        return jnp.concatenate([rows[...] for rows in maps], axis=0)
    return jnp.concatenate([rows[...].astype(f32) for rows in maps], axis=0).astype(bf16)


def out_map_rows(map_refs, parts):
    rows = map_refs[0].shape[0] // 2
    pairs = [ref if rows % 16 == 0 else ref[...].astype(f32) for ref in map_refs]
    sent = (0, *pair_masks(parts))
    picked = []
    for mask in (0, *far_first_masks(parts)):
        pair = pairs[sent.index(mask & ~FIRST_HOP)]
        at = slice(rows, 2 * rows) if mask & FIRST_HOP else slice(0, rows)
        picked.append(pair.at[at] if rows % 16 == 0 else pair[at])
    return map_rows(picked)


def fetch(sources, targets, semaphores):
    copies = [
        pltpu.make_async_copy(source, target, semaphores.at[index])
        for index, (source, target) in enumerate(zip(sources, targets))
    ]
    for copy in copies:
        copy.start()
    return copies


def prepare_kernel(*refs):
    sources, (scaled_ref, cum_ref), kept_refs = refs[:8], refs[8:10], refs[10:16]
    step_ref, rate_ref, semaphores = refs[16:]
    inputs_ref = kept_refs[0]
    copies = fetch(sources, (step_ref, rate_ref, *kept_refs), semaphores)
    heads, tokens = step_ref.shape
    width = inputs_ref.shape[1]
    row = lax.broadcasted_iota(jnp.int32, (GROUP, GROUP), 0)
    col = lax.broadcasted_iota(jnp.int32, (GROUP, GROUP), 1)
    until = jnp.where(row <= col, 1.0, 0.0)
    expand = expander(heads, width, 2).astype(bf16)
    copies[0].wait()
    copies[1].wait()
    step = step_ref[...]
    log_decay = -step * column_of(rate_ref[...])
    factors = []
    for group in range(tokens // GROUP):
        at = group_slice(group)
        cum = jnp.dot(log_decay[:, at], until, precision=HIGHEST, preferred_element_type=f32)
        cum_ref[:, at] = cum
        factors.append(two_parts(jnp.exp(-cum) * step[:, at]))
    factor = jnp.concatenate(factors, axis=1)
    copies[2].wait()
    for cols in blocks_of(width):
        scale = transposed_dot(factor, expand[:, cols])
        scaled_ref[:, cols] = (inputs_ref[:, cols].astype(f32) * scale).astype(bf16)
    for copy in copies[3:]:
        copy.wait()


def join_kernel(mine_ref, theirs_ref, both_ref):
    rows = mine_ref.shape[0]
    both_ref[:rows, :] = mine_ref[...]
    both_ref[rows:, :] = theirs_ref[...]


def states_kernel(parts, sides, *refs):
    map_refs, (scaled_ref, cum_ref), out_refs = refs[:parts], refs[parts : parts + 2], refs[parts + 2 :]
    shard_refs = out_refs[:sides]
    heads, tokens = cum_ref.shape
    width = scaled_ref.shape[1]
    in_map = map_rows(map_refs)
    size = in_map.shape[0]
    cum = cum_ref[...]
    states, decays = [], []
    for group in range(tokens // GROUP):
        at = group_slice(group)
        decay = head_row(heads, width, jnp.exp(cum[:, at.stop - 1 : at.stop]))
        raw = jnp.dot(in_map[:, at], scaled_ref[at, :], preferred_element_type=f32)
        states.append(raw * decay)
        decays.append(decay)
    total, decay = states[0], decays[0]
    for group in range(1, len(states)):
        total = total * decays[group] + states[group]
        decay = decay * decays[group]
    columns = width // sides
    core = lax.rem(lax.axis_index("seq"), 2)
    for ref, first in zip(shard_refs, (core == 0, core == 1)):
        at = slice(0, columns)
        ref[:size, :] = jnp.where(first, total[:, at], total[:, width - columns :]).astype(bf16)
        row = jnp.where(first, decay[:, at], decay[:, width - columns :])
        ref[size:, :] = jnp.broadcast_to(row, (DECAY_ROWS, columns)).astype(bf16)
    for index, (later, _, start, stop) in enumerate(local_spans(len(states))):
        span = states[start]
        for group in range(start + 1, later):
            span = span * decays[group]
            if group < stop:
                span = span + states[group]
        out_refs[sides][index * size : (index + 1) * size, :] = span.astype(bf16)


def merge_kernel(size, mine_ref, theirs_ref, pair_ref):
    core = lax.rem(lax.axis_index("seq"), 2)
    mine, theirs = mine_ref[...], theirs_ref[...]
    older = jnp.where(core == 1, theirs, mine).astype(f32)
    newer = jnp.where(core == 1, mine, theirs).astype(f32)
    decay = newer[size : size + 1]
    pair_ref[:size, :] = (older[:size] * decay + newer[:size]).astype(bf16)
    pair_ref[size:, :] = (older[size:] * decay).astype(bf16)


def factor_kernel(spans, levels, *refs):
    inputs_ref, gate_ref, mix_ref, skip_ref, cum_ref, _ = refs[:6]
    base_ref, own_ref, far_ref = refs[6:9]
    span_refs = refs[9:]
    heads, tokens = cum_ref.shape
    width = inputs_ref.shape[1]
    groups = tokens // GROUP
    first = groups.bit_length()
    expand = expander(heads, width, 2).astype(bf16)
    skip = head_row(heads, width, column_of(skip_ref[...]))
    before = jnp.zeros((heads, 1), f32)
    for group in range(groups):
        at = group_slice(group)
        cum = cum_ref[:, at]
        decay = jnp.exp(cum)
        own_mix = two_parts(mix_ref[0, :, at] * decay)
        span_mixes = [
            (index, two_parts(mix_ref[1 + bit, :, at] * decay))
            for index, (later, bit, _, _) in enumerate(spans)
            if later == group
        ]
        decay = jnp.exp(cum + before)
        before = before + cum[:, GROUP - 1 : GROUP]
        far_mixes = [two_parts(mix_ref[first + level, :, at] * decay) for level in range(levels)]
        for cols in blocks_of(width):
            gate = gate_ref[at, cols].astype(f32)
            swish = gate / (1.0 + jnp.exp(-gate))
            base_ref[at, cols] = skip[:, cols] * inputs_ref[at, cols].astype(f32) * swish
            own_ref[at, cols] = transposed_dot(own_mix, expand[:, cols]) * swish
            for level, mix in enumerate(far_mixes):
                far_ref[level, at, cols] = (transposed_dot(mix, expand[:, cols]) * swish).astype(bf16)
            for index, mix in span_mixes:
                span_refs[0][index, :, cols] = (transposed_dot(mix, expand[:, cols]) * swish).astype(bf16)


def near_body(spans, paired, start, scores_ref, turned_ref, refs, near_ref):
    base_ref, own_ref, far_ref, core_ref, scaled_ref = refs[:5]
    span_refs = refs[5:]
    tokens, size = turned_ref.shape
    has_core = lax.rem(lax.axis_index("seq"), 2) == 1
    for group in range(tokens // GROUP):
        at = group_slice(group)
        for cols in blocks_of(near_ref.shape[1]):
            of = pl.ds(pl.multiple_of(start + cols.start, BLOCK), BLOCK)
            own = jnp.dot(scores_ref[at, :], scaled_ref[at, of], preferred_element_type=f32)
            total = base_ref[at, of] + own_ref[at, of] * own
            for index, (later, _, _, _) in enumerate(spans):
                if later == group:
                    rows = slice(index * size, (index + 1) * size)
                    reach = jnp.dot(turned_ref[at, :], span_refs[0][rows, of], preferred_element_type=f32)
                    total = total + span_refs[1][index, :, of].astype(f32) * reach
            if paired:
                reach = jnp.dot(turned_ref[at, :], core_ref[:size, cols], preferred_element_type=f32)
                reach = jnp.where(has_core, reach, 0.0)
                total = total + far_ref[0, at, of].astype(f32) * reach
            near_ref[at, cols] = total


def near_kernel(parts, spans, paired, _, *refs):
    count = parts + parts // 2
    in_refs, out_refs, rest = refs[:parts], refs[parts:count], refs[count:-3]
    near_ref, turned_ref, scores_ref = refs[-3:]
    in_map = map_rows(in_refs)
    turned = jnp.transpose(out_map_rows(out_refs, parts))
    turned_ref[...] = turned
    row = lax.broadcasted_iota(jnp.int32, (GROUP, GROUP), 0)
    col = lax.broadcasted_iota(jnp.int32, (GROUP, GROUP), 1)
    for group in range(turned.shape[0] // GROUP):
        at = group_slice(group)
        scores = jnp.dot(turned[at], in_map[:, at], preferred_element_type=f32)
        scores_ref[at, :] = jnp.where(row >= col, scores, 0.0).astype(bf16)
    start = lax.rem(lax.axis_index("seq"), 2) * near_ref.shape[1] if paired else 0
    near_body(spans, paired, start, scores_ref, turned_ref, rest, near_ref)


def other_near_kernel(spans, scores_ref, turned_ref, _, *refs):
    near_ref = refs[-1]
    start = (1 - lax.rem(lax.axis_index("seq"), 2)) * near_ref.shape[1]
    near_body(spans, True, start, scores_ref, turned_ref, refs[:-1], near_ref)


def far_body(turned_ref, near_ref, far_ref, gain_ref, start, columns, levels, state_of, gated_ref):
    tokens = far_ref.shape[1]
    squares = jnp.zeros((tokens, 128), f32)
    for cols in blocks_of(columns):
        at = pl.ds(pl.multiple_of(start + cols.start, BLOCK), BLOCK)
        total = near_ref[:, cols]
        for level in levels:
            state = state_of(level, cols, at).astype(bf16)
            reach = jnp.dot(turned_ref[...], state, preferred_element_type=f32)
            total = total + far_ref[level, :, at].astype(f32) * reach
        gated_ref[:, cols] = total * gain_ref[:, at]
        total = total * total
        for part in range(0, BLOCK, 128):
            squares = squares + total[:, part : part + 128]
    return squares


def row_sums(squares):
    high = squares.astype(bf16)
    low = (squares - high.astype(f32)).astype(bf16)
    parts = jnp.concatenate([high, low], axis=1)
    ones = jnp.ones((16, parts.shape[1]), bf16)
    return lax.dot_general(ones, parts, (((1,), (1,)), ((), ())), preferred_element_type=f32)[:1]


def far_kernel(turned_ref, near_ref, far_ref, gain_ref, *refs):
    state_refs = refs[:-2]
    gated_ref, sums_ref = refs[-2:]

    def state_of(level, cols, _):
        return state_refs[level][:, cols]

    width = near_ref.shape[1]
    levels = range(far_ref.shape[0])
    squares = far_body(turned_ref, near_ref, far_ref, gain_ref, 0, width, levels, state_of, gated_ref)
    sums_ref[...] = row_sums(squares)


def combine_kernel(size, x_ref, y_ref, diagonal_ref, spans_ref):
    rank = lax.axis_index("seq")
    along_x = lax.rem(lax.div(rank, 2), 2)
    along_y = lax.div(rank, 4)

    def parts_of(ref):
        return ref[:size, :].astype(f32), ref[size:, :].astype(f32)[:1]

    x_state, x_decay = parts_of(x_ref)
    y_state, y_decay = parts_of(y_ref)
    d_state, d_decay = parts_of(diagonal_ref)
    newer = jnp.where(along_x == 1, y_state, d_state)
    newer_decay = jnp.where(along_x == 1, y_decay, d_decay)
    older = jnp.where(along_x == 1, d_state, y_state)
    running = jnp.where(along_x == 1, x_decay, 1.0)
    running = jnp.where(along_y == 1, running, 0.0)
    spans_ref[:size, :] = jnp.where(along_x == 1, x_state, 0.0).astype(bf16)
    spans_ref[size:, :] = ((older * newer_decay + newer) * running).astype(bf16)


def far_kernel_of_half(own, *refs):
    turned_ref, near_ref, far_ref, gain_ref, core_ref, spans_ref = refs[:6]
    gated_ref, sums_ref = refs[-2:]
    size = turned_ref.shape[1]
    core = lax.rem(lax.axis_index("seq"), 2)
    half = spans_ref.shape[1]
    start = (core if own else 1 - core) * half

    def state_of(level, cols, at):
        core_decay = core_ref[size:, cols].astype(f32)[:1]
        running = jnp.where(core == 1, core_decay, 1.0)
        return spans_ref[(level - 1) * size : level * size, cols].astype(f32) * running

    squares = far_body(turned_ref, near_ref, far_ref, gain_ref, start, half, (1, 2), state_of, gated_ref)
    sums_ref[...] = squares if own else row_sums(squares + refs[6][...])


def norm_kernel(parts, columns, *refs):
    gated_refs, (out_hbm, out_ref, semaphores) = refs[parts:-3], refs[-3:]
    total = refs[0][...]
    for ref in refs[1:parts]:
        total = total + ref[...]
    scale = lax.rsqrt(total / columns + 1e-05)
    pieces, rest = [], scale
    for _ in range(3):
        pieces.append(rest.astype(bf16).astype(f32))
        rest = rest - pieces[-1]
    tokens = scale.shape[1]
    pieces.append(jnp.zeros((16 - len(pieces), tokens), f32))
    scale = transposed_dot(jnp.concatenate(pieces, axis=0).astype(bf16), jnp.ones((16, 128), bf16))
    width = gated_refs[0].shape[1]
    core = lax.rem(lax.axis_index("seq"), 2)
    sides = (core, 1 - core) if len(gated_refs) == 2 else (0,)
    chunk = tokens // NORM_CHUNKS
    copies = []
    for index in range(NORM_CHUNKS):
        rows = slice(index * chunk, (index + 1) * chunk)
        for ref, side in zip(gated_refs, sides):
            for col in range(0, width, 128):
                at = pl.ds(pl.multiple_of(side * width + col, 128), 128)
                out_ref[rows, at] = (ref[rows, col : col + 128] * scale[rows]).astype(bf16)
        copies.append(pltpu.make_async_copy(out_ref.at[rows], out_hbm.at[rows], semaphores.at[index]))
        copies[-1].start()
    for copy in copies:
        copy.wait()


def call(kernel, out_shape, args, flops=0, bytes_accessed=0, hbm=0, scratch=None, out_space=pltpu.VMEM):
    specs = [pl.BlockSpec(memory_space=pl.ANY)] * hbm + [pl.BlockSpec(memory_space=pltpu.VMEM)] * (len(args) - hbm)
    args = [pltpu.with_memory_space_constraint(arg, pltpu.HBM) for arg in args[:hbm]] + list(args[hbm:])
    if scratch is None:
        scratch = [pltpu.VMEM(arg.shape, arg.dtype) for arg in args[:hbm]]
        scratch += [pltpu.SemaphoreType.DMA((hbm,))] if hbm else []
    return pl.pallas_call(
        kernel,
        out_shape=out_shape,
        in_specs=specs,
        out_specs=jax.tree.map(lambda _: pl.BlockSpec(memory_space=out_space), out_shape),
        scratch_shapes=scratch,
        compiler_params=pltpu.CompilerParams(vmem_limit_bytes=VMEM_LIMIT),
        cost_estimate=pl.CostEstimate(flops=flops, bytes_accessed=bytes_accessed, transcendentals=0),
    )(*args)


def shaped(shape, dtype):
    return jax.ShapeDtypeStruct(shape, dtype)


def flip(array, axis, mask):
    return lax.ppermute(array, axis, [(i, i ^ mask) for i in range(lax.axis_size(axis))])


def from_each(array, axis, masks):
    return [flip(array, axis, mask) for mask in masks]


def merged(older, newer, size):
    older, newer = older.astype(f32), newer.astype(f32)
    decay = newer[size : size + 1]
    return jnp.concatenate([older[:size] * decay + newer[:size], older[size:] * decay], axis=0).astype(bf16)


def far_states(shard, size):
    rank = lax.axis_index("seq")
    levels = lax.axis_size("seq").bit_length() - 1
    states = []
    running = jnp.ones((1, shard.shape[1]), f32)
    for level in range(levels):
        theirs = flip(shard, "seq", 1 << level)
        upper = jnp.right_shift(rank, level) % 2 == 1
        states.append(jnp.where(upper, theirs[:size].astype(f32) * running, 0.0).astype(bf16))
        running = jnp.where(upper, running * theirs[size : size + 1].astype(f32), running)
        shard = merged(jnp.where(upper, theirs, shard), jnp.where(upper, shard, theirs), size)
    return states


def on_device(inputs, gate, input_map, output_map, step, decay_rate, level_mix, skip, norm_gain):
    tokens, width = inputs.shape
    heads = step.shape[0]
    parts = lax.axis_size("head")
    levels = lax.axis_size("seq").bit_length() - 1
    size = input_map.shape[0] * parts
    groups = tokens // GROUP
    spans = local_spans(groups)
    dense = 2 * tokens * GROUP * width
    area = tokens * width
    others = from_each(input_map, "head", far_first_masks(parts))
    kept = inputs, gate, level_mix, skip[None, :], input_map, output_map
    scaled, cum, *kept = call(
        prepare_kernel,
        (
            *(shaped((tokens, width), bf16), shaped((heads, tokens), f32)),
            *(shaped(array.shape, array.dtype) for array in kept),
        ),
        (step, decay_rate[None, :], *kept),
        flops=16 * dense,
        bytes_accessed=4 * area,
        hbm=8,
        scratch=[pltpu.VMEM(step.shape, f32), pltpu.VMEM((1, heads), f32), pltpu.SemaphoreType.DMA((8,))],
    )
    inputs, gate, level_mix, skip, input_map, output_map = kept
    in_maps = [input_map, *others]
    pairs = lax.axis_size("seq") == 8 and parts == 4
    sides = 2 if pairs else 1
    shard_shape = shaped((size + DECAY_ROWS, width // sides), bf16)
    span_shape = [shaped((len(spans) * size, width), bf16)] if spans else []
    shard, *rest = call(
        functools.partial(states_kernel, parts, sides),
        (*[shard_shape] * sides, *span_shape),
        (*in_maps, scaled, cum),
        flops=dense,
        bytes_accessed=4 * area,
    )
    span_states = rest[sides - 1 :]
    if pairs:
        theirs = flip(rest[0], "seq", 1)
        message = call(
            functools.partial(merge_kernel, size), shard_shape, (shard, theirs), bytes_accessed=area
        )
        other_theirs = flip(lax.optimization_barrier((shard, message))[0], "seq", 1)
    else:
        other_theirs = theirs = message = shard
    output_map, _ = lax.optimization_barrier((output_map, shard))
    beside = flip(output_map, "head", FIRST_HOP)
    rows = output_map.shape[0]
    if rows % 16 == 0:
        both = call(
            join_kernel,
            shaped((2 * rows, tokens), bf16),
            (output_map, beside),
            bytes_accessed=8 * rows * tokens,
        )
    else:
        both = jnp.concatenate([output_map, beside], axis=0)
    out_maps = [both, *from_each(both, "head", pair_masks(parts))]
    factor_shape = [shaped((len(spans), GROUP, width), bf16)] if spans else []
    base, own_factor, far, *span_factors = call(
        functools.partial(factor_kernel, spans, levels),
        (
            *(shaped((tokens, width), f32), shaped((tokens, width), f32)),
            *(shaped((levels, tokens, width), bf16), *factor_shape),
        ),
        (inputs, gate, level_mix, skip, cum, message),
        flops=5 * dense,
        bytes_accessed=0,
    )
    near_args = base, own_factor, far, theirs, scaled, *span_states, *span_factors
    near_shape = shaped((tokens, width // 2 if pairs else width), f32)
    near, turned, scores = call(
        functools.partial(near_kernel, parts, spans, pairs),
        (near_shape, shaped((tokens, size), bf16), shaped((tokens, GROUP), bf16)),
        (other_theirs, *in_maps, *out_maps, *near_args),
    )
    gain = norm_gain[None, :]
    sums_shape = shaped((1, tokens), f32)
    if pairs:
        received = [flip(message, "seq", mask) for mask in (6, 4, 2)]
        *received, near, far = lax.optimization_barrier((*received, near, far))
        own = call(
            functools.partial(combine_kernel, size),
            shaped((2 * size, width // 2), bf16),
            received[::-1],
            bytes_accessed=area,
        )
        other = flip(own, "seq", 1)
        near_args = base, own_factor, far, other_theirs, scaled, *span_states, *span_factors
        other_near = call(
            functools.partial(other_near_kernel, spans), near_shape, (scores, turned, own, *near_args), flops=dense
        )
        gated_shape = shaped((tokens, width // 2), f32)
        own_gated, own_squares = call(
            functools.partial(far_kernel_of_half, True),
            (gated_shape, shaped((tokens, 128), f32)),
            (turned, near, far, gain, theirs, own),
            flops=2 * dense,
            bytes_accessed=6 * area,
        )
        other_gated, sums = call(
            functools.partial(far_kernel_of_half, False),
            (gated_shape, sums_shape),
            (turned, other_near, far, gain, other_theirs, other, own_squares),
            flops=2 * dense,
            bytes_accessed=6 * area,
        )
        gated = (own_gated, other_gated)
    else:
        *gated, sums = call(
            far_kernel,
            (shaped((tokens, width), f32), sums_shape),
            (turned, near, far, gain, *far_states(shard, size)),
            flops=4 * dense,
            bytes_accessed=12 * area,
        )
    last = [sums, *from_each(sums, "head", far_first_masks(parts))]
    return call(
        functools.partial(norm_kernel, len(last), width * parts),
        shaped((tokens, width), bf16),
        (*last, *gated),
        flops=dense,
        bytes_accessed=6 * area,
        scratch=[pltpu.VMEM((tokens, width), bf16), pltpu.SemaphoreType.DMA((NORM_CHUNKS,))],
        out_space=pl.ANY,
    )


def solution(mesh):
    return jax.shard_map(
        on_device,
        mesh=mesh,
        in_specs=(
            P("seq", "head"),
            P("seq", "head"),
            P("head", "seq"),
            P("head", "seq"),
            P("head", "seq"),
            P("head"),
            P(None, "head", "seq"),
            P("head"),
            P("head"),
        ),
        out_specs=P("seq", "head"),
        check_vma=False,
    )
```

```python
import functools

import jax
import jax.numpy as jnp
from jax import lax
from jax.experimental import pallas as pl
from jax.experimental.pallas import tpu as pltpu
from jax.sharding import PartitionSpec as P

P_SIZE = 64
GROUP = 256
DECAY_ROWS = 8
BLOCK = 256
NORM_CHUNKS = 4
FIRST_HOP = 1
VMEM_LIMIT = 40 * 1024 * 1024

f32, bf16 = jnp.float32, jnp.bfloat16
HIGHEST = lax.Precision.HIGHEST
TRANSPOSED = (((0,), (0,)), ((), ()))


def expander(heads, width, copies):
    row = lax.broadcasted_iota(jnp.int32, (copies * heads, width), 0)
    col = lax.broadcasted_iota(jnp.int32, (copies * heads, width), 1)
    return jnp.where(lax.rem(row, heads) == lax.div(col, P_SIZE), 1.0, 0.0)


def far_first_masks(size):
    return (*range(2, size), 1)


def pair_masks(size):
    return tuple(mask for mask in range(1, size) if not mask & FIRST_HOP)


def two_parts(factor):
    high = factor.astype(bf16).astype(f32)
    return jnp.concatenate([high, factor - high], axis=0).astype(bf16)


def transposed_dot(left, right):
    return lax.dot_general(left, right, TRANSPOSED, preferred_element_type=f32)


def head_row(heads, width, column):
    return jnp.sum(expander(heads, width, 1) * column, axis=0, keepdims=True)


def group_slice(group):
    return slice(group * GROUP, (group + 1) * GROUP)


def blocks_of(width):
    return [slice(at, at + BLOCK) for at in range(0, width, BLOCK)]


def local_spans(groups):
    spans = []
    for later in range(groups):
        for bit in range(groups.bit_length() - 1):
            if later >> bit & 1:
                start = later >> bit + 1 << bit + 1
                spans.append((later, bit, start, start + 2**bit))
    return spans


def column_of(row):
    size = row.shape[1]
    at = lax.broadcasted_iota(jnp.int32, (size, size), 0) == lax.broadcasted_iota(jnp.int32, (size, size), 1)
    return jnp.sum(jnp.where(at, row, 0.0), axis=1, keepdims=True)


def map_rows(maps):
    if all(rows.shape[0] % 16 == 0 for rows in maps):
        return jnp.concatenate([rows[...] for rows in maps], axis=0)
    return jnp.concatenate([rows[...].astype(f32) for rows in maps], axis=0).astype(bf16)


def out_map_rows(map_refs, parts):
    rows = map_refs[0].shape[0] // 2
    pairs = [ref if rows % 16 == 0 else ref[...].astype(f32) for ref in map_refs]
    sent = (0, *pair_masks(parts))
    picked = []
    for mask in (0, *far_first_masks(parts)):
        pair = pairs[sent.index(mask & ~FIRST_HOP)]
        at = slice(rows, 2 * rows) if mask & FIRST_HOP else slice(0, rows)
        picked.append(pair.at[at] if rows % 16 == 0 else pair[at])
    return map_rows(picked)


def fetch(sources, targets, semaphores):
    copies = [
        pltpu.make_async_copy(source, target, semaphores.at[index])
        for index, (source, target) in enumerate(zip(sources, targets))
    ]
    for copy in copies:
        copy.start()
    return copies


def prepare_kernel(*refs):
    sources, (scaled_ref, cum_ref), kept_refs = refs[:8], refs[8:10], refs[10:16]
    step_ref, rate_ref, semaphores = refs[16:]
    inputs_ref = kept_refs[0]
    copies = fetch(sources, (step_ref, rate_ref, *kept_refs), semaphores)
    heads, tokens = step_ref.shape
    width = inputs_ref.shape[1]
    row = lax.broadcasted_iota(jnp.int32, (GROUP, GROUP), 0)
    col = lax.broadcasted_iota(jnp.int32, (GROUP, GROUP), 1)
    until = jnp.where(row <= col, 1.0, 0.0)
    expand = expander(heads, width, 2).astype(bf16)
    copies[0].wait()
    copies[1].wait()
    step = step_ref[...]
    log_decay = -step * column_of(rate_ref[...])
    factors = []
    for group in range(tokens // GROUP):
        at = group_slice(group)
        cum = jnp.dot(log_decay[:, at], until, precision=HIGHEST, preferred_element_type=f32)
        cum_ref[:, at] = cum
        factors.append(two_parts(jnp.exp(-cum) * step[:, at]))
    factor = jnp.concatenate(factors, axis=1)
    copies[2].wait()
    for cols in blocks_of(width):
        scale = transposed_dot(factor, expand[:, cols])
        scaled_ref[:, cols] = (inputs_ref[:, cols].astype(f32) * scale).astype(bf16)
    for copy in copies[3:]:
        copy.wait()


def join_kernel(mine_ref, theirs_ref, _, both_ref):
    rows = mine_ref.shape[0]
    both_ref[:rows, :] = mine_ref[...]
    both_ref[rows:, :] = theirs_ref[...]


def states_kernel(parts, sides, *refs):
    map_refs, (scaled_ref, cum_ref), out_refs = refs[:parts], refs[parts : parts + 2], refs[parts + 2 :]
    shard_refs = out_refs[:sides]
    heads, tokens = cum_ref.shape
    width = scaled_ref.shape[1]
    in_map = map_rows(map_refs)
    size = in_map.shape[0]
    cum = cum_ref[...]
    states, decays = [], []
    for group in range(tokens // GROUP):
        at = group_slice(group)
        decay = head_row(heads, width, jnp.exp(cum[:, at.stop - 1 : at.stop]))
        raw = jnp.dot(in_map[:, at], scaled_ref[at, :], preferred_element_type=f32)
        states.append(raw * decay)
        decays.append(decay)
    total, decay = states[0], decays[0]
    for group in range(1, len(states)):
        total = total * decays[group] + states[group]
        decay = decay * decays[group]
    columns = width // sides
    core = lax.rem(lax.axis_index("seq"), 2)
    for ref, first in zip(shard_refs, (core == 0, core == 1)):
        at = slice(0, columns)
        ref[:size, :] = jnp.where(first, total[:, at], total[:, width - columns :]).astype(bf16)
        row = jnp.where(first, decay[:, at], decay[:, width - columns :])
        ref[size:, :] = jnp.broadcast_to(row, (DECAY_ROWS, columns)).astype(bf16)
    for index, (later, _, start, stop) in enumerate(local_spans(len(states))):
        span = states[start]
        for group in range(start + 1, later):
            span = span * decays[group]
            if group < stop:
                span = span + states[group]
        out_refs[sides][index * size : (index + 1) * size, :] = span.astype(bf16)


def merge_kernel(size, mine_ref, theirs_ref, _, pair_ref):
    core = lax.rem(lax.axis_index("seq"), 2)
    mine, theirs = mine_ref[...], theirs_ref[...]
    older = jnp.where(core == 1, theirs, mine).astype(f32)
    newer = jnp.where(core == 1, mine, theirs).astype(f32)
    decay = newer[size : size + 1]
    pair_ref[:size, :] = (older[:size] * decay + newer[:size]).astype(bf16)
    pair_ref[size:, :] = (older[size:] * decay).astype(bf16)


def factor_kernel(spans, levels, *refs):
    inputs_ref, gate_ref, mix_ref, skip_ref, cum_ref, _ = refs[:6]
    base_ref, own_ref, far_ref = refs[6:9]
    span_refs = refs[9:]
    heads, tokens = cum_ref.shape
    width = inputs_ref.shape[1]
    groups = tokens // GROUP
    first = groups.bit_length()
    expand = expander(heads, width, 2).astype(bf16)
    skip = head_row(heads, width, column_of(skip_ref[...]))
    before = jnp.zeros((heads, 1), f32)
    for group in range(groups):
        at = group_slice(group)
        cum = cum_ref[:, at]
        decay = jnp.exp(cum)
        own_mix = two_parts(mix_ref[0, :, at] * decay)
        span_mixes = [
            (index, two_parts(mix_ref[1 + bit, :, at] * decay))
            for index, (later, bit, _, _) in enumerate(spans)
            if later == group
        ]
        decay = jnp.exp(cum + before)
        before = before + cum[:, GROUP - 1 : GROUP]
        far_mixes = [two_parts(mix_ref[first + level, :, at] * decay) for level in range(levels)]
        for cols in blocks_of(width):
            gate = gate_ref[at, cols].astype(f32)
            swish = gate / (1.0 + jnp.exp(-gate))
            base_ref[at, cols] = skip[:, cols] * inputs_ref[at, cols].astype(f32) * swish
            own_ref[at, cols] = transposed_dot(own_mix, expand[:, cols]) * swish
            for level, mix in enumerate(far_mixes):
                far_ref[level, at, cols] = (transposed_dot(mix, expand[:, cols]) * swish).astype(bf16)
            for index, mix in span_mixes:
                span_refs[0][index, :, cols] = (transposed_dot(mix, expand[:, cols]) * swish).astype(bf16)


def near_body(spans, paired, start, scores_ref, turned_ref, refs, near_ref):
    base_ref, own_ref, far_ref, core_ref, scaled_ref = refs[:5]
    span_refs = refs[5:]
    tokens, size = turned_ref.shape
    has_core = lax.rem(lax.axis_index("seq"), 2) == 1
    for group in range(tokens // GROUP):
        at = group_slice(group)
        for cols in blocks_of(near_ref.shape[1]):
            of = pl.ds(pl.multiple_of(start + cols.start, BLOCK), BLOCK)
            own = jnp.dot(scores_ref[at, :], scaled_ref[at, of], preferred_element_type=f32)
            total = base_ref[at, of] + own_ref[at, of] * own
            for index, (later, _, _, _) in enumerate(spans):
                if later == group:
                    rows = slice(index * size, (index + 1) * size)
                    reach = jnp.dot(turned_ref[at, :], span_refs[0][rows, of], preferred_element_type=f32)
                    total = total + span_refs[1][index, :, of].astype(f32) * reach
            if paired:
                reach = jnp.dot(turned_ref[at, :], core_ref[:size, cols], preferred_element_type=f32)
                reach = jnp.where(has_core, reach, 0.0)
                total = total + far_ref[0, at, of].astype(f32) * reach
            near_ref[at, cols] = total


def near_kernel(parts, spans, paired, _, *refs):
    count = parts + parts // 2
    in_refs, out_refs, rest = refs[:parts], refs[parts:count], refs[count:-3]
    near_ref, turned_ref, scores_ref = refs[-3:]
    in_map = map_rows(in_refs)
    turned = jnp.transpose(out_map_rows(out_refs, parts))
    turned_ref[...] = turned
    row = lax.broadcasted_iota(jnp.int32, (GROUP, GROUP), 0)
    col = lax.broadcasted_iota(jnp.int32, (GROUP, GROUP), 1)
    for group in range(turned.shape[0] // GROUP):
        at = group_slice(group)
        scores = jnp.dot(turned[at], in_map[:, at], preferred_element_type=f32)
        scores_ref[at, :] = jnp.where(row >= col, scores, 0.0).astype(bf16)
    start = lax.rem(lax.axis_index("seq"), 2) * near_ref.shape[1] if paired else 0
    near_body(spans, paired, start, scores_ref, turned_ref, rest, near_ref)


def other_near_kernel(spans, scores_ref, turned_ref, _, *refs):
    near_ref = refs[-1]
    start = (1 - lax.rem(lax.axis_index("seq"), 2)) * near_ref.shape[1]
    near_body(spans, True, start, scores_ref, turned_ref, refs[:-1], near_ref)


def far_body(turned_ref, near_ref, far_ref, gain_ref, start, columns, levels, state_of, gated_ref):
    tokens = far_ref.shape[1]
    squares = jnp.zeros((tokens, 128), f32)
    for cols in blocks_of(columns):
        at = pl.ds(pl.multiple_of(start + cols.start, BLOCK), BLOCK)
        total = near_ref[:, cols]
        for level in levels:
            state = state_of(level, cols, at).astype(bf16)
            reach = jnp.dot(turned_ref[...], state, preferred_element_type=f32)
            total = total + far_ref[level, :, at].astype(f32) * reach
        gated_ref[:, cols] = total * gain_ref[:, at]
        total = total * total
        for part in range(0, BLOCK, 128):
            squares = squares + total[:, part : part + 128]
    return squares


def row_sums(squares):
    high = squares.astype(bf16)
    low = (squares - high.astype(f32)).astype(bf16)
    parts = jnp.concatenate([high, low], axis=1)
    ones = jnp.ones((16, parts.shape[1]), bf16)
    return lax.dot_general(ones, parts, (((1,), (1,)), ((), ())), preferred_element_type=f32)[:1]


def far_kernel(turned_ref, near_ref, far_ref, gain_ref, *refs):
    state_refs = refs[:-2]
    gated_ref, sums_ref = refs[-2:]

    def state_of(level, cols, _):
        return state_refs[level][:, cols]

    width = near_ref.shape[1]
    levels = range(far_ref.shape[0])
    squares = far_body(turned_ref, near_ref, far_ref, gain_ref, 0, width, levels, state_of, gated_ref)
    sums_ref[...] = row_sums(squares)


def combine_kernel(size, x_ref, y_ref, diagonal_ref, spans_ref):
    rank = lax.axis_index("seq")
    along_x = lax.rem(lax.div(rank, 2), 2)
    along_y = lax.div(rank, 4)

    def parts_of(ref):
        return ref[:size, :].astype(f32), ref[size:, :].astype(f32)[:1]

    x_state, x_decay = parts_of(x_ref)
    y_state, y_decay = parts_of(y_ref)
    d_state, d_decay = parts_of(diagonal_ref)
    newer = jnp.where(along_x == 1, y_state, d_state)
    newer_decay = jnp.where(along_x == 1, y_decay, d_decay)
    older = jnp.where(along_x == 1, d_state, y_state)
    running = jnp.where(along_x == 1, x_decay, 1.0)
    running = jnp.where(along_y == 1, running, 0.0)
    spans_ref[:size, :] = jnp.where(along_x == 1, x_state, 0.0).astype(bf16)
    spans_ref[size:, :] = ((older * newer_decay + newer) * running).astype(bf16)


def far_kernel_of_half(own, *refs):
    turned_ref, near_ref, far_ref, gain_ref, core_ref, spans_ref = refs[:6]
    gated_ref, sums_ref = refs[-2:]
    size = turned_ref.shape[1]
    core = lax.rem(lax.axis_index("seq"), 2)
    half = spans_ref.shape[1]
    start = (core if own else 1 - core) * half

    def state_of(level, cols, at):
        core_decay = core_ref[size:, cols].astype(f32)[:1]
        running = jnp.where(core == 1, core_decay, 1.0)
        return spans_ref[(level - 1) * size : level * size, cols].astype(f32) * running

    squares = far_body(turned_ref, near_ref, far_ref, gain_ref, start, half, (1, 2), state_of, gated_ref)
    sums_ref[...] = squares if own else row_sums(squares + refs[6][...])


def norm_kernel(parts, columns, *refs):
    gated_refs, (out_hbm, out_ref, semaphores) = refs[parts:-3], refs[-3:]
    total = refs[0][...]
    for ref in refs[1:parts]:
        total = total + ref[...]
    scale = lax.rsqrt(total / columns + 1e-05)
    pieces, rest = [], scale
    for _ in range(3):
        pieces.append(rest.astype(bf16).astype(f32))
        rest = rest - pieces[-1]
    tokens = scale.shape[1]
    pieces.append(jnp.zeros((16 - len(pieces), tokens), f32))
    scale = transposed_dot(jnp.concatenate(pieces, axis=0).astype(bf16), jnp.ones((16, 128), bf16))
    width = gated_refs[0].shape[1]
    core = lax.rem(lax.axis_index("seq"), 2)
    sides = (core, 1 - core) if len(gated_refs) == 2 else (0,)
    chunk = tokens // NORM_CHUNKS
    copies = []
    for index in range(NORM_CHUNKS):
        rows = slice(index * chunk, (index + 1) * chunk)
        for ref, side in zip(gated_refs, sides):
            for col in range(0, width, 128):
                at = pl.ds(pl.multiple_of(side * width + col, 128), 128)
                out_ref[rows, at] = (ref[rows, col : col + 128] * scale[rows]).astype(bf16)
        copies.append(pltpu.make_async_copy(out_ref.at[rows], out_hbm.at[rows], semaphores.at[index]))
        copies[-1].start()
    for copy in copies:
        copy.wait()


def call(kernel, out_shape, args, flops=0, bytes_accessed=0, hbm=0, scratch=None, out_space=pltpu.VMEM):
    specs = [pl.BlockSpec(memory_space=pl.ANY)] * hbm + [pl.BlockSpec(memory_space=pltpu.VMEM)] * (len(args) - hbm)
    args = [pltpu.with_memory_space_constraint(arg, pltpu.HBM) for arg in args[:hbm]] + list(args[hbm:])
    if scratch is None:
        scratch = [pltpu.VMEM(arg.shape, arg.dtype) for arg in args[:hbm]]
        scratch += [pltpu.SemaphoreType.DMA((hbm,))] if hbm else []
    return pl.pallas_call(
        kernel,
        out_shape=out_shape,
        in_specs=specs,
        out_specs=jax.tree.map(lambda _: pl.BlockSpec(memory_space=out_space), out_shape),
        scratch_shapes=scratch,
        compiler_params=pltpu.CompilerParams(vmem_limit_bytes=VMEM_LIMIT),
        cost_estimate=pl.CostEstimate(flops=flops, bytes_accessed=bytes_accessed, transcendentals=0),
    )(*args)


def shaped(shape, dtype):
    return jax.ShapeDtypeStruct(shape, dtype)


def flip(array, axis, mask):
    return lax.ppermute(array, axis, [(i, i ^ mask) for i in range(lax.axis_size(axis))])


def from_each(array, axis, masks):
    return [flip(array, axis, mask) for mask in masks]


def merged(older, newer, size):
    older, newer = older.astype(f32), newer.astype(f32)
    decay = newer[size : size + 1]
    return jnp.concatenate([older[:size] * decay + newer[:size], older[size:] * decay], axis=0).astype(bf16)


def far_states(shard, size):
    rank = lax.axis_index("seq")
    levels = lax.axis_size("seq").bit_length() - 1
    states = []
    running = jnp.ones((1, shard.shape[1]), f32)
    for level in range(levels):
        theirs = flip(shard, "seq", 1 << level)
        upper = jnp.right_shift(rank, level) % 2 == 1
        states.append(jnp.where(upper, theirs[:size].astype(f32) * running, 0.0).astype(bf16))
        running = jnp.where(upper, running * theirs[size : size + 1].astype(f32), running)
        shard = merged(jnp.where(upper, theirs, shard), jnp.where(upper, shard, theirs), size)
    return states


def on_device(inputs, gate, input_map, output_map, step, decay_rate, level_mix, skip, norm_gain):
    tokens, width = inputs.shape
    heads = step.shape[0]
    parts = lax.axis_size("head")
    levels = lax.axis_size("seq").bit_length() - 1
    size = input_map.shape[0] * parts
    groups = tokens // GROUP
    spans = local_spans(groups)
    dense = 2 * tokens * GROUP * width
    area = tokens * width
    others = from_each(input_map, "head", far_first_masks(parts))
    kept = inputs, gate, level_mix, skip[None, :], input_map, output_map
    beside = flip(output_map, "head", FIRST_HOP)
    scaled, cum, *kept = call(
        prepare_kernel,
        (
            *(shaped((tokens, width), bf16), shaped((heads, tokens), f32)),
            *(shaped(array.shape, array.dtype) for array in kept),
        ),
        (step, decay_rate[None, :], *kept),
        flops=16 * dense,
        bytes_accessed=4 * area,
        hbm=8,
        scratch=[pltpu.VMEM(step.shape, f32), pltpu.VMEM((1, heads), f32), pltpu.SemaphoreType.DMA((8,))],
    )
    inputs, gate, level_mix, skip, input_map, output_map = kept
    in_maps = [input_map, *others]
    pairs = lax.axis_size("seq") == 8 and parts == 4
    sides = 2 if pairs else 1
    shard_shape = shaped((size + DECAY_ROWS, width // sides), bf16)
    span_shape = [shaped((len(spans) * size, width), bf16)] if spans else []
    shard, *rest = call(
        functools.partial(states_kernel, parts, sides),
        (*[shard_shape] * sides, *span_shape),
        (*in_maps, scaled, cum),
        flops=dense,
    )
    span_states = rest[sides - 1 :]
    rows = output_map.shape[0]
    if rows % 16 == 0:
        both = call(
            join_kernel,
            shaped((2 * rows, tokens), bf16),
            (output_map, beside, shard),
            flops=8 * dense,
        )
    else:
        both = jnp.concatenate([output_map, beside], axis=0)
    if pairs:
        theirs = flip(rest[0], "seq", 1)
        message = call(
            functools.partial(merge_kernel, size), shard_shape, (shard, theirs, both), flops=0
        )
        other_theirs = flip(lax.optimization_barrier((shard, message))[0], "seq", 1)
    else:
        other_theirs = theirs = message = shard
    out_maps = [both, *from_each(both, "head", pair_masks(parts))]
    factor_shape = [shaped((len(spans), GROUP, width), bf16)] if spans else []
    base, own_factor, far, *span_factors = call(
        functools.partial(factor_kernel, spans, levels),
        (
            *(shaped((tokens, width), f32), shaped((tokens, width), f32)),
            *(shaped((levels, tokens, width), bf16), *factor_shape),
        ),
        (inputs, gate, level_mix, skip, cum, message),
        flops=5 * dense,
        bytes_accessed=0,
    )
    near_args = base, own_factor, far, theirs, scaled, *span_states, *span_factors
    near_shape = shaped((tokens, width // 2 if pairs else width), f32)
    near, turned, scores = call(
        functools.partial(near_kernel, parts, spans, pairs),
        (near_shape, shaped((tokens, size), bf16), shaped((tokens, GROUP), bf16)),
        (other_theirs, *in_maps, *out_maps, *near_args),
    )
    gain = norm_gain[None, :]
    sums_shape = shaped((1, tokens), f32)
    if pairs:
        received = [flip(message, "seq", mask) for mask in (6, 4, 2)]
        *received, near, far = lax.optimization_barrier((*received, near, far))
        own = call(
            functools.partial(combine_kernel, size),
            shaped((2 * size, width // 2), bf16),
            received[::-1],
            bytes_accessed=area,
        )
        other = flip(own, "seq", 1)
        near_args = base, own_factor, far, other_theirs, scaled, *span_states, *span_factors
        other_near = call(
            functools.partial(other_near_kernel, spans), near_shape, (scores, turned, own, *near_args), flops=dense
        )
        gated_shape = shaped((tokens, width // 2), f32)
        own_gated, own_squares = call(
            functools.partial(far_kernel_of_half, True),
            (gated_shape, shaped((tokens, 128), f32)),
            (turned, near, far, gain, theirs, own),
            flops=2 * dense,
            bytes_accessed=6 * area,
        )
        other_gated, sums = call(
            functools.partial(far_kernel_of_half, False),
            (gated_shape, sums_shape),
            (turned, other_near, far, gain, other_theirs, other, own_squares),
            flops=2 * dense,
            bytes_accessed=6 * area,
        )
        gated = (own_gated, other_gated)
    else:
        *gated, sums = call(
            far_kernel,
            (shaped((tokens, width), f32), sums_shape),
            (turned, near, far, gain, *far_states(shard, size)),
            flops=4 * dense,
            bytes_accessed=12 * area,
        )
    last = [sums, *from_each(sums, "head", far_first_masks(parts))]
    return call(
        functools.partial(norm_kernel, len(last), width * parts),
        shaped((tokens, width), bf16),
        (*last, *gated),
        flops=dense,
        bytes_accessed=6 * area,
        scratch=[pltpu.VMEM((tokens, width), bf16), pltpu.SemaphoreType.DMA((NORM_CHUNKS,))],
        out_space=pl.ANY,
    )


def solution(mesh):
    return jax.shard_map(
        on_device,
        mesh=mesh,
        in_specs=(
            P("seq", "head"),
            P("seq", "head"),
            P("head", "seq"),
            P("head", "seq"),
            P("head", "seq"),
            P("head"),
            P(None, "head", "seq"),
            P("head"),
            P("head"),
        ),
        out_specs=P("seq", "head"),
        check_vma=False,
    )
```

```python
import functools

import jax
import jax.numpy as jnp
from jax import lax
from jax.experimental import pallas as pl
from jax.experimental.pallas import tpu as pltpu
from jax.sharding import PartitionSpec as P

P_SIZE = 64
GROUP = 256
DECAY_ROWS = 8
BLOCK = 256
NORM_CHUNKS = 4
FIRST_HOP = 2
VMEM_LIMIT = 40 * 1024 * 1024

f32, bf16 = jnp.float32, jnp.bfloat16
HIGHEST = lax.Precision.HIGHEST
TRANSPOSED = (((0,), (0,)), ((), ()))


def expander(heads, width, copies):
    row = lax.broadcasted_iota(jnp.int32, (copies * heads, width), 0)
    col = lax.broadcasted_iota(jnp.int32, (copies * heads, width), 1)
    return jnp.where(lax.rem(row, heads) == lax.div(col, P_SIZE), 1.0, 0.0)


def far_first_masks(size):
    return (*range(2, size), 1)


def pair_masks(size):
    return tuple(mask for mask in range(1, size) if not mask & FIRST_HOP)


def two_parts(factor):
    high = factor.astype(bf16).astype(f32)
    return jnp.concatenate([high, factor - high], axis=0).astype(bf16)


def transposed_dot(left, right):
    return lax.dot_general(left, right, TRANSPOSED, preferred_element_type=f32)


def head_row(heads, width, column):
    return jnp.sum(expander(heads, width, 1) * column, axis=0, keepdims=True)


def group_slice(group):
    return slice(group * GROUP, (group + 1) * GROUP)


def blocks_of(width):
    return [slice(at, at + BLOCK) for at in range(0, width, BLOCK)]


def local_spans(groups):
    spans = []
    for later in range(groups):
        for bit in range(groups.bit_length() - 1):
            if later >> bit & 1:
                start = later >> bit + 1 << bit + 1
                spans.append((later, bit, start, start + 2**bit))
    return spans


def column_of(row):
    size = row.shape[1]
    at = lax.broadcasted_iota(jnp.int32, (size, size), 0) == lax.broadcasted_iota(jnp.int32, (size, size), 1)
    return jnp.sum(jnp.where(at, row, 0.0), axis=1, keepdims=True)


def map_rows(maps):
    if all(rows.shape[0] % 16 == 0 for rows in maps):
        return jnp.concatenate([rows[...] for rows in maps], axis=0)
    return jnp.concatenate([rows[...].astype(f32) for rows in maps], axis=0).astype(bf16)


def out_map_rows(map_refs, parts):
    rows = map_refs[0].shape[0] // 2
    pairs = [ref if rows % 16 == 0 else ref[...].astype(f32) for ref in map_refs]
    sent = (0, *pair_masks(parts))
    picked = []
    for mask in (0, *far_first_masks(parts)):
        pair = pairs[sent.index(mask & ~FIRST_HOP)]
        at = slice(rows, 2 * rows) if mask & FIRST_HOP else slice(0, rows)
        picked.append(pair.at[at] if rows % 16 == 0 else pair[at])
    return map_rows(picked)


def fetch(sources, targets, semaphores):
    copies = [
        pltpu.make_async_copy(source, target, semaphores.at[index])
        for index, (source, target) in enumerate(zip(sources, targets))
    ]
    for copy in copies:
        copy.start()
    return copies


def prepare_kernel(*refs):
    sources, (scaled_ref, cum_ref), kept_refs = refs[:9], refs[9:11], refs[11:18]
    step_ref, rate_ref, semaphores = refs[18:]
    inputs_ref = kept_refs[0]
    copies = fetch(sources, (step_ref, rate_ref, *kept_refs), semaphores)
    heads, tokens = step_ref.shape
    width = inputs_ref.shape[1]
    row = lax.broadcasted_iota(jnp.int32, (GROUP, GROUP), 0)
    col = lax.broadcasted_iota(jnp.int32, (GROUP, GROUP), 1)
    until = jnp.where(row <= col, 1.0, 0.0)
    expand = expander(heads, width, 2).astype(bf16)
    copies[0].wait()
    copies[1].wait()
    step = step_ref[...]
    log_decay = -step * column_of(rate_ref[...])
    factors = []
    for group in range(tokens // GROUP):
        at = group_slice(group)
        cum = jnp.dot(log_decay[:, at], until, precision=HIGHEST, preferred_element_type=f32)
        cum_ref[:, at] = cum
        factors.append(two_parts(jnp.exp(-cum) * step[:, at]))
    factor = jnp.concatenate(factors, axis=1)
    copies[2].wait()
    for cols in blocks_of(width):
        scale = transposed_dot(factor, expand[:, cols])
        scaled_ref[:, cols] = (inputs_ref[:, cols].astype(f32) * scale).astype(bf16)
    for copy in copies[3:]:
        copy.wait()


def join_kernel(mine_ref, theirs_ref, _, both_ref):
    rows = mine_ref.shape[0]
    both_ref[:rows, :] = mine_ref[...]
    both_ref[rows:, :] = theirs_ref[...]


def states_kernel(parts, sides, *refs):
    map_refs, (scaled_ref, cum_ref), out_refs = refs[:parts], refs[parts : parts + 2], refs[parts + 2 :]
    shard_refs = out_refs[:sides]
    heads, tokens = cum_ref.shape
    width = scaled_ref.shape[1]
    in_map = map_rows(map_refs)
    size = in_map.shape[0]
    cum = cum_ref[...]
    states, decays = [], []
    for group in range(tokens // GROUP):
        at = group_slice(group)
        decay = head_row(heads, width, jnp.exp(cum[:, at.stop - 1 : at.stop]))
        raw = jnp.dot(in_map[:, at], scaled_ref[at, :], preferred_element_type=f32)
        states.append(raw * decay)
        decays.append(decay)
    total, decay = states[0], decays[0]
    for group in range(1, len(states)):
        total = total * decays[group] + states[group]
        decay = decay * decays[group]
    columns = width // sides
    core = lax.rem(lax.axis_index("seq"), 2)
    for ref, first in zip(shard_refs, (core == 0, core == 1)):
        at = slice(0, columns)
        ref[:size, :] = jnp.where(first, total[:, at], total[:, width - columns :]).astype(bf16)
        row = jnp.where(first, decay[:, at], decay[:, width - columns :])
        ref[size:, :] = jnp.broadcast_to(row, (DECAY_ROWS, columns)).astype(bf16)
    for index, (later, _, start, stop) in enumerate(local_spans(len(states))):
        span = states[start]
        for group in range(start + 1, later):
            span = span * decays[group]
            if group < stop:
                span = span + states[group]
        out_refs[sides][index * size : (index + 1) * size, :] = span.astype(bf16)


def merge_kernel(size, mine_ref, theirs_ref, _, pair_ref):
    core = lax.rem(lax.axis_index("seq"), 2)
    mine, theirs = mine_ref[...], theirs_ref[...]
    older = jnp.where(core == 1, theirs, mine).astype(f32)
    newer = jnp.where(core == 1, mine, theirs).astype(f32)
    decay = newer[size : size + 1]
    pair_ref[:size, :] = (older[:size] * decay + newer[:size]).astype(bf16)
    pair_ref[size:, :] = (older[size:] * decay).astype(bf16)


def factor_kernel(spans, levels, *refs):
    inputs_ref, gate_ref, mix_ref, skip_ref, cum_ref, _ = refs[:6]
    base_ref, own_ref, far_ref = refs[6:9]
    span_refs = refs[9:]
    heads, tokens = cum_ref.shape
    width = inputs_ref.shape[1]
    groups = tokens // GROUP
    first = groups.bit_length()
    expand = expander(heads, width, 2).astype(bf16)
    skip = head_row(heads, width, column_of(skip_ref[...]))
    before = jnp.zeros((heads, 1), f32)
    for group in range(groups):
        at = group_slice(group)
        cum = cum_ref[:, at]
        decay = jnp.exp(cum)
        own_mix = two_parts(mix_ref[0, :, at] * decay)
        span_mixes = [
            (index, two_parts(mix_ref[1 + bit, :, at] * decay))
            for index, (later, bit, _, _) in enumerate(spans)
            if later == group
        ]
        decay = jnp.exp(cum + before)
        before = before + cum[:, GROUP - 1 : GROUP]
        far_mixes = [two_parts(mix_ref[first + level, :, at] * decay) for level in range(levels)]
        for cols in blocks_of(width):
            gate = gate_ref[at, cols].astype(f32)
            swish = gate / (1.0 + jnp.exp(-gate))
            base_ref[at, cols] = skip[:, cols] * inputs_ref[at, cols].astype(f32) * swish
            own_ref[at, cols] = transposed_dot(own_mix, expand[:, cols]) * swish
            for level, mix in enumerate(far_mixes):
                far_ref[level, at, cols] = (transposed_dot(mix, expand[:, cols]) * swish).astype(bf16)
            for index, mix in span_mixes:
                span_refs[0][index, :, cols] = (transposed_dot(mix, expand[:, cols]) * swish).astype(bf16)


def near_body(spans, paired, start, scores_ref, turned_ref, refs, near_ref):
    base_ref, own_ref, far_ref, core_ref, scaled_ref = refs[:5]
    span_refs = refs[5:]
    tokens, size = turned_ref.shape
    has_core = lax.rem(lax.axis_index("seq"), 2) == 1
    for group in range(tokens // GROUP):
        at = group_slice(group)
        for cols in blocks_of(near_ref.shape[1]):
            of = pl.ds(pl.multiple_of(start + cols.start, BLOCK), BLOCK)
            own = jnp.dot(scores_ref[at, :], scaled_ref[at, of], preferred_element_type=f32)
            total = base_ref[at, of] + own_ref[at, of] * own
            for index, (later, _, _, _) in enumerate(spans):
                if later == group:
                    rows = slice(index * size, (index + 1) * size)
                    reach = jnp.dot(turned_ref[at, :], span_refs[0][rows, of], preferred_element_type=f32)
                    total = total + span_refs[1][index, :, of].astype(f32) * reach
            if paired:
                reach = jnp.dot(turned_ref[at, :], core_ref[:size, cols], preferred_element_type=f32)
                reach = jnp.where(has_core, reach, 0.0)
                total = total + far_ref[0, at, of].astype(f32) * reach
            near_ref[at, cols] = total


def near_kernel(parts, spans, paired, _, *refs):
    count = parts + parts // 2
    in_refs, out_refs, rest = refs[:parts], refs[parts:count], refs[count:-3]
    near_ref, turned_ref, scores_ref = refs[-3:]
    in_map = map_rows(in_refs)
    turned = jnp.transpose(out_map_rows(out_refs, parts))
    turned_ref[...] = turned
    row = lax.broadcasted_iota(jnp.int32, (GROUP, GROUP), 0)
    col = lax.broadcasted_iota(jnp.int32, (GROUP, GROUP), 1)
    for group in range(turned.shape[0] // GROUP):
        at = group_slice(group)
        scores = jnp.dot(turned[at], in_map[:, at], preferred_element_type=f32)
        scores_ref[at, :] = jnp.where(row >= col, scores, 0.0).astype(bf16)
    start = lax.rem(lax.axis_index("seq"), 2) * near_ref.shape[1] if paired else 0
    near_body(spans, paired, start, scores_ref, turned_ref, rest, near_ref)


def other_near_kernel(spans, scores_ref, turned_ref, _, *refs):
    near_ref = refs[-1]
    start = (1 - lax.rem(lax.axis_index("seq"), 2)) * near_ref.shape[1]
    near_body(spans, True, start, scores_ref, turned_ref, refs[:-1], near_ref)


def far_body(turned_ref, near_ref, far_ref, gain_ref, start, columns, levels, state_of, gated_ref):
    tokens = far_ref.shape[1]
    squares = jnp.zeros((tokens, 128), f32)
    for cols in blocks_of(columns):
        at = pl.ds(pl.multiple_of(start + cols.start, BLOCK), BLOCK)
        total = near_ref[:, cols]
        for level in levels:
            state = state_of(level, cols, at).astype(bf16)
            reach = jnp.dot(turned_ref[...], state, preferred_element_type=f32)
            total = total + far_ref[level, :, at].astype(f32) * reach
        gated_ref[:, cols] = total * gain_ref[:, at]
        total = total * total
        for part in range(0, BLOCK, 128):
            squares = squares + total[:, part : part + 128]
    return squares


def row_sums(squares):
    high = squares.astype(bf16)
    low = (squares - high.astype(f32)).astype(bf16)
    parts = jnp.concatenate([high, low], axis=1)
    ones = jnp.ones((16, parts.shape[1]), bf16)
    return lax.dot_general(ones, parts, (((1,), (1,)), ((), ())), preferred_element_type=f32)[:1]


def far_kernel(turned_ref, near_ref, far_ref, gain_ref, *refs):
    state_refs = refs[:-2]
    gated_ref, sums_ref = refs[-2:]

    def state_of(level, cols, _):
        return state_refs[level][:, cols]

    width = near_ref.shape[1]
    levels = range(far_ref.shape[0])
    squares = far_body(turned_ref, near_ref, far_ref, gain_ref, 0, width, levels, state_of, gated_ref)
    sums_ref[...] = row_sums(squares)


def combine_kernel(size, x_ref, y_ref, diagonal_ref, spans_ref):
    rank = lax.axis_index("seq")
    along_x = lax.rem(lax.div(rank, 2), 2)
    along_y = lax.div(rank, 4)

    def parts_of(ref):
        return ref[:size, :].astype(f32), ref[size:, :].astype(f32)[:1]

    x_state, x_decay = parts_of(x_ref)
    y_state, y_decay = parts_of(y_ref)
    d_state, d_decay = parts_of(diagonal_ref)
    newer = jnp.where(along_x == 1, y_state, d_state)
    newer_decay = jnp.where(along_x == 1, y_decay, d_decay)
    older = jnp.where(along_x == 1, d_state, y_state)
    running = jnp.where(along_x == 1, x_decay, 1.0)
    running = jnp.where(along_y == 1, running, 0.0)
    spans_ref[:size, :] = jnp.where(along_x == 1, x_state, 0.0).astype(bf16)
    spans_ref[size:, :] = ((older * newer_decay + newer) * running).astype(bf16)


def far_kernel_of_half(own, *refs):
    turned_ref, near_ref, far_ref, gain_ref, core_ref, spans_ref = refs[:6]
    gated_ref, sums_ref = refs[-2:]
    size = turned_ref.shape[1]
    core = lax.rem(lax.axis_index("seq"), 2)
    half = spans_ref.shape[1]
    start = (core if own else 1 - core) * half

    def state_of(level, cols, at):
        core_decay = core_ref[size:, cols].astype(f32)[:1]
        running = jnp.where(core == 1, core_decay, 1.0)
        return spans_ref[(level - 1) * size : level * size, cols].astype(f32) * running

    squares = far_body(turned_ref, near_ref, far_ref, gain_ref, start, half, (1, 2), state_of, gated_ref)
    sums_ref[...] = squares if own else row_sums(squares + refs[6][...])


def norm_kernel(parts, columns, *refs):
    gated_refs, (out_hbm, out_ref, semaphores) = refs[parts:-3], refs[-3:]
    total = refs[0][...]
    for ref in refs[1:parts]:
        total = total + ref[...]
    scale = lax.rsqrt(total / columns + 1e-05)
    pieces, rest = [], scale
    for _ in range(3):
        pieces.append(rest.astype(bf16).astype(f32))
        rest = rest - pieces[-1]
    tokens = scale.shape[1]
    pieces.append(jnp.zeros((16 - len(pieces), tokens), f32))
    scale = transposed_dot(jnp.concatenate(pieces, axis=0).astype(bf16), jnp.ones((16, 128), bf16))
    width = gated_refs[0].shape[1]
    core = lax.rem(lax.axis_index("seq"), 2)
    sides = (core, 1 - core) if len(gated_refs) == 2 else (0,)
    chunk = tokens // NORM_CHUNKS
    copies = []
    for index in range(NORM_CHUNKS):
        rows = slice(index * chunk, (index + 1) * chunk)
        for ref, side in zip(gated_refs, sides):
            for col in range(0, width, 128):
                at = pl.ds(pl.multiple_of(side * width + col, 128), 128)
                out_ref[rows, at] = (ref[rows, col : col + 128] * scale[rows]).astype(bf16)
        copies.append(pltpu.make_async_copy(out_ref.at[rows], out_hbm.at[rows], semaphores.at[index]))
        copies[-1].start()
    for copy in copies:
        copy.wait()


def call(kernel, out_shape, args, flops=0, bytes_accessed=0, hbm=0, scratch=None, out_space=pltpu.VMEM):
    specs = [pl.BlockSpec(memory_space=pl.ANY)] * hbm + [pl.BlockSpec(memory_space=pltpu.VMEM)] * (len(args) - hbm)
    args = [pltpu.with_memory_space_constraint(arg, pltpu.HBM) for arg in args[:hbm]] + list(args[hbm:])
    if scratch is None:
        scratch = [pltpu.VMEM(arg.shape, arg.dtype) for arg in args[:hbm]]
        scratch += [pltpu.SemaphoreType.DMA((hbm,))] if hbm else []
    return pl.pallas_call(
        kernel,
        out_shape=out_shape,
        in_specs=specs,
        out_specs=jax.tree.map(lambda _: pl.BlockSpec(memory_space=out_space), out_shape),
        scratch_shapes=scratch,
        compiler_params=pltpu.CompilerParams(vmem_limit_bytes=VMEM_LIMIT),
        cost_estimate=pl.CostEstimate(flops=flops, bytes_accessed=bytes_accessed, transcendentals=0),
    )(*args)


def shaped(shape, dtype):
    return jax.ShapeDtypeStruct(shape, dtype)


def flip(array, axis, mask):
    return lax.ppermute(array, axis, [(i, i ^ mask) for i in range(lax.axis_size(axis))])


def from_each(array, axis, masks):
    return [flip(array, axis, mask) for mask in masks]


def around(array, axis):
    size = lax.axis_size(axis)
    return [lax.ppermute(array, axis, [(i, (i + shift) % size) for i in range(size)]) for shift in range(1, size)]


def merged(older, newer, size):
    older, newer = older.astype(f32), newer.astype(f32)
    decay = newer[size : size + 1]
    return jnp.concatenate([older[:size] * decay + newer[:size], older[size:] * decay], axis=0).astype(bf16)


def far_states(shard, size):
    rank = lax.axis_index("seq")
    levels = lax.axis_size("seq").bit_length() - 1
    states = []
    running = jnp.ones((1, shard.shape[1]), f32)
    for level in range(levels):
        theirs = flip(shard, "seq", 1 << level)
        upper = jnp.right_shift(rank, level) % 2 == 1
        states.append(jnp.where(upper, theirs[:size].astype(f32) * running, 0.0).astype(bf16))
        running = jnp.where(upper, running * theirs[size : size + 1].astype(f32), running)
        shard = merged(jnp.where(upper, theirs, shard), jnp.where(upper, shard, theirs), size)
    return states


def on_device(inputs, gate, input_map, output_map, step, decay_rate, level_mix, skip, norm_gain):
    tokens, width = inputs.shape
    heads = step.shape[0]
    parts = lax.axis_size("head")
    levels = lax.axis_size("seq").bit_length() - 1
    size = input_map.shape[0] * parts
    groups = tokens // GROUP
    spans = local_spans(groups)
    dense = 2 * tokens * GROUP * width
    area = tokens * width
    others = from_each(input_map, "head", far_first_masks(parts))
    kept = inputs, gate, level_mix, skip[None, :], input_map, output_map, norm_gain[None, :]
    beside = flip(output_map, "head", FIRST_HOP)
    scaled, cum, *kept = call(
        prepare_kernel,
        (
            *(shaped((tokens, width), bf16), shaped((heads, tokens), f32)),
            *(shaped(array.shape, array.dtype) for array in kept),
        ),
        (step, decay_rate[None, :], *kept),
        flops=16 * dense,
        bytes_accessed=4 * area,
        hbm=9,
        scratch=[pltpu.VMEM(step.shape, f32), pltpu.VMEM((1, heads), f32), pltpu.SemaphoreType.DMA((9,))],
    )
    inputs, gate, level_mix, skip, input_map, output_map, gain = kept
    in_maps = [input_map, *others]
    pairs = lax.axis_size("seq") == 8 and parts == 4
    sides = 2 if pairs else 1
    shard_shape = shaped((size + DECAY_ROWS, width // sides), bf16)
    span_shape = [shaped((len(spans) * size, width), bf16)] if spans else []
    shard, *rest = call(
        functools.partial(states_kernel, parts, sides),
        (*[shard_shape] * sides, *span_shape),
        (*in_maps, scaled, cum),
        flops=dense,
    )
    span_states = rest[sides - 1 :]
    rows = output_map.shape[0]
    if rows % 16 == 0:
        both = call(
            join_kernel,
            shaped((2 * rows, tokens), bf16),
            (output_map, beside, shard),
            flops=8 * dense,
        )
    else:
        both = jnp.concatenate([output_map, beside], axis=0)
    if pairs:
        theirs = flip(rest[0], "seq", 1)
        message = call(
            functools.partial(merge_kernel, size), shard_shape, (shard, theirs, both), flops=0
        )
        other_theirs = flip(lax.optimization_barrier((shard, message))[0], "seq", 1)
    else:
        other_theirs = theirs = message = shard
    out_maps = [both, *from_each(both, "head", pair_masks(parts))]
    factor_shape = [shaped((len(spans), GROUP, width), bf16)] if spans else []
    base, own_factor, far, *span_factors = call(
        functools.partial(factor_kernel, spans, levels),
        (
            *(shaped((tokens, width), f32), shaped((tokens, width), f32)),
            *(shaped((levels, tokens, width), bf16), *factor_shape),
        ),
        (inputs, gate, level_mix, skip, cum, message),
        flops=5 * dense,
        bytes_accessed=0,
    )
    near_args = base, own_factor, far, theirs, scaled, *span_states, *span_factors
    near_shape = shaped((tokens, width // 2 if pairs else width), f32)
    near, turned, scores = call(
        functools.partial(near_kernel, parts, spans, pairs),
        (near_shape, shaped((tokens, size), bf16), shaped((tokens, GROUP), bf16)),
        (other_theirs, *in_maps, *out_maps, *near_args),
    )
    sums_shape = shaped((1, tokens), f32)
    if pairs:
        received = [flip(message, "seq", mask) for mask in (6, 4, 2)]
        *received, near, far = lax.optimization_barrier((*received, near, far))
        own = call(
            functools.partial(combine_kernel, size),
            shaped((2 * size, width // 2), bf16),
            received[::-1],
            bytes_accessed=area,
        )
        other = flip(own, "seq", 1)
        near_args = base, own_factor, far, other_theirs, scaled, *span_states, *span_factors
        other_near = call(
            functools.partial(other_near_kernel, spans), near_shape, (scores, turned, own, *near_args), flops=dense
        )
        gated_shape = shaped((tokens, width // 2), f32)
        own_gated, own_squares = call(
            functools.partial(far_kernel_of_half, True),
            (gated_shape, shaped((tokens, 128), f32)),
            (turned, near, far, gain, theirs, own),
            flops=2 * dense,
            bytes_accessed=6 * area,
        )
        other_gated, sums = call(
            functools.partial(far_kernel_of_half, False),
            (gated_shape, sums_shape),
            (turned, other_near, far, gain, other_theirs, other, own_squares),
            flops=2 * dense,
            bytes_accessed=6 * area,
        )
        gated = (own_gated, other_gated)
    else:
        *gated, sums = call(
            far_kernel,
            (shaped((tokens, width), f32), sums_shape),
            (turned, near, far, gain, *far_states(shard, size)),
            flops=4 * dense,
            bytes_accessed=12 * area,
        )
    last = [sums, *around(sums, "head")]
    return call(
        functools.partial(norm_kernel, len(last), width * parts),
        shaped((tokens, width), bf16),
        (*last, *gated),
        flops=dense,
        bytes_accessed=6 * area,
        scratch=[pltpu.VMEM((tokens, width), bf16), pltpu.SemaphoreType.DMA((NORM_CHUNKS,))],
        out_space=pl.ANY,
    )


def solution(mesh):
    return jax.shard_map(
        on_device,
        mesh=mesh,
        in_specs=(
            P("seq", "head"),
            P("seq", "head"),
            P("head", "seq"),
            P("head", "seq"),
            P("head", "seq"),
            P("head"),
            P(None, "head", "seq"),
            P("head"),
            P("head"),
        ),
        out_specs=P("seq", "head"),
        check_vma=False,
    )
```

```python
import functools

import jax
import jax.numpy as jnp
from jax import lax
from jax.experimental import pallas as pl
from jax.experimental.pallas import tpu as pltpu
from jax.sharding import PartitionSpec as P

P_SIZE = 64
GROUP = 256
DECAY_ROWS = 8
BLOCK = 256
NORM_CHUNKS = 4
FIRST_HOP = 2
VMEM_LIMIT = 40 * 1024 * 1024

f32, bf16 = jnp.float32, jnp.bfloat16
HIGHEST = lax.Precision.HIGHEST
TRANSPOSED = (((0,), (0,)), ((), ()))


def expander(heads, width, copies):
    row = lax.broadcasted_iota(jnp.int32, (copies * heads, width), 0)
    col = lax.broadcasted_iota(jnp.int32, (copies * heads, width), 1)
    return jnp.where(lax.rem(row, heads) == lax.div(col, P_SIZE), 1.0, 0.0)


def far_first_masks(size):
    return (*range(2, size), 1)


def pair_masks(size):
    return tuple(mask for mask in range(1, size) if not mask & FIRST_HOP)


def two_parts(factor):
    high = factor.astype(bf16).astype(f32)
    return jnp.concatenate([high, factor - high], axis=0).astype(bf16)


def transposed_dot(left, right):
    return lax.dot_general(left, right, TRANSPOSED, preferred_element_type=f32)


def head_row(heads, width, column):
    return jnp.sum(expander(heads, width, 1) * column, axis=0, keepdims=True)


def group_slice(group):
    return slice(group * GROUP, (group + 1) * GROUP)


def blocks_of(width):
    return [slice(at, at + BLOCK) for at in range(0, width, BLOCK)]


def local_spans(groups):
    spans = []
    for later in range(groups):
        for bit in range(groups.bit_length() - 1):
            if later >> bit & 1:
                start = later >> bit + 1 << bit + 1
                spans.append((later, bit, start, start + 2**bit))
    return spans


def column_of(row):
    size = row.shape[1]
    at = lax.broadcasted_iota(jnp.int32, (size, size), 0) == lax.broadcasted_iota(jnp.int32, (size, size), 1)
    return jnp.sum(jnp.where(at, row, 0.0), axis=1, keepdims=True)


def map_rows(maps):
    if all(rows.shape[0] % 16 == 0 for rows in maps):
        return jnp.concatenate([rows[...] for rows in maps], axis=0)
    return jnp.concatenate([rows[...].astype(f32) for rows in maps], axis=0).astype(bf16)


def out_map_rows(map_refs, parts):
    rows = map_refs[0].shape[0] // 2
    pairs = [ref if rows % 16 == 0 else ref[...].astype(f32) for ref in map_refs]
    sent = (0, *pair_masks(parts))
    picked = []
    for mask in (0, *far_first_masks(parts)):
        pair = pairs[sent.index(mask & ~FIRST_HOP)]
        at = slice(rows, 2 * rows) if mask & FIRST_HOP else slice(0, rows)
        picked.append(pair.at[at] if rows % 16 == 0 else pair[at])
    return map_rows(picked)


def fetch(sources, targets, semaphores):
    copies = [
        pltpu.make_async_copy(source, target, semaphores.at[index])
        for index, (source, target) in enumerate(zip(sources, targets))
    ]
    for copy in copies:
        copy.start()
    return copies


def prepare_kernel(*refs):
    sources, (scaled_ref, cum_ref), kept_refs = refs[:9], refs[9:11], refs[11:18]
    step_ref, rate_ref, semaphores = refs[18:]
    inputs_ref = kept_refs[0]
    copies = fetch(sources, (step_ref, rate_ref, *kept_refs), semaphores)
    heads, tokens = step_ref.shape
    width = inputs_ref.shape[1]
    row = lax.broadcasted_iota(jnp.int32, (GROUP, GROUP), 0)
    col = lax.broadcasted_iota(jnp.int32, (GROUP, GROUP), 1)
    until = jnp.where(row <= col, 1.0, 0.0)
    expand = expander(heads, width, 2).astype(bf16)
    copies[0].wait()
    copies[1].wait()
    step = step_ref[...]
    log_decay = -step * column_of(rate_ref[...])
    factors = []
    for group in range(tokens // GROUP):
        at = group_slice(group)
        cum = jnp.dot(log_decay[:, at], until, precision=HIGHEST, preferred_element_type=f32)
        cum_ref[:, at] = cum
        factors.append(two_parts(jnp.exp(-cum) * step[:, at]))
    factor = jnp.concatenate(factors, axis=1)
    copies[2].wait()
    for cols in blocks_of(width):
        scale = transposed_dot(factor, expand[:, cols])
        scaled_ref[:, cols] = (inputs_ref[:, cols].astype(f32) * scale).astype(bf16)
    for copy in copies[3:]:
        copy.wait()


def join_kernel(mine_ref, theirs_ref, _, both_ref):
    rows = mine_ref.shape[0]
    both_ref[:rows, :] = mine_ref[...]
    both_ref[rows:, :] = theirs_ref[...]


def states_kernel(parts, sides, *refs):
    map_refs, (scaled_ref, cum_ref), out_refs = refs[:parts], refs[parts : parts + 2], refs[parts + 2 :]
    shard_refs = out_refs[:sides]
    heads, tokens = cum_ref.shape
    width = scaled_ref.shape[1]
    in_map = map_rows(map_refs)
    size = in_map.shape[0]
    cum = cum_ref[...]
    states, decays = [], []
    for group in range(tokens // GROUP):
        at = group_slice(group)
        decay = head_row(heads, width, jnp.exp(cum[:, at.stop - 1 : at.stop]))
        raw = jnp.dot(in_map[:, at], scaled_ref[at, :], preferred_element_type=f32)
        states.append(raw * decay)
        decays.append(decay)
    total, decay = states[0], decays[0]
    for group in range(1, len(states)):
        total = total * decays[group] + states[group]
        decay = decay * decays[group]
    columns = width // sides
    core = lax.rem(lax.axis_index("seq"), 2)
    for ref, first in zip(shard_refs, (core == 0, core == 1)):
        at = slice(0, columns)
        ref[:size, :] = jnp.where(first, total[:, at], total[:, width - columns :]).astype(bf16)
        row = jnp.where(first, decay[:, at], decay[:, width - columns :])
        ref[size:, :] = jnp.broadcast_to(row, (DECAY_ROWS, columns)).astype(bf16)
    for index, (later, _, start, stop) in enumerate(local_spans(len(states))):
        span = states[start]
        for group in range(start + 1, later):
            span = span * decays[group]
            if group < stop:
                span = span + states[group]
        out_refs[sides][index * size : (index + 1) * size, :] = span.astype(bf16)


def merge_kernel(size, mine_ref, theirs_ref, _, pair_ref):
    core = lax.rem(lax.axis_index("seq"), 2)
    mine, theirs = mine_ref[...], theirs_ref[...]
    older = jnp.where(core == 1, theirs, mine).astype(f32)
    newer = jnp.where(core == 1, mine, theirs).astype(f32)
    decay = newer[size : size + 1]
    pair_ref[:size, :] = (older[:size] * decay + newer[:size]).astype(bf16)
    pair_ref[size:, :] = (older[size:] * decay).astype(bf16)


def factor_kernel(spans, levels, *refs):
    inputs_ref, gate_ref, mix_ref, skip_ref, cum_ref, _ = refs[:6]
    base_ref, own_ref, far_ref = refs[6:9]
    span_refs = refs[9:]
    heads, tokens = cum_ref.shape
    width = inputs_ref.shape[1]
    groups = tokens // GROUP
    first = groups.bit_length()
    expand = expander(heads, width, 2).astype(bf16)
    skip = head_row(heads, width, column_of(skip_ref[...]))
    before = jnp.zeros((heads, 1), f32)
    for group in range(groups):
        at = group_slice(group)
        cum = cum_ref[:, at]
        decay = jnp.exp(cum)
        own_mix = two_parts(mix_ref[0, :, at] * decay)
        span_mixes = [
            (index, two_parts(mix_ref[1 + bit, :, at] * decay))
            for index, (later, bit, _, _) in enumerate(spans)
            if later == group
        ]
        decay = jnp.exp(cum + before)
        before = before + cum[:, GROUP - 1 : GROUP]
        far_mixes = [two_parts(mix_ref[first + level, :, at] * decay) for level in range(levels)]
        for cols in blocks_of(width):
            gate = gate_ref[at, cols].astype(f32)
            swish = gate / (1.0 + jnp.exp(-gate))
            base_ref[at, cols] = skip[:, cols] * inputs_ref[at, cols].astype(f32) * swish
            own_ref[at, cols] = transposed_dot(own_mix, expand[:, cols]) * swish
            for level, mix in enumerate(far_mixes):
                far_ref[level, at, cols] = (transposed_dot(mix, expand[:, cols]) * swish).astype(bf16)
            for index, mix in span_mixes:
                span_refs[0][index, :, cols] = (transposed_dot(mix, expand[:, cols]) * swish).astype(bf16)


def near_body(spans, paired, start, scores_ref, turned_ref, refs, near_ref):
    base_ref, own_ref, far_ref, core_ref, scaled_ref = refs[:5]
    span_refs = refs[5:]
    tokens, size = turned_ref.shape
    has_core = lax.rem(lax.axis_index("seq"), 2) == 1
    for group in range(tokens // GROUP):
        at = group_slice(group)
        for cols in blocks_of(near_ref.shape[1]):
            of = pl.ds(pl.multiple_of(start + cols.start, BLOCK), BLOCK)
            own = jnp.dot(scores_ref[at, :], scaled_ref[at, of], preferred_element_type=f32)
            total = base_ref[at, of] + own_ref[at, of] * own
            for index, (later, _, _, _) in enumerate(spans):
                if later == group:
                    rows = slice(index * size, (index + 1) * size)
                    reach = jnp.dot(turned_ref[at, :], span_refs[0][rows, of], preferred_element_type=f32)
                    total = total + span_refs[1][index, :, of].astype(f32) * reach
            if paired:
                reach = jnp.dot(turned_ref[at, :], core_ref[:size, cols], preferred_element_type=f32)
                reach = jnp.where(has_core, reach, 0.0)
                total = total + far_ref[0, at, of].astype(f32) * reach
            near_ref[at, cols] = total


def near_kernel(parts, spans, paired, *refs):
    count = parts + parts // 2
    in_refs, out_refs, rest = refs[:parts], refs[parts:count], refs[count:-3]
    near_ref, turned_ref, scores_ref = refs[-3:]
    in_map = map_rows(in_refs)
    turned = jnp.transpose(out_map_rows(out_refs, parts))
    turned_ref[...] = turned
    row = lax.broadcasted_iota(jnp.int32, (GROUP, GROUP), 0)
    col = lax.broadcasted_iota(jnp.int32, (GROUP, GROUP), 1)
    for group in range(turned.shape[0] // GROUP):
        at = group_slice(group)
        scores = jnp.dot(turned[at], in_map[:, at], preferred_element_type=f32)
        scores_ref[at, :] = jnp.where(row >= col, scores, 0.0).astype(bf16)
    start = lax.rem(lax.axis_index("seq"), 2) * near_ref.shape[1] if paired else 0
    near_body(spans, paired, start, scores_ref, turned_ref, rest, near_ref)


def other_near_kernel(spans, scores_ref, turned_ref, _, *refs):
    near_ref = refs[-1]
    start = (1 - lax.rem(lax.axis_index("seq"), 2)) * near_ref.shape[1]
    near_body(spans, True, start, scores_ref, turned_ref, refs[:-1], near_ref)


def far_body(turned_ref, near_ref, far_ref, gain_ref, start, columns, levels, state_of, gated_ref):
    tokens = far_ref.shape[1]
    squares = jnp.zeros((tokens, 128), f32)
    for cols in blocks_of(columns):
        at = pl.ds(pl.multiple_of(start + cols.start, BLOCK), BLOCK)
        total = near_ref[:, cols]
        for level in levels:
            state = state_of(level, cols, at).astype(bf16)
            reach = jnp.dot(turned_ref[...], state, preferred_element_type=f32)
            total = total + far_ref[level, :, at].astype(f32) * reach
        gated_ref[:, cols] = total * gain_ref[:, at]
        total = total * total
        for part in range(0, BLOCK, 128):
            squares = squares + total[:, part : part + 128]
    return squares


def row_sums(squares):
    high = squares.astype(bf16)
    low = (squares - high.astype(f32)).astype(bf16)
    parts = jnp.concatenate([high, low], axis=1)
    ones = jnp.ones((16, parts.shape[1]), bf16)
    return lax.dot_general(ones, parts, (((1,), (1,)), ((), ())), preferred_element_type=f32)[:1]


def far_kernel(turned_ref, near_ref, far_ref, gain_ref, *refs):
    state_refs = refs[:-2]
    gated_ref, sums_ref = refs[-2:]

    def state_of(level, cols, _):
        return state_refs[level][:, cols]

    width = near_ref.shape[1]
    levels = range(far_ref.shape[0])
    squares = far_body(turned_ref, near_ref, far_ref, gain_ref, 0, width, levels, state_of, gated_ref)
    sums_ref[...] = row_sums(squares)


def combine_kernel(size, x_ref, y_ref, diagonal_ref, spans_ref):
    rank = lax.axis_index("seq")
    along_x = lax.rem(lax.div(rank, 2), 2)
    along_y = lax.div(rank, 4)

    def parts_of(ref):
        return ref[:size, :].astype(f32), ref[size:, :].astype(f32)[:1]

    x_state, x_decay = parts_of(x_ref)
    y_state, y_decay = parts_of(y_ref)
    d_state, d_decay = parts_of(diagonal_ref)
    newer = jnp.where(along_x == 1, y_state, d_state)
    newer_decay = jnp.where(along_x == 1, y_decay, d_decay)
    older = jnp.where(along_x == 1, d_state, y_state)
    running = jnp.where(along_x == 1, x_decay, 1.0)
    running = jnp.where(along_y == 1, running, 0.0)
    spans_ref[:size, :] = jnp.where(along_x == 1, x_state, 0.0).astype(bf16)
    spans_ref[size:, :] = ((older * newer_decay + newer) * running).astype(bf16)


def far_kernel_of_half(own, *refs):
    turned_ref, near_ref, far_ref, gain_ref, core_ref, spans_ref = refs[:6]
    gated_ref, sums_ref = refs[-2:]
    size = turned_ref.shape[1]
    core = lax.rem(lax.axis_index("seq"), 2)
    half = spans_ref.shape[1]
    start = (core if own else 1 - core) * half

    def state_of(level, cols, at):
        core_decay = core_ref[size:, cols].astype(f32)[:1]
        running = jnp.where(core == 1, core_decay, 1.0)
        return spans_ref[(level - 1) * size : level * size, cols].astype(f32) * running

    squares = far_body(turned_ref, near_ref, far_ref, gain_ref, start, half, (1, 2), state_of, gated_ref)
    sums_ref[...] = squares if own else row_sums(squares + refs[6][...])


def norm_kernel(parts, columns, *refs):
    gated_refs, (out_hbm, out_ref, semaphores) = refs[parts:-3], refs[-3:]
    total = refs[0][...]
    for ref in refs[1:parts]:
        total = total + ref[...]
    scale = lax.rsqrt(total / columns + 1e-05)
    pieces, rest = [], scale
    for _ in range(3):
        pieces.append(rest.astype(bf16).astype(f32))
        rest = rest - pieces[-1]
    tokens = scale.shape[1]
    pieces.append(jnp.zeros((16 - len(pieces), tokens), f32))
    scale = transposed_dot(jnp.concatenate(pieces, axis=0).astype(bf16), jnp.ones((16, 128), bf16))
    width = gated_refs[0].shape[1]
    core = lax.rem(lax.axis_index("seq"), 2)
    sides = (core, 1 - core) if len(gated_refs) == 2 else (0,)
    chunk = tokens // NORM_CHUNKS
    copies = []
    for index in range(NORM_CHUNKS):
        rows = slice(index * chunk, (index + 1) * chunk)
        for ref, side in zip(gated_refs, sides):
            for col in range(0, width, 128):
                at = pl.ds(pl.multiple_of(side * width + col, 128), 128)
                out_ref[rows, at] = (ref[rows, col : col + 128] * scale[rows]).astype(bf16)
        copies.append(pltpu.make_async_copy(out_ref.at[rows], out_hbm.at[rows], semaphores.at[index]))
        copies[-1].start()
    for copy in copies:
        copy.wait()


def call(kernel, out_shape, args, flops=0, bytes_accessed=0, hbm=0, scratch=None, out_space=pltpu.VMEM):
    specs = [pl.BlockSpec(memory_space=pl.ANY)] * hbm + [pl.BlockSpec(memory_space=pltpu.VMEM)] * (len(args) - hbm)
    args = [pltpu.with_memory_space_constraint(arg, pltpu.HBM) for arg in args[:hbm]] + list(args[hbm:])
    if scratch is None:
        scratch = [pltpu.VMEM(arg.shape, arg.dtype) for arg in args[:hbm]]
        scratch += [pltpu.SemaphoreType.DMA((hbm,))] if hbm else []
    return pl.pallas_call(
        kernel,
        out_shape=out_shape,
        in_specs=specs,
        out_specs=jax.tree.map(lambda _: pl.BlockSpec(memory_space=out_space), out_shape),
        scratch_shapes=scratch,
        compiler_params=pltpu.CompilerParams(vmem_limit_bytes=VMEM_LIMIT),
        cost_estimate=pl.CostEstimate(flops=flops, bytes_accessed=bytes_accessed, transcendentals=0),
    )(*args)


def shaped(shape, dtype):
    return jax.ShapeDtypeStruct(shape, dtype)


def flip(array, axis, mask):
    return lax.ppermute(array, axis, [(i, i ^ mask) for i in range(lax.axis_size(axis))])


def from_each(array, axis, masks):
    return [flip(array, axis, mask) for mask in masks]


def around(array, axis):
    size = lax.axis_size(axis)
    return [lax.ppermute(array, axis, [(i, (i + shift) % size) for i in range(size)]) for shift in range(1, size)]


def merged(older, newer, size):
    older, newer = older.astype(f32), newer.astype(f32)
    decay = newer[size : size + 1]
    return jnp.concatenate([older[:size] * decay + newer[:size], older[size:] * decay], axis=0).astype(bf16)


def far_states(shard, size):
    rank = lax.axis_index("seq")
    levels = lax.axis_size("seq").bit_length() - 1
    states = []
    running = jnp.ones((1, shard.shape[1]), f32)
    for level in range(levels):
        theirs = flip(shard, "seq", 1 << level)
        upper = jnp.right_shift(rank, level) % 2 == 1
        states.append(jnp.where(upper, theirs[:size].astype(f32) * running, 0.0).astype(bf16))
        running = jnp.where(upper, running * theirs[size : size + 1].astype(f32), running)
        shard = merged(jnp.where(upper, theirs, shard), jnp.where(upper, shard, theirs), size)
    return states


def on_device(inputs, gate, input_map, output_map, step, decay_rate, level_mix, skip, norm_gain):
    tokens, width = inputs.shape
    heads = step.shape[0]
    parts = lax.axis_size("head")
    levels = lax.axis_size("seq").bit_length() - 1
    size = input_map.shape[0] * parts
    groups = tokens // GROUP
    spans = local_spans(groups)
    dense = 2 * tokens * GROUP * width
    area = tokens * width
    others = from_each(input_map, "head", far_first_masks(parts))
    kept = inputs, gate, level_mix, skip[None, :], input_map, output_map, norm_gain[None, :]
    beside = flip(output_map, "head", FIRST_HOP)
    scaled, cum, *kept = call(
        prepare_kernel,
        (
            *(shaped((tokens, width), bf16), shaped((heads, tokens), f32)),
            *(shaped(array.shape, array.dtype) for array in kept),
        ),
        (step, decay_rate[None, :], *kept),
        flops=16 * dense,
        bytes_accessed=4 * area,
        hbm=9,
        scratch=[pltpu.VMEM(step.shape, f32), pltpu.VMEM((1, heads), f32), pltpu.SemaphoreType.DMA((9,))],
    )
    inputs, gate, level_mix, skip, input_map, output_map, gain = kept
    in_maps = [input_map, *others]
    pairs = lax.axis_size("seq") == 8 and parts == 4
    sides = 2 if pairs else 1
    shard_shape = shaped((size + DECAY_ROWS, width // sides), bf16)
    span_shape = [shaped((len(spans) * size, width), bf16)] if spans else []
    shard, *rest = call(
        functools.partial(states_kernel, parts, sides),
        (*[shard_shape] * sides, *span_shape),
        (*in_maps, scaled, cum),
        flops=dense,
    )
    span_states = rest[sides - 1 :]
    rows = output_map.shape[0]
    if rows % 16 == 0:
        both = call(
            join_kernel,
            shaped((2 * rows, tokens), bf16),
            (output_map, beside, shard),
            flops=8 * dense,
        )
    else:
        both = jnp.concatenate([output_map, beside], axis=0)
    if pairs:
        theirs = flip(rest[0], "seq", 1)
        message = call(
            functools.partial(merge_kernel, size), shard_shape, (shard, theirs, both), flops=0
        )
        other_theirs = flip(lax.optimization_barrier((shard, message))[0], "seq", 1)
    else:
        other_theirs = theirs = message = shard
    out_maps = [both, *from_each(both, "head", pair_masks(parts))]
    factor_shape = [shaped((len(spans), GROUP, width), bf16)] if spans else []
    base, own_factor, far, *span_factors = call(
        functools.partial(factor_kernel, spans, levels),
        (
            *(shaped((tokens, width), f32), shaped((tokens, width), f32)),
            *(shaped((levels, tokens, width), bf16), *factor_shape),
        ),
        (inputs, gate, level_mix, skip, cum, message),
        flops=5 * dense,
        bytes_accessed=0,
    )
    near_args = base, own_factor, far, theirs, scaled, *span_states, *span_factors
    near_shape = shaped((tokens, width // 2 if pairs else width), f32)
    near, turned, scores = call(
        functools.partial(near_kernel, parts, spans, pairs),
        (near_shape, shaped((tokens, size), bf16), shaped((tokens, GROUP), bf16)),
        (*in_maps, *out_maps, *near_args),
    )
    sums_shape = shaped((1, tokens), f32)
    if pairs:
        received = [flip(message, "seq", mask) for mask in (6, 4, 2)]
        *received, other_theirs, near, far = lax.optimization_barrier((*received, other_theirs, near, far))
        own = call(
            functools.partial(combine_kernel, size),
            shaped((2 * size, width // 2), bf16),
            received[::-1],
            bytes_accessed=area,
        )
        other = flip(own, "seq", 1)
        near_args = base, own_factor, far, other_theirs, scaled, *span_states, *span_factors
        other_near = call(
            functools.partial(other_near_kernel, spans), near_shape, (scores, turned, own, *near_args), flops=dense
        )
        gated_shape = shaped((tokens, width // 2), f32)
        own_gated, own_squares = call(
            functools.partial(far_kernel_of_half, True),
            (gated_shape, shaped((tokens, 128), f32)),
            (turned, near, far, gain, theirs, own),
            flops=2 * dense,
            bytes_accessed=6 * area,
        )
        other_gated, sums = call(
            functools.partial(far_kernel_of_half, False),
            (gated_shape, sums_shape),
            (turned, other_near, far, gain, other_theirs, other, own_squares),
            flops=2 * dense,
            bytes_accessed=6 * area,
        )
        gated = (own_gated, other_gated)
    else:
        *gated, sums = call(
            far_kernel,
            (shaped((tokens, width), f32), sums_shape),
            (turned, near, far, gain, *far_states(shard, size)),
            flops=4 * dense,
            bytes_accessed=12 * area,
        )
    last = [sums, *around(sums, "head")]
    return call(
        functools.partial(norm_kernel, len(last), width * parts),
        shaped((tokens, width), bf16),
        (*last, *gated),
        flops=dense,
        bytes_accessed=6 * area,
        scratch=[pltpu.VMEM((tokens, width), bf16), pltpu.SemaphoreType.DMA((NORM_CHUNKS,))],
        out_space=pl.ANY,
    )


def solution(mesh):
    return jax.shard_map(
        on_device,
        mesh=mesh,
        in_specs=(
            P("seq", "head"),
            P("seq", "head"),
            P("head", "seq"),
            P("head", "seq"),
            P("head", "seq"),
            P("head"),
            P(None, "head", "seq"),
            P("head"),
            P("head"),
        ),
        out_specs=P("seq", "head"),
        check_vma=False,
    )
```

```python
import functools

import jax
import jax.numpy as jnp
from jax import lax
from jax.experimental import pallas as pl
from jax.experimental.pallas import tpu as pltpu
from jax.sharding import PartitionSpec as P

P_SIZE = 64
GROUP = 256
DECAY_ROWS = 8
BLOCK = 256
NORM_CHUNKS = 4
FIRST_HOP = 2
VMEM_LIMIT = 40 * 1024 * 1024

f32, bf16 = jnp.float32, jnp.bfloat16
HIGHEST = lax.Precision.HIGHEST
TRANSPOSED = (((0,), (0,)), ((), ()))


def expander(heads, width, copies):
    row = lax.broadcasted_iota(jnp.int32, (copies * heads, width), 0)
    col = lax.broadcasted_iota(jnp.int32, (copies * heads, width), 1)
    return jnp.where(lax.rem(row, heads) == lax.div(col, P_SIZE), 1.0, 0.0)


def far_first_masks(size):
    return (*range(2, size), 1)


def pair_masks(size):
    return tuple(mask for mask in range(1, size) if not mask & FIRST_HOP)


def two_parts(factor):
    high = factor.astype(bf16).astype(f32)
    return jnp.concatenate([high, factor - high], axis=0).astype(bf16)


def transposed_dot(left, right):
    return lax.dot_general(left, right, TRANSPOSED, preferred_element_type=f32)


def head_row(heads, width, column):
    return jnp.sum(expander(heads, width, 1) * column, axis=0, keepdims=True)


def group_slice(group):
    return slice(group * GROUP, (group + 1) * GROUP)


def blocks_of(width):
    return [slice(at, at + BLOCK) for at in range(0, width, BLOCK)]


def local_spans(groups):
    spans = []
    for later in range(groups):
        for bit in range(groups.bit_length() - 1):
            if later >> bit & 1:
                start = later >> bit + 1 << bit + 1
                spans.append((later, bit, start, start + 2**bit))
    return spans


def column_of(row):
    size = row.shape[1]
    at = lax.broadcasted_iota(jnp.int32, (size, size), 0) == lax.broadcasted_iota(jnp.int32, (size, size), 1)
    return jnp.sum(jnp.where(at, row, 0.0), axis=1, keepdims=True)


def map_rows(maps):
    if all(rows.shape[0] % 16 == 0 for rows in maps):
        return jnp.concatenate([rows[...] for rows in maps], axis=0)
    return jnp.concatenate([rows[...].astype(f32) for rows in maps], axis=0).astype(bf16)


def out_map_rows(map_refs, parts):
    rows = map_refs[0].shape[0] // 2
    pairs = [ref if rows % 16 == 0 else ref[...].astype(f32) for ref in map_refs]
    sent = (0, *pair_masks(parts))
    picked = []
    for mask in (0, *far_first_masks(parts)):
        pair = pairs[sent.index(mask & ~FIRST_HOP)]
        at = slice(rows, 2 * rows) if mask & FIRST_HOP else slice(0, rows)
        picked.append(pair.at[at] if rows % 16 == 0 else pair[at])
    return map_rows(picked)


def fetch(sources, targets, semaphores):
    copies = [
        pltpu.make_async_copy(source, target, semaphores.at[index])
        for index, (source, target) in enumerate(zip(sources, targets))
    ]
    for copy in copies:
        copy.start()
    return copies


def prepare_kernel(*refs):
    sources, (scaled_ref, cum_ref), kept_refs = refs[:9], refs[9:11], refs[11:18]
    step_ref, rate_ref, semaphores = refs[18:]
    inputs_ref = kept_refs[0]
    copies = fetch(sources, (step_ref, rate_ref, *kept_refs), semaphores)
    heads, tokens = step_ref.shape
    width = inputs_ref.shape[1]
    row = lax.broadcasted_iota(jnp.int32, (GROUP, GROUP), 0)
    col = lax.broadcasted_iota(jnp.int32, (GROUP, GROUP), 1)
    until = jnp.where(row <= col, 1.0, 0.0)
    expand = expander(heads, width, 2).astype(bf16)
    copies[0].wait()
    copies[1].wait()
    step = step_ref[...]
    log_decay = -step * column_of(rate_ref[...])
    factors = []
    for group in range(tokens // GROUP):
        at = group_slice(group)
        cum = jnp.dot(log_decay[:, at], until, precision=HIGHEST, preferred_element_type=f32)
        cum_ref[:, at] = cum
        factors.append(two_parts(jnp.exp(-cum) * step[:, at]))
    factor = jnp.concatenate(factors, axis=1)
    copies[2].wait()
    for cols in blocks_of(width):
        scale = transposed_dot(factor, expand[:, cols])
        scaled_ref[:, cols] = (inputs_ref[:, cols].astype(f32) * scale).astype(bf16)
    for copy in copies[3:]:
        copy.wait()


def join_kernel(mine_ref, theirs_ref, _, both_ref):
    rows = mine_ref.shape[0]
    both_ref[:rows, :] = mine_ref[...]
    both_ref[rows:, :] = theirs_ref[...]


def states_kernel(parts, sides, *refs):
    map_refs, (scaled_ref, cum_ref), out_refs = refs[:parts], refs[parts : parts + 2], refs[parts + 2 :]
    shard_refs = out_refs[:sides]
    heads, tokens = cum_ref.shape
    width = scaled_ref.shape[1]
    in_map = map_rows(map_refs)
    size = in_map.shape[0]
    cum = cum_ref[...]
    states, decays = [], []
    for group in range(tokens // GROUP):
        at = group_slice(group)
        decay = head_row(heads, width, jnp.exp(cum[:, at.stop - 1 : at.stop]))
        raw = jnp.dot(in_map[:, at], scaled_ref[at, :], preferred_element_type=f32)
        states.append(raw * decay)
        decays.append(decay)
    total, decay = states[0], decays[0]
    for group in range(1, len(states)):
        total = total * decays[group] + states[group]
        decay = decay * decays[group]
    columns = width // sides
    core = lax.rem(lax.axis_index("seq"), 2)
    for ref, first in zip(shard_refs, (core == 0, core == 1)):
        at = slice(0, columns)
        ref[:size, :] = jnp.where(first, total[:, at], total[:, width - columns :]).astype(bf16)
        row = jnp.where(first, decay[:, at], decay[:, width - columns :])
        ref[size:, :] = jnp.broadcast_to(row, (DECAY_ROWS, columns)).astype(bf16)
    for index, (later, _, start, stop) in enumerate(local_spans(len(states))):
        span = states[start]
        for group in range(start + 1, later):
            span = span * decays[group]
            if group < stop:
                span = span + states[group]
        out_refs[sides][index * size : (index + 1) * size, :] = span.astype(bf16)


def merge_kernel(size, mine_ref, theirs_ref, _, pair_ref):
    core = lax.rem(lax.axis_index("seq"), 2)
    mine, theirs = mine_ref[...], theirs_ref[...]
    older = jnp.where(core == 1, theirs, mine).astype(f32)
    newer = jnp.where(core == 1, mine, theirs).astype(f32)
    decay = newer[size : size + 1]
    pair_ref[:size, :] = (older[:size] * decay + newer[:size]).astype(bf16)
    pair_ref[size:, :] = (older[size:] * decay).astype(bf16)


def factor_kernel(spans, levels, *refs):
    inputs_ref, gate_ref, mix_ref, skip_ref, cum_ref, _ = refs[:6]
    base_ref, own_ref, far_ref = refs[6:9]
    span_refs = refs[9:]
    heads, tokens = cum_ref.shape
    width = inputs_ref.shape[1]
    groups = tokens // GROUP
    first = groups.bit_length()
    expand = expander(heads, width, 2).astype(bf16)
    skip = head_row(heads, width, column_of(skip_ref[...]))
    before = jnp.zeros((heads, 1), f32)
    for group in range(groups):
        at = group_slice(group)
        cum = cum_ref[:, at]
        decay = jnp.exp(cum)
        own_mix = two_parts(mix_ref[0, :, at] * decay)
        span_mixes = [
            (index, two_parts(mix_ref[1 + bit, :, at] * decay))
            for index, (later, bit, _, _) in enumerate(spans)
            if later == group
        ]
        decay = jnp.exp(cum + before)
        before = before + cum[:, GROUP - 1 : GROUP]
        far_mixes = [two_parts(mix_ref[first + level, :, at] * decay) for level in range(levels)]
        for cols in blocks_of(width):
            gate = gate_ref[at, cols].astype(f32)
            swish = gate / (1.0 + jnp.exp(-gate))
            base_ref[at, cols] = skip[:, cols] * inputs_ref[at, cols].astype(f32) * swish
            own_ref[at, cols] = transposed_dot(own_mix, expand[:, cols]) * swish
            for level, mix in enumerate(far_mixes):
                far_ref[level, at, cols] = (transposed_dot(mix, expand[:, cols]) * swish).astype(bf16)
            for index, mix in span_mixes:
                span_refs[0][index, :, cols] = (transposed_dot(mix, expand[:, cols]) * swish).astype(bf16)


def near_body(spans, paired, start, scores_ref, turned_ref, refs, near_ref):
    base_ref, own_ref, far_ref, core_ref, scaled_ref = refs[:5]
    span_refs = refs[5:]
    tokens, size = turned_ref.shape
    has_core = lax.rem(lax.axis_index("seq"), 2) == 1
    for group in range(tokens // GROUP):
        at = group_slice(group)
        for cols in blocks_of(near_ref.shape[1]):
            of = pl.ds(pl.multiple_of(start + cols.start, BLOCK), BLOCK)
            own = jnp.dot(scores_ref[at, :], scaled_ref[at, of], preferred_element_type=f32)
            total = base_ref[at, of] + own_ref[at, of] * own
            for index, (later, _, _, _) in enumerate(spans):
                if later == group:
                    rows = slice(index * size, (index + 1) * size)
                    reach = jnp.dot(turned_ref[at, :], span_refs[0][rows, of], preferred_element_type=f32)
                    total = total + span_refs[1][index, :, of].astype(f32) * reach
            if paired:
                reach = jnp.dot(turned_ref[at, :], core_ref[:size, cols], preferred_element_type=f32)
                reach = jnp.where(has_core, reach, 0.0)
                total = total + far_ref[0, at, of].astype(f32) * reach
            near_ref[at, cols] = total


def near_kernel(parts, spans, paired, *refs):
    count = parts + parts // 2
    in_refs, out_refs, rest = refs[:parts], refs[parts:count], refs[count:-3]
    near_ref, turned_ref, scores_ref = refs[-3:]
    in_map = map_rows(in_refs)
    turned = jnp.transpose(out_map_rows(out_refs, parts))
    turned_ref[...] = turned
    row = lax.broadcasted_iota(jnp.int32, (GROUP, GROUP), 0)
    col = lax.broadcasted_iota(jnp.int32, (GROUP, GROUP), 1)
    for group in range(turned.shape[0] // GROUP):
        at = group_slice(group)
        scores = jnp.dot(turned[at], in_map[:, at], preferred_element_type=f32)
        scores_ref[at, :] = jnp.where(row >= col, scores, 0.0).astype(bf16)
    start = lax.rem(lax.axis_index("seq"), 2) * near_ref.shape[1] if paired else 0
    near_body(spans, paired, start, scores_ref, turned_ref, rest, near_ref)


def other_near_kernel(spans, scores_ref, turned_ref, _, *refs):
    near_ref = refs[-1]
    start = (1 - lax.rem(lax.axis_index("seq"), 2)) * near_ref.shape[1]
    near_body(spans, True, start, scores_ref, turned_ref, refs[:-1], near_ref)


def far_body(turned_ref, near_ref, far_ref, gain_ref, start, columns, levels, state_of, gated_ref):
    tokens = far_ref.shape[1]
    squares = jnp.zeros((tokens, 128), f32)
    for cols in blocks_of(columns):
        at = pl.ds(pl.multiple_of(start + cols.start, BLOCK), BLOCK)
        total = near_ref[:, cols]
        for level in levels:
            state = state_of(level, cols, at).astype(bf16)
            reach = jnp.dot(turned_ref[...], state, preferred_element_type=f32)
            total = total + far_ref[level, :, at].astype(f32) * reach
        gated_ref[:, cols] = total * gain_ref[:, at]
        total = total * total
        for part in range(0, BLOCK, 128):
            squares = squares + total[:, part : part + 128]
    return squares


def row_sums(squares):
    high = squares.astype(bf16)
    low = (squares - high.astype(f32)).astype(bf16)
    parts = jnp.concatenate([high, low], axis=1)
    ones = jnp.ones((16, parts.shape[1]), bf16)
    return lax.dot_general(ones, parts, (((1,), (1,)), ((), ())), preferred_element_type=f32)[:1]


def far_kernel(turned_ref, near_ref, far_ref, gain_ref, *refs):
    state_refs = refs[:-2]
    gated_ref, sums_ref = refs[-2:]

    def state_of(level, cols, _):
        return state_refs[level][:, cols]

    width = near_ref.shape[1]
    levels = range(far_ref.shape[0])
    squares = far_body(turned_ref, near_ref, far_ref, gain_ref, 0, width, levels, state_of, gated_ref)
    sums_ref[...] = row_sums(squares)


def combine_kernel(size, x_ref, y_ref, diagonal_ref, spans_ref):
    rank = lax.axis_index("seq")
    along_x = lax.rem(lax.div(rank, 2), 2)
    along_y = lax.div(rank, 4)

    def parts_of(ref):
        return ref[:size, :].astype(f32), ref[size:, :].astype(f32)[:1]

    x_state, x_decay = parts_of(x_ref)
    y_state, y_decay = parts_of(y_ref)
    d_state, d_decay = parts_of(diagonal_ref)
    newer = jnp.where(along_x == 1, y_state, d_state)
    newer_decay = jnp.where(along_x == 1, y_decay, d_decay)
    older = jnp.where(along_x == 1, d_state, y_state)
    running = jnp.where(along_x == 1, x_decay, 1.0)
    running = jnp.where(along_y == 1, running, 0.0)
    spans_ref[:size, :] = jnp.where(along_x == 1, x_state, 0.0).astype(bf16)
    spans_ref[size:, :] = ((older * newer_decay + newer) * running).astype(bf16)


def far_kernel_of_half(own, *refs):
    turned_ref, near_ref, far_ref, gain_ref, core_ref, spans_ref = refs[:6]
    gated_ref, sums_ref = refs[-2:]
    size = turned_ref.shape[1]
    core = lax.rem(lax.axis_index("seq"), 2)
    half = spans_ref.shape[1]
    start = (core if own else 1 - core) * half

    def state_of(level, cols, at):
        core_decay = core_ref[size:, cols].astype(f32)[:1]
        running = jnp.where(core == 1, core_decay, 1.0)
        return spans_ref[(level - 1) * size : level * size, cols].astype(f32) * running

    squares = far_body(turned_ref, near_ref, far_ref, gain_ref, start, half, (1, 2), state_of, gated_ref)
    sums_ref[...] = squares if own else row_sums(squares + refs[6][...])


def norm_kernel(parts, columns, *refs):
    gated_refs, (out_hbm, out_ref, semaphores) = refs[parts:-3], refs[-3:]
    total = refs[0][...]
    for ref in refs[1:parts]:
        total = total + ref[...]
    scale = lax.rsqrt(total / columns + 1e-05)
    pieces, rest = [], scale
    for _ in range(3):
        pieces.append(rest.astype(bf16).astype(f32))
        rest = rest - pieces[-1]
    tokens = scale.shape[1]
    pieces.append(jnp.zeros((16 - len(pieces), tokens), f32))
    scale = transposed_dot(jnp.concatenate(pieces, axis=0).astype(bf16), jnp.ones((16, 128), bf16))
    width = gated_refs[0].shape[1]
    core = lax.rem(lax.axis_index("seq"), 2)
    sides = (core, 1 - core) if len(gated_refs) == 2 else (0,)
    chunk = tokens // NORM_CHUNKS
    copies = []
    for index in range(NORM_CHUNKS):
        rows = slice(index * chunk, (index + 1) * chunk)
        for ref, side in zip(gated_refs, sides):
            for col in range(0, width, 128):
                at = pl.ds(pl.multiple_of(side * width + col, 128), 128)
                out_ref[rows, at] = (ref[rows, col : col + 128] * scale[rows]).astype(bf16)
        copies.append(pltpu.make_async_copy(out_ref.at[rows], out_hbm.at[rows], semaphores.at[index]))
        copies[-1].start()
    for copy in copies:
        copy.wait()


def call(kernel, out_shape, args, flops=0, bytes_accessed=0, hbm=0, scratch=None, out_space=pltpu.VMEM):
    specs = [pl.BlockSpec(memory_space=pl.ANY)] * hbm + [pl.BlockSpec(memory_space=pltpu.VMEM)] * (len(args) - hbm)
    args = [pltpu.with_memory_space_constraint(arg, pltpu.HBM) for arg in args[:hbm]] + list(args[hbm:])
    if scratch is None:
        scratch = [pltpu.VMEM(arg.shape, arg.dtype) for arg in args[:hbm]]
        scratch += [pltpu.SemaphoreType.DMA((hbm,))] if hbm else []
    return pl.pallas_call(
        kernel,
        out_shape=out_shape,
        in_specs=specs,
        out_specs=jax.tree.map(lambda _: pl.BlockSpec(memory_space=out_space), out_shape),
        scratch_shapes=scratch,
        compiler_params=pltpu.CompilerParams(vmem_limit_bytes=VMEM_LIMIT),
        cost_estimate=pl.CostEstimate(flops=flops, bytes_accessed=bytes_accessed, transcendentals=0),
    )(*args)


def shaped(shape, dtype):
    return jax.ShapeDtypeStruct(shape, dtype)


def flip(array, axis, mask):
    return lax.ppermute(array, axis, [(i, i ^ mask) for i in range(lax.axis_size(axis))])


def from_each(array, axis, masks):
    return [flip(array, axis, mask) for mask in masks]


def around(array, axis):
    size = lax.axis_size(axis)
    return [lax.ppermute(array, axis, [(i, (i + shift) % size) for i in range(size)]) for shift in range(1, size)]


def merged(older, newer, size):
    older, newer = older.astype(f32), newer.astype(f32)
    decay = newer[size : size + 1]
    return jnp.concatenate([older[:size] * decay + newer[:size], older[size:] * decay], axis=0).astype(bf16)


def far_states(shard, size):
    rank = lax.axis_index("seq")
    levels = lax.axis_size("seq").bit_length() - 1
    states = []
    running = jnp.ones((1, shard.shape[1]), f32)
    for level in range(levels):
        theirs = flip(shard, "seq", 1 << level)
        upper = jnp.right_shift(rank, level) % 2 == 1
        states.append(jnp.where(upper, theirs[:size].astype(f32) * running, 0.0).astype(bf16))
        running = jnp.where(upper, running * theirs[size : size + 1].astype(f32), running)
        shard = merged(jnp.where(upper, theirs, shard), jnp.where(upper, shard, theirs), size)
    return states


def on_device(inputs, gate, input_map, output_map, step, decay_rate, level_mix, skip, norm_gain):
    tokens, width = inputs.shape
    heads = step.shape[0]
    parts = lax.axis_size("head")
    levels = lax.axis_size("seq").bit_length() - 1
    size = input_map.shape[0] * parts
    groups = tokens // GROUP
    spans = local_spans(groups)
    dense = 2 * tokens * GROUP * width
    area = tokens * width
    others = from_each(input_map, "head", far_first_masks(parts))
    kept = inputs, gate, level_mix, skip[None, :], input_map, output_map, norm_gain[None, :]
    beside = flip(output_map, "head", FIRST_HOP)
    scaled, cum, *kept = call(
        prepare_kernel,
        (
            *(shaped((tokens, width), bf16), shaped((heads, tokens), f32)),
            *(shaped(array.shape, array.dtype) for array in kept),
        ),
        (step, decay_rate[None, :], *kept),
        flops=16 * dense,
        bytes_accessed=4 * area,
        hbm=9,
        scratch=[pltpu.VMEM(step.shape, f32), pltpu.VMEM((1, heads), f32), pltpu.SemaphoreType.DMA((9,))],
    )
    inputs, gate, level_mix, skip, input_map, output_map, gain = kept
    in_maps = [input_map, *others]
    pairs = lax.axis_size("seq") == 8 and parts == 4
    sides = 2 if pairs else 1
    shard_shape = shaped((size + DECAY_ROWS, width // sides), bf16)
    span_shape = [shaped((len(spans) * size, width), bf16)] if spans else []
    shard, *rest = call(
        functools.partial(states_kernel, parts, sides),
        (*[shard_shape] * sides, *span_shape),
        (*in_maps, scaled, cum),
        flops=dense,
    )
    span_states = rest[sides - 1 :]
    rows = output_map.shape[0]
    if rows % 16 == 0:
        both = call(
            join_kernel,
            shaped((2 * rows, tokens), bf16),
            (output_map, beside, shard),
            flops=8 * dense,
        )
    else:
        both = jnp.concatenate([output_map, beside], axis=0)
    if pairs:
        theirs = flip(rest[0], "seq", 1)
        message = call(
            functools.partial(merge_kernel, size), shard_shape, (shard, theirs, both), flops=0
        )
        other_theirs = flip(lax.optimization_barrier((shard, message))[0], "seq", 1)
    else:
        other_theirs = theirs = message = shard
    out_maps = [both, *from_each(both, "head", pair_masks(parts))]
    factor_shape = [shaped((len(spans), GROUP, width), bf16)] if spans else []
    base, own_factor, far, *span_factors = call(
        functools.partial(factor_kernel, spans, levels),
        (
            *(shaped((tokens, width), f32), shaped((tokens, width), f32)),
            *(shaped((levels, tokens, width), bf16), *factor_shape),
        ),
        (inputs, gate, level_mix, skip, cum, message),
        flops=5 * dense,
        bytes_accessed=0,
    )
    near_args = base, own_factor, far, theirs, scaled, *span_states, *span_factors
    near_shape = shaped((tokens, width // 2 if pairs else width), f32)
    near, turned, scores = call(
        functools.partial(near_kernel, parts, spans, pairs),
        (near_shape, shaped((tokens, size), bf16), shaped((tokens, GROUP), bf16)),
        (*in_maps, *out_maps, *near_args),
    )
    sums_shape = shaped((1, tokens), f32)
    if pairs:
        received = [flip(message, "seq", mask) for mask in (6, 4, 2)]
        *received, other_theirs, near, far = lax.optimization_barrier((*received, other_theirs, near, far))
        own = call(
            functools.partial(combine_kernel, size),
            shaped((2 * size, width // 2), bf16),
            received[::-1],
            bytes_accessed=area,
        )
        other = lax.ppermute(own, "seq", [(i, i ^ 1) for i in range(2, lax.axis_size("seq"))])
        near_args = base, own_factor, far, other_theirs, scaled, *span_states, *span_factors
        other_near = call(
            functools.partial(other_near_kernel, spans), near_shape, (scores, turned, own, *near_args), flops=dense
        )
        gated_shape = shaped((tokens, width // 2), f32)
        own_gated, own_squares = call(
            functools.partial(far_kernel_of_half, True),
            (gated_shape, shaped((tokens, 128), f32)),
            (turned, near, far, gain, theirs, own),
            flops=2 * dense,
            bytes_accessed=6 * area,
        )
        other_gated, sums = call(
            functools.partial(far_kernel_of_half, False),
            (gated_shape, sums_shape),
            (turned, other_near, far, gain, other_theirs, other, own_squares),
            flops=2 * dense,
            bytes_accessed=6 * area,
        )
        gated = (own_gated, other_gated)
    else:
        *gated, sums = call(
            far_kernel,
            (shaped((tokens, width), f32), sums_shape),
            (turned, near, far, gain, *far_states(shard, size)),
            flops=4 * dense,
            bytes_accessed=12 * area,
        )
    last = [sums, *around(sums, "head")]
    return call(
        functools.partial(norm_kernel, len(last), width * parts),
        shaped((tokens, width), bf16),
        (*last, *gated),
        flops=dense,
        bytes_accessed=6 * area,
        scratch=[pltpu.VMEM((tokens, width), bf16), pltpu.SemaphoreType.DMA((NORM_CHUNKS,))],
        out_space=pl.ANY,
    )


def solution(mesh):
    return jax.shard_map(
        on_device,
        mesh=mesh,
        in_specs=(
            P("seq", "head"),
            P("seq", "head"),
            P("head", "seq"),
            P("head", "seq"),
            P("head", "seq"),
            P("head"),
            P(None, "head", "seq"),
            P("head"),
            P("head"),
        ),
        out_specs=P("seq", "head"),
        check_vma=False,
    )
```

```python
import functools

import jax
import jax.numpy as jnp
from jax import lax
from jax.experimental import pallas as pl
from jax.experimental.pallas import tpu as pltpu
from jax.sharding import PartitionSpec as P

P_SIZE = 64
GROUP = 256
DECAY_ROWS = 8
BLOCK = 256
NORM_CHUNKS = 4
FIRST_HOP = 2
VMEM_LIMIT = 40 * 1024 * 1024

f32, bf16 = jnp.float32, jnp.bfloat16
HIGHEST = lax.Precision.HIGHEST
TRANSPOSED = (((0,), (0,)), ((), ()))


def expander(heads, width, copies):
    row = lax.broadcasted_iota(jnp.int32, (copies * heads, width), 0)
    col = lax.broadcasted_iota(jnp.int32, (copies * heads, width), 1)
    return jnp.where(lax.rem(row, heads) == lax.div(col, P_SIZE), 1.0, 0.0)


def far_first_masks(size):
    return (*range(2, size), 1)


def pair_masks(size):
    return tuple(mask for mask in range(1, size) if not mask & FIRST_HOP)


def two_parts(factor):
    high = factor.astype(bf16).astype(f32)
    return jnp.concatenate([high, factor - high], axis=0).astype(bf16)


def transposed_dot(left, right):
    return lax.dot_general(left, right, TRANSPOSED, preferred_element_type=f32)


def head_row(heads, width, column):
    return jnp.sum(expander(heads, width, 1) * column, axis=0, keepdims=True)


def group_slice(group):
    return slice(group * GROUP, (group + 1) * GROUP)


def blocks_of(width):
    return [slice(at, at + BLOCK) for at in range(0, width, BLOCK)]


def local_spans(groups):
    spans = []
    for later in range(groups):
        for bit in range(groups.bit_length() - 1):
            if later >> bit & 1:
                start = later >> bit + 1 << bit + 1
                spans.append((later, bit, start, start + 2**bit))
    return spans


def column_of(row):
    size = row.shape[1]
    at = lax.broadcasted_iota(jnp.int32, (size, size), 0) == lax.broadcasted_iota(jnp.int32, (size, size), 1)
    return jnp.sum(jnp.where(at, row, 0.0), axis=1, keepdims=True)


def map_rows(maps):
    if all(rows.shape[0] % 16 == 0 for rows in maps):
        return jnp.concatenate([rows[...] for rows in maps], axis=0)
    return jnp.concatenate([rows[...].astype(f32) for rows in maps], axis=0).astype(bf16)


def out_map_rows(map_refs, parts):
    rows = map_refs[0].shape[0] // 2
    pairs = [ref if rows % 16 == 0 else ref[...].astype(f32) for ref in map_refs]
    sent = (0, *pair_masks(parts))
    picked = []
    for mask in (0, *far_first_masks(parts)):
        pair = pairs[sent.index(mask & ~FIRST_HOP)]
        at = slice(rows, 2 * rows) if mask & FIRST_HOP else slice(0, rows)
        picked.append(pair.at[at] if rows % 16 == 0 else pair[at])
    return map_rows(picked)


def fetch(sources, targets, semaphores):
    copies = [
        pltpu.make_async_copy(source, target, semaphores.at[index])
        for index, (source, target) in enumerate(zip(sources, targets))
    ]
    for copy in copies:
        copy.start()
    return copies


def prepare_kernel(*refs):
    sources, (scaled_ref, cum_ref), kept_refs = refs[:9], refs[9:11], refs[11:18]
    step_ref, rate_ref, semaphores = refs[18:]
    inputs_ref = kept_refs[0]
    copies = fetch(sources, (step_ref, rate_ref, *kept_refs), semaphores)
    heads, tokens = step_ref.shape
    width = inputs_ref.shape[1]
    row = lax.broadcasted_iota(jnp.int32, (GROUP, GROUP), 0)
    col = lax.broadcasted_iota(jnp.int32, (GROUP, GROUP), 1)
    until = jnp.where(row <= col, 1.0, 0.0)
    expand = expander(heads, width, 2).astype(bf16)
    copies[0].wait()
    copies[1].wait()
    step = step_ref[...]
    log_decay = -step * column_of(rate_ref[...])
    factors = []
    for group in range(tokens // GROUP):
        at = group_slice(group)
        cum = jnp.dot(log_decay[:, at], until, precision=HIGHEST, preferred_element_type=f32)
        cum_ref[:, at] = cum
        factors.append(two_parts(jnp.exp(-cum) * step[:, at]))
    factor = jnp.concatenate(factors, axis=1)
    copies[2].wait()
    for cols in blocks_of(width):
        scale = transposed_dot(factor, expand[:, cols])
        scaled_ref[:, cols] = (inputs_ref[:, cols].astype(f32) * scale).astype(bf16)
    for copy in copies[3:]:
        copy.wait()


def join_kernel(mine_ref, theirs_ref, _, both_ref):
    rows = mine_ref.shape[0]
    both_ref[:rows, :] = mine_ref[...]
    both_ref[rows:, :] = theirs_ref[...]


def states_kernel(parts, sides, *refs):
    map_refs, (scaled_ref, cum_ref), out_refs = refs[:parts], refs[parts : parts + 2], refs[parts + 2 :]
    shard_refs = out_refs[:sides]
    heads, tokens = cum_ref.shape
    width = scaled_ref.shape[1]
    in_map = map_rows(map_refs)
    size = in_map.shape[0]
    cum = cum_ref[...]
    states, decays = [], []
    for group in range(tokens // GROUP):
        at = group_slice(group)
        decay = head_row(heads, width, jnp.exp(cum[:, at.stop - 1 : at.stop]))
        raw = jnp.dot(in_map[:, at], scaled_ref[at, :], preferred_element_type=f32)
        states.append(raw * decay)
        decays.append(decay)
    total, decay = states[0], decays[0]
    for group in range(1, len(states)):
        total = total * decays[group] + states[group]
        decay = decay * decays[group]
    columns = width // sides
    core = lax.rem(lax.axis_index("seq"), 2)
    for ref, first in zip(shard_refs, (core == 0, core == 1)):
        at = slice(0, columns)
        ref[:size, :] = jnp.where(first, total[:, at], total[:, width - columns :]).astype(bf16)
        row = jnp.where(first, decay[:, at], decay[:, width - columns :])
        ref[size:, :] = jnp.broadcast_to(row, (DECAY_ROWS, columns)).astype(bf16)
    for index, (later, _, start, stop) in enumerate(local_spans(len(states))):
        span = states[start]
        for group in range(start + 1, later):
            span = span * decays[group]
            if group < stop:
                span = span + states[group]
        out_refs[sides][index * size : (index + 1) * size, :] = span.astype(bf16)


def merge_kernel(size, mine_ref, theirs_ref, _, pair_ref):
    core = lax.rem(lax.axis_index("seq"), 2)
    mine, theirs = mine_ref[...], theirs_ref[...]
    older = jnp.where(core == 1, theirs, mine).astype(f32)
    newer = jnp.where(core == 1, mine, theirs).astype(f32)
    decay = newer[size : size + 1]
    pair_ref[:size, :] = (older[:size] * decay + newer[:size]).astype(bf16)
    pair_ref[size:, :] = (older[size:] * decay).astype(bf16)


def factor_kernel(spans, levels, *refs):
    inputs_ref, gate_ref, mix_ref, skip_ref, cum_ref, _ = refs[:6]
    base_ref, own_ref, far_ref = refs[6:9]
    span_refs = refs[9:]
    heads, tokens = cum_ref.shape
    width = inputs_ref.shape[1]
    groups = tokens // GROUP
    first = groups.bit_length()
    expand = expander(heads, width, 2).astype(bf16)
    skip = head_row(heads, width, column_of(skip_ref[...]))
    before = jnp.zeros((heads, 1), f32)
    for group in range(groups):
        at = group_slice(group)
        cum = cum_ref[:, at]
        decay = jnp.exp(cum)
        own_mix = two_parts(mix_ref[0, :, at] * decay)
        span_mixes = [
            (index, two_parts(mix_ref[1 + bit, :, at] * decay))
            for index, (later, bit, _, _) in enumerate(spans)
            if later == group
        ]
        decay = jnp.exp(cum + before)
        before = before + cum[:, GROUP - 1 : GROUP]
        far_mixes = [two_parts(mix_ref[first + level, :, at] * decay) for level in range(levels)]
        for cols in blocks_of(width):
            gate = gate_ref[at, cols].astype(f32)
            swish = gate / (1.0 + jnp.exp(-gate))
            base_ref[at, cols] = skip[:, cols] * inputs_ref[at, cols].astype(f32) * swish
            own_ref[at, cols] = transposed_dot(own_mix, expand[:, cols]) * swish
            for level, mix in enumerate(far_mixes):
                far_ref[level, at, cols] = (transposed_dot(mix, expand[:, cols]) * swish).astype(bf16)
            for index, mix in span_mixes:
                span_refs[0][index, :, cols] = (transposed_dot(mix, expand[:, cols]) * swish).astype(bf16)


def near_body(spans, paired, start, scores_ref, turned_ref, refs, near_ref):
    base_ref, own_ref, far_ref, core_ref, scaled_ref = refs[:5]
    span_refs = refs[5:]
    tokens, size = turned_ref.shape
    has_core = lax.rem(lax.axis_index("seq"), 2) == 1
    for group in range(tokens // GROUP):
        at = group_slice(group)
        for cols in blocks_of(near_ref.shape[1]):
            of = pl.ds(pl.multiple_of(start + cols.start, BLOCK), BLOCK)
            own = jnp.dot(scores_ref[at, :], scaled_ref[at, of], preferred_element_type=f32)
            total = base_ref[at, of] + own_ref[at, of] * own
            for index, (later, _, _, _) in enumerate(spans):
                if later == group:
                    rows = slice(index * size, (index + 1) * size)
                    reach = jnp.dot(turned_ref[at, :], span_refs[0][rows, of], preferred_element_type=f32)
                    total = total + span_refs[1][index, :, of].astype(f32) * reach
            if paired:
                reach = jnp.dot(turned_ref[at, :], core_ref[:size, cols], preferred_element_type=f32)
                reach = jnp.where(has_core, reach, 0.0)
                total = total + far_ref[0, at, of].astype(f32) * reach
            near_ref[at, cols] = total


def near_kernel(parts, spans, paired, *refs):
    count = parts + parts // 2
    in_refs, out_refs, rest = refs[:parts], refs[parts:count], refs[count:-3]
    near_ref, turned_ref, scores_ref = refs[-3:]
    in_map = map_rows(in_refs)
    turned = jnp.transpose(out_map_rows(out_refs, parts))
    turned_ref[...] = turned
    row = lax.broadcasted_iota(jnp.int32, (GROUP, GROUP), 0)
    col = lax.broadcasted_iota(jnp.int32, (GROUP, GROUP), 1)
    for group in range(turned.shape[0] // GROUP):
        at = group_slice(group)
        scores = jnp.dot(turned[at], in_map[:, at], preferred_element_type=f32)
        scores_ref[at, :] = jnp.where(row >= col, scores, 0.0).astype(bf16)
    start = lax.rem(lax.axis_index("seq"), 2) * near_ref.shape[1] if paired else 0
    near_body(spans, paired, start, scores_ref, turned_ref, rest, near_ref)


def other_near_kernel(spans, scores_ref, turned_ref, *refs):
    near_ref = refs[-1]
    start = (1 - lax.rem(lax.axis_index("seq"), 2)) * near_ref.shape[1]
    near_body(spans, True, start, scores_ref, turned_ref, refs[:-1], near_ref)


def far_body(turned_ref, near_ref, far_ref, gain_ref, start, columns, levels, state_of, gated_ref):
    tokens = far_ref.shape[1]
    squares = jnp.zeros((tokens, 128), f32)
    for cols in blocks_of(columns):
        at = pl.ds(pl.multiple_of(start + cols.start, BLOCK), BLOCK)
        total = near_ref[:, cols]
        for level in levels:
            state = state_of(level, cols, at).astype(bf16)
            reach = jnp.dot(turned_ref[...], state, preferred_element_type=f32)
            total = total + far_ref[level, :, at].astype(f32) * reach
        gated_ref[:, cols] = total * gain_ref[:, at]
        total = total * total
        for part in range(0, BLOCK, 128):
            squares = squares + total[:, part : part + 128]
    return squares


def row_sums(squares):
    high = squares.astype(bf16)
    low = (squares - high.astype(f32)).astype(bf16)
    parts = jnp.concatenate([high, low], axis=1)
    ones = jnp.ones((16, parts.shape[1]), bf16)
    return lax.dot_general(ones, parts, (((1,), (1,)), ((), ())), preferred_element_type=f32)[:1]


def far_kernel(turned_ref, near_ref, far_ref, gain_ref, *refs):
    state_refs = refs[:-2]
    gated_ref, sums_ref = refs[-2:]

    def state_of(level, cols, _):
        return state_refs[level][:, cols]

    width = near_ref.shape[1]
    levels = range(far_ref.shape[0])
    squares = far_body(turned_ref, near_ref, far_ref, gain_ref, 0, width, levels, state_of, gated_ref)
    sums_ref[...] = row_sums(squares)


def combine_kernel(size, x_ref, y_ref, diagonal_ref, spans_ref):
    rank = lax.axis_index("seq")
    along_x = lax.rem(lax.div(rank, 2), 2)
    along_y = lax.div(rank, 4)

    def parts_of(ref):
        return ref[:size, :].astype(f32), ref[size:, :].astype(f32)[:1]

    x_state, x_decay = parts_of(x_ref)
    y_state, y_decay = parts_of(y_ref)
    d_state, d_decay = parts_of(diagonal_ref)
    newer = jnp.where(along_x == 1, y_state, d_state)
    newer_decay = jnp.where(along_x == 1, y_decay, d_decay)
    older = jnp.where(along_x == 1, d_state, y_state)
    running = jnp.where(along_x == 1, x_decay, 1.0)
    running = jnp.where(along_y == 1, running, 0.0)
    spans_ref[:size, :] = jnp.where(along_x == 1, x_state, 0.0).astype(bf16)
    spans_ref[size:, :] = ((older * newer_decay + newer) * running).astype(bf16)


def far_kernel_of_half(own, *refs):
    turned_ref, near_ref, far_ref, gain_ref, core_ref, spans_ref = refs[:6]
    gated_ref, sums_ref = refs[-2:]
    size = turned_ref.shape[1]
    core = lax.rem(lax.axis_index("seq"), 2)
    half = spans_ref.shape[1]
    start = (core if own else 1 - core) * half

    def state_of(level, cols, at):
        core_decay = core_ref[size:, cols].astype(f32)[:1]
        running = jnp.where(core == 1, core_decay, 1.0)
        return spans_ref[(level - 1) * size : level * size, cols].astype(f32) * running

    squares = far_body(turned_ref, near_ref, far_ref, gain_ref, start, half, (1, 2), state_of, gated_ref)
    sums_ref[...] = squares if own else row_sums(squares + refs[6][...])


def norm_kernel(parts, columns, *refs):
    gated_refs, (out_hbm, out_ref, semaphores) = refs[parts:-3], refs[-3:]
    total = refs[0][...]
    for ref in refs[1:parts]:
        total = total + ref[...]
    scale = lax.rsqrt(total / columns + 1e-05)
    pieces, rest = [], scale
    for _ in range(3):
        pieces.append(rest.astype(bf16).astype(f32))
        rest = rest - pieces[-1]
    tokens = scale.shape[1]
    pieces.append(jnp.zeros((16 - len(pieces), tokens), f32))
    scale = transposed_dot(jnp.concatenate(pieces, axis=0).astype(bf16), jnp.ones((16, 128), bf16))
    width = gated_refs[0].shape[1]
    core = lax.rem(lax.axis_index("seq"), 2)
    sides = (core, 1 - core) if len(gated_refs) == 2 else (0,)
    chunk = tokens // NORM_CHUNKS
    copies = []
    for index in range(NORM_CHUNKS):
        rows = slice(index * chunk, (index + 1) * chunk)
        for ref, side in zip(gated_refs, sides):
            for col in range(0, width, 128):
                at = pl.ds(pl.multiple_of(side * width + col, 128), 128)
                out_ref[rows, at] = (ref[rows, col : col + 128] * scale[rows]).astype(bf16)
        copies.append(pltpu.make_async_copy(out_ref.at[rows], out_hbm.at[rows], semaphores.at[index]))
        copies[-1].start()
    for copy in copies:
        copy.wait()


def call(kernel, out_shape, args, flops=0, bytes_accessed=0, hbm=0, scratch=None, out_space=pltpu.VMEM):
    specs = [pl.BlockSpec(memory_space=pl.ANY)] * hbm + [pl.BlockSpec(memory_space=pltpu.VMEM)] * (len(args) - hbm)
    args = [pltpu.with_memory_space_constraint(arg, pltpu.HBM) for arg in args[:hbm]] + list(args[hbm:])
    if scratch is None:
        scratch = [pltpu.VMEM(arg.shape, arg.dtype) for arg in args[:hbm]]
        scratch += [pltpu.SemaphoreType.DMA((hbm,))] if hbm else []
    return pl.pallas_call(
        kernel,
        out_shape=out_shape,
        in_specs=specs,
        out_specs=jax.tree.map(lambda _: pl.BlockSpec(memory_space=out_space), out_shape),
        scratch_shapes=scratch,
        compiler_params=pltpu.CompilerParams(vmem_limit_bytes=VMEM_LIMIT),
        cost_estimate=pl.CostEstimate(flops=flops, bytes_accessed=bytes_accessed, transcendentals=0),
    )(*args)


def shaped(shape, dtype):
    return jax.ShapeDtypeStruct(shape, dtype)


def flip(array, axis, mask):
    return lax.ppermute(array, axis, [(i, i ^ mask) for i in range(lax.axis_size(axis))])


def from_each(array, axis, masks):
    return [flip(array, axis, mask) for mask in masks]


def around(array, axis):
    size = lax.axis_size(axis)
    return [lax.ppermute(array, axis, [(i, (i + shift) % size) for i in range(size)]) for shift in range(1, size)]


def merged(older, newer, size):
    older, newer = older.astype(f32), newer.astype(f32)
    decay = newer[size : size + 1]
    return jnp.concatenate([older[:size] * decay + newer[:size], older[size:] * decay], axis=0).astype(bf16)


def far_states(shard, size):
    rank = lax.axis_index("seq")
    levels = lax.axis_size("seq").bit_length() - 1
    states = []
    running = jnp.ones((1, shard.shape[1]), f32)
    for level in range(levels):
        theirs = flip(shard, "seq", 1 << level)
        upper = jnp.right_shift(rank, level) % 2 == 1
        states.append(jnp.where(upper, theirs[:size].astype(f32) * running, 0.0).astype(bf16))
        running = jnp.where(upper, running * theirs[size : size + 1].astype(f32), running)
        shard = merged(jnp.where(upper, theirs, shard), jnp.where(upper, shard, theirs), size)
    return states


def on_device(inputs, gate, input_map, output_map, step, decay_rate, level_mix, skip, norm_gain):
    tokens, width = inputs.shape
    heads = step.shape[0]
    parts = lax.axis_size("head")
    levels = lax.axis_size("seq").bit_length() - 1
    size = input_map.shape[0] * parts
    groups = tokens // GROUP
    spans = local_spans(groups)
    dense = 2 * tokens * GROUP * width
    area = tokens * width
    others = from_each(input_map, "head", far_first_masks(parts))
    kept = inputs, gate, level_mix, skip[None, :], input_map, output_map, norm_gain[None, :]
    beside = flip(output_map, "head", FIRST_HOP)
    scaled, cum, *kept = call(
        prepare_kernel,
        (
            *(shaped((tokens, width), bf16), shaped((heads, tokens), f32)),
            *(shaped(array.shape, array.dtype) for array in kept),
        ),
        (step, decay_rate[None, :], *kept),
        flops=16 * dense,
        bytes_accessed=4 * area,
        hbm=9,
        scratch=[pltpu.VMEM(step.shape, f32), pltpu.VMEM((1, heads), f32), pltpu.SemaphoreType.DMA((9,))],
    )
    inputs, gate, level_mix, skip, input_map, output_map, gain = kept
    in_maps = [input_map, *others]
    pairs = lax.axis_size("seq") == 8 and parts == 4
    sides = 2 if pairs else 1
    shard_shape = shaped((size + DECAY_ROWS, width // sides), bf16)
    span_shape = [shaped((len(spans) * size, width), bf16)] if spans else []
    shard, *rest = call(
        functools.partial(states_kernel, parts, sides),
        (*[shard_shape] * sides, *span_shape),
        (*in_maps, scaled, cum),
        flops=dense,
    )
    span_states = rest[sides - 1 :]
    rows = output_map.shape[0]
    if rows % 16 == 0:
        both = call(
            join_kernel,
            shaped((2 * rows, tokens), bf16),
            (output_map, beside, shard),
            flops=8 * dense,
        )
    else:
        both = jnp.concatenate([output_map, beside], axis=0)
    if pairs:
        theirs = flip(rest[0], "seq", 1)
        message = call(
            functools.partial(merge_kernel, size), shard_shape, (shard, theirs, both), flops=0
        )
        other_theirs = flip(lax.optimization_barrier((shard, message))[0], "seq", 1)
    else:
        other_theirs = theirs = message = shard
    out_maps = [both, *from_each(both, "head", pair_masks(parts))]
    factor_shape = [shaped((len(spans), GROUP, width), bf16)] if spans else []
    base, own_factor, far, *span_factors = call(
        functools.partial(factor_kernel, spans, levels),
        (
            *(shaped((tokens, width), f32), shaped((tokens, width), f32)),
            *(shaped((levels, tokens, width), bf16), *factor_shape),
        ),
        (inputs, gate, level_mix, skip, cum, message),
        flops=5 * dense,
        bytes_accessed=0,
    )
    near_args = base, own_factor, far, theirs, scaled, *span_states, *span_factors
    near_shape = shaped((tokens, width // 2 if pairs else width), f32)
    near, turned, scores = call(
        functools.partial(near_kernel, parts, spans, pairs),
        (near_shape, shaped((tokens, size), bf16), shaped((tokens, GROUP), bf16)),
        (*in_maps, *out_maps, *near_args),
    )
    sums_shape = shaped((1, tokens), f32)
    if pairs:
        received = [flip(message, "seq", mask) for mask in (6, 4, 2)]
        near_args = base, own_factor, far, other_theirs, scaled, *span_states, *span_factors
        other_near = call(
            functools.partial(other_near_kernel, spans), near_shape, (scores, turned, *near_args), flops=0
        )
        *received, near, far, other_near = lax.optimization_barrier((*received, near, far, other_near))
        own = call(
            functools.partial(combine_kernel, size),
            shaped((2 * size, width // 2), bf16),
            received[::-1],
            bytes_accessed=area,
        )
        other = lax.ppermute(own, "seq", [(i, i ^ 1 if i >= 2 else i) for i in range(lax.axis_size("seq"))])
        near_args = base, own_factor, far, other_theirs, scaled, *span_states, *span_factors
        gated_shape = shaped((tokens, width // 2), f32)
        own_gated, own_squares = call(
            functools.partial(far_kernel_of_half, True),
            (gated_shape, shaped((tokens, 128), f32)),
            (turned, near, far, gain, theirs, own),
            flops=2 * dense,
            bytes_accessed=6 * area,
        )
        other_gated, sums = call(
            functools.partial(far_kernel_of_half, False),
            (gated_shape, sums_shape),
            (turned, other_near, far, gain, other_theirs, other, own_squares),
            flops=2 * dense,
            bytes_accessed=6 * area,
        )
        gated = (own_gated, other_gated)
    else:
        *gated, sums = call(
            far_kernel,
            (shaped((tokens, width), f32), sums_shape),
            (turned, near, far, gain, *far_states(shard, size)),
            flops=4 * dense,
            bytes_accessed=12 * area,
        )
    last = [sums, *around(sums, "head")]
    return call(
        functools.partial(norm_kernel, len(last), width * parts),
        shaped((tokens, width), bf16),
        (*last, *gated),
        flops=dense,
        bytes_accessed=6 * area,
        scratch=[pltpu.VMEM((tokens, width), bf16), pltpu.SemaphoreType.DMA((NORM_CHUNKS,))],
        out_space=pl.ANY,
    )


def solution(mesh):
    return jax.shard_map(
        on_device,
        mesh=mesh,
        in_specs=(
            P("seq", "head"),
            P("seq", "head"),
            P("head", "seq"),
            P("head", "seq"),
            P("head", "seq"),
            P("head"),
            P(None, "head", "seq"),
            P("head"),
            P("head"),
        ),
        out_specs=P("seq", "head"),
        check_vma=False,
    )
```

```python
import functools

import jax
import jax.numpy as jnp
from jax import lax
from jax.experimental import pallas as pl
from jax.experimental.pallas import tpu as pltpu
from jax.sharding import PartitionSpec as P

P_SIZE = 64
GROUP = 256
DECAY_ROWS = 8
BLOCK = 256
NORM_CHUNKS = 4
FIRST_HOP = 2
CYCLE = [(2 * chip + core, 2 * target + core) for chip, target in ((0, 3), (3, 1), (1, 2), (2, 0)) for core in (0, 1)]
VMEM_LIMIT = 40 * 1024 * 1024

f32, bf16 = jnp.float32, jnp.bfloat16
HIGHEST = lax.Precision.HIGHEST
TRANSPOSED = (((0,), (0,)), ((), ()))


def expander(heads, width, copies):
    row = lax.broadcasted_iota(jnp.int32, (copies * heads, width), 0)
    col = lax.broadcasted_iota(jnp.int32, (copies * heads, width), 1)
    return jnp.where(lax.rem(row, heads) == lax.div(col, P_SIZE), 1.0, 0.0)


def far_first_masks(size):
    return (*range(2, size), 1)


def pair_masks(size):
    return tuple(mask for mask in range(1, size) if not mask & FIRST_HOP)


def two_parts(factor):
    high = factor.astype(bf16).astype(f32)
    return jnp.concatenate([high, factor - high], axis=0).astype(bf16)


def transposed_dot(left, right):
    return lax.dot_general(left, right, TRANSPOSED, preferred_element_type=f32)


def head_row(heads, width, column):
    return jnp.sum(expander(heads, width, 1) * column, axis=0, keepdims=True)


def group_slice(group):
    return slice(group * GROUP, (group + 1) * GROUP)


def blocks_of(width):
    return [slice(at, at + BLOCK) for at in range(0, width, BLOCK)]


def local_spans(groups):
    spans = []
    for later in range(groups):
        for bit in range(groups.bit_length() - 1):
            if later >> bit & 1:
                start = later >> bit + 1 << bit + 1
                spans.append((later, bit, start, start + 2**bit))
    return spans


def column_of(row):
    size = row.shape[1]
    at = lax.broadcasted_iota(jnp.int32, (size, size), 0) == lax.broadcasted_iota(jnp.int32, (size, size), 1)
    return jnp.sum(jnp.where(at, row, 0.0), axis=1, keepdims=True)


def map_rows(maps):
    if all(rows.shape[0] % 16 == 0 for rows in maps):
        return jnp.concatenate([rows[...] for rows in maps], axis=0)
    return jnp.concatenate([rows[...].astype(f32) for rows in maps], axis=0).astype(bf16)


def out_map_rows(map_refs, parts):
    rows = map_refs[0].shape[0] // 2
    pairs = [ref if rows % 16 == 0 else ref[...].astype(f32) for ref in map_refs]
    sent = (0, *pair_masks(parts))
    picked = []
    for mask in (0, *far_first_masks(parts)):
        pair = pairs[sent.index(mask & ~FIRST_HOP)]
        at = slice(rows, 2 * rows) if mask & FIRST_HOP else slice(0, rows)
        picked.append(pair.at[at] if rows % 16 == 0 else pair[at])
    return map_rows(picked)


def fetch(sources, targets, semaphores):
    copies = [
        pltpu.make_async_copy(source, target, semaphores.at[index])
        for index, (source, target) in enumerate(zip(sources, targets))
    ]
    for copy in copies:
        copy.start()
    return copies


def prepare_kernel(*refs):
    sources, (scaled_ref, cum_ref), kept_refs = refs[:9], refs[9:11], refs[11:18]
    step_ref, rate_ref, semaphores = refs[18:]
    inputs_ref = kept_refs[0]
    copies = fetch(sources, (step_ref, rate_ref, *kept_refs), semaphores)
    heads, tokens = step_ref.shape
    width = inputs_ref.shape[1]
    row = lax.broadcasted_iota(jnp.int32, (GROUP, GROUP), 0)
    col = lax.broadcasted_iota(jnp.int32, (GROUP, GROUP), 1)
    until = jnp.where(row <= col, 1.0, 0.0)
    expand = expander(heads, width, 2).astype(bf16)
    copies[0].wait()
    copies[1].wait()
    step = step_ref[...]
    log_decay = -step * column_of(rate_ref[...])
    factors = []
    for group in range(tokens // GROUP):
        at = group_slice(group)
        cum = jnp.dot(log_decay[:, at], until, precision=HIGHEST, preferred_element_type=f32)
        cum_ref[:, at] = cum
        factors.append(two_parts(jnp.exp(-cum) * step[:, at]))
    factor = jnp.concatenate(factors, axis=1)
    copies[2].wait()
    for cols in blocks_of(width):
        scale = transposed_dot(factor, expand[:, cols])
        scaled_ref[:, cols] = (inputs_ref[:, cols].astype(f32) * scale).astype(bf16)
    for copy in copies[3:]:
        copy.wait()


def join_kernel(mine_ref, theirs_ref, _, both_ref):
    rows = mine_ref.shape[0]
    both_ref[:rows, :] = mine_ref[...]
    both_ref[rows:, :] = theirs_ref[...]


def states_kernel(parts, sides, *refs):
    map_refs, (scaled_ref, cum_ref), out_refs = refs[:parts], refs[parts : parts + 2], refs[parts + 2 :]
    shard_refs = out_refs[:sides]
    heads, tokens = cum_ref.shape
    width = scaled_ref.shape[1]
    in_map = map_rows(map_refs)
    size = in_map.shape[0]
    cum = cum_ref[...]
    states, decays = [], []
    for group in range(tokens // GROUP):
        at = group_slice(group)
        decay = head_row(heads, width, jnp.exp(cum[:, at.stop - 1 : at.stop]))
        raw = jnp.dot(in_map[:, at], scaled_ref[at, :], preferred_element_type=f32)
        states.append(raw * decay)
        decays.append(decay)
    total, decay = states[0], decays[0]
    for group in range(1, len(states)):
        total = total * decays[group] + states[group]
        decay = decay * decays[group]
    columns = width // sides
    core = lax.rem(lax.axis_index("seq"), 2)
    for ref, first in zip(shard_refs, (core == 0, core == 1)):
        at = slice(0, columns)
        ref[:size, :] = jnp.where(first, total[:, at], total[:, width - columns :]).astype(bf16)
        row = jnp.where(first, decay[:, at], decay[:, width - columns :])
        ref[size:, :] = jnp.broadcast_to(row, (DECAY_ROWS, columns)).astype(bf16)
    for index, (later, _, start, stop) in enumerate(local_spans(len(states))):
        span = states[start]
        for group in range(start + 1, later):
            span = span * decays[group]
            if group < stop:
                span = span + states[group]
        out_refs[sides][index * size : (index + 1) * size, :] = span.astype(bf16)


def merge_kernel(size, mine_ref, theirs_ref, _, pair_ref):
    core = lax.rem(lax.axis_index("seq"), 2)
    mine, theirs = mine_ref[...], theirs_ref[...]
    older = jnp.where(core == 1, theirs, mine).astype(f32)
    newer = jnp.where(core == 1, mine, theirs).astype(f32)
    decay = newer[size : size + 1]
    pair_ref[:size, :] = (older[:size] * decay + newer[:size]).astype(bf16)
    pair_ref[size:, :] = (older[size:] * decay).astype(bf16)


def factor_kernel(spans, levels, *refs):
    inputs_ref, gate_ref, mix_ref, skip_ref, cum_ref, _ = refs[:6]
    base_ref, own_ref, far_ref = refs[6:9]
    span_refs = refs[9:]
    heads, tokens = cum_ref.shape
    width = inputs_ref.shape[1]
    groups = tokens // GROUP
    first = groups.bit_length()
    expand = expander(heads, width, 2).astype(bf16)
    skip = head_row(heads, width, column_of(skip_ref[...]))
    before = jnp.zeros((heads, 1), f32)
    for group in range(groups):
        at = group_slice(group)
        cum = cum_ref[:, at]
        decay = jnp.exp(cum)
        own_mix = two_parts(mix_ref[0, :, at] * decay)
        span_mixes = [
            (index, two_parts(mix_ref[1 + bit, :, at] * decay))
            for index, (later, bit, _, _) in enumerate(spans)
            if later == group
        ]
        decay = jnp.exp(cum + before)
        before = before + cum[:, GROUP - 1 : GROUP]
        far_mixes = [two_parts(mix_ref[first + level, :, at] * decay) for level in range(levels)]
        for cols in blocks_of(width):
            gate = gate_ref[at, cols].astype(f32)
            swish = gate / (1.0 + jnp.exp(-gate))
            base_ref[at, cols] = skip[:, cols] * inputs_ref[at, cols].astype(f32) * swish
            own_ref[at, cols] = transposed_dot(own_mix, expand[:, cols]) * swish
            for level, mix in enumerate(far_mixes):
                far_ref[level, at, cols] = (transposed_dot(mix, expand[:, cols]) * swish).astype(bf16)
            for index, mix in span_mixes:
                span_refs[0][index, :, cols] = (transposed_dot(mix, expand[:, cols]) * swish).astype(bf16)


def near_body(spans, paired, start, scores_ref, turned_ref, refs, near_ref):
    base_ref, own_ref, far_ref, core_ref, scaled_ref = refs[:5]
    span_refs = refs[5:]
    tokens, size = turned_ref.shape
    has_core = lax.rem(lax.axis_index("seq"), 2) == 1
    for group in range(tokens // GROUP):
        at = group_slice(group)
        for cols in blocks_of(near_ref.shape[1]):
            of = pl.ds(pl.multiple_of(start + cols.start, BLOCK), BLOCK)
            own = jnp.dot(scores_ref[at, :], scaled_ref[at, of], preferred_element_type=f32)
            total = base_ref[at, of] + own_ref[at, of] * own
            for index, (later, _, _, _) in enumerate(spans):
                if later == group:
                    rows = slice(index * size, (index + 1) * size)
                    reach = jnp.dot(turned_ref[at, :], span_refs[0][rows, of], preferred_element_type=f32)
                    total = total + span_refs[1][index, :, of].astype(f32) * reach
            if paired:
                reach = jnp.dot(turned_ref[at, :], core_ref[:size, cols], preferred_element_type=f32)
                reach = jnp.where(has_core, reach, 0.0)
                total = total + far_ref[0, at, of].astype(f32) * reach
            near_ref[at, cols] = total


def near_kernel(parts, spans, paired, *refs):
    count = parts + parts // 2
    in_refs, out_refs, rest = refs[:parts], refs[parts:count], refs[count:-3]
    near_ref, turned_ref, scores_ref = refs[-3:]
    in_map = map_rows(in_refs)
    turned = jnp.transpose(out_map_rows(out_refs, parts))
    turned_ref[...] = turned
    row = lax.broadcasted_iota(jnp.int32, (GROUP, GROUP), 0)
    col = lax.broadcasted_iota(jnp.int32, (GROUP, GROUP), 1)
    for group in range(turned.shape[0] // GROUP):
        at = group_slice(group)
        scores = jnp.dot(turned[at], in_map[:, at], preferred_element_type=f32)
        scores_ref[at, :] = jnp.where(row >= col, scores, 0.0).astype(bf16)
    start = lax.rem(lax.axis_index("seq"), 2) * near_ref.shape[1] if paired else 0
    near_body(spans, paired, start, scores_ref, turned_ref, rest, near_ref)


def other_near_kernel(spans, scores_ref, turned_ref, _, *refs):
    near_ref = refs[-1]
    start = (1 - lax.rem(lax.axis_index("seq"), 2)) * near_ref.shape[1]
    near_body(spans, True, start, scores_ref, turned_ref, refs[:-1], near_ref)


def far_body(turned_ref, near_ref, far_ref, gain_ref, start, columns, levels, state_of, gated_ref):
    tokens = far_ref.shape[1]
    squares = jnp.zeros((tokens, 128), f32)
    for cols in blocks_of(columns):
        at = pl.ds(pl.multiple_of(start + cols.start, BLOCK), BLOCK)
        total = near_ref[:, cols]
        for level in levels:
            state = state_of(level, cols, at).astype(bf16)
            reach = jnp.dot(turned_ref[...], state, preferred_element_type=f32)
            total = total + far_ref[level, :, at].astype(f32) * reach
        gated_ref[:, cols] = total * gain_ref[:, at]
        total = total * total
        for part in range(0, BLOCK, 128):
            squares = squares + total[:, part : part + 128]
    return squares


def row_sums(squares):
    high = squares.astype(bf16)
    low = (squares - high.astype(f32)).astype(bf16)
    parts = jnp.concatenate([high, low], axis=1)
    ones = jnp.ones((16, parts.shape[1]), bf16)
    return lax.dot_general(ones, parts, (((1,), (1,)), ((), ())), preferred_element_type=f32)[:1]


def far_kernel(turned_ref, near_ref, far_ref, gain_ref, *refs):
    state_refs = refs[:-2]
    gated_ref, sums_ref = refs[-2:]

    def state_of(level, cols, _):
        return state_refs[level][:, cols]

    width = near_ref.shape[1]
    levels = range(far_ref.shape[0])
    squares = far_body(turned_ref, near_ref, far_ref, gain_ref, 0, width, levels, state_of, gated_ref)
    sums_ref[...] = row_sums(squares)


def combine_kernel(size, x_ref, y_ref, diagonal_ref, spans_ref):
    rank = lax.axis_index("seq")
    along_x = lax.rem(lax.div(rank, 2), 2)
    along_y = lax.div(rank, 4)

    def parts_of(ref):
        return ref[:size, :].astype(f32), ref[size:, :].astype(f32)[:1]

    x_state, x_decay = parts_of(x_ref)
    y_state, y_decay = parts_of(y_ref)
    d_state, d_decay = parts_of(diagonal_ref)
    newer = jnp.where(along_x == 1, y_state, d_state)
    newer_decay = jnp.where(along_x == 1, y_decay, d_decay)
    older = jnp.where(along_x == 1, d_state, y_state)
    running = jnp.where(along_x == 1, x_decay, 1.0)
    running = jnp.where(along_y == 1, running, 0.0)
    spans_ref[:size, :] = jnp.where(along_x == 1, x_state, 0.0).astype(bf16)
    spans_ref[size:, :] = ((older * newer_decay + newer) * running).astype(bf16)


def far_kernel_of_half(own, *refs):
    turned_ref, near_ref, far_ref, gain_ref, core_ref, spans_ref = refs[:6]
    gated_ref, sums_ref = refs[-2:]
    size = turned_ref.shape[1]
    core = lax.rem(lax.axis_index("seq"), 2)
    half = spans_ref.shape[1]
    start = (core if own else 1 - core) * half

    def state_of(level, cols, at):
        core_decay = core_ref[size:, cols].astype(f32)[:1]
        running = jnp.where(core == 1, core_decay, 1.0)
        return spans_ref[(level - 1) * size : level * size, cols].astype(f32) * running

    squares = far_body(turned_ref, near_ref, far_ref, gain_ref, start, half, (1, 2), state_of, gated_ref)
    sums_ref[...] = squares if own else row_sums(squares + refs[6][...])


def norm_kernel(parts, columns, *refs):
    gated_refs, (out_hbm, out_ref, semaphores) = refs[parts:-3], refs[-3:]
    total = refs[0][...]
    for ref in refs[1:parts]:
        total = total + ref[...]
    scale = lax.rsqrt(total / columns + 1e-05)
    pieces, rest = [], scale
    for _ in range(3):
        pieces.append(rest.astype(bf16).astype(f32))
        rest = rest - pieces[-1]
    tokens = scale.shape[1]
    pieces.append(jnp.zeros((16 - len(pieces), tokens), f32))
    scale = transposed_dot(jnp.concatenate(pieces, axis=0).astype(bf16), jnp.ones((16, 128), bf16))
    width = gated_refs[0].shape[1]
    core = lax.rem(lax.axis_index("seq"), 2)
    sides = (core, 1 - core) if len(gated_refs) == 2 else (0,)
    chunk = tokens // NORM_CHUNKS
    copies = []
    for index in range(NORM_CHUNKS):
        rows = slice(index * chunk, (index + 1) * chunk)
        for ref, side in zip(gated_refs, sides):
            for col in range(0, width, 128):
                at = pl.ds(pl.multiple_of(side * width + col, 128), 128)
                out_ref[rows, at] = (ref[rows, col : col + 128] * scale[rows]).astype(bf16)
        copies.append(pltpu.make_async_copy(out_ref.at[rows], out_hbm.at[rows], semaphores.at[index]))
        copies[-1].start()
    for copy in copies:
        copy.wait()


def call(kernel, out_shape, args, flops=0, bytes_accessed=0, hbm=0, scratch=None, out_space=pltpu.VMEM):
    specs = [pl.BlockSpec(memory_space=pl.ANY)] * hbm + [pl.BlockSpec(memory_space=pltpu.VMEM)] * (len(args) - hbm)
    args = [pltpu.with_memory_space_constraint(arg, pltpu.HBM) for arg in args[:hbm]] + list(args[hbm:])
    if scratch is None:
        scratch = [pltpu.VMEM(arg.shape, arg.dtype) for arg in args[:hbm]]
        scratch += [pltpu.SemaphoreType.DMA((hbm,))] if hbm else []
    return pl.pallas_call(
        kernel,
        out_shape=out_shape,
        in_specs=specs,
        out_specs=jax.tree.map(lambda _: pl.BlockSpec(memory_space=out_space), out_shape),
        scratch_shapes=scratch,
        compiler_params=pltpu.CompilerParams(vmem_limit_bytes=VMEM_LIMIT),
        cost_estimate=pl.CostEstimate(flops=flops, bytes_accessed=bytes_accessed, transcendentals=0),
    )(*args)


def shaped(shape, dtype):
    return jax.ShapeDtypeStruct(shape, dtype)


def flip(array, axis, mask):
    return lax.ppermute(array, axis, [(i, i ^ mask) for i in range(lax.axis_size(axis))])


def from_each(array, axis, masks):
    return [flip(array, axis, mask) for mask in masks]


def around(array, axis):
    size = lax.axis_size(axis)
    return [lax.ppermute(array, axis, [(i, (i + shift) % size) for i in range(size)]) for shift in range(1, size)]


def merged(older, newer, size):
    older, newer = older.astype(f32), newer.astype(f32)
    decay = newer[size : size + 1]
    return jnp.concatenate([older[:size] * decay + newer[:size], older[size:] * decay], axis=0).astype(bf16)


def far_states(shard, size):
    rank = lax.axis_index("seq")
    levels = lax.axis_size("seq").bit_length() - 1
    states = []
    running = jnp.ones((1, shard.shape[1]), f32)
    for level in range(levels):
        theirs = flip(shard, "seq", 1 << level)
        upper = jnp.right_shift(rank, level) % 2 == 1
        states.append(jnp.where(upper, theirs[:size].astype(f32) * running, 0.0).astype(bf16))
        running = jnp.where(upper, running * theirs[size : size + 1].astype(f32), running)
        shard = merged(jnp.where(upper, theirs, shard), jnp.where(upper, shard, theirs), size)
    return states


def on_device(inputs, gate, input_map, output_map, step, decay_rate, level_mix, skip, norm_gain):
    tokens, width = inputs.shape
    heads = step.shape[0]
    parts = lax.axis_size("head")
    levels = lax.axis_size("seq").bit_length() - 1
    size = input_map.shape[0] * parts
    groups = tokens // GROUP
    spans = local_spans(groups)
    dense = 2 * tokens * GROUP * width
    area = tokens * width
    others = from_each(input_map, "head", far_first_masks(parts))
    kept = inputs, gate, level_mix, skip[None, :], input_map, output_map, norm_gain[None, :]
    beside = flip(output_map, "head", FIRST_HOP)
    scaled, cum, *kept = call(
        prepare_kernel,
        (
            *(shaped((tokens, width), bf16), shaped((heads, tokens), f32)),
            *(shaped(array.shape, array.dtype) for array in kept),
        ),
        (step, decay_rate[None, :], *kept),
        flops=16 * dense,
        bytes_accessed=4 * area,
        hbm=9,
        scratch=[pltpu.VMEM(step.shape, f32), pltpu.VMEM((1, heads), f32), pltpu.SemaphoreType.DMA((9,))],
    )
    inputs, gate, level_mix, skip, input_map, output_map, gain = kept
    in_maps = [input_map, *others]
    pairs = lax.axis_size("seq") == 8 and parts == 4
    sides = 2 if pairs else 1
    shard_shape = shaped((size + DECAY_ROWS, width // sides), bf16)
    span_shape = [shaped((len(spans) * size, width), bf16)] if spans else []
    shard, *rest = call(
        functools.partial(states_kernel, parts, sides),
        (*[shard_shape] * sides, *span_shape),
        (*in_maps, scaled, cum),
        flops=dense,
    )
    span_states = rest[sides - 1 :]
    rows = output_map.shape[0]
    if rows % 16 == 0:
        both = call(
            join_kernel,
            shaped((2 * rows, tokens), bf16),
            (output_map, beside, shard),
            flops=8 * dense,
        )
    else:
        both = jnp.concatenate([output_map, beside], axis=0)
    if pairs:
        theirs = flip(rest[0], "seq", 1)
        message = call(
            functools.partial(merge_kernel, size), shard_shape, (shard, theirs, both), flops=0
        )
        other_theirs = flip(lax.optimization_barrier((shard, message))[0], "seq", 1)
    else:
        other_theirs = theirs = message = shard
    out_maps = [both, *from_each(both, "head", pair_masks(parts))]
    factor_shape = [shaped((len(spans), GROUP, width), bf16)] if spans else []
    base, own_factor, far, *span_factors = call(
        functools.partial(factor_kernel, spans, levels),
        (
            *(shaped((tokens, width), f32), shaped((tokens, width), f32)),
            *(shaped((levels, tokens, width), bf16), *factor_shape),
        ),
        (inputs, gate, level_mix, skip, cum, message),
        flops=5 * dense,
        bytes_accessed=0,
    )
    near_args = base, own_factor, far, theirs, scaled, *span_states, *span_factors
    near_shape = shaped((tokens, width // 2 if pairs else width), f32)
    near, turned, scores = call(
        functools.partial(near_kernel, parts, spans, pairs),
        (near_shape, shaped((tokens, size), bf16), shaped((tokens, GROUP), bf16)),
        (*in_maps, *out_maps, *near_args),
    )
    sums_shape = shaped((1, tokens), f32)
    if pairs:
        received = [flip(message, "seq", 4), flip(message, "seq", 2), lax.ppermute(message, "seq", CYCLE)]
        *received, other_theirs, near, far = lax.optimization_barrier((*received, other_theirs, near, far))
        own = call(
            functools.partial(combine_kernel, size),
            shaped((2 * size, width // 2), bf16),
            (received[1], received[0], received[2]),
            bytes_accessed=area,
        )
        other = flip(own, "seq", 1)
        near_args = base, own_factor, far, other_theirs, scaled, *span_states, *span_factors
        other_near = call(
            functools.partial(other_near_kernel, spans), near_shape, (scores, turned, own, *near_args), flops=dense
        )
        gated_shape = shaped((tokens, width // 2), f32)
        own_gated, own_squares = call(
            functools.partial(far_kernel_of_half, True),
            (gated_shape, shaped((tokens, 128), f32)),
            (turned, near, far, gain, theirs, own),
            flops=2 * dense,
            bytes_accessed=6 * area,
        )
        other_gated, sums = call(
            functools.partial(far_kernel_of_half, False),
            (gated_shape, sums_shape),
            (turned, other_near, far, gain, other_theirs, other, own_squares),
            flops=2 * dense,
            bytes_accessed=6 * area,
        )
        gated = (own_gated, other_gated)
    else:
        *gated, sums = call(
            far_kernel,
            (shaped((tokens, width), f32), sums_shape),
            (turned, near, far, gain, *far_states(shard, size)),
            flops=4 * dense,
            bytes_accessed=12 * area,
        )
    last = [sums, *around(sums, "head")]
    return call(
        functools.partial(norm_kernel, len(last), width * parts),
        shaped((tokens, width), bf16),
        (*last, *gated),
        flops=dense,
        bytes_accessed=6 * area,
        scratch=[pltpu.VMEM((tokens, width), bf16), pltpu.SemaphoreType.DMA((NORM_CHUNKS,))],
        out_space=pl.ANY,
    )


def solution(mesh):
    return jax.shard_map(
        on_device,
        mesh=mesh,
        in_specs=(
            P("seq", "head"),
            P("seq", "head"),
            P("head", "seq"),
            P("head", "seq"),
            P("head", "seq"),
            P("head"),
            P(None, "head", "seq"),
            P("head"),
            P("head"),
        ),
        out_specs=P("seq", "head"),
        check_vma=False,
    )
```

```python
import functools

import jax
import jax.numpy as jnp
from jax import lax
from jax.experimental import pallas as pl
from jax.experimental.pallas import tpu as pltpu
from jax.sharding import PartitionSpec as P

P_SIZE = 64
GROUP = 256
DECAY_ROWS = 8
BLOCK = 256
NORM_CHUNKS = 4
FIRST_HOP = 2
CYCLE = [(2 * chip + core, 2 * target + core) for chip, target in ((0, 3), (3, 1), (1, 2), (2, 0)) for core in (0, 1)]
VMEM_LIMIT = 40 * 1024 * 1024

f32, bf16 = jnp.float32, jnp.bfloat16
HIGHEST = lax.Precision.HIGHEST
TRANSPOSED = (((0,), (0,)), ((), ()))


def expander(heads, width, copies):
    row = lax.broadcasted_iota(jnp.int32, (copies * heads, width), 0)
    col = lax.broadcasted_iota(jnp.int32, (copies * heads, width), 1)
    return jnp.where(lax.rem(row, heads) == lax.div(col, P_SIZE), 1.0, 0.0)


def far_first_masks(size):
    return (*range(2, size), 1)


def pair_masks(size):
    return tuple(mask for mask in range(1, size) if not mask & FIRST_HOP)


def two_parts(factor):
    high = factor.astype(bf16).astype(f32)
    return jnp.concatenate([high, factor - high], axis=0).astype(bf16)


def transposed_dot(left, right):
    return lax.dot_general(left, right, TRANSPOSED, preferred_element_type=f32)


def head_row(heads, width, column):
    return jnp.sum(expander(heads, width, 1) * column, axis=0, keepdims=True)


def group_slice(group):
    return slice(group * GROUP, (group + 1) * GROUP)


def blocks_of(width):
    return [slice(at, at + BLOCK) for at in range(0, width, BLOCK)]


def local_spans(groups):
    spans = []
    for later in range(groups):
        for bit in range(groups.bit_length() - 1):
            if later >> bit & 1:
                start = later >> bit + 1 << bit + 1
                spans.append((later, bit, start, start + 2**bit))
    return spans


def column_of(row):
    size = row.shape[1]
    at = lax.broadcasted_iota(jnp.int32, (size, size), 0) == lax.broadcasted_iota(jnp.int32, (size, size), 1)
    return jnp.sum(jnp.where(at, row, 0.0), axis=1, keepdims=True)


def map_rows(maps):
    if all(rows.shape[0] % 16 == 0 for rows in maps):
        return jnp.concatenate([rows[...] for rows in maps], axis=0)
    return jnp.concatenate([rows[...].astype(f32) for rows in maps], axis=0).astype(bf16)


def out_map_rows(map_refs, parts):
    rows = map_refs[0].shape[0] // 2
    pairs = [ref if rows % 16 == 0 else ref[...].astype(f32) for ref in map_refs]
    sent = (0, *pair_masks(parts))
    picked = []
    for mask in (0, *far_first_masks(parts)):
        pair = pairs[sent.index(mask & ~FIRST_HOP)]
        at = slice(rows, 2 * rows) if mask & FIRST_HOP else slice(0, rows)
        picked.append(pair.at[at] if rows % 16 == 0 else pair[at])
    return map_rows(picked)


def fetch(sources, targets, semaphores):
    copies = [
        pltpu.make_async_copy(source, target, semaphores.at[index])
        for index, (source, target) in enumerate(zip(sources, targets))
    ]
    for copy in copies:
        copy.start()
    return copies


def prepare_kernel(*refs):
    sources, (scaled_ref, cum_ref), kept_refs = refs[:9], refs[9:11], refs[11:18]
    step_ref, rate_ref, semaphores = refs[18:]
    inputs_ref = kept_refs[0]
    copies = fetch(sources, (step_ref, rate_ref, *kept_refs), semaphores)
    heads, tokens = step_ref.shape
    width = inputs_ref.shape[1]
    row = lax.broadcasted_iota(jnp.int32, (GROUP, GROUP), 0)
    col = lax.broadcasted_iota(jnp.int32, (GROUP, GROUP), 1)
    until = jnp.where(row <= col, 1.0, 0.0)
    expand = expander(heads, width, 2).astype(bf16)
    copies[0].wait()
    copies[1].wait()
    step = step_ref[...]
    log_decay = -step * column_of(rate_ref[...])
    factors = []
    for group in range(tokens // GROUP):
        at = group_slice(group)
        cum = jnp.dot(log_decay[:, at], until, precision=HIGHEST, preferred_element_type=f32)
        cum_ref[:, at] = cum
        factors.append(two_parts(jnp.exp(-cum) * step[:, at]))
    factor = jnp.concatenate(factors, axis=1)
    copies[2].wait()
    for cols in blocks_of(width):
        scale = transposed_dot(factor, expand[:, cols])
        scaled_ref[:, cols] = (inputs_ref[:, cols].astype(f32) * scale).astype(bf16)
    for copy in copies[3:]:
        copy.wait()


def join_kernel(mine_ref, theirs_ref, _, both_ref):
    rows = mine_ref.shape[0]
    both_ref[:rows, :] = mine_ref[...]
    both_ref[rows:, :] = theirs_ref[...]


def states_kernel(parts, sides, *refs):
    map_refs, (scaled_ref, cum_ref), out_refs = refs[:parts], refs[parts : parts + 2], refs[parts + 2 :]
    shard_refs = out_refs[:sides]
    heads, tokens = cum_ref.shape
    width = scaled_ref.shape[1]
    in_map = map_rows(map_refs)
    size = in_map.shape[0]
    cum = cum_ref[...]
    states, decays = [], []
    for group in range(tokens // GROUP):
        at = group_slice(group)
        decay = head_row(heads, width, jnp.exp(cum[:, at.stop - 1 : at.stop]))
        raw = jnp.dot(in_map[:, at], scaled_ref[at, :], preferred_element_type=f32)
        states.append(raw * decay)
        decays.append(decay)
    total, decay = states[0], decays[0]
    for group in range(1, len(states)):
        total = total * decays[group] + states[group]
        decay = decay * decays[group]
    columns = width // sides
    core = lax.rem(lax.axis_index("seq"), 2)
    for ref, first in zip(shard_refs, (core == 0, core == 1)):
        at = slice(0, columns)
        ref[:size, :] = jnp.where(first, total[:, at], total[:, width - columns :]).astype(bf16)
        row = jnp.where(first, decay[:, at], decay[:, width - columns :])
        ref[size:, :] = jnp.broadcast_to(row, (DECAY_ROWS, columns)).astype(bf16)
    for index, (later, _, start, stop) in enumerate(local_spans(len(states))):
        span = states[start]
        for group in range(start + 1, later):
            span = span * decays[group]
            if group < stop:
                span = span + states[group]
        out_refs[sides][index * size : (index + 1) * size, :] = span.astype(bf16)


def merge_kernel(size, mine_ref, theirs_ref, _, pair_ref):
    core = lax.rem(lax.axis_index("seq"), 2)
    mine, theirs = mine_ref[...], theirs_ref[...]
    older = jnp.where(core == 1, theirs, mine).astype(f32)
    newer = jnp.where(core == 1, mine, theirs).astype(f32)
    decay = newer[size : size + 1]
    pair_ref[:size, :] = (older[:size] * decay + newer[:size]).astype(bf16)
    pair_ref[size:, :] = (older[size:] * decay).astype(bf16)


def factor_kernel(spans, levels, *refs):
    inputs_ref, gate_ref, mix_ref, skip_ref, cum_ref, _ = refs[:6]
    base_ref, own_ref, far_ref = refs[6:9]
    span_refs = refs[9:]
    heads, tokens = cum_ref.shape
    width = inputs_ref.shape[1]
    groups = tokens // GROUP
    first = groups.bit_length()
    expand = expander(heads, width, 2).astype(bf16)
    skip = head_row(heads, width, column_of(skip_ref[...]))
    before = jnp.zeros((heads, 1), f32)
    for group in range(groups):
        at = group_slice(group)
        cum = cum_ref[:, at]
        decay = jnp.exp(cum)
        own_mix = two_parts(mix_ref[0, :, at] * decay)
        span_mixes = [
            (index, two_parts(mix_ref[1 + bit, :, at] * decay))
            for index, (later, bit, _, _) in enumerate(spans)
            if later == group
        ]
        decay = jnp.exp(cum + before)
        before = before + cum[:, GROUP - 1 : GROUP]
        far_mixes = [two_parts(mix_ref[first + level, :, at] * decay) for level in range(levels)]
        for cols in blocks_of(width):
            gate = gate_ref[at, cols].astype(f32)
            swish = gate / (1.0 + jnp.exp(-gate))
            base_ref[at, cols] = skip[:, cols] * inputs_ref[at, cols].astype(f32) * swish
            own_ref[at, cols] = transposed_dot(own_mix, expand[:, cols]) * swish
            for level, mix in enumerate(far_mixes):
                far_ref[level, at, cols] = (transposed_dot(mix, expand[:, cols]) * swish).astype(bf16)
            for index, mix in span_mixes:
                span_refs[0][index, :, cols] = (transposed_dot(mix, expand[:, cols]) * swish).astype(bf16)


def near_body(spans, paired, start, scores_ref, turned_ref, refs, near_ref):
    base_ref, own_ref, far_ref, core_ref, scaled_ref = refs[:5]
    span_refs = refs[5:]
    tokens, size = turned_ref.shape
    has_core = lax.rem(lax.axis_index("seq"), 2) == 1
    for group in range(tokens // GROUP):
        at = group_slice(group)
        for cols in blocks_of(near_ref.shape[1]):
            of = pl.ds(pl.multiple_of(start + cols.start, BLOCK), BLOCK)
            own = jnp.dot(scores_ref[at, :], scaled_ref[at, of], preferred_element_type=f32)
            total = base_ref[at, of] + own_ref[at, of] * own
            for index, (later, _, _, _) in enumerate(spans):
                if later == group:
                    rows = slice(index * size, (index + 1) * size)
                    reach = jnp.dot(turned_ref[at, :], span_refs[0][rows, of], preferred_element_type=f32)
                    total = total + span_refs[1][index, :, of].astype(f32) * reach
            if paired:
                reach = jnp.dot(turned_ref[at, :], core_ref[:size, cols], preferred_element_type=f32)
                reach = jnp.where(has_core, reach, 0.0)
                total = total + far_ref[0, at, of].astype(f32) * reach
            near_ref[at, cols] = total


def near_kernel(parts, spans, paired, *refs):
    count = parts + parts // 2
    in_refs, out_refs, rest = refs[:parts], refs[parts:count], refs[count:-3]
    near_ref, turned_ref, scores_ref = refs[-3:]
    in_map = map_rows(in_refs)
    turned = jnp.transpose(out_map_rows(out_refs, parts))
    turned_ref[...] = turned
    row = lax.broadcasted_iota(jnp.int32, (GROUP, GROUP), 0)
    col = lax.broadcasted_iota(jnp.int32, (GROUP, GROUP), 1)
    for group in range(turned.shape[0] // GROUP):
        at = group_slice(group)
        scores = jnp.dot(turned[at], in_map[:, at], preferred_element_type=f32)
        scores_ref[at, :] = jnp.where(row >= col, scores, 0.0).astype(bf16)
    start = lax.rem(lax.axis_index("seq"), 2) * near_ref.shape[1] if paired else 0
    near_body(spans, paired, start, scores_ref, turned_ref, rest, near_ref)


def other_near_kernel(spans, scores_ref, turned_ref, _, *refs):
    near_ref = refs[-1]
    start = (1 - lax.rem(lax.axis_index("seq"), 2)) * near_ref.shape[1]
    near_body(spans, True, start, scores_ref, turned_ref, refs[:-1], near_ref)


def far_body(turned_ref, near_ref, far_ref, gain_ref, start, columns, levels, state_of, gated_ref):
    tokens = far_ref.shape[1]
    squares = jnp.zeros((tokens, 128), f32)
    for cols in blocks_of(columns):
        at = pl.ds(pl.multiple_of(start + cols.start, BLOCK), BLOCK)
        total = near_ref[:, cols]
        for level in levels:
            state = state_of(level, cols, at).astype(bf16)
            reach = jnp.dot(turned_ref[...], state, preferred_element_type=f32)
            total = total + far_ref[level, :, at].astype(f32) * reach
        gated_ref[:, cols] = total * gain_ref[:, at]
        total = total * total
        for part in range(0, BLOCK, 128):
            squares = squares + total[:, part : part + 128]
    return squares


def row_sums(squares):
    high = squares.astype(bf16)
    low = (squares - high.astype(f32)).astype(bf16)
    parts = jnp.concatenate([high, low], axis=1)
    sums = jnp.dot(parts, jnp.ones((parts.shape[1], 128), bf16), preferred_element_type=f32)
    row = lax.broadcasted_iota(jnp.int32, (128, 128), 0)
    col = lax.broadcasted_iota(jnp.int32, (128, 128), 1)
    blocks = [
        jnp.sum(jnp.where(row == col, sums[at : at + 128], 0.0), axis=0, keepdims=True)
        for at in range(0, sums.shape[0], 128)
    ]
    return jnp.concatenate(blocks, axis=1)


def far_kernel(turned_ref, near_ref, far_ref, gain_ref, *refs):
    state_refs = refs[:-2]
    gated_ref, sums_ref = refs[-2:]

    def state_of(level, cols, _):
        return state_refs[level][:, cols]

    width = near_ref.shape[1]
    levels = range(far_ref.shape[0])
    squares = far_body(turned_ref, near_ref, far_ref, gain_ref, 0, width, levels, state_of, gated_ref)
    sums_ref[...] = row_sums(squares)


def combine_kernel(size, x_ref, y_ref, diagonal_ref, spans_ref):
    rank = lax.axis_index("seq")
    along_x = lax.rem(lax.div(rank, 2), 2)
    along_y = lax.div(rank, 4)

    def parts_of(ref):
        return ref[:size, :].astype(f32), ref[size:, :].astype(f32)[:1]

    x_state, x_decay = parts_of(x_ref)
    y_state, y_decay = parts_of(y_ref)
    d_state, d_decay = parts_of(diagonal_ref)
    newer = jnp.where(along_x == 1, y_state, d_state)
    newer_decay = jnp.where(along_x == 1, y_decay, d_decay)
    older = jnp.where(along_x == 1, d_state, y_state)
    running = jnp.where(along_x == 1, x_decay, 1.0)
    running = jnp.where(along_y == 1, running, 0.0)
    spans_ref[:size, :] = jnp.where(along_x == 1, x_state, 0.0).astype(bf16)
    spans_ref[size:, :] = ((older * newer_decay + newer) * running).astype(bf16)


def far_kernel_of_half(own, *refs):
    turned_ref, near_ref, far_ref, gain_ref, core_ref, spans_ref = refs[:6]
    gated_ref, sums_ref = refs[-2:]
    size = turned_ref.shape[1]
    core = lax.rem(lax.axis_index("seq"), 2)
    half = spans_ref.shape[1]
    start = (core if own else 1 - core) * half

    def state_of(level, cols, at):
        core_decay = core_ref[size:, cols].astype(f32)[:1]
        running = jnp.where(core == 1, core_decay, 1.0)
        return spans_ref[(level - 1) * size : level * size, cols].astype(f32) * running

    squares = far_body(turned_ref, near_ref, far_ref, gain_ref, start, half, (1, 2), state_of, gated_ref)
    sums_ref[...] = squares if own else row_sums(squares + refs[6][...])


def norm_kernel(parts, columns, *refs):
    gated_refs, (out_hbm, out_ref, semaphores) = refs[parts:-3], refs[-3:]
    total = refs[0][...]
    for ref in refs[1:parts]:
        total = total + ref[...]
    scale = lax.rsqrt(total / columns + 1e-05)
    tokens = scale.shape[1]
    scale = jnp.broadcast_to(scale, (8, tokens))
    width = gated_refs[0].shape[1]
    core = lax.rem(lax.axis_index("seq"), 2)
    sides = (core, 1 - core) if len(gated_refs) == 2 else (0,)
    chunk = tokens // NORM_CHUNKS
    copies = []
    for index in range(NORM_CHUNKS):
        rows = slice(index * chunk, (index + 1) * chunk)
        column = jnp.transpose(scale[:, rows])[:, :1]
        for ref, side in zip(gated_refs, sides):
            at = pl.ds(pl.multiple_of(side * width, width), width)
            out_ref[rows, at] = (ref[rows, :] * column).astype(bf16)
        copies.append(pltpu.make_async_copy(out_ref.at[rows], out_hbm.at[rows], semaphores.at[index]))
        copies[-1].start()
    for copy in copies:
        copy.wait()


def call(kernel, out_shape, args, flops=0, bytes_accessed=0, hbm=0, scratch=None, out_space=pltpu.VMEM):
    specs = [pl.BlockSpec(memory_space=pl.ANY)] * hbm + [pl.BlockSpec(memory_space=pltpu.VMEM)] * (len(args) - hbm)
    args = [pltpu.with_memory_space_constraint(arg, pltpu.HBM) for arg in args[:hbm]] + list(args[hbm:])
    if scratch is None:
        scratch = [pltpu.VMEM(arg.shape, arg.dtype) for arg in args[:hbm]]
        scratch += [pltpu.SemaphoreType.DMA((hbm,))] if hbm else []
    return pl.pallas_call(
        kernel,
        out_shape=out_shape,
        in_specs=specs,
        out_specs=jax.tree.map(lambda _: pl.BlockSpec(memory_space=out_space), out_shape),
        scratch_shapes=scratch,
        compiler_params=pltpu.CompilerParams(vmem_limit_bytes=VMEM_LIMIT),
        cost_estimate=pl.CostEstimate(flops=flops, bytes_accessed=bytes_accessed, transcendentals=0),
    )(*args)


def shaped(shape, dtype):
    return jax.ShapeDtypeStruct(shape, dtype)


def flip(array, axis, mask):
    return lax.ppermute(array, axis, [(i, i ^ mask) for i in range(lax.axis_size(axis))])


def from_each(array, axis, masks):
    return [flip(array, axis, mask) for mask in masks]


def around(array, axis):
    size = lax.axis_size(axis)
    return [lax.ppermute(array, axis, [(i, (i + shift) % size) for i in range(size)]) for shift in range(1, size)]


def merged(older, newer, size):
    older, newer = older.astype(f32), newer.astype(f32)
    decay = newer[size : size + 1]
    return jnp.concatenate([older[:size] * decay + newer[:size], older[size:] * decay], axis=0).astype(bf16)


def far_states(shard, size):
    rank = lax.axis_index("seq")
    levels = lax.axis_size("seq").bit_length() - 1
    states = []
    running = jnp.ones((1, shard.shape[1]), f32)
    for level in range(levels):
        theirs = flip(shard, "seq", 1 << level)
        upper = jnp.right_shift(rank, level) % 2 == 1
        states.append(jnp.where(upper, theirs[:size].astype(f32) * running, 0.0).astype(bf16))
        running = jnp.where(upper, running * theirs[size : size + 1].astype(f32), running)
        shard = merged(jnp.where(upper, theirs, shard), jnp.where(upper, shard, theirs), size)
    return states


def on_device(inputs, gate, input_map, output_map, step, decay_rate, level_mix, skip, norm_gain):
    tokens, width = inputs.shape
    heads = step.shape[0]
    parts = lax.axis_size("head")
    levels = lax.axis_size("seq").bit_length() - 1
    size = input_map.shape[0] * parts
    groups = tokens // GROUP
    spans = local_spans(groups)
    dense = 2 * tokens * GROUP * width
    area = tokens * width
    others = from_each(input_map, "head", far_first_masks(parts))
    kept = inputs, gate, level_mix, skip[None, :], input_map, output_map, norm_gain[None, :]
    beside = flip(output_map, "head", FIRST_HOP)
    scaled, cum, *kept = call(
        prepare_kernel,
        (
            *(shaped((tokens, width), bf16), shaped((heads, tokens), f32)),
            *(shaped(array.shape, array.dtype) for array in kept),
        ),
        (step, decay_rate[None, :], *kept),
        flops=16 * dense,
        bytes_accessed=4 * area,
        hbm=9,
        scratch=[pltpu.VMEM(step.shape, f32), pltpu.VMEM((1, heads), f32), pltpu.SemaphoreType.DMA((9,))],
    )
    inputs, gate, level_mix, skip, input_map, output_map, gain = kept
    in_maps = [input_map, *others]
    pairs = lax.axis_size("seq") == 8 and parts == 4
    sides = 2 if pairs else 1
    shard_shape = shaped((size + DECAY_ROWS, width // sides), bf16)
    span_shape = [shaped((len(spans) * size, width), bf16)] if spans else []
    shard, *rest = call(
        functools.partial(states_kernel, parts, sides),
        (*[shard_shape] * sides, *span_shape),
        (*in_maps, scaled, cum),
        flops=dense,
    )
    span_states = rest[sides - 1 :]
    rows = output_map.shape[0]
    if rows % 16 == 0:
        both = call(
            join_kernel,
            shaped((2 * rows, tokens), bf16),
            (output_map, beside, shard),
            flops=8 * dense,
        )
    else:
        both = jnp.concatenate([output_map, beside], axis=0)
    if pairs:
        theirs = flip(rest[0], "seq", 1)
        message = call(
            functools.partial(merge_kernel, size), shard_shape, (shard, theirs, both), flops=0
        )
        other_theirs = flip(lax.optimization_barrier((shard, message))[0], "seq", 1)
    else:
        other_theirs = theirs = message = shard
    out_maps = [both, *from_each(both, "head", pair_masks(parts))]
    factor_shape = [shaped((len(spans), GROUP, width), bf16)] if spans else []
    base, own_factor, far, *span_factors = call(
        functools.partial(factor_kernel, spans, levels),
        (
            *(shaped((tokens, width), f32), shaped((tokens, width), f32)),
            *(shaped((levels, tokens, width), bf16), *factor_shape),
        ),
        (inputs, gate, level_mix, skip, cum, message),
        flops=5 * dense,
        bytes_accessed=0,
    )
    near_args = base, own_factor, far, theirs, scaled, *span_states, *span_factors
    near_shape = shaped((tokens, width // 2 if pairs else width), f32)
    near, turned, scores = call(
        functools.partial(near_kernel, parts, spans, pairs),
        (near_shape, shaped((tokens, size), bf16), shaped((tokens, GROUP), bf16)),
        (*in_maps, *out_maps, *near_args),
    )
    sums_shape = shaped((1, tokens), f32)
    if pairs:
        received = [lax.ppermute(message, "seq", CYCLE), flip(message, "seq", 4), flip(message, "seq", 2)]
        *received, other_theirs, near, far = lax.optimization_barrier((*received, other_theirs, near, far))
        own = call(
            functools.partial(combine_kernel, size),
            shaped((2 * size, width // 2), bf16),
            received[::-1],
            bytes_accessed=area,
        )
        other = flip(own, "seq", 1)
        near_args = base, own_factor, far, other_theirs, scaled, *span_states, *span_factors
        other_near = call(
            functools.partial(other_near_kernel, spans), near_shape, (scores, turned, own, *near_args), flops=dense
        )
        gated_shape = shaped((tokens, width // 2), f32)
        own_gated, own_squares = call(
            functools.partial(far_kernel_of_half, True),
            (gated_shape, shaped((tokens, 128), f32)),
            (turned, near, far, gain, theirs, own),
            flops=2 * dense,
            bytes_accessed=6 * area,
        )
        other_gated, sums = call(
            functools.partial(far_kernel_of_half, False),
            (gated_shape, sums_shape),
            (turned, other_near, far, gain, other_theirs, other, own_squares),
            flops=2 * dense,
            bytes_accessed=6 * area,
        )
        gated = (own_gated, other_gated)
    else:
        *gated, sums = call(
            far_kernel,
            (shaped((tokens, width), f32), sums_shape),
            (turned, near, far, gain, *far_states(shard, size)),
            flops=4 * dense,
            bytes_accessed=12 * area,
        )
    last = [sums, *around(sums, "head")]
    return call(
        functools.partial(norm_kernel, len(last), width * parts),
        shaped((tokens, width), bf16),
        (*last, *gated),
        flops=dense,
        bytes_accessed=6 * area,
        scratch=[pltpu.VMEM((tokens, width), bf16), pltpu.SemaphoreType.DMA((NORM_CHUNKS,))],
        out_space=pl.ANY,
    )


def solution(mesh):
    return jax.shard_map(
        on_device,
        mesh=mesh,
        in_specs=(
            P("seq", "head"),
            P("seq", "head"),
            P("head", "seq"),
            P("head", "seq"),
            P("head", "seq"),
            P("head"),
            P(None, "head", "seq"),
            P("head"),
            P("head"),
        ),
        out_specs=P("seq", "head"),
        check_vma=False,
    )
```

```python
import functools

import jax
import jax.numpy as jnp
from jax import lax
from jax.experimental import pallas as pl
from jax.experimental.pallas import tpu as pltpu
from jax.sharding import PartitionSpec as P

P_SIZE = 64
GROUP = 256
DECAY_ROWS = 8
BLOCK = 256
NORM_CHUNKS = 4
FIRST_HOP = 2
CYCLE = [(2 * chip + core, 2 * target + core) for chip, target in ((0, 3), (3, 1), (1, 2), (2, 0)) for core in (0, 1)]
VMEM_LIMIT = 40 * 1024 * 1024

f32, bf16 = jnp.float32, jnp.bfloat16
HIGHEST = lax.Precision.HIGHEST
TRANSPOSED = (((0,), (0,)), ((), ()))


def expander(heads, width, copies):
    row = lax.broadcasted_iota(jnp.int32, (copies * heads, width), 0)
    col = lax.broadcasted_iota(jnp.int32, (copies * heads, width), 1)
    return jnp.where(lax.rem(row, heads) == lax.div(col, P_SIZE), 1.0, 0.0)


def far_first_masks(size):
    return (*range(2, size), 1)


def pair_masks(size):
    return tuple(mask for mask in range(1, size) if not mask & FIRST_HOP)


def two_parts(factor):
    high = factor.astype(bf16).astype(f32)
    return jnp.concatenate([high, factor - high], axis=0).astype(bf16)


def transposed_dot(left, right):
    return lax.dot_general(left, right, TRANSPOSED, preferred_element_type=f32)


def head_row(heads, width, column):
    return jnp.sum(expander(heads, width, 1) * column, axis=0, keepdims=True)


def group_slice(group):
    return slice(group * GROUP, (group + 1) * GROUP)


def blocks_of(width):
    return [slice(at, at + BLOCK) for at in range(0, width, BLOCK)]


def local_spans(groups):
    spans = []
    for later in range(groups):
        for bit in range(groups.bit_length() - 1):
            if later >> bit & 1:
                start = later >> bit + 1 << bit + 1
                spans.append((later, bit, start, start + 2**bit))
    return spans


def column_of(row):
    size = row.shape[1]
    at = lax.broadcasted_iota(jnp.int32, (size, size), 0) == lax.broadcasted_iota(jnp.int32, (size, size), 1)
    return jnp.sum(jnp.where(at, row, 0.0), axis=1, keepdims=True)


def map_rows(maps):
    if all(rows.shape[0] % 16 == 0 for rows in maps):
        return jnp.concatenate([rows[...] for rows in maps], axis=0)
    return jnp.concatenate([rows[...].astype(f32) for rows in maps], axis=0).astype(bf16)


def out_map_rows(map_refs, parts):
    rows = map_refs[0].shape[0] // 2
    pairs = [ref if rows % 16 == 0 else ref[...].astype(f32) for ref in map_refs]
    sent = (0, *pair_masks(parts))
    picked = []
    for mask in (0, *far_first_masks(parts)):
        pair = pairs[sent.index(mask & ~FIRST_HOP)]
        at = slice(rows, 2 * rows) if mask & FIRST_HOP else slice(0, rows)
        picked.append(pair.at[at] if rows % 16 == 0 else pair[at])
    return map_rows(picked)


def fetch(sources, targets, semaphores):
    copies = [
        pltpu.make_async_copy(source, target, semaphores.at[index])
        for index, (source, target) in enumerate(zip(sources, targets))
    ]
    for copy in copies:
        copy.start()
    return copies


def prepare_kernel(*refs):
    sources, (scaled_ref, cum_ref), kept_refs = refs[:9], refs[9:11], refs[11:18]
    step_ref, rate_ref, semaphores = refs[18:]
    inputs_ref = kept_refs[0]
    copies = fetch(sources, (step_ref, rate_ref, *kept_refs), semaphores)
    heads, tokens = step_ref.shape
    width = inputs_ref.shape[1]
    row = lax.broadcasted_iota(jnp.int32, (GROUP, GROUP), 0)
    col = lax.broadcasted_iota(jnp.int32, (GROUP, GROUP), 1)
    until = jnp.where(row <= col, 1.0, 0.0)
    expand = expander(heads, width, 2).astype(bf16)
    copies[0].wait()
    copies[1].wait()
    step = step_ref[...]
    log_decay = -step * column_of(rate_ref[...])
    factors = []
    for group in range(tokens // GROUP):
        at = group_slice(group)
        cum = jnp.dot(log_decay[:, at], until, precision=HIGHEST, preferred_element_type=f32)
        cum_ref[:, at] = cum
        factors.append(two_parts(jnp.exp(-cum) * step[:, at]))
    factor = jnp.concatenate(factors, axis=1)
    copies[2].wait()
    for cols in blocks_of(width):
        scale = transposed_dot(factor, expand[:, cols])
        scaled_ref[:, cols] = (inputs_ref[:, cols].astype(f32) * scale).astype(bf16)
    for copy in copies[3:]:
        copy.wait()


def join_kernel(mine_ref, theirs_ref, _, both_ref):
    rows = mine_ref.shape[0]
    both_ref[:rows, :] = mine_ref[...]
    both_ref[rows:, :] = theirs_ref[...]


def states_kernel(parts, sides, *refs):
    map_refs, (scaled_ref, cum_ref), out_refs = refs[:parts], refs[parts : parts + 2], refs[parts + 2 :]
    shard_refs = out_refs[:sides]
    heads, tokens = cum_ref.shape
    width = scaled_ref.shape[1]
    in_map = map_rows(map_refs)
    size = in_map.shape[0]
    cum = cum_ref[...]
    states, decays = [], []
    for group in range(tokens // GROUP):
        at = group_slice(group)
        decay = head_row(heads, width, jnp.exp(cum[:, at.stop - 1 : at.stop]))
        raw = jnp.dot(in_map[:, at], scaled_ref[at, :], preferred_element_type=f32)
        states.append(raw * decay)
        decays.append(decay)
    total, decay = states[0], decays[0]
    for group in range(1, len(states)):
        total = total * decays[group] + states[group]
        decay = decay * decays[group]
    columns = width // sides
    core = lax.rem(lax.axis_index("seq"), 2)
    for ref, first in zip(shard_refs, (core == 0, core == 1)):
        at = slice(0, columns)
        ref[:size, :] = jnp.where(first, total[:, at], total[:, width - columns :]).astype(bf16)
        row = jnp.where(first, decay[:, at], decay[:, width - columns :])
        ref[size:, :] = jnp.broadcast_to(row, (DECAY_ROWS, columns)).astype(bf16)
    for index, (later, _, start, stop) in enumerate(local_spans(len(states))):
        span = states[start]
        for group in range(start + 1, later):
            span = span * decays[group]
            if group < stop:
                span = span + states[group]
        out_refs[sides][index * size : (index + 1) * size, :] = span.astype(bf16)


def merge_kernel(size, mine_ref, theirs_ref, _, pair_ref):
    core = lax.rem(lax.axis_index("seq"), 2)
    mine, theirs = mine_ref[...], theirs_ref[...]
    older = jnp.where(core == 1, theirs, mine).astype(f32)
    newer = jnp.where(core == 1, mine, theirs).astype(f32)
    decay = newer[size : size + 1]
    pair_ref[:size, :] = (older[:size] * decay + newer[:size]).astype(bf16)
    pair_ref[size:, :] = (older[size:] * decay).astype(bf16)


def factor_kernel(spans, levels, *refs):
    inputs_ref, gate_ref, mix_ref, skip_ref, cum_ref, _ = refs[:6]
    base_ref, own_ref, far_ref = refs[6:9]
    span_refs = refs[9:]
    heads, tokens = cum_ref.shape
    width = inputs_ref.shape[1]
    groups = tokens // GROUP
    first = groups.bit_length()
    expand = expander(heads, width, 2).astype(bf16)
    skip = head_row(heads, width, column_of(skip_ref[...]))
    before = jnp.zeros((heads, 1), f32)
    for group in range(groups):
        at = group_slice(group)
        cum = cum_ref[:, at]
        decay = jnp.exp(cum)
        own_mix = two_parts(mix_ref[0, :, at] * decay)
        span_mixes = [
            (index, two_parts(mix_ref[1 + bit, :, at] * decay))
            for index, (later, bit, _, _) in enumerate(spans)
            if later == group
        ]
        decay = jnp.exp(cum + before)
        before = before + cum[:, GROUP - 1 : GROUP]
        far_mixes = [two_parts(mix_ref[first + level, :, at] * decay) for level in range(levels)]
        for cols in blocks_of(width):
            gate = gate_ref[at, cols].astype(f32)
            swish = gate / (1.0 + jnp.exp(-gate))
            base_ref[at, cols] = skip[:, cols] * inputs_ref[at, cols].astype(f32) * swish
            own_ref[at, cols] = transposed_dot(own_mix, expand[:, cols]) * swish
            for level, mix in enumerate(far_mixes):
                far_ref[level, at, cols] = (transposed_dot(mix, expand[:, cols]) * swish).astype(bf16)
            for index, mix in span_mixes:
                span_refs[0][index, :, cols] = (transposed_dot(mix, expand[:, cols]) * swish).astype(bf16)


def near_body(spans, paired, start, scores_ref, turned_ref, refs, near_ref):
    base_ref, own_ref, far_ref, core_ref, scaled_ref = refs[:5]
    span_refs = refs[5:]
    tokens, size = turned_ref.shape
    has_core = lax.rem(lax.axis_index("seq"), 2) == 1
    for group in range(tokens // GROUP):
        at = group_slice(group)
        for cols in blocks_of(near_ref.shape[1]):
            of = pl.ds(pl.multiple_of(start + cols.start, BLOCK), BLOCK)
            own = jnp.dot(scores_ref[at, :], scaled_ref[at, of], preferred_element_type=f32)
            total = base_ref[at, of] + own_ref[at, of] * own
            for index, (later, _, _, _) in enumerate(spans):
                if later == group:
                    rows = slice(index * size, (index + 1) * size)
                    reach = jnp.dot(turned_ref[at, :], span_refs[0][rows, of], preferred_element_type=f32)
                    total = total + span_refs[1][index, :, of].astype(f32) * reach
            if paired:
                reach = jnp.dot(turned_ref[at, :], core_ref[:size, cols], preferred_element_type=f32)
                reach = jnp.where(has_core, reach, 0.0)
                total = total + far_ref[0, at, of].astype(f32) * reach
            near_ref[at, cols] = total


def near_kernel(parts, spans, paired, *refs):
    count = parts + parts // 2
    in_refs, out_refs, rest = refs[:parts], refs[parts:count], refs[count:-3]
    near_ref, turned_ref, scores_ref = refs[-3:]
    in_map = map_rows(in_refs)
    turned = jnp.transpose(out_map_rows(out_refs, parts))
    turned_ref[...] = turned
    row = lax.broadcasted_iota(jnp.int32, (GROUP, GROUP), 0)
    col = lax.broadcasted_iota(jnp.int32, (GROUP, GROUP), 1)
    for group in range(turned.shape[0] // GROUP):
        at = group_slice(group)
        scores = jnp.dot(turned[at], in_map[:, at], preferred_element_type=f32)
        scores_ref[at, :] = jnp.where(row >= col, scores, 0.0).astype(bf16)
    start = lax.rem(lax.axis_index("seq"), 2) * near_ref.shape[1] if paired else 0
    near_body(spans, paired, start, scores_ref, turned_ref, rest, near_ref)


def other_near_kernel(spans, scores_ref, turned_ref, _, *refs):
    near_ref = refs[-1]
    start = (1 - lax.rem(lax.axis_index("seq"), 2)) * near_ref.shape[1]
    near_body(spans, True, start, scores_ref, turned_ref, refs[:-1], near_ref)


def far_body(turned_ref, near_ref, far_ref, gain_ref, start, columns, levels, state_of, gated_ref):
    tokens = far_ref.shape[1]
    squares = jnp.zeros((tokens, 128), f32)
    for cols in blocks_of(columns):
        at = pl.ds(pl.multiple_of(start + cols.start, BLOCK), BLOCK)
        total = near_ref[:, cols]
        for level in levels:
            state = state_of(level, cols, at).astype(bf16)
            reach = jnp.dot(turned_ref[...], state, preferred_element_type=f32)
            total = total + far_ref[level, :, at].astype(f32) * reach
        gated_ref[:, cols] = total * gain_ref[:, at]
        total = total * total
        for part in range(0, BLOCK, 128):
            squares = squares + total[:, part : part + 128]
    return squares


def row_sums(squares):
    high = squares.astype(bf16)
    low = (squares - high.astype(f32)).astype(bf16)
    parts = jnp.concatenate([high, low], axis=1)
    ones = jnp.ones((16, parts.shape[1]), bf16)
    return lax.dot_general(ones, parts, (((1,), (1,)), ((), ())), preferred_element_type=f32)[:1]


def far_kernel(turned_ref, near_ref, far_ref, gain_ref, *refs):
    state_refs = refs[:-2]
    gated_ref, sums_ref = refs[-2:]

    def state_of(level, cols, _):
        return state_refs[level][:, cols]

    width = near_ref.shape[1]
    levels = range(far_ref.shape[0])
    squares = far_body(turned_ref, near_ref, far_ref, gain_ref, 0, width, levels, state_of, gated_ref)
    sums_ref[...] = row_sums(squares)


def combine_kernel(size, x_ref, y_ref, diagonal_ref, spans_ref):
    rank = lax.axis_index("seq")
    along_x = lax.rem(lax.div(rank, 2), 2)
    along_y = lax.div(rank, 4)

    def parts_of(ref):
        return ref[:size, :].astype(f32), ref[size:, :].astype(f32)[:1]

    _, x_decay = parts_of(x_ref)
    y_state, y_decay = parts_of(y_ref)
    d_state, d_decay = parts_of(diagonal_ref)
    newer = jnp.where(along_x == 1, y_state, d_state)
    newer_decay = jnp.where(along_x == 1, y_decay, d_decay)
    older = jnp.where(along_x == 1, d_state, y_state)
    running = jnp.where(along_x == 1, x_decay, 1.0)
    running = jnp.where(along_y == 1, running, 0.0)
    spans_ref[...] = ((older * newer_decay + newer) * running).astype(bf16)


def far_kernel_of_half(own, *refs):
    turned_ref, near_ref, far_ref, gain_ref, core_ref, x_ref, span_ref = refs[:7]
    gated_ref, sums_ref = refs[-2:]
    size = turned_ref.shape[1]
    rank = lax.axis_index("seq")
    core = lax.rem(rank, 2)
    along_x = lax.rem(lax.div(rank, 2), 2)
    half = span_ref.shape[1]
    start = (core if own else 1 - core) * half

    def state_of(level, cols, at):
        core_decay = core_ref[size:, cols].astype(f32)[:1]
        running = jnp.where(core == 1, core_decay, 1.0)
        if level == 1:
            return x_ref[:size, cols].astype(f32) * jnp.where(along_x == 1, running, 0.0)
        return span_ref[:, cols].astype(f32) * running

    squares = far_body(turned_ref, near_ref, far_ref, gain_ref, start, half, (1, 2), state_of, gated_ref)
    sums_ref[...] = squares if own else row_sums(squares + refs[7][...])


def norm_kernel(parts, columns, *refs):
    gated_refs, (out_hbm, out_ref, semaphores) = refs[parts:-3], refs[-3:]
    total = refs[0][...]
    for ref in refs[1:parts]:
        total = total + ref[...]
    scale = lax.rsqrt(total / columns + 1e-05)
    tokens = scale.shape[1]
    scale = jnp.broadcast_to(scale, (8, tokens))
    width = gated_refs[0].shape[1]
    core = lax.rem(lax.axis_index("seq"), 2)
    sides = (core, 1 - core) if len(gated_refs) == 2 else (0,)
    chunk = tokens // NORM_CHUNKS
    copies = []
    for index in range(NORM_CHUNKS):
        rows = slice(index * chunk, (index + 1) * chunk)
        column = jnp.transpose(scale[:, rows])[:, :1]
        for ref, side in zip(gated_refs, sides):
            at = pl.ds(pl.multiple_of(side * width, width), width)
            out_ref[rows, at] = (ref[rows, :] * column).astype(bf16)
        copies.append(pltpu.make_async_copy(out_ref.at[rows], out_hbm.at[rows], semaphores.at[index]))
        copies[-1].start()
    for copy in copies:
        copy.wait()


def call(kernel, out_shape, args, flops=0, bytes_accessed=0, hbm=0, scratch=None, out_space=pltpu.VMEM):
    specs = [pl.BlockSpec(memory_space=pl.ANY)] * hbm + [pl.BlockSpec(memory_space=pltpu.VMEM)] * (len(args) - hbm)
    args = [pltpu.with_memory_space_constraint(arg, pltpu.HBM) for arg in args[:hbm]] + list(args[hbm:])
    if scratch is None:
        scratch = [pltpu.VMEM(arg.shape, arg.dtype) for arg in args[:hbm]]
        scratch += [pltpu.SemaphoreType.DMA((hbm,))] if hbm else []
    return pl.pallas_call(
        kernel,
        out_shape=out_shape,
        in_specs=specs,
        out_specs=jax.tree.map(lambda _: pl.BlockSpec(memory_space=out_space), out_shape),
        scratch_shapes=scratch,
        compiler_params=pltpu.CompilerParams(vmem_limit_bytes=VMEM_LIMIT),
        cost_estimate=pl.CostEstimate(flops=flops, bytes_accessed=bytes_accessed, transcendentals=0),
    )(*args)


def shaped(shape, dtype):
    return jax.ShapeDtypeStruct(shape, dtype)


def flip(array, axis, mask):
    return lax.ppermute(array, axis, [(i, i ^ mask) for i in range(lax.axis_size(axis))])


def from_each(array, axis, masks):
    return [flip(array, axis, mask) for mask in masks]


def around(array, axis):
    size = lax.axis_size(axis)
    return [lax.ppermute(array, axis, [(i, (i + shift) % size) for i in range(size)]) for shift in range(1, size)]


def merged(older, newer, size):
    older, newer = older.astype(f32), newer.astype(f32)
    decay = newer[size : size + 1]
    return jnp.concatenate([older[:size] * decay + newer[:size], older[size:] * decay], axis=0).astype(bf16)


def far_states(shard, size):
    rank = lax.axis_index("seq")
    levels = lax.axis_size("seq").bit_length() - 1
    states = []
    running = jnp.ones((1, shard.shape[1]), f32)
    for level in range(levels):
        theirs = flip(shard, "seq", 1 << level)
        upper = jnp.right_shift(rank, level) % 2 == 1
        states.append(jnp.where(upper, theirs[:size].astype(f32) * running, 0.0).astype(bf16))
        running = jnp.where(upper, running * theirs[size : size + 1].astype(f32), running)
        shard = merged(jnp.where(upper, theirs, shard), jnp.where(upper, shard, theirs), size)
    return states


def on_device(inputs, gate, input_map, output_map, step, decay_rate, level_mix, skip, norm_gain):
    tokens, width = inputs.shape
    heads = step.shape[0]
    parts = lax.axis_size("head")
    levels = lax.axis_size("seq").bit_length() - 1
    size = input_map.shape[0] * parts
    groups = tokens // GROUP
    spans = local_spans(groups)
    dense = 2 * tokens * GROUP * width
    area = tokens * width
    others = from_each(input_map, "head", far_first_masks(parts))
    kept = inputs, gate, level_mix, skip[None, :], input_map, output_map, norm_gain[None, :]
    beside = flip(output_map, "head", FIRST_HOP)
    scaled, cum, *kept = call(
        prepare_kernel,
        (
            *(shaped((tokens, width), bf16), shaped((heads, tokens), f32)),
            *(shaped(array.shape, array.dtype) for array in kept),
        ),
        (step, decay_rate[None, :], *kept),
        flops=16 * dense,
        bytes_accessed=4 * area,
        hbm=9,
        scratch=[pltpu.VMEM(step.shape, f32), pltpu.VMEM((1, heads), f32), pltpu.SemaphoreType.DMA((9,))],
    )
    inputs, gate, level_mix, skip, input_map, output_map, gain = kept
    in_maps = [input_map, *others]
    pairs = lax.axis_size("seq") == 8 and parts == 4
    sides = 2 if pairs else 1
    shard_shape = shaped((size + DECAY_ROWS, width // sides), bf16)
    span_shape = [shaped((len(spans) * size, width), bf16)] if spans else []
    shard, *rest = call(
        functools.partial(states_kernel, parts, sides),
        (*[shard_shape] * sides, *span_shape),
        (*in_maps, scaled, cum),
        flops=dense,
    )
    span_states = rest[sides - 1 :]
    rows = output_map.shape[0]
    if rows % 16 == 0:
        both = call(
            join_kernel,
            shaped((2 * rows, tokens), bf16),
            (output_map, beside, shard),
            flops=8 * dense,
        )
    else:
        both = jnp.concatenate([output_map, beside], axis=0)
    if pairs:
        theirs = flip(rest[0], "seq", 1)
        message = call(
            functools.partial(merge_kernel, size), shard_shape, (shard, theirs, both), flops=0
        )
        other_theirs = flip(lax.optimization_barrier((shard, message))[0], "seq", 1)
    else:
        other_theirs = theirs = message = shard
    out_maps = [both, *from_each(both, "head", pair_masks(parts))]
    factor_shape = [shaped((len(spans), GROUP, width), bf16)] if spans else []
    base, own_factor, far, *span_factors = call(
        functools.partial(factor_kernel, spans, levels),
        (
            *(shaped((tokens, width), f32), shaped((tokens, width), f32)),
            *(shaped((levels, tokens, width), bf16), *factor_shape),
        ),
        (inputs, gate, level_mix, skip, cum, message),
        flops=5 * dense,
        bytes_accessed=0,
    )
    near_args = base, own_factor, far, theirs, scaled, *span_states, *span_factors
    near_shape = shaped((tokens, width // 2 if pairs else width), f32)
    near, turned, scores = call(
        functools.partial(near_kernel, parts, spans, pairs),
        (near_shape, shaped((tokens, size), bf16), shaped((tokens, GROUP), bf16)),
        (*in_maps, *out_maps, *near_args),
    )
    sums_shape = shaped((1, tokens), f32)
    if pairs:
        received = [flip(message, "seq", 4), flip(message, "seq", 2), lax.ppermute(message, "seq", CYCLE)]
        from_y, from_x, from_cycle = received
        from_y, from_x, near, far = lax.optimization_barrier((from_y, from_x, near, far))
        from_cycle, other_theirs, near = lax.optimization_barrier((from_cycle, other_theirs, near))
        own = call(
            functools.partial(combine_kernel, size),
            shaped((size, width // 2), bf16),
            (from_x, from_y, from_cycle),
            bytes_accessed=area,
        )
        other = flip(own, "seq", 1)
        other_x = flip(from_x, "seq", 1)
        near_args = base, own_factor, far, other_theirs, scaled, *span_states, *span_factors
        other_near = call(
            functools.partial(other_near_kernel, spans), near_shape, (scores, turned, own, *near_args), flops=dense
        )
        gated_shape = shaped((tokens, width // 2), f32)
        own_gated, own_squares = call(
            functools.partial(far_kernel_of_half, True),
            (gated_shape, shaped((tokens, 128), f32)),
            (turned, near, far, gain, theirs, from_x, own),
            flops=2 * dense,
            bytes_accessed=6 * area,
        )
        other_gated, sums = call(
            functools.partial(far_kernel_of_half, False),
            (gated_shape, sums_shape),
            (turned, other_near, far, gain, other_theirs, other_x, other, own_squares),
            flops=2 * dense,
            bytes_accessed=6 * area,
        )
        gated = (own_gated, other_gated)
    else:
        *gated, sums = call(
            far_kernel,
            (shaped((tokens, width), f32), sums_shape),
            (turned, near, far, gain, *far_states(shard, size)),
            flops=4 * dense,
            bytes_accessed=12 * area,
        )
    last = [sums, *around(sums, "head")]
    return call(
        functools.partial(norm_kernel, len(last), width * parts),
        shaped((tokens, width), bf16),
        (*last, *gated),
        flops=dense,
        bytes_accessed=6 * area,
        scratch=[pltpu.VMEM((tokens, width), bf16), pltpu.SemaphoreType.DMA((NORM_CHUNKS,))],
        out_space=pl.ANY,
    )


def solution(mesh):
    return jax.shard_map(
        on_device,
        mesh=mesh,
        in_specs=(
            P("seq", "head"),
            P("seq", "head"),
            P("head", "seq"),
            P("head", "seq"),
            P("head", "seq"),
            P("head"),
            P(None, "head", "seq"),
            P("head"),
            P("head"),
        ),
        out_specs=P("seq", "head"),
        check_vma=False,
    )
```

```python
import functools

import jax
import jax.numpy as jnp
from jax import lax
from jax.experimental import pallas as pl
from jax.experimental.pallas import tpu as pltpu
from jax.sharding import PartitionSpec as P

P_SIZE = 64
GROUP = 256
DECAY_ROWS = 8
BLOCK = 256
NORM_CHUNKS = 4
FIRST_HOP = 2
CYCLE = [(2 * chip + core, 2 * target + core) for chip, target in ((0, 3), (3, 1), (1, 2), (2, 0)) for core in (0, 1)]
VMEM_LIMIT = 40 * 1024 * 1024

f32, bf16 = jnp.float32, jnp.bfloat16
HIGHEST = lax.Precision.HIGHEST
TRANSPOSED = (((0,), (0,)), ((), ()))


def expander(heads, width, copies):
    row = lax.broadcasted_iota(jnp.int32, (copies * heads, width), 0)
    col = lax.broadcasted_iota(jnp.int32, (copies * heads, width), 1)
    return jnp.where(lax.rem(row, heads) == lax.div(col, P_SIZE), 1.0, 0.0)


def far_first_masks(size):
    return (*range(2, size), 1)


def pair_masks(size):
    return tuple(mask for mask in range(1, size) if not mask & FIRST_HOP)


def two_parts(factor):
    high = factor.astype(bf16).astype(f32)
    return jnp.concatenate([high, factor - high], axis=0).astype(bf16)


def transposed_dot(left, right):
    return lax.dot_general(left, right, TRANSPOSED, preferred_element_type=f32)


def head_row(heads, width, column):
    return jnp.sum(expander(heads, width, 1) * column, axis=0, keepdims=True)


def group_slice(group):
    return slice(group * GROUP, (group + 1) * GROUP)


def blocks_of(width):
    return [slice(at, at + BLOCK) for at in range(0, width, BLOCK)]


def local_spans(groups):
    spans = []
    for later in range(groups):
        for bit in range(groups.bit_length() - 1):
            if later >> bit & 1:
                start = later >> bit + 1 << bit + 1
                spans.append((later, bit, start, start + 2**bit))
    return spans


def column_of(row):
    size = row.shape[1]
    at = lax.broadcasted_iota(jnp.int32, (size, size), 0) == lax.broadcasted_iota(jnp.int32, (size, size), 1)
    return jnp.sum(jnp.where(at, row, 0.0), axis=1, keepdims=True)


def map_rows(maps):
    if all(rows.shape[0] % 16 == 0 for rows in maps):
        return jnp.concatenate([rows[...] for rows in maps], axis=0)
    return jnp.concatenate([rows[...].astype(f32) for rows in maps], axis=0).astype(bf16)


def out_map_rows(map_refs, parts):
    rows = map_refs[0].shape[0] // 2
    pairs = [ref if rows % 16 == 0 else ref[...].astype(f32) for ref in map_refs]
    sent = (0, *pair_masks(parts))
    picked = []
    for mask in (0, *far_first_masks(parts)):
        pair = pairs[sent.index(mask & ~FIRST_HOP)]
        at = slice(rows, 2 * rows) if mask & FIRST_HOP else slice(0, rows)
        picked.append(pair.at[at] if rows % 16 == 0 else pair[at])
    return map_rows(picked)


def fetch(sources, targets, semaphores):
    copies = [
        pltpu.make_async_copy(source, target, semaphores.at[index])
        for index, (source, target) in enumerate(zip(sources, targets))
    ]
    for copy in copies:
        copy.start()
    return copies


def prepare_kernel(*refs):
    sources, (scaled_ref, cum_ref), kept_refs = refs[:9], refs[9:11], refs[11:18]
    step_ref, rate_ref, semaphores = refs[18:]
    inputs_ref = kept_refs[0]
    copies = fetch(sources, (step_ref, rate_ref, *kept_refs), semaphores)
    heads, tokens = step_ref.shape
    width = inputs_ref.shape[1]
    row = lax.broadcasted_iota(jnp.int32, (GROUP, GROUP), 0)
    col = lax.broadcasted_iota(jnp.int32, (GROUP, GROUP), 1)
    until = jnp.where(row <= col, 1.0, 0.0)
    expand = expander(heads, width, 2).astype(bf16)
    copies[0].wait()
    copies[1].wait()
    step = step_ref[...]
    log_decay = -step * column_of(rate_ref[...])
    factors = []
    for group in range(tokens // GROUP):
        at = group_slice(group)
        cum = jnp.dot(log_decay[:, at], until, precision=HIGHEST, preferred_element_type=f32)
        cum_ref[:, at] = cum
        factors.append(two_parts(jnp.exp(-cum) * step[:, at]))
    factor = jnp.concatenate(factors, axis=1)
    copies[2].wait()
    for cols in blocks_of(width):
        scale = transposed_dot(factor, expand[:, cols])
        scaled_ref[:, cols] = (inputs_ref[:, cols].astype(f32) * scale).astype(bf16)
    for copy in copies[3:]:
        copy.wait()


def join_kernel(mine_ref, theirs_ref, _, both_ref):
    rows = mine_ref.shape[0]
    both_ref[:rows, :] = mine_ref[...]
    both_ref[rows:, :] = theirs_ref[...]


def states_kernel(parts, sides, *refs):
    map_refs, (scaled_ref, cum_ref), out_refs = refs[:parts], refs[parts : parts + 2], refs[parts + 2 :]
    shard_refs = out_refs[:sides]
    heads, tokens = cum_ref.shape
    width = scaled_ref.shape[1]
    in_map = map_rows(map_refs)
    size = in_map.shape[0]
    cum = cum_ref[...]
    states, decays = [], []
    for group in range(tokens // GROUP):
        at = group_slice(group)
        decay = head_row(heads, width, jnp.exp(cum[:, at.stop - 1 : at.stop]))
        raw = jnp.dot(in_map[:, at], scaled_ref[at, :], preferred_element_type=f32)
        states.append(raw * decay)
        decays.append(decay)
    total, decay = states[0], decays[0]
    for group in range(1, len(states)):
        total = total * decays[group] + states[group]
        decay = decay * decays[group]
    columns = width // sides
    core = lax.rem(lax.axis_index("seq"), 2)
    for ref, first in zip(shard_refs, (core == 0, core == 1)):
        at = slice(0, columns)
        ref[:size, :] = jnp.where(first, total[:, at], total[:, width - columns :]).astype(bf16)
        row = jnp.where(first, decay[:, at], decay[:, width - columns :])
        ref[size:, :] = jnp.broadcast_to(row, (DECAY_ROWS, columns)).astype(bf16)
    for index, (later, _, start, stop) in enumerate(local_spans(len(states))):
        span = states[start]
        for group in range(start + 1, later):
            span = span * decays[group]
            if group < stop:
                span = span + states[group]
        out_refs[sides][index * size : (index + 1) * size, :] = span.astype(bf16)


def merge_kernel(size, mine_ref, theirs_ref, _, pair_ref):
    core = lax.rem(lax.axis_index("seq"), 2)
    mine, theirs = mine_ref[...], theirs_ref[...]
    older = jnp.where(core == 1, theirs, mine).astype(f32)
    newer = jnp.where(core == 1, mine, theirs).astype(f32)
    decay = newer[size : size + 1]
    pair_ref[:size, :] = (older[:size] * decay + newer[:size]).astype(bf16)
    pair_ref[size:, :] = (older[size:] * decay).astype(bf16)


def factor_kernel(spans, levels, *refs):
    inputs_ref, gate_ref, mix_ref, skip_ref, cum_ref, _ = refs[:6]
    base_ref, own_ref, far_ref = refs[6:9]
    span_refs = refs[9:]
    heads, tokens = cum_ref.shape
    width = inputs_ref.shape[1]
    groups = tokens // GROUP
    first = groups.bit_length()
    expand = expander(heads, width, 2).astype(bf16)
    skip = head_row(heads, width, column_of(skip_ref[...]))
    before = jnp.zeros((heads, 1), f32)
    for group in range(groups):
        at = group_slice(group)
        cum = cum_ref[:, at]
        decay = jnp.exp(cum)
        own_mix = two_parts(mix_ref[0, :, at] * decay)
        span_mixes = [
            (index, two_parts(mix_ref[1 + bit, :, at] * decay))
            for index, (later, bit, _, _) in enumerate(spans)
            if later == group
        ]
        decay = jnp.exp(cum + before)
        before = before + cum[:, GROUP - 1 : GROUP]
        far_mixes = [two_parts(mix_ref[first + level, :, at] * decay) for level in range(levels)]
        for cols in blocks_of(width):
            gate = gate_ref[at, cols].astype(f32)
            swish = gate / (1.0 + jnp.exp(-gate))
            base_ref[at, cols] = skip[:, cols] * inputs_ref[at, cols].astype(f32) * swish
            own_ref[at, cols] = transposed_dot(own_mix, expand[:, cols]) * swish
            for level, mix in enumerate(far_mixes):
                far_ref[level, at, cols] = (transposed_dot(mix, expand[:, cols]) * swish).astype(bf16)
            for index, mix in span_mixes:
                span_refs[0][index, :, cols] = (transposed_dot(mix, expand[:, cols]) * swish).astype(bf16)


def near_body(spans, has_core, start, scores_ref, turned_ref, refs, near_ref):
    base_ref, own_ref, far_ref, core_ref, scaled_ref = refs[:5]
    span_refs = refs[5:]
    tokens, size = turned_ref.shape
    for group in range(tokens // GROUP):
        at = group_slice(group)
        for cols in blocks_of(near_ref.shape[1]):
            of = pl.ds(pl.multiple_of(start + cols.start, BLOCK), BLOCK)
            own = jnp.dot(scores_ref[at, :], scaled_ref[at, of], preferred_element_type=f32)
            total = base_ref[at, of] + own_ref[at, of] * own
            for index, (later, _, _, _) in enumerate(spans):
                if later == group:
                    rows = slice(index * size, (index + 1) * size)
                    reach = jnp.dot(turned_ref[at, :], span_refs[0][rows, of], preferred_element_type=f32)
                    total = total + span_refs[1][index, :, of].astype(f32) * reach
            if has_core:
                reach = jnp.dot(turned_ref[at, :], core_ref[:size, cols], preferred_element_type=f32)
                total = total + far_ref[0, at, of].astype(f32) * reach
            near_ref[at, cols] = total


def near_of_core(spans, own, scores_ref, turned_ref, refs, near_ref):
    core = lax.rem(lax.axis_index("seq"), 2)
    for has_core in (0, 1):

        @pl.when(core == has_core)
        def _():
            start = (has_core if own else 1 - has_core) * near_ref.shape[1]
            near_body(spans, has_core, start, scores_ref, turned_ref, refs, near_ref)


def near_kernel(parts, spans, paired, *refs):
    count = parts + parts // 2
    in_refs, out_refs, rest = refs[:parts], refs[parts:count], refs[count:-3]
    near_ref, turned_ref, scores_ref = refs[-3:]
    in_map = map_rows(in_refs)
    turned = jnp.transpose(out_map_rows(out_refs, parts))
    turned_ref[...] = turned
    row = lax.broadcasted_iota(jnp.int32, (GROUP, GROUP), 0)
    col = lax.broadcasted_iota(jnp.int32, (GROUP, GROUP), 1)
    for group in range(turned.shape[0] // GROUP):
        at = group_slice(group)
        scores = jnp.dot(turned[at], in_map[:, at], preferred_element_type=f32)
        scores_ref[at, :] = jnp.where(row >= col, scores, 0.0).astype(bf16)
    if paired:
        near_of_core(spans, True, scores_ref, turned_ref, rest, near_ref)
    else:
        near_body(spans, False, 0, scores_ref, turned_ref, rest, near_ref)


def other_near_kernel(spans, scores_ref, turned_ref, _, *refs):
    near_of_core(spans, False, scores_ref, turned_ref, refs[:-1], refs[-1])


def far_body(turned_ref, near_ref, far_ref, gain_ref, start, columns, levels, state_of, gated_ref):
    tokens = far_ref.shape[1]
    squares = jnp.zeros((tokens, 128), f32)
    for cols in blocks_of(columns):
        at = pl.ds(pl.multiple_of(start + cols.start, BLOCK), BLOCK)
        total = near_ref[:, cols]
        for level in levels:
            state = state_of(level, cols, at).astype(bf16)
            reach = jnp.dot(turned_ref[...], state, preferred_element_type=f32)
            total = total + far_ref[level, :, at].astype(f32) * reach
        gated_ref[:, cols] = total * gain_ref[:, at]
        total = total * total
        for part in range(0, BLOCK, 128):
            squares = squares + total[:, part : part + 128]
    return squares


def row_sums(squares):
    high = squares.astype(bf16)
    low = (squares - high.astype(f32)).astype(bf16)
    parts = jnp.concatenate([high, low], axis=1)
    ones = jnp.ones((16, parts.shape[1]), bf16)
    return lax.dot_general(ones, parts, (((1,), (1,)), ((), ())), preferred_element_type=f32)[:1]


def far_kernel(turned_ref, near_ref, far_ref, gain_ref, *refs):
    state_refs = refs[:-2]
    gated_ref, sums_ref = refs[-2:]

    def state_of(level, cols, _):
        return state_refs[level][:, cols]

    width = near_ref.shape[1]
    levels = range(far_ref.shape[0])
    squares = far_body(turned_ref, near_ref, far_ref, gain_ref, 0, width, levels, state_of, gated_ref)
    sums_ref[...] = row_sums(squares)


def combine_kernel(size, x_ref, y_ref, diagonal_ref, spans_ref):
    rank = lax.axis_index("seq")
    along_x = lax.rem(lax.div(rank, 2), 2)
    along_y = lax.div(rank, 4)

    def parts_of(ref):
        return ref[:size, :].astype(f32), ref[size:, :].astype(f32)[:1]

    _, x_decay = parts_of(x_ref)
    y_state, y_decay = parts_of(y_ref)
    d_state, d_decay = parts_of(diagonal_ref)
    newer = jnp.where(along_x == 1, y_state, d_state)
    newer_decay = jnp.where(along_x == 1, y_decay, d_decay)
    older = jnp.where(along_x == 1, d_state, y_state)
    running = jnp.where(along_x == 1, x_decay, 1.0)
    running = jnp.where(along_y == 1, running, 0.0)
    spans_ref[...] = ((older * newer_decay + newer) * running).astype(bf16)


def far_kernel_of_half(own, *refs):
    turned_ref, near_ref, far_ref, gain_ref, core_ref, x_ref, span_ref = refs[:7]
    gated_ref, sums_ref = refs[-2:]
    size = turned_ref.shape[1]
    rank = lax.axis_index("seq")
    core = lax.rem(rank, 2)
    along_x = lax.rem(lax.div(rank, 2), 2)
    along_y = lax.div(rank, 4)
    half = span_ref.shape[1]
    start = (core if own else 1 - core) * half

    def state_of(level, cols, at):
        core_decay = core_ref[size:, cols].astype(f32)[:1]
        running = jnp.where(core == 1, core_decay, 1.0)
        if level == 1:
            return x_ref[:size, cols].astype(f32) * running
        return span_ref[:, cols].astype(f32) * running

    for has_x, has_y in ((0, 0), (0, 1), (1, 0), (1, 1)):

        @pl.when((along_x == has_x) & (along_y == has_y))
        def _():
            levels = (1,) * has_x + (2,) * has_y
            squares = far_body(turned_ref, near_ref, far_ref, gain_ref, start, half, levels, state_of, gated_ref)
            sums_ref[...] = squares if own else row_sums(squares + refs[7][...])


def norm_kernel(parts, columns, *refs):
    gated_refs, (out_hbm, out_ref, semaphores) = refs[parts:-3], refs[-3:]
    total = refs[0][...]
    for ref in refs[1:parts]:
        total = total + ref[...]
    scale = lax.rsqrt(total / columns + 1e-05)
    tokens = scale.shape[1]
    scale = jnp.broadcast_to(scale, (8, tokens))
    width = gated_refs[0].shape[1]
    core = lax.rem(lax.axis_index("seq"), 2)
    sides = (core, 1 - core) if len(gated_refs) == 2 else (0,)
    chunk = tokens // NORM_CHUNKS
    copies = []
    for index in range(NORM_CHUNKS):
        rows = slice(index * chunk, (index + 1) * chunk)
        column = jnp.transpose(scale[:, rows])[:, :1]
        for ref, side in zip(gated_refs, sides):
            at = pl.ds(pl.multiple_of(side * width, width), width)
            out_ref[rows, at] = (ref[rows, :] * column).astype(bf16)
        copies.append(pltpu.make_async_copy(out_ref.at[rows], out_hbm.at[rows], semaphores.at[index]))
        copies[-1].start()
    for copy in copies:
        copy.wait()


def call(kernel, out_shape, args, flops=0, bytes_accessed=0, hbm=0, scratch=None, out_space=pltpu.VMEM):
    specs = [pl.BlockSpec(memory_space=pl.ANY)] * hbm + [pl.BlockSpec(memory_space=pltpu.VMEM)] * (len(args) - hbm)
    args = [pltpu.with_memory_space_constraint(arg, pltpu.HBM) for arg in args[:hbm]] + list(args[hbm:])
    if scratch is None:
        scratch = [pltpu.VMEM(arg.shape, arg.dtype) for arg in args[:hbm]]
        scratch += [pltpu.SemaphoreType.DMA((hbm,))] if hbm else []
    return pl.pallas_call(
        kernel,
        out_shape=out_shape,
        in_specs=specs,
        out_specs=jax.tree.map(lambda _: pl.BlockSpec(memory_space=out_space), out_shape),
        scratch_shapes=scratch,
        compiler_params=pltpu.CompilerParams(vmem_limit_bytes=VMEM_LIMIT),
        cost_estimate=pl.CostEstimate(flops=flops, bytes_accessed=bytes_accessed, transcendentals=0),
    )(*args)


def shaped(shape, dtype):
    return jax.ShapeDtypeStruct(shape, dtype)


def flip(array, axis, mask):
    return lax.ppermute(array, axis, [(i, i ^ mask) for i in range(lax.axis_size(axis))])


def from_each(array, axis, masks):
    return [flip(array, axis, mask) for mask in masks]


def around(array, axis):
    size = lax.axis_size(axis)
    return [lax.ppermute(array, axis, [(i, (i + shift) % size) for i in range(size)]) for shift in range(1, size)]


def merged(older, newer, size):
    older, newer = older.astype(f32), newer.astype(f32)
    decay = newer[size : size + 1]
    return jnp.concatenate([older[:size] * decay + newer[:size], older[size:] * decay], axis=0).astype(bf16)


def far_states(shard, size):
    rank = lax.axis_index("seq")
    levels = lax.axis_size("seq").bit_length() - 1
    states = []
    running = jnp.ones((1, shard.shape[1]), f32)
    for level in range(levels):
        theirs = flip(shard, "seq", 1 << level)
        upper = jnp.right_shift(rank, level) % 2 == 1
        states.append(jnp.where(upper, theirs[:size].astype(f32) * running, 0.0).astype(bf16))
        running = jnp.where(upper, running * theirs[size : size + 1].astype(f32), running)
        shard = merged(jnp.where(upper, theirs, shard), jnp.where(upper, shard, theirs), size)
    return states


def on_device(inputs, gate, input_map, output_map, step, decay_rate, level_mix, skip, norm_gain):
    tokens, width = inputs.shape
    heads = step.shape[0]
    parts = lax.axis_size("head")
    levels = lax.axis_size("seq").bit_length() - 1
    size = input_map.shape[0] * parts
    groups = tokens // GROUP
    spans = local_spans(groups)
    dense = 2 * tokens * GROUP * width
    area = tokens * width
    others = from_each(input_map, "head", far_first_masks(parts))
    kept = inputs, gate, level_mix, skip[None, :], input_map, output_map, norm_gain[None, :]
    beside = flip(output_map, "head", FIRST_HOP)
    scaled, cum, *kept = call(
        prepare_kernel,
        (
            *(shaped((tokens, width), bf16), shaped((heads, tokens), f32)),
            *(shaped(array.shape, array.dtype) for array in kept),
        ),
        (step, decay_rate[None, :], *kept),
        flops=16 * dense,
        bytes_accessed=4 * area,
        hbm=9,
        scratch=[pltpu.VMEM(step.shape, f32), pltpu.VMEM((1, heads), f32), pltpu.SemaphoreType.DMA((9,))],
    )
    inputs, gate, level_mix, skip, input_map, output_map, gain = kept
    in_maps = [input_map, *others]
    pairs = lax.axis_size("seq") == 8 and parts == 4
    sides = 2 if pairs else 1
    shard_shape = shaped((size + DECAY_ROWS, width // sides), bf16)
    span_shape = [shaped((len(spans) * size, width), bf16)] if spans else []
    shard, *rest = call(
        functools.partial(states_kernel, parts, sides),
        (*[shard_shape] * sides, *span_shape),
        (*in_maps, scaled, cum),
        flops=dense,
    )
    span_states = rest[sides - 1 :]
    rows = output_map.shape[0]
    if rows % 16 == 0:
        both = call(
            join_kernel,
            shaped((2 * rows, tokens), bf16),
            (output_map, beside, shard),
            flops=8 * dense,
        )
    else:
        both = jnp.concatenate([output_map, beside], axis=0)
    if pairs:
        theirs = flip(rest[0], "seq", 1)
        message = call(
            functools.partial(merge_kernel, size), shard_shape, (shard, theirs, both), flops=0
        )
        other_theirs = flip(lax.optimization_barrier((shard, message))[0], "seq", 1)
    else:
        other_theirs = theirs = message = shard
    out_maps = [both, *from_each(both, "head", pair_masks(parts))]
    factor_shape = [shaped((len(spans), GROUP, width), bf16)] if spans else []
    base, own_factor, far, *span_factors = call(
        functools.partial(factor_kernel, spans, levels),
        (
            *(shaped((tokens, width), f32), shaped((tokens, width), f32)),
            *(shaped((levels, tokens, width), bf16), *factor_shape),
        ),
        (inputs, gate, level_mix, skip, cum, message),
        flops=5 * dense,
        bytes_accessed=0,
    )
    near_args = base, own_factor, far, theirs, scaled, *span_states, *span_factors
    near_shape = shaped((tokens, width // 2 if pairs else width), f32)
    near, turned, scores = call(
        functools.partial(near_kernel, parts, spans, pairs),
        (near_shape, shaped((tokens, size), bf16), shaped((tokens, GROUP), bf16)),
        (*in_maps, *out_maps, *near_args),
    )
    sums_shape = shaped((1, tokens), f32)
    if pairs:
        received = [flip(message, "seq", 4), flip(message, "seq", 2), lax.ppermute(message, "seq", CYCLE)]
        from_y, from_x, from_cycle = received
        from_y, from_x, near, far = lax.optimization_barrier((from_y, from_x, near, far))
        from_cycle, other_theirs, near = lax.optimization_barrier((from_cycle, other_theirs, near))
        own = call(
            functools.partial(combine_kernel, size),
            shaped((size, width // 2), bf16),
            (from_x, from_y, from_cycle),
            bytes_accessed=area,
        )
        other = flip(own, "seq", 1)
        other_x = flip(from_x, "seq", 1)
        near_args = base, own_factor, far, other_theirs, scaled, *span_states, *span_factors
        other_near = call(
            functools.partial(other_near_kernel, spans), near_shape, (scores, turned, own, *near_args), flops=dense
        )
        gated_shape = shaped((tokens, width // 2), f32)
        own_gated, own_squares = call(
            functools.partial(far_kernel_of_half, True),
            (gated_shape, shaped((tokens, 128), f32)),
            (turned, near, far, gain, theirs, from_x, own),
            flops=2 * dense,
            bytes_accessed=6 * area,
        )
        other_gated, sums = call(
            functools.partial(far_kernel_of_half, False),
            (gated_shape, sums_shape),
            (turned, other_near, far, gain, other_theirs, other_x, other, own_squares),
            flops=2 * dense,
            bytes_accessed=6 * area,
        )
        gated = (own_gated, other_gated)
    else:
        *gated, sums = call(
            far_kernel,
            (shaped((tokens, width), f32), sums_shape),
            (turned, near, far, gain, *far_states(shard, size)),
            flops=4 * dense,
            bytes_accessed=12 * area,
        )
    last = [sums, *around(sums, "head")]
    return call(
        functools.partial(norm_kernel, len(last), width * parts),
        shaped((tokens, width), bf16),
        (*last, *gated),
        flops=dense,
        bytes_accessed=6 * area,
        scratch=[pltpu.VMEM((tokens, width), bf16), pltpu.SemaphoreType.DMA((NORM_CHUNKS,))],
        out_space=pl.ANY,
    )


def solution(mesh):
    return jax.shard_map(
        on_device,
        mesh=mesh,
        in_specs=(
            P("seq", "head"),
            P("seq", "head"),
            P("head", "seq"),
            P("head", "seq"),
            P("head", "seq"),
            P("head"),
            P(None, "head", "seq"),
            P("head"),
            P("head"),
        ),
        out_specs=P("seq", "head"),
        check_vma=False,
    )
```

```python
import functools

import jax
import jax.numpy as jnp
from jax import lax
from jax.experimental import pallas as pl
from jax.experimental.pallas import tpu as pltpu
from jax.sharding import PartitionSpec as P

P_SIZE = 64
GROUP = 256
DECAY_ROWS = 8
BLOCK = 256
NORM_CHUNKS = 4
FIRST_HOP = 2
LATER_SHIFTS = (2, 1, 3)
CYCLE = [(2 * chip + core, 2 * target + core) for chip, target in ((0, 3), (3, 1), (1, 2), (2, 0)) for core in (0, 1)]
VMEM_LIMIT = 40 * 1024 * 1024

f32, bf16 = jnp.float32, jnp.bfloat16
HIGHEST = lax.Precision.HIGHEST
TRANSPOSED = (((0,), (0,)), ((), ()))


def expander(heads, width, copies):
    row = lax.broadcasted_iota(jnp.int32, (copies * heads, width), 0)
    col = lax.broadcasted_iota(jnp.int32, (copies * heads, width), 1)
    return jnp.where(lax.rem(row, heads) == lax.div(col, P_SIZE), 1.0, 0.0)


def far_first_masks(size):
    return (*range(2, size), 1)


def pair_masks(size):
    return tuple(mask for mask in range(1, size) if not mask & FIRST_HOP)


def two_parts(factor):
    high = factor.astype(bf16).astype(f32)
    return jnp.concatenate([high, factor - high], axis=0).astype(bf16)


def transposed_dot(left, right):
    return lax.dot_general(left, right, TRANSPOSED, preferred_element_type=f32)


def head_row(heads, width, column):
    return jnp.sum(expander(heads, width, 1) * column, axis=0, keepdims=True)


def group_slice(group):
    return slice(group * GROUP, (group + 1) * GROUP)


def blocks_of(width):
    return [slice(at, at + BLOCK) for at in range(0, width, BLOCK)]


def local_spans(groups):
    spans = []
    for later in range(groups):
        for bit in range(groups.bit_length() - 1):
            if later >> bit & 1:
                start = later >> bit + 1 << bit + 1
                spans.append((later, bit, start, start + 2**bit))
    return spans


def column_of(row):
    size = row.shape[1]
    at = lax.broadcasted_iota(jnp.int32, (size, size), 0) == lax.broadcasted_iota(jnp.int32, (size, size), 1)
    return jnp.sum(jnp.where(at, row, 0.0), axis=1, keepdims=True)


def map_rows(maps):
    if all(rows.shape[0] % 16 == 0 for rows in maps):
        return jnp.concatenate([rows[...] for rows in maps], axis=0)
    return jnp.concatenate([rows[...].astype(f32) for rows in maps], axis=0).astype(bf16)


def out_map_rows(map_refs, parts):
    rows = map_refs[0].shape[0] // 2
    pairs = [ref if rows % 16 == 0 else ref[...].astype(f32) for ref in map_refs]
    sent = (0, *pair_masks(parts))
    picked = []
    for mask in (0, *far_first_masks(parts)):
        pair = pairs[sent.index(mask & ~FIRST_HOP)]
        at = slice(rows, 2 * rows) if mask & FIRST_HOP else slice(0, rows)
        picked.append(pair.at[at] if rows % 16 == 0 else pair[at])
    return map_rows(picked)


def fetch(sources, targets, semaphores):
    copies = [
        pltpu.make_async_copy(source, target, semaphores.at[index])
        for index, (source, target) in enumerate(zip(sources, targets))
    ]
    for copy in copies:
        copy.start()
    return copies


def prepare_kernel(*refs):
    sources, (scaled_ref, cum_ref), kept_refs = refs[:9], refs[9:11], refs[11:18]
    step_ref, rate_ref, semaphores = refs[18:]
    inputs_ref = kept_refs[0]
    copies = fetch(sources, (step_ref, rate_ref, *kept_refs), semaphores)
    heads, tokens = step_ref.shape
    width = inputs_ref.shape[1]
    row = lax.broadcasted_iota(jnp.int32, (GROUP, GROUP), 0)
    col = lax.broadcasted_iota(jnp.int32, (GROUP, GROUP), 1)
    until = jnp.where(row <= col, 1.0, 0.0)
    expand = expander(heads, width, 2).astype(bf16)
    copies[0].wait()
    copies[1].wait()
    step = step_ref[...]
    log_decay = -step * column_of(rate_ref[...])
    factors = []
    for group in range(tokens // GROUP):
        at = group_slice(group)
        cum = jnp.dot(log_decay[:, at], until, precision=HIGHEST, preferred_element_type=f32)
        cum_ref[:, at] = cum
        factors.append(two_parts(jnp.exp(-cum) * step[:, at]))
    factor = jnp.concatenate(factors, axis=1)
    copies[2].wait()
    for cols in blocks_of(width):
        scale = transposed_dot(factor, expand[:, cols])
        scaled_ref[:, cols] = (inputs_ref[:, cols].astype(f32) * scale).astype(bf16)
    for copy in copies[3:]:
        copy.wait()


def join_kernel(mine_ref, theirs_ref, _, both_ref):
    rows = mine_ref.shape[0]
    both_ref[:rows, :] = mine_ref[...]
    both_ref[rows:, :] = theirs_ref[...]


def states_kernel(parts, sides, *refs):
    map_refs, (scaled_ref, cum_ref), out_refs = refs[:parts], refs[parts : parts + 2], refs[parts + 2 :]
    shard_refs = out_refs[:sides]
    heads, tokens = cum_ref.shape
    width = scaled_ref.shape[1]
    in_map = map_rows(map_refs)
    size = in_map.shape[0]
    cum = cum_ref[...]
    states, decays = [], []
    for group in range(tokens // GROUP):
        at = group_slice(group)
        decay = head_row(heads, width, jnp.exp(cum[:, at.stop - 1 : at.stop]))
        raw = jnp.dot(in_map[:, at], scaled_ref[at, :], preferred_element_type=f32)
        states.append(raw * decay)
        decays.append(decay)
    total, decay = states[0], decays[0]
    for group in range(1, len(states)):
        total = total * decays[group] + states[group]
        decay = decay * decays[group]
    columns = width // sides
    core = lax.rem(lax.axis_index("seq"), 2)
    for ref, first in zip(shard_refs, (core == 0, core == 1)):
        at = slice(0, columns)
        ref[:size, :] = jnp.where(first, total[:, at], total[:, width - columns :]).astype(bf16)
        row = jnp.where(first, decay[:, at], decay[:, width - columns :])
        ref[size:, :] = jnp.broadcast_to(row, (DECAY_ROWS, columns)).astype(bf16)
    for index, (later, _, start, stop) in enumerate(local_spans(len(states))):
        span = states[start]
        for group in range(start + 1, later):
            span = span * decays[group]
            if group < stop:
                span = span + states[group]
        out_refs[sides][index * size : (index + 1) * size, :] = span.astype(bf16)


def merge_kernel(size, mine_ref, theirs_ref, _, pair_ref):
    core = lax.rem(lax.axis_index("seq"), 2)
    mine, theirs = mine_ref[...], theirs_ref[...]
    older = jnp.where(core == 1, theirs, mine).astype(f32)
    newer = jnp.where(core == 1, mine, theirs).astype(f32)
    decay = newer[size : size + 1]
    pair_ref[:size, :] = (older[:size] * decay + newer[:size]).astype(bf16)
    pair_ref[size:, :] = (older[size:] * decay).astype(bf16)


def factor_kernel(spans, levels, *refs):
    inputs_ref, gate_ref, mix_ref, skip_ref, cum_ref, _ = refs[:6]
    base_ref, own_ref, far_ref = refs[6:9]
    span_refs = refs[9:]
    heads, tokens = cum_ref.shape
    width = inputs_ref.shape[1]
    groups = tokens // GROUP
    first = groups.bit_length()
    expand = expander(heads, width, 2).astype(bf16)
    skip = head_row(heads, width, column_of(skip_ref[...]))
    before = jnp.zeros((heads, 1), f32)
    for group in range(groups):
        at = group_slice(group)
        cum = cum_ref[:, at]
        decay = jnp.exp(cum)
        own_mix = two_parts(mix_ref[0, :, at] * decay)
        span_mixes = [
            (index, two_parts(mix_ref[1 + bit, :, at] * decay))
            for index, (later, bit, _, _) in enumerate(spans)
            if later == group
        ]
        decay = jnp.exp(cum + before)
        before = before + cum[:, GROUP - 1 : GROUP]
        far_mixes = [two_parts(mix_ref[first + level, :, at] * decay) for level in range(levels)]
        for cols in blocks_of(width):
            gate = gate_ref[at, cols].astype(f32)
            swish = gate / (1.0 + jnp.exp(-gate))
            base_ref[at, cols] = skip[:, cols] * inputs_ref[at, cols].astype(f32) * swish
            own_ref[at, cols] = transposed_dot(own_mix, expand[:, cols]) * swish
            for level, mix in enumerate(far_mixes):
                far_ref[level, at, cols] = (transposed_dot(mix, expand[:, cols]) * swish).astype(bf16)
            for index, mix in span_mixes:
                span_refs[0][index, :, cols] = (transposed_dot(mix, expand[:, cols]) * swish).astype(bf16)


def near_body(spans, has_core, start, scores_ref, turned_ref, refs, near_ref):
    base_ref, own_ref, far_ref, core_ref, scaled_ref = refs[:5]
    span_refs = refs[5:]
    tokens, size = turned_ref.shape
    for group in range(tokens // GROUP):
        at = group_slice(group)
        for cols in blocks_of(near_ref.shape[1]):
            of = pl.ds(pl.multiple_of(start + cols.start, BLOCK), BLOCK)
            own = jnp.dot(scores_ref[at, :], scaled_ref[at, of], preferred_element_type=f32)
            total = base_ref[at, of] + own_ref[at, of] * own
            for index, (later, _, _, _) in enumerate(spans):
                if later == group:
                    rows = slice(index * size, (index + 1) * size)
                    reach = jnp.dot(turned_ref[at, :], span_refs[0][rows, of], preferred_element_type=f32)
                    total = total + span_refs[1][index, :, of].astype(f32) * reach
            if has_core:
                reach = jnp.dot(turned_ref[at, :], core_ref[:size, cols], preferred_element_type=f32)
                total = total + far_ref[0, at, of].astype(f32) * reach
            near_ref[at, cols] = total


def near_of_core(spans, own, scores_ref, turned_ref, refs, near_ref):
    core = lax.rem(lax.axis_index("seq"), 2)
    for has_core in (0, 1):

        @pl.when(core == has_core)
        def _():
            start = (has_core if own else 1 - has_core) * near_ref.shape[1]
            near_body(spans, has_core, start, scores_ref, turned_ref, refs, near_ref)


def near_kernel(parts, spans, paired, *refs):
    count = parts + parts // 2
    in_refs, out_refs, rest = refs[:parts], refs[parts:count], refs[count:-3]
    near_ref, turned_ref, scores_ref = refs[-3:]
    in_map = map_rows(in_refs)
    turned = jnp.transpose(out_map_rows(out_refs, parts))
    turned_ref[...] = turned
    row = lax.broadcasted_iota(jnp.int32, (GROUP, GROUP), 0)
    col = lax.broadcasted_iota(jnp.int32, (GROUP, GROUP), 1)
    for group in range(turned.shape[0] // GROUP):
        at = group_slice(group)
        scores = jnp.dot(turned[at], in_map[:, at], preferred_element_type=f32)
        scores_ref[at, :] = jnp.where(row >= col, scores, 0.0).astype(bf16)
    if paired:
        near_of_core(spans, True, scores_ref, turned_ref, rest, near_ref)
    else:
        near_body(spans, False, 0, scores_ref, turned_ref, rest, near_ref)


def other_near_kernel(spans, scores_ref, turned_ref, _, *refs):
    near_of_core(spans, False, scores_ref, turned_ref, refs[:-1], refs[-1])


def far_body(turned_ref, near_ref, far_ref, gain_ref, start, columns, levels, state_of, gated_ref):
    tokens = far_ref.shape[1]
    squares = jnp.zeros((tokens, 128), f32)
    for cols in blocks_of(columns):
        at = pl.ds(pl.multiple_of(start + cols.start, BLOCK), BLOCK)
        total = near_ref[:, cols]
        for level in levels:
            state = state_of(level, cols, at).astype(bf16)
            reach = jnp.dot(turned_ref[...], state, preferred_element_type=f32)
            total = total + far_ref[level, :, at].astype(f32) * reach
        gated_ref[:, cols] = total * gain_ref[:, at]
        total = total * total
        for part in range(0, BLOCK, 128):
            squares = squares + total[:, part : part + 128]
    return squares


def row_sums(squares):
    high = squares.astype(bf16)
    low = (squares - high.astype(f32)).astype(bf16)
    parts = jnp.concatenate([high, low], axis=1)
    ones = jnp.ones((16, parts.shape[1]), bf16)
    return lax.dot_general(ones, parts, (((1,), (1,)), ((), ())), preferred_element_type=f32)[:1]


def far_kernel(turned_ref, near_ref, far_ref, gain_ref, *refs):
    state_refs = refs[:-2]
    gated_ref, sums_ref = refs[-2:]

    def state_of(level, cols, _):
        return state_refs[level][:, cols]

    width = near_ref.shape[1]
    levels = range(far_ref.shape[0])
    squares = far_body(turned_ref, near_ref, far_ref, gain_ref, 0, width, levels, state_of, gated_ref)
    sums_ref[...] = row_sums(squares)


def combine_kernel(size, x_ref, y_ref, diagonal_ref, spans_ref):
    rank = lax.axis_index("seq")
    along_x = lax.rem(lax.div(rank, 2), 2)
    along_y = lax.div(rank, 4)

    def parts_of(ref):
        return ref[:size, :].astype(f32), ref[size:, :].astype(f32)[:1]

    _, x_decay = parts_of(x_ref)
    y_state, y_decay = parts_of(y_ref)
    d_state, d_decay = parts_of(diagonal_ref)
    newer = jnp.where(along_x == 1, y_state, d_state)
    newer_decay = jnp.where(along_x == 1, y_decay, d_decay)
    older = jnp.where(along_x == 1, d_state, y_state)
    running = jnp.where(along_x == 1, x_decay, 1.0)
    running = jnp.where(along_y == 1, running, 0.0)
    spans_ref[...] = ((older * newer_decay + newer) * running).astype(bf16)


def far_kernel_of_half(own, *refs):
    turned_ref, near_ref, far_ref, gain_ref, core_ref, x_ref, span_ref = refs[:7]
    gated_ref, sums_ref = refs[-2:]
    size = turned_ref.shape[1]
    rank = lax.axis_index("seq")
    core = lax.rem(rank, 2)
    along_x = lax.rem(lax.div(rank, 2), 2)
    along_y = lax.div(rank, 4)
    half = span_ref.shape[1]
    start = (core if own else 1 - core) * half

    def state_of(level, cols, at):
        core_decay = core_ref[size:, cols].astype(f32)[:1]
        running = jnp.where(core == 1, core_decay, 1.0)
        if level == 1:
            return x_ref[:size, cols].astype(f32) * running
        return span_ref[:, cols].astype(f32) * running

    for has_x, has_y in ((0, 0), (0, 1), (1, 0), (1, 1)):

        @pl.when((along_x == has_x) & (along_y == has_y))
        def _():
            levels = (1,) * has_x + (2,) * has_y
            squares = far_body(turned_ref, near_ref, far_ref, gain_ref, start, half, levels, state_of, gated_ref)
            sums_ref[...] = squares if own else row_sums(squares + refs[7][...])


def norm_kernel(parts, columns, *refs):
    gated_refs, (out_hbm, out_ref, semaphores) = refs[parts:-3], refs[-3:]
    total = refs[0][...]
    for ref in refs[1:parts]:
        total = total + ref[...]
    scale = lax.rsqrt(total / columns + 1e-05)
    tokens = scale.shape[1]
    scale = jnp.broadcast_to(scale, (8, tokens))
    width = gated_refs[0].shape[1]
    core = lax.rem(lax.axis_index("seq"), 2)
    sides = (core, 1 - core) if len(gated_refs) == 2 else (0,)
    chunk = tokens // NORM_CHUNKS
    copies = []
    for index in range(NORM_CHUNKS):
        rows = slice(index * chunk, (index + 1) * chunk)
        column = jnp.transpose(scale[:, rows])[:, :1]
        for ref, side in zip(gated_refs, sides):
            at = pl.ds(pl.multiple_of(side * width, width), width)
            out_ref[rows, at] = (ref[rows, :] * column).astype(bf16)
        copies.append(pltpu.make_async_copy(out_ref.at[rows], out_hbm.at[rows], semaphores.at[index]))
        copies[-1].start()
    for copy in copies:
        copy.wait()


def call(kernel, out_shape, args, flops=0, bytes_accessed=0, hbm=0, scratch=None, out_space=pltpu.VMEM):
    specs = [pl.BlockSpec(memory_space=pl.ANY)] * hbm + [pl.BlockSpec(memory_space=pltpu.VMEM)] * (len(args) - hbm)
    args = [pltpu.with_memory_space_constraint(arg, pltpu.HBM) for arg in args[:hbm]] + list(args[hbm:])
    if scratch is None:
        scratch = [pltpu.VMEM(arg.shape, arg.dtype) for arg in args[:hbm]]
        scratch += [pltpu.SemaphoreType.DMA((hbm,))] if hbm else []
    return pl.pallas_call(
        kernel,
        out_shape=out_shape,
        in_specs=specs,
        out_specs=jax.tree.map(lambda _: pl.BlockSpec(memory_space=out_space), out_shape),
        scratch_shapes=scratch,
        compiler_params=pltpu.CompilerParams(vmem_limit_bytes=VMEM_LIMIT),
        cost_estimate=pl.CostEstimate(flops=flops, bytes_accessed=bytes_accessed, transcendentals=0),
    )(*args)


def shaped(shape, dtype):
    return jax.ShapeDtypeStruct(shape, dtype)


def flip(array, axis, mask):
    return lax.ppermute(array, axis, [(i, i ^ mask) for i in range(lax.axis_size(axis))])


def from_each(array, axis, masks):
    return [flip(array, axis, mask) for mask in masks]


def around(array, paired):
    shards, size = lax.axis_size("seq"), lax.axis_size("head")
    received = []
    for step in range(1, size):
        pairs = []
        for shard in range(shards):
            shift = LATER_SHIFTS[step - 1] if paired and shard >= shards // 2 else step
            pairs += [(shard * size + i, shard * size + (i + shift) % size) for i in range(size)]
        received.append(lax.ppermute(array, ("seq", "head"), pairs))
    return received


def merged(older, newer, size):
    older, newer = older.astype(f32), newer.astype(f32)
    decay = newer[size : size + 1]
    return jnp.concatenate([older[:size] * decay + newer[:size], older[size:] * decay], axis=0).astype(bf16)


def far_states(shard, size):
    rank = lax.axis_index("seq")
    levels = lax.axis_size("seq").bit_length() - 1
    states = []
    running = jnp.ones((1, shard.shape[1]), f32)
    for level in range(levels):
        theirs = flip(shard, "seq", 1 << level)
        upper = jnp.right_shift(rank, level) % 2 == 1
        states.append(jnp.where(upper, theirs[:size].astype(f32) * running, 0.0).astype(bf16))
        running = jnp.where(upper, running * theirs[size : size + 1].astype(f32), running)
        shard = merged(jnp.where(upper, theirs, shard), jnp.where(upper, shard, theirs), size)
    return states


def on_device(inputs, gate, input_map, output_map, step, decay_rate, level_mix, skip, norm_gain):
    tokens, width = inputs.shape
    heads = step.shape[0]
    parts = lax.axis_size("head")
    levels = lax.axis_size("seq").bit_length() - 1
    size = input_map.shape[0] * parts
    groups = tokens // GROUP
    spans = local_spans(groups)
    dense = 2 * tokens * GROUP * width
    area = tokens * width
    others = from_each(input_map, "head", far_first_masks(parts))
    kept = inputs, gate, level_mix, skip[None, :], input_map, output_map, norm_gain[None, :]
    beside = flip(output_map, "head", FIRST_HOP)
    scaled, cum, *kept = call(
        prepare_kernel,
        (
            *(shaped((tokens, width), bf16), shaped((heads, tokens), f32)),
            *(shaped(array.shape, array.dtype) for array in kept),
        ),
        (step, decay_rate[None, :], *kept),
        flops=16 * dense,
        bytes_accessed=4 * area,
        hbm=9,
        scratch=[pltpu.VMEM(step.shape, f32), pltpu.VMEM((1, heads), f32), pltpu.SemaphoreType.DMA((9,))],
    )
    inputs, gate, level_mix, skip, input_map, output_map, gain = kept
    in_maps = [input_map, *others]
    pairs = lax.axis_size("seq") == 8 and parts == 4
    sides = 2 if pairs else 1
    shard_shape = shaped((size + DECAY_ROWS, width // sides), bf16)
    span_shape = [shaped((len(spans) * size, width), bf16)] if spans else []
    shard, *rest = call(
        functools.partial(states_kernel, parts, sides),
        (*[shard_shape] * sides, *span_shape),
        (*in_maps, scaled, cum),
        flops=dense,
    )
    span_states = rest[sides - 1 :]
    rows = output_map.shape[0]
    if rows % 16 == 0:
        both = call(
            join_kernel,
            shaped((2 * rows, tokens), bf16),
            (output_map, beside, shard),
            flops=8 * dense,
        )
    else:
        both = jnp.concatenate([output_map, beside], axis=0)
    if pairs:
        theirs = flip(rest[0], "seq", 1)
        message = call(
            functools.partial(merge_kernel, size), shard_shape, (shard, theirs, both), flops=0
        )
        other_theirs = flip(lax.optimization_barrier((shard, message))[0], "seq", 1)
    else:
        other_theirs = theirs = message = shard
    out_maps = [both, *from_each(both, "head", pair_masks(parts))]
    factor_shape = [shaped((len(spans), GROUP, width), bf16)] if spans else []
    base, own_factor, far, *span_factors = call(
        functools.partial(factor_kernel, spans, levels),
        (
            *(shaped((tokens, width), f32), shaped((tokens, width), f32)),
            *(shaped((levels, tokens, width), bf16), *factor_shape),
        ),
        (inputs, gate, level_mix, skip, cum, message),
        flops=5 * dense,
        bytes_accessed=0,
    )
    near_args = base, own_factor, far, theirs, scaled, *span_states, *span_factors
    near_shape = shaped((tokens, width // 2 if pairs else width), f32)
    near, turned, scores = call(
        functools.partial(near_kernel, parts, spans, pairs),
        (near_shape, shaped((tokens, size), bf16), shaped((tokens, GROUP), bf16)),
        (*in_maps, *out_maps, *near_args),
    )
    sums_shape = shaped((1, tokens), f32)
    if pairs:
        received = [flip(message, "seq", 4), flip(message, "seq", 2), lax.ppermute(message, "seq", CYCLE)]
        from_y, from_x, from_cycle = received
        from_y, from_x, near, far = lax.optimization_barrier((from_y, from_x, near, far))
        from_cycle, other_theirs, near = lax.optimization_barrier((from_cycle, other_theirs, near))
        own = call(
            functools.partial(combine_kernel, size),
            shaped((size, width // 2), bf16),
            (from_x, from_y, from_cycle),
            bytes_accessed=area,
        )
        other = flip(own, "seq", 1)
        other_x = flip(from_x, "seq", 1)
        near_args = base, own_factor, far, other_theirs, scaled, *span_states, *span_factors
        other_near = call(
            functools.partial(other_near_kernel, spans), near_shape, (scores, turned, own, *near_args), flops=dense
        )
        gated_shape = shaped((tokens, width // 2), f32)
        own_gated, own_squares = call(
            functools.partial(far_kernel_of_half, True),
            (gated_shape, shaped((tokens, 128), f32)),
            (turned, near, far, gain, theirs, from_x, own),
            flops=2 * dense,
            bytes_accessed=6 * area,
        )
        other_gated, sums = call(
            functools.partial(far_kernel_of_half, False),
            (gated_shape, sums_shape),
            (turned, other_near, far, gain, other_theirs, other_x, other, own_squares),
            flops=2 * dense,
            bytes_accessed=6 * area,
        )
        gated = (own_gated, other_gated)
    else:
        *gated, sums = call(
            far_kernel,
            (shaped((tokens, width), f32), sums_shape),
            (turned, near, far, gain, *far_states(shard, size)),
            flops=4 * dense,
            bytes_accessed=12 * area,
        )
    last = [sums, *around(sums, pairs)]
    return call(
        functools.partial(norm_kernel, len(last), width * parts),
        shaped((tokens, width), bf16),
        (*last, *gated),
        flops=dense,
        bytes_accessed=6 * area,
        scratch=[pltpu.VMEM((tokens, width), bf16), pltpu.SemaphoreType.DMA((NORM_CHUNKS,))],
        out_space=pl.ANY,
    )


def solution(mesh):
    return jax.shard_map(
        on_device,
        mesh=mesh,
        in_specs=(
            P("seq", "head"),
            P("seq", "head"),
            P("head", "seq"),
            P("head", "seq"),
            P("head", "seq"),
            P("head"),
            P(None, "head", "seq"),
            P("head"),
            P("head"),
        ),
        out_specs=P("seq", "head"),
        check_vma=False,
    )
```

```python
import functools

import jax
import jax.numpy as jnp
from jax import lax
from jax.experimental import pallas as pl
from jax.experimental.pallas import tpu as pltpu
from jax.sharding import PartitionSpec as P

P_SIZE = 64
GROUP = 256
DECAY_ROWS = 16
BLOCK = 256
NORM_CHUNKS = 4
FIRST_HOP = 2
LATER_SHIFTS = (2, 1, 3)
CYCLE = [(2 * chip + core, 2 * target + core) for chip, target in ((0, 3), (3, 1), (1, 2), (2, 0)) for core in (0, 1)]
VMEM_LIMIT = 40 * 1024 * 1024

f32, bf16 = jnp.float32, jnp.bfloat16
HIGHEST = lax.Precision.HIGHEST
TRANSPOSED = (((0,), (0,)), ((), ()))


def expander(heads, width, copies):
    row = lax.broadcasted_iota(jnp.int32, (copies * heads, width), 0)
    col = lax.broadcasted_iota(jnp.int32, (copies * heads, width), 1)
    return jnp.where(lax.rem(row, heads) == lax.div(col, P_SIZE), 1.0, 0.0)


def far_first_masks(size):
    return (*range(2, size), 1)


def pair_masks(size):
    return tuple(mask for mask in range(1, size) if not mask & FIRST_HOP)


def two_parts(factor):
    high = factor.astype(bf16).astype(f32)
    return jnp.concatenate([high, factor - high], axis=0).astype(bf16)


def transposed_dot(left, right):
    return lax.dot_general(left, right, TRANSPOSED, preferred_element_type=f32)


def head_row(heads, width, column):
    return jnp.sum(expander(heads, width, 1) * column, axis=0, keepdims=True)


def group_slice(group):
    return slice(group * GROUP, (group + 1) * GROUP)


def blocks_of(width):
    return [slice(at, at + BLOCK) for at in range(0, width, BLOCK)]


def local_spans(groups):
    spans = []
    for later in range(groups):
        for bit in range(groups.bit_length() - 1):
            if later >> bit & 1:
                start = later >> bit + 1 << bit + 1
                spans.append((later, bit, start, start + 2**bit))
    return spans


def column_of(row):
    size = row.shape[1]
    at = lax.broadcasted_iota(jnp.int32, (size, size), 0) == lax.broadcasted_iota(jnp.int32, (size, size), 1)
    return jnp.sum(jnp.where(at, row, 0.0), axis=1, keepdims=True)


def map_rows(maps):
    if all(rows.shape[0] % 16 == 0 for rows in maps):
        return jnp.concatenate([rows[...] for rows in maps], axis=0)
    return jnp.concatenate([rows[...].astype(f32) for rows in maps], axis=0).astype(bf16)


def out_map_rows(map_refs, parts):
    rows = map_refs[0].shape[0] // 2
    pairs = [ref if rows % 16 == 0 else ref[...].astype(f32) for ref in map_refs]
    sent = (0, *pair_masks(parts))
    picked = []
    for mask in (0, *far_first_masks(parts)):
        pair = pairs[sent.index(mask & ~FIRST_HOP)]
        at = slice(rows, 2 * rows) if mask & FIRST_HOP else slice(0, rows)
        picked.append(pair.at[at] if rows % 16 == 0 else pair[at])
    return map_rows(picked)


def fetch(sources, targets, semaphores):
    copies = [
        pltpu.make_async_copy(source, target, semaphores.at[index])
        for index, (source, target) in enumerate(zip(sources, targets))
    ]
    for copy in copies:
        copy.start()
    return copies


def prepare_kernel(*refs):
    sources, (scaled_ref, cum_ref), kept_refs = refs[:9], refs[9:11], refs[11:18]
    step_ref, rate_ref, semaphores = refs[18:]
    inputs_ref = kept_refs[0]
    copies = fetch(sources, (step_ref, rate_ref, *kept_refs), semaphores)
    heads, tokens = step_ref.shape
    width = inputs_ref.shape[1]
    row = lax.broadcasted_iota(jnp.int32, (GROUP, GROUP), 0)
    col = lax.broadcasted_iota(jnp.int32, (GROUP, GROUP), 1)
    until = jnp.where(row <= col, 1.0, 0.0)
    expand = expander(heads, width, 2).astype(bf16)
    copies[0].wait()
    copies[1].wait()
    step = step_ref[...]
    log_decay = -step * column_of(rate_ref[...])
    factors = []
    for group in range(tokens // GROUP):
        at = group_slice(group)
        cum = jnp.dot(log_decay[:, at], until, precision=HIGHEST, preferred_element_type=f32)
        cum_ref[:, at] = cum
        factors.append(two_parts(jnp.exp(-cum) * step[:, at]))
    factor = jnp.concatenate(factors, axis=1)
    copies[2].wait()
    for cols in blocks_of(width):
        scale = transposed_dot(factor, expand[:, cols])
        scaled_ref[:, cols] = (inputs_ref[:, cols].astype(f32) * scale).astype(bf16)
    for copy in copies[3:]:
        copy.wait()


def join_kernel(mine_ref, theirs_ref, _, both_ref):
    rows = mine_ref.shape[0]
    both_ref[:rows, :] = mine_ref[...]
    both_ref[rows:, :] = theirs_ref[...]


def states_kernel(parts, sides, *refs):
    map_refs, (scaled_ref, cum_ref), out_refs = refs[:parts], refs[parts : parts + 2], refs[parts + 2 :]
    shard_refs = out_refs[:sides]
    heads, tokens = cum_ref.shape
    width = scaled_ref.shape[1]
    in_map = map_rows(map_refs)
    size = in_map.shape[0]
    cum = cum_ref[...]
    states, decays = [], []
    for group in range(tokens // GROUP):
        at = group_slice(group)
        decay = head_row(heads, width, jnp.exp(cum[:, at.stop - 1 : at.stop]))
        raw = jnp.dot(in_map[:, at], scaled_ref[at, :], preferred_element_type=f32)
        states.append(raw * decay)
        decays.append(decay)
    total, decay = states[0], decays[0]
    for group in range(1, len(states)):
        total = total * decays[group] + states[group]
        decay = decay * decays[group]
    columns = width // sides
    core = lax.rem(lax.axis_index("seq"), 2)
    for ref, first in zip(shard_refs, (core == 0, core == 1)):
        at = slice(0, columns)
        ref[:size, :] = jnp.where(first, total[:, at], total[:, width - columns :]).astype(bf16)
        row = jnp.where(first, decay[:, at], decay[:, width - columns :])
        ref[size:, :] = jnp.broadcast_to(row, (DECAY_ROWS, columns)).astype(bf16)
    for index, (later, _, start, stop) in enumerate(local_spans(len(states))):
        span = states[start]
        for group in range(start + 1, later):
            span = span * decays[group]
            if group < stop:
                span = span + states[group]
        out_refs[sides][index * size : (index + 1) * size, :] = span.astype(bf16)


def merge_kernel(size, mine_ref, theirs_ref, _, pair_ref):
    core = lax.rem(lax.axis_index("seq"), 2)
    mine, theirs = mine_ref[...], theirs_ref[...]
    older = jnp.where(core == 1, theirs, mine).astype(f32)
    newer = jnp.where(core == 1, mine, theirs).astype(f32)
    decay = newer[size : size + 1]
    pair_ref[:size, :] = (older[:size] * decay + newer[:size]).astype(bf16)
    pair_ref[size:, :] = (older[size:] * decay).astype(bf16)


def factor_kernel(spans, levels, *refs):
    inputs_ref, gate_ref, mix_ref, skip_ref, cum_ref, _ = refs[:6]
    base_ref, own_ref, far_ref = refs[6:9]
    span_refs = refs[9:]
    heads, tokens = cum_ref.shape
    width = inputs_ref.shape[1]
    groups = tokens // GROUP
    first = groups.bit_length()
    expand = expander(heads, width, 2).astype(bf16)
    skip = head_row(heads, width, column_of(skip_ref[...]))
    before = jnp.zeros((heads, 1), f32)
    for group in range(groups):
        at = group_slice(group)
        cum = cum_ref[:, at]
        decay = jnp.exp(cum)
        own_mix = two_parts(mix_ref[0, :, at] * decay)
        span_mixes = [
            (index, two_parts(mix_ref[1 + bit, :, at] * decay))
            for index, (later, bit, _, _) in enumerate(spans)
            if later == group
        ]
        decay = jnp.exp(cum + before)
        before = before + cum[:, GROUP - 1 : GROUP]
        far_mixes = [two_parts(mix_ref[first + level, :, at] * decay) for level in range(levels)]
        for cols in blocks_of(width):
            gate = gate_ref[at, cols].astype(f32)
            swish = gate / (1.0 + jnp.exp(-gate))
            base_ref[at, cols] = skip[:, cols] * inputs_ref[at, cols].astype(f32) * swish
            own_ref[at, cols] = transposed_dot(own_mix, expand[:, cols]) * swish
            for level, mix in enumerate(far_mixes):
                far_ref[level, at, cols] = (transposed_dot(mix, expand[:, cols]) * swish).astype(bf16)
            for index, mix in span_mixes:
                span_refs[0][index, :, cols] = (transposed_dot(mix, expand[:, cols]) * swish).astype(bf16)


def near_body(spans, has_core, start, scores_ref, turned_ref, refs, near_ref):
    base_ref, own_ref, far_ref, core_ref, scaled_ref = refs[:5]
    span_refs = refs[5:]
    tokens, size = turned_ref.shape
    for group in range(tokens // GROUP):
        at = group_slice(group)
        for cols in blocks_of(near_ref.shape[1]):
            of = pl.ds(pl.multiple_of(start + cols.start, BLOCK), BLOCK)
            own = jnp.dot(scores_ref[at, :], scaled_ref[at, of], preferred_element_type=f32)
            total = base_ref[at, of] + own_ref[at, of] * own
            for index, (later, _, _, _) in enumerate(spans):
                if later == group:
                    rows = slice(index * size, (index + 1) * size)
                    reach = jnp.dot(turned_ref[at, :], span_refs[0][rows, of], preferred_element_type=f32)
                    total = total + span_refs[1][index, :, of].astype(f32) * reach
            if has_core:
                reach = jnp.dot(turned_ref[at, :], core_ref[:size, cols], preferred_element_type=f32)
                total = total + far_ref[0, at, of].astype(f32) * reach
            near_ref[at, cols] = total


def near_of_core(spans, own, scores_ref, turned_ref, refs, near_ref):
    core = lax.rem(lax.axis_index("seq"), 2)
    for has_core in (0, 1):

        @pl.when(core == has_core)
        def _():
            start = (has_core if own else 1 - has_core) * near_ref.shape[1]
            near_body(spans, has_core, start, scores_ref, turned_ref, refs, near_ref)


def near_kernel(parts, spans, paired, *refs):
    count = parts + parts // 2
    in_refs, out_refs, rest = refs[:parts], refs[parts:count], refs[count:-3]
    near_ref, turned_ref, scores_ref = refs[-3:]
    in_map = map_rows(in_refs)
    turned = jnp.transpose(out_map_rows(out_refs, parts))
    turned_ref[...] = turned
    row = lax.broadcasted_iota(jnp.int32, (GROUP, GROUP), 0)
    col = lax.broadcasted_iota(jnp.int32, (GROUP, GROUP), 1)
    for group in range(turned.shape[0] // GROUP):
        at = group_slice(group)
        scores = jnp.dot(turned[at], in_map[:, at], preferred_element_type=f32)
        scores_ref[at, :] = jnp.where(row >= col, scores, 0.0).astype(bf16)
    if paired:
        near_of_core(spans, True, scores_ref, turned_ref, rest, near_ref)
    else:
        near_body(spans, False, 0, scores_ref, turned_ref, rest, near_ref)


def other_near_kernel(spans, scores_ref, turned_ref, _, *refs):
    near_of_core(spans, False, scores_ref, turned_ref, refs[:-1], refs[-1])


def far_body(turned_ref, near_ref, far_ref, gain_ref, start, columns, levels, state_of, gated_ref):
    tokens = far_ref.shape[1]
    squares = jnp.zeros((tokens, 128), f32)
    for cols in blocks_of(columns):
        at = pl.ds(pl.multiple_of(start + cols.start, BLOCK), BLOCK)
        total = near_ref[:, cols]
        for level in levels:
            state = state_of(level, cols, at).astype(bf16)
            reach = jnp.dot(turned_ref[...], state, preferred_element_type=f32)
            total = total + far_ref[level, :, at].astype(f32) * reach
        gated_ref[:, cols] = total * gain_ref[:, at]
        total = total * total
        for part in range(0, BLOCK, 128):
            squares = squares + total[:, part : part + 128]
    return squares


def row_sums(squares):
    high = squares.astype(bf16)
    low = (squares - high.astype(f32)).astype(bf16)
    parts = jnp.concatenate([high, low], axis=1)
    ones = jnp.ones((16, parts.shape[1]), bf16)
    return lax.dot_general(ones, parts, (((1,), (1,)), ((), ())), preferred_element_type=f32)[:1]


def far_kernel(turned_ref, near_ref, far_ref, gain_ref, *refs):
    state_refs = refs[:-2]
    gated_ref, sums_ref = refs[-2:]

    def state_of(level, cols, _):
        return state_refs[level][:, cols]

    width = near_ref.shape[1]
    levels = range(far_ref.shape[0])
    squares = far_body(turned_ref, near_ref, far_ref, gain_ref, 0, width, levels, state_of, gated_ref)
    sums_ref[...] = row_sums(squares)


def combine_kernel(size, x_ref, y_ref, diagonal_ref, spans_ref):
    rank = lax.axis_index("seq")
    along_x = lax.rem(lax.div(rank, 2), 2)
    along_y = lax.div(rank, 4)

    def parts_of(ref):
        return ref[:size, :].astype(f32), ref[size:, :].astype(f32)[:1]

    _, x_decay = parts_of(x_ref)
    y_state, y_decay = parts_of(y_ref)
    d_state, d_decay = parts_of(diagonal_ref)
    newer = jnp.where(along_x == 1, y_state, d_state)
    newer_decay = jnp.where(along_x == 1, y_decay, d_decay)
    older = jnp.where(along_x == 1, d_state, y_state)
    running = jnp.where(along_x == 1, x_decay, 1.0)
    running = jnp.where(along_y == 1, running, 0.0)
    spans_ref[...] = ((older * newer_decay + newer) * running).astype(bf16)


def far_kernel_of_half(own, *refs):
    turned_ref, near_ref, far_ref, gain_ref, core_ref, x_ref, span_ref = refs[:7]
    gated_ref, sums_ref = refs[-2:]
    size = turned_ref.shape[1]
    rank = lax.axis_index("seq")
    core = lax.rem(rank, 2)
    along_x = lax.rem(lax.div(rank, 2), 2)
    along_y = lax.div(rank, 4)
    half = span_ref.shape[1]
    start = (core if own else 1 - core) * half

    def state_of(level, cols, at):
        core_decay = core_ref[size:, cols].astype(f32)[:1]
        running = jnp.where(core == 1, core_decay, 1.0)
        if level == 1:
            return x_ref[:size, cols].astype(f32) * running
        return span_ref[:, cols].astype(f32) * running

    for has_x, has_y in ((0, 0), (0, 1), (1, 0), (1, 1)):

        @pl.when((along_x == has_x) & (along_y == has_y))
        def _():
            levels = (1,) * has_x + (2,) * has_y
            squares = far_body(turned_ref, near_ref, far_ref, gain_ref, start, half, levels, state_of, gated_ref)
            sums_ref[...] = squares if own else row_sums(squares + refs[7][...])


def norm_kernel(parts, columns, *refs):
    gated_refs, (out_hbm, out_ref, semaphores) = refs[parts:-3], refs[-3:]
    total = refs[0][...]
    for ref in refs[1:parts]:
        total = total + ref[...]
    scale = lax.rsqrt(total / columns + 1e-05)
    tokens = scale.shape[1]
    scale = jnp.broadcast_to(scale, (8, tokens))
    width = gated_refs[0].shape[1]
    core = lax.rem(lax.axis_index("seq"), 2)
    sides = (core, 1 - core) if len(gated_refs) == 2 else (0,)
    chunk = tokens // NORM_CHUNKS
    copies = []
    for index in range(NORM_CHUNKS):
        rows = slice(index * chunk, (index + 1) * chunk)
        column = jnp.transpose(scale[:, rows])[:, :1]
        for ref, side in zip(gated_refs, sides):
            at = pl.ds(pl.multiple_of(side * width, width), width)
            out_ref[rows, at] = (ref[rows, :] * column).astype(bf16)
        copies.append(pltpu.make_async_copy(out_ref.at[rows], out_hbm.at[rows], semaphores.at[index]))
        copies[-1].start()
    for copy in copies:
        copy.wait()


def call(kernel, out_shape, args, flops=0, bytes_accessed=0, hbm=0, scratch=None, out_space=pltpu.VMEM):
    specs = [pl.BlockSpec(memory_space=pl.ANY)] * hbm + [pl.BlockSpec(memory_space=pltpu.VMEM)] * (len(args) - hbm)
    args = [pltpu.with_memory_space_constraint(arg, pltpu.HBM) for arg in args[:hbm]] + list(args[hbm:])
    if scratch is None:
        scratch = [pltpu.VMEM(arg.shape, arg.dtype) for arg in args[:hbm]]
        scratch += [pltpu.SemaphoreType.DMA((hbm,))] if hbm else []
    return pl.pallas_call(
        kernel,
        out_shape=out_shape,
        in_specs=specs,
        out_specs=jax.tree.map(lambda _: pl.BlockSpec(memory_space=out_space), out_shape),
        scratch_shapes=scratch,
        compiler_params=pltpu.CompilerParams(vmem_limit_bytes=VMEM_LIMIT),
        cost_estimate=pl.CostEstimate(flops=flops, bytes_accessed=bytes_accessed, transcendentals=0),
    )(*args)


def shaped(shape, dtype):
    return jax.ShapeDtypeStruct(shape, dtype)


def flip(array, axis, mask):
    return lax.ppermute(array, axis, [(i, i ^ mask) for i in range(lax.axis_size(axis))])


def from_each(array, axis, masks):
    return [flip(array, axis, mask) for mask in masks]


def around(array, paired):
    shards, size = lax.axis_size("seq"), lax.axis_size("head")
    received = []
    for step in range(1, size):
        pairs = []
        for shard in range(shards):
            shift = LATER_SHIFTS[step - 1] if paired and shard >= shards // 2 else step
            pairs += [(shard * size + i, shard * size + (i + shift) % size) for i in range(size)]
        received.append(lax.ppermute(array, ("seq", "head"), pairs))
    return received


def merged(older, newer, size):
    older, newer = older.astype(f32), newer.astype(f32)
    decay = newer[size : size + 1]
    return jnp.concatenate([older[:size] * decay + newer[:size], older[size:] * decay], axis=0).astype(bf16)


def far_states(shard, size):
    rank = lax.axis_index("seq")
    levels = lax.axis_size("seq").bit_length() - 1
    states = []
    running = jnp.ones((1, shard.shape[1]), f32)
    for level in range(levels):
        theirs = flip(shard, "seq", 1 << level)
        upper = jnp.right_shift(rank, level) % 2 == 1
        states.append(jnp.where(upper, theirs[:size].astype(f32) * running, 0.0).astype(bf16))
        running = jnp.where(upper, running * theirs[size : size + 1].astype(f32), running)
        shard = merged(jnp.where(upper, theirs, shard), jnp.where(upper, shard, theirs), size)
    return states


def on_device(inputs, gate, input_map, output_map, step, decay_rate, level_mix, skip, norm_gain):
    tokens, width = inputs.shape
    heads = step.shape[0]
    parts = lax.axis_size("head")
    levels = lax.axis_size("seq").bit_length() - 1
    size = input_map.shape[0] * parts
    groups = tokens // GROUP
    spans = local_spans(groups)
    dense = 2 * tokens * GROUP * width
    area = tokens * width
    others = from_each(input_map, "head", far_first_masks(parts))
    kept = inputs, gate, level_mix, skip[None, :], input_map, output_map, norm_gain[None, :]
    beside = flip(output_map, "head", FIRST_HOP)
    scaled, cum, *kept = call(
        prepare_kernel,
        (
            *(shaped((tokens, width), bf16), shaped((heads, tokens), f32)),
            *(shaped(array.shape, array.dtype) for array in kept),
        ),
        (step, decay_rate[None, :], *kept),
        flops=16 * dense,
        bytes_accessed=4 * area,
        hbm=9,
        scratch=[pltpu.VMEM(step.shape, f32), pltpu.VMEM((1, heads), f32), pltpu.SemaphoreType.DMA((9,))],
    )
    inputs, gate, level_mix, skip, input_map, output_map, gain = kept
    in_maps = [input_map, *others]
    pairs = lax.axis_size("seq") == 8 and parts == 4
    sides = 2 if pairs else 1
    shard_shape = shaped((size + DECAY_ROWS, width // sides), bf16)
    span_shape = [shaped((len(spans) * size, width), bf16)] if spans else []
    shard, *rest = call(
        functools.partial(states_kernel, parts, sides),
        (*[shard_shape] * sides, *span_shape),
        (*in_maps, scaled, cum),
        flops=dense,
    )
    span_states = rest[sides - 1 :]
    rows = output_map.shape[0]
    if rows % 16 == 0:
        both = call(
            join_kernel,
            shaped((2 * rows, tokens), bf16),
            (output_map, beside, shard),
            flops=8 * dense,
        )
    else:
        both = jnp.concatenate([output_map, beside], axis=0)
    if pairs:
        theirs = flip(rest[0], "seq", 1)
        message = call(
            functools.partial(merge_kernel, size), shard_shape, (shard, theirs, both), flops=0
        )
        other_theirs = flip(lax.optimization_barrier((shard, message))[0], "seq", 1)
    else:
        other_theirs = theirs = message = shard
    out_maps = [both, *from_each(both, "head", pair_masks(parts))]
    factor_shape = [shaped((len(spans), GROUP, width), bf16)] if spans else []
    base, own_factor, far, *span_factors = call(
        functools.partial(factor_kernel, spans, levels),
        (
            *(shaped((tokens, width), f32), shaped((tokens, width), f32)),
            *(shaped((levels, tokens, width), bf16), *factor_shape),
        ),
        (inputs, gate, level_mix, skip, cum, message),
        flops=5 * dense,
        bytes_accessed=0,
    )
    near_args = base, own_factor, far, theirs, scaled, *span_states, *span_factors
    near_shape = shaped((tokens, width // 2 if pairs else width), f32)
    near, turned, scores = call(
        functools.partial(near_kernel, parts, spans, pairs),
        (near_shape, shaped((tokens, size), bf16), shaped((tokens, GROUP), bf16)),
        (*in_maps, *out_maps, *near_args),
    )
    sums_shape = shaped((1, tokens), f32)
    if pairs:
        received = [flip(message, "seq", 4), flip(message, "seq", 2), lax.ppermute(message, "seq", CYCLE)]
        from_y, from_x, from_cycle = received
        from_y, from_x, near, far = lax.optimization_barrier((from_y, from_x, near, far))
        from_cycle, other_theirs, near = lax.optimization_barrier((from_cycle, other_theirs, near))
        own = call(
            functools.partial(combine_kernel, size),
            shaped((size, width // 2), bf16),
            (from_x, from_y, from_cycle),
            bytes_accessed=area,
        )
        other = flip(own, "seq", 1)
        other_x = flip(from_x, "seq", 1)
        near_args = base, own_factor, far, other_theirs, scaled, *span_states, *span_factors
        other_near = call(
            functools.partial(other_near_kernel, spans), near_shape, (scores, turned, own, *near_args), flops=dense
        )
        gated_shape = shaped((tokens, width // 2), f32)
        own_gated, own_squares = call(
            functools.partial(far_kernel_of_half, True),
            (gated_shape, shaped((tokens, 128), f32)),
            (turned, near, far, gain, theirs, from_x, own),
            flops=2 * dense,
            bytes_accessed=6 * area,
        )
        other_gated, sums = call(
            functools.partial(far_kernel_of_half, False),
            (gated_shape, sums_shape),
            (turned, other_near, far, gain, other_theirs, other_x, other, own_squares),
            flops=2 * dense,
            bytes_accessed=6 * area,
        )
        gated = (own_gated, other_gated)
    else:
        *gated, sums = call(
            far_kernel,
            (shaped((tokens, width), f32), sums_shape),
            (turned, near, far, gain, *far_states(shard, size)),
            flops=4 * dense,
            bytes_accessed=12 * area,
        )
    last = [sums, *around(sums, pairs)]
    return call(
        functools.partial(norm_kernel, len(last), width * parts),
        shaped((tokens, width), bf16),
        (*last, *gated),
        flops=dense,
        bytes_accessed=6 * area,
        scratch=[pltpu.VMEM((tokens, width), bf16), pltpu.SemaphoreType.DMA((NORM_CHUNKS,))],
        out_space=pl.ANY,
    )


def solution(mesh):
    return jax.shard_map(
        on_device,
        mesh=mesh,
        in_specs=(
            P("seq", "head"),
            P("seq", "head"),
            P("head", "seq"),
            P("head", "seq"),
            P("head", "seq"),
            P("head"),
            P(None, "head", "seq"),
            P("head"),
            P("head"),
        ),
        out_specs=P("seq", "head"),
        check_vma=False,
    )
```

```python
import functools

import jax
import jax.numpy as jnp
from jax import lax
from jax.experimental import pallas as pl
from jax.experimental.pallas import tpu as pltpu
from jax.sharding import PartitionSpec as P

P_SIZE = 64
GROUP = 256
DECAY_ROWS = 8
BLOCK = 256
NORM_CHUNKS = 4
FIRST_HOP = 2
LATER_SHIFTS = (2, 1, 3)
CYCLE = [(2 * chip + core, 2 * target + core) for chip, target in ((0, 3), (3, 1), (1, 2), (2, 0)) for core in (0, 1)]
VMEM_LIMIT = 40 * 1024 * 1024

f32, bf16 = jnp.float32, jnp.bfloat16
HIGHEST = lax.Precision.HIGHEST
TRANSPOSED = (((0,), (0,)), ((), ()))


def expander(heads, width, copies):
    row = lax.broadcasted_iota(jnp.int32, (copies * heads, width), 0)
    col = lax.broadcasted_iota(jnp.int32, (copies * heads, width), 1)
    return jnp.where(lax.rem(row, heads) == lax.div(col, P_SIZE), 1.0, 0.0)


def far_first_masks(size):
    return (*range(2, size), 1)


def pair_masks(size):
    return tuple(mask for mask in range(1, size) if not mask & FIRST_HOP)


def two_parts(factor):
    high = factor.astype(bf16).astype(f32)
    return jnp.concatenate([high, factor - high], axis=0).astype(bf16)


def transposed_dot(left, right):
    return lax.dot_general(left, right, TRANSPOSED, preferred_element_type=f32)


def head_row(heads, width, column):
    return jnp.sum(expander(heads, width, 1) * column, axis=0, keepdims=True)


def group_slice(group):
    return slice(group * GROUP, (group + 1) * GROUP)


def blocks_of(width):
    return [slice(at, at + BLOCK) for at in range(0, width, BLOCK)]


def local_spans(groups):
    spans = []
    for later in range(groups):
        for bit in range(groups.bit_length() - 1):
            if later >> bit & 1:
                start = later >> bit + 1 << bit + 1
                spans.append((later, bit, start, start + 2**bit))
    return spans


def column_of(row):
    size = row.shape[1]
    at = lax.broadcasted_iota(jnp.int32, (size, size), 0) == lax.broadcasted_iota(jnp.int32, (size, size), 1)
    return jnp.sum(jnp.where(at, row, 0.0), axis=1, keepdims=True)


def map_rows(maps):
    if all(rows.shape[0] % 16 == 0 for rows in maps):
        return jnp.concatenate([rows[...] for rows in maps], axis=0)
    return jnp.concatenate([rows[...].astype(f32) for rows in maps], axis=0).astype(bf16)


def out_map_rows(map_refs, parts):
    rows = map_refs[0].shape[0] // 2
    pairs = [ref if rows % 16 == 0 else ref[...].astype(f32) for ref in map_refs]
    sent = (0, *pair_masks(parts))
    picked = []
    for mask in (0, *far_first_masks(parts)):
        pair = pairs[sent.index(mask & ~FIRST_HOP)]
        at = slice(rows, 2 * rows) if mask & FIRST_HOP else slice(0, rows)
        picked.append(pair.at[at] if rows % 16 == 0 else pair[at])
    return map_rows(picked)


def fetch(sources, targets, semaphores):
    copies = [
        pltpu.make_async_copy(source, target, semaphores.at[index])
        for index, (source, target) in enumerate(zip(sources, targets))
    ]
    for copy in copies:
        copy.start()
    return copies


def prepare_kernel(*refs):
    sources, (scaled_ref, cum_ref), kept_refs = refs[:9], refs[9:11], refs[11:18]
    step_ref, rate_ref, semaphores = refs[18:]
    inputs_ref = kept_refs[0]
    copies = fetch(sources, (step_ref, rate_ref, *kept_refs), semaphores)
    heads, tokens = step_ref.shape
    width = inputs_ref.shape[1]
    row = lax.broadcasted_iota(jnp.int32, (GROUP, GROUP), 0)
    col = lax.broadcasted_iota(jnp.int32, (GROUP, GROUP), 1)
    until = jnp.where(row <= col, 1.0, 0.0)
    expand = expander(heads, width, 2).astype(bf16)
    copies[0].wait()
    copies[1].wait()
    step = step_ref[...]
    log_decay = -step * column_of(rate_ref[...])
    factors = []
    for group in range(tokens // GROUP):
        at = group_slice(group)
        cum = jnp.dot(log_decay[:, at], until, precision=HIGHEST, preferred_element_type=f32)
        cum_ref[:, at] = cum
        factors.append(two_parts(jnp.exp(-cum) * step[:, at]))
    factor = jnp.concatenate(factors, axis=1)
    copies[2].wait()
    for cols in blocks_of(width):
        scale = transposed_dot(factor, expand[:, cols])
        scaled_ref[:, cols] = (inputs_ref[:, cols].astype(f32) * scale).astype(bf16)
    for copy in copies[3:]:
        copy.wait()


def join_kernel(mine_ref, theirs_ref, _, both_ref):
    rows = mine_ref.shape[0]
    both_ref[:rows, :] = mine_ref[...]
    both_ref[rows:, :] = theirs_ref[...]


def states_kernel(parts, sides, *refs):
    map_refs, (scaled_ref, cum_ref), out_refs = refs[:parts], refs[parts : parts + 2], refs[parts + 2 :]
    shard_refs = out_refs[:sides]
    heads, tokens = cum_ref.shape
    width = scaled_ref.shape[1]
    in_map = map_rows(map_refs)
    size = in_map.shape[0]
    cum = cum_ref[...]
    states, decays = [], []
    for group in range(tokens // GROUP):
        at = group_slice(group)
        decay = head_row(heads, width, jnp.exp(cum[:, at.stop - 1 : at.stop]))
        raw = jnp.dot(in_map[:, at], scaled_ref[at, :], preferred_element_type=f32)
        states.append(raw * decay)
        decays.append(decay)
    total, decay = states[0], decays[0]
    for group in range(1, len(states)):
        total = total * decays[group] + states[group]
        decay = decay * decays[group]
    columns = width // sides
    core = lax.rem(lax.axis_index("seq"), 2)
    for ref, first in zip(shard_refs, (core == 0, core == 1)):
        at = slice(0, columns)
        ref[:size, :] = jnp.where(first, total[:, at], total[:, width - columns :]).astype(bf16)
        row = jnp.where(first, decay[:, at], decay[:, width - columns :])
        ref[size:, :] = jnp.broadcast_to(row, (DECAY_ROWS, columns)).astype(bf16)
    for index, (later, _, start, stop) in enumerate(local_spans(len(states))):
        span = states[start]
        for group in range(start + 1, later):
            span = span * decays[group]
            if group < stop:
                span = span + states[group]
        out_refs[sides][index * size : (index + 1) * size, :] = span.astype(bf16)


def merge_kernel(size, mine_ref, theirs_ref, _, pair_ref):
    core = lax.rem(lax.axis_index("seq"), 2)
    mine, theirs = mine_ref[...], theirs_ref[...]
    older = jnp.where(core == 1, theirs, mine).astype(f32)
    newer = jnp.where(core == 1, mine, theirs).astype(f32)
    decay = newer[size : size + 1]
    pair_ref[:size, :] = (older[:size] * decay + newer[:size]).astype(bf16)
    pair_ref[size:, :] = (older[size:] * decay).astype(bf16)


def factor_kernel(spans, levels, *refs):
    inputs_ref, gate_ref, mix_ref, skip_ref, cum_ref, _ = refs[:6]
    base_ref, own_ref, far_ref = refs[6:9]
    span_refs = refs[9:]
    heads, tokens = cum_ref.shape
    width = inputs_ref.shape[1]
    groups = tokens // GROUP
    first = groups.bit_length()
    expand = expander(heads, width, 2).astype(bf16)
    skip = head_row(heads, width, column_of(skip_ref[...]))
    before = jnp.zeros((heads, 1), f32)
    for group in range(groups):
        at = group_slice(group)
        cum = cum_ref[:, at]
        decay = jnp.exp(cum)
        own_mix = two_parts(mix_ref[0, :, at] * decay)
        span_mixes = [
            (index, two_parts(mix_ref[1 + bit, :, at] * decay))
            for index, (later, bit, _, _) in enumerate(spans)
            if later == group
        ]
        decay = jnp.exp(cum + before)
        before = before + cum[:, GROUP - 1 : GROUP]
        far_mixes = [two_parts(mix_ref[first + level, :, at] * decay) for level in range(levels)]
        for cols in blocks_of(width):
            gate = gate_ref[at, cols].astype(f32)
            swish = gate / (1.0 + jnp.exp(-gate))
            base_ref[at, cols] = skip[:, cols] * inputs_ref[at, cols].astype(f32) * swish
            own_ref[at, cols] = transposed_dot(own_mix, expand[:, cols]) * swish
            for level, mix in enumerate(far_mixes):
                far_ref[level, at, cols] = (transposed_dot(mix, expand[:, cols]) * swish).astype(bf16)
            for index, mix in span_mixes:
                span_refs[0][index, :, cols] = (transposed_dot(mix, expand[:, cols]) * swish).astype(bf16)


def near_body(spans, has_core, start, scores_ref, turned_ref, refs, near_ref, x_ref=None):
    base_ref, own_ref, far_ref, core_ref, scaled_ref = refs[:5]
    span_refs = refs[5:]
    tokens, size = turned_ref.shape
    for group in range(tokens // GROUP):
        at = group_slice(group)
        for cols in blocks_of(near_ref.shape[1]):
            of = pl.ds(pl.multiple_of(start + cols.start, BLOCK), BLOCK)
            own = jnp.dot(scores_ref[at, :], scaled_ref[at, of], preferred_element_type=f32)
            total = base_ref[at, of] + own_ref[at, of] * own
            for index, (later, _, _, _) in enumerate(spans):
                if later == group:
                    rows = slice(index * size, (index + 1) * size)
                    reach = jnp.dot(turned_ref[at, :], span_refs[0][rows, of], preferred_element_type=f32)
                    total = total + span_refs[1][index, :, of].astype(f32) * reach
            if has_core:
                reach = jnp.dot(turned_ref[at, :], core_ref[:size, cols], preferred_element_type=f32)
                total = total + far_ref[0, at, of].astype(f32) * reach
            if x_ref is not None:
                state = x_ref[:size, cols]
                if has_core:
                    state = (state.astype(f32) * core_ref[size:, cols].astype(f32)[:1]).astype(bf16)
                reach = jnp.dot(turned_ref[at, :], state, preferred_element_type=f32)
                total = total + far_ref[1, at, of].astype(f32) * reach
            near_ref[at, cols] = total


def near_of_core(spans, scores_ref, turned_ref, refs, near_ref, x_ref=None):
    rank = lax.axis_index("seq")
    core = lax.rem(rank, 2)
    along_x = lax.rem(lax.div(rank, 2), 2)
    for has_core in (0, 1):
        for has_x in (0,) if x_ref is None else (0, 1):

            @pl.when((core == has_core) if x_ref is None else (core == has_core) & (along_x == has_x))
            def _():
                start = (has_core if x_ref is None else 1 - has_core) * near_ref.shape[1]
                x_state = x_ref if has_x else None
                near_body(spans, has_core, start, scores_ref, turned_ref, refs, near_ref, x_state)


def near_kernel(parts, spans, paired, *refs):
    count = parts + parts // 2
    in_refs, out_refs, rest = refs[:parts], refs[parts:count], refs[count:-3]
    near_ref, turned_ref, scores_ref = refs[-3:]
    in_map = map_rows(in_refs)
    turned = jnp.transpose(out_map_rows(out_refs, parts))
    turned_ref[...] = turned
    row = lax.broadcasted_iota(jnp.int32, (GROUP, GROUP), 0)
    col = lax.broadcasted_iota(jnp.int32, (GROUP, GROUP), 1)
    for group in range(turned.shape[0] // GROUP):
        at = group_slice(group)
        scores = jnp.dot(turned[at], in_map[:, at], preferred_element_type=f32)
        scores_ref[at, :] = jnp.where(row >= col, scores, 0.0).astype(bf16)
    if paired:
        near_of_core(spans, scores_ref, turned_ref, rest, near_ref)
    else:
        near_body(spans, False, 0, scores_ref, turned_ref, rest, near_ref)


def other_near_kernel(spans, scores_ref, turned_ref, x_ref, _, *refs):
    near_of_core(spans, scores_ref, turned_ref, refs[:-1], refs[-1], x_ref)


def far_body(turned_ref, near_ref, far_ref, gain_ref, start, columns, levels, state_of, gated_ref):
    tokens = far_ref.shape[1]
    squares = jnp.zeros((tokens, 128), f32)
    for cols in blocks_of(columns):
        at = pl.ds(pl.multiple_of(start + cols.start, BLOCK), BLOCK)
        total = near_ref[:, cols]
        for level in levels:
            state = state_of(level, cols, at).astype(bf16)
            reach = jnp.dot(turned_ref[...], state, preferred_element_type=f32)
            total = total + far_ref[level, :, at].astype(f32) * reach
        gated_ref[:, cols] = total * gain_ref[:, at]
        total = total * total
        for part in range(0, BLOCK, 128):
            squares = squares + total[:, part : part + 128]
    return squares


def row_sums(squares):
    high = squares.astype(bf16)
    low = (squares - high.astype(f32)).astype(bf16)
    parts = jnp.concatenate([high, low], axis=1)
    ones = jnp.ones((16, parts.shape[1]), bf16)
    return lax.dot_general(ones, parts, (((1,), (1,)), ((), ())), preferred_element_type=f32)[:1]


def far_kernel(turned_ref, near_ref, far_ref, gain_ref, *refs):
    state_refs = refs[:-2]
    gated_ref, sums_ref = refs[-2:]

    def state_of(level, cols, _):
        return state_refs[level][:, cols]

    width = near_ref.shape[1]
    levels = range(far_ref.shape[0])
    squares = far_body(turned_ref, near_ref, far_ref, gain_ref, 0, width, levels, state_of, gated_ref)
    sums_ref[...] = row_sums(squares)


def combine_kernel(size, x_ref, y_ref, diagonal_ref, spans_ref):
    rank = lax.axis_index("seq")
    along_x = lax.rem(lax.div(rank, 2), 2)
    along_y = lax.div(rank, 4)

    def parts_of(ref):
        return ref[:size, :].astype(f32), ref[size:, :].astype(f32)[:1]

    _, x_decay = parts_of(x_ref)
    y_state, y_decay = parts_of(y_ref)
    d_state, d_decay = parts_of(diagonal_ref)
    newer = jnp.where(along_x == 1, y_state, d_state)
    newer_decay = jnp.where(along_x == 1, y_decay, d_decay)
    older = jnp.where(along_x == 1, d_state, y_state)
    running = jnp.where(along_x == 1, x_decay, 1.0)
    running = jnp.where(along_y == 1, running, 0.0)
    spans_ref[...] = ((older * newer_decay + newer) * running).astype(bf16)


def far_kernel_of_half(own, *refs):
    turned_ref, near_ref, far_ref, gain_ref, core_ref, x_ref, span_ref = refs[:7]
    gated_ref, sums_ref = refs[-2:]
    size = turned_ref.shape[1]
    rank = lax.axis_index("seq")
    core = lax.rem(rank, 2)
    along_x = lax.rem(lax.div(rank, 2), 2)
    along_y = lax.div(rank, 4)
    half = span_ref.shape[1]
    start = (core if own else 1 - core) * half

    def state_of(level, cols, at):
        core_decay = core_ref[size:, cols].astype(f32)[:1]
        running = jnp.where(core == 1, core_decay, 1.0)
        if level == 1:
            return x_ref[:size, cols].astype(f32) * running
        return span_ref[:, cols].astype(f32) * running

    for has_x, has_y in ((0, 0), (0, 1), (1, 0), (1, 1)):

        @pl.when((along_x == has_x) & (along_y == has_y))
        def _():
            levels = ((1,) * has_x if own else ()) + (2,) * has_y
            squares = far_body(turned_ref, near_ref, far_ref, gain_ref, start, half, levels, state_of, gated_ref)
            sums_ref[...] = squares if own else row_sums(squares + refs[7][...])


def norm_kernel(parts, columns, *refs):
    gated_refs, (out_hbm, out_ref, semaphores) = refs[parts:-3], refs[-3:]
    total = refs[0][...]
    for ref in refs[1:parts]:
        total = total + ref[...]
    scale = lax.rsqrt(total / columns + 1e-05)
    tokens = scale.shape[1]
    scale = jnp.broadcast_to(scale, (8, tokens))
    width = gated_refs[0].shape[1]
    core = lax.rem(lax.axis_index("seq"), 2)
    sides = (core, 1 - core) if len(gated_refs) == 2 else (0,)
    chunk = tokens // NORM_CHUNKS
    copies = []
    for index in range(NORM_CHUNKS):
        rows = slice(index * chunk, (index + 1) * chunk)
        column = jnp.transpose(scale[:, rows])[:, :1]
        for ref, side in zip(gated_refs, sides):
            at = pl.ds(pl.multiple_of(side * width, width), width)
            out_ref[rows, at] = (ref[rows, :] * column).astype(bf16)
        copies.append(pltpu.make_async_copy(out_ref.at[rows], out_hbm.at[rows], semaphores.at[index]))
        copies[-1].start()
    for copy in copies:
        copy.wait()


def call(kernel, out_shape, args, flops=0, bytes_accessed=0, hbm=0, scratch=None, out_space=pltpu.VMEM):
    specs = [pl.BlockSpec(memory_space=pl.ANY)] * hbm + [pl.BlockSpec(memory_space=pltpu.VMEM)] * (len(args) - hbm)
    args = [pltpu.with_memory_space_constraint(arg, pltpu.HBM) for arg in args[:hbm]] + list(args[hbm:])
    if scratch is None:
        scratch = [pltpu.VMEM(arg.shape, arg.dtype) for arg in args[:hbm]]
        scratch += [pltpu.SemaphoreType.DMA((hbm,))] if hbm else []
    return pl.pallas_call(
        kernel,
        out_shape=out_shape,
        in_specs=specs,
        out_specs=jax.tree.map(lambda _: pl.BlockSpec(memory_space=out_space), out_shape),
        scratch_shapes=scratch,
        compiler_params=pltpu.CompilerParams(vmem_limit_bytes=VMEM_LIMIT),
        cost_estimate=pl.CostEstimate(flops=flops, bytes_accessed=bytes_accessed, transcendentals=0),
    )(*args)


def shaped(shape, dtype):
    return jax.ShapeDtypeStruct(shape, dtype)


def flip(array, axis, mask):
    return lax.ppermute(array, axis, [(i, i ^ mask) for i in range(lax.axis_size(axis))])


def from_each(array, axis, masks):
    return [flip(array, axis, mask) for mask in masks]


def around(array, paired):
    shards, size = lax.axis_size("seq"), lax.axis_size("head")
    received = []
    for step in range(1, size):
        pairs = []
        for shard in range(shards):
            shift = LATER_SHIFTS[step - 1] if paired and shard >= shards // 2 else step
            pairs += [(shard * size + i, shard * size + (i + shift) % size) for i in range(size)]
        received.append(lax.ppermute(array, ("seq", "head"), pairs))
    return received


def merged(older, newer, size):
    older, newer = older.astype(f32), newer.astype(f32)
    decay = newer[size : size + 1]
    return jnp.concatenate([older[:size] * decay + newer[:size], older[size:] * decay], axis=0).astype(bf16)


def far_states(shard, size):
    rank = lax.axis_index("seq")
    levels = lax.axis_size("seq").bit_length() - 1
    states = []
    running = jnp.ones((1, shard.shape[1]), f32)
    for level in range(levels):
        theirs = flip(shard, "seq", 1 << level)
        upper = jnp.right_shift(rank, level) % 2 == 1
        states.append(jnp.where(upper, theirs[:size].astype(f32) * running, 0.0).astype(bf16))
        running = jnp.where(upper, running * theirs[size : size + 1].astype(f32), running)
        shard = merged(jnp.where(upper, theirs, shard), jnp.where(upper, shard, theirs), size)
    return states


def on_device(inputs, gate, input_map, output_map, step, decay_rate, level_mix, skip, norm_gain):
    tokens, width = inputs.shape
    heads = step.shape[0]
    parts = lax.axis_size("head")
    levels = lax.axis_size("seq").bit_length() - 1
    size = input_map.shape[0] * parts
    groups = tokens // GROUP
    spans = local_spans(groups)
    dense = 2 * tokens * GROUP * width
    area = tokens * width
    others = from_each(input_map, "head", far_first_masks(parts))
    kept = inputs, gate, level_mix, skip[None, :], input_map, output_map, norm_gain[None, :]
    beside = flip(output_map, "head", FIRST_HOP)
    scaled, cum, *kept = call(
        prepare_kernel,
        (
            *(shaped((tokens, width), bf16), shaped((heads, tokens), f32)),
            *(shaped(array.shape, array.dtype) for array in kept),
        ),
        (step, decay_rate[None, :], *kept),
        flops=16 * dense,
        bytes_accessed=4 * area,
        hbm=9,
        scratch=[pltpu.VMEM(step.shape, f32), pltpu.VMEM((1, heads), f32), pltpu.SemaphoreType.DMA((9,))],
    )
    inputs, gate, level_mix, skip, input_map, output_map, gain = kept
    in_maps = [input_map, *others]
    pairs = lax.axis_size("seq") == 8 and parts == 4
    sides = 2 if pairs else 1
    shard_shape = shaped((size + DECAY_ROWS, width // sides), bf16)
    span_shape = [shaped((len(spans) * size, width), bf16)] if spans else []
    shard, *rest = call(
        functools.partial(states_kernel, parts, sides),
        (*[shard_shape] * sides, *span_shape),
        (*in_maps, scaled, cum),
        flops=dense,
    )
    span_states = rest[sides - 1 :]
    rows = output_map.shape[0]
    if rows % 16 == 0:
        both = call(
            join_kernel,
            shaped((2 * rows, tokens), bf16),
            (output_map, beside, shard),
            flops=8 * dense,
        )
    else:
        both = jnp.concatenate([output_map, beside], axis=0)
    if pairs:
        theirs = flip(rest[0], "seq", 1)
        message = call(
            functools.partial(merge_kernel, size), shard_shape, (shard, theirs, both), flops=0
        )
        other_theirs = flip(lax.optimization_barrier((shard, message))[0], "seq", 1)
    else:
        other_theirs = theirs = message = shard
    out_maps = [both, *from_each(both, "head", pair_masks(parts))]
    factor_shape = [shaped((len(spans), GROUP, width), bf16)] if spans else []
    base, own_factor, far, *span_factors = call(
        functools.partial(factor_kernel, spans, levels),
        (
            *(shaped((tokens, width), f32), shaped((tokens, width), f32)),
            *(shaped((levels, tokens, width), bf16), *factor_shape),
        ),
        (inputs, gate, level_mix, skip, cum, message),
        flops=5 * dense,
        bytes_accessed=0,
    )
    near_args = base, own_factor, far, theirs, scaled, *span_states, *span_factors
    near_shape = shaped((tokens, width // 2 if pairs else width), f32)
    near, turned, scores = call(
        functools.partial(near_kernel, parts, spans, pairs),
        (near_shape, shaped((tokens, size), bf16), shaped((tokens, GROUP), bf16)),
        (*in_maps, *out_maps, *near_args),
    )
    sums_shape = shaped((1, tokens), f32)
    if pairs:
        received = [flip(message, "seq", 4), flip(message, "seq", 2), lax.ppermute(message, "seq", CYCLE)]
        from_y, from_x, from_cycle = received
        from_y, from_x, near, far = lax.optimization_barrier((from_y, from_x, near, far))
        from_cycle, other_theirs, near = lax.optimization_barrier((from_cycle, other_theirs, near))
        own = call(
            functools.partial(combine_kernel, size),
            shaped((size, width // 2), bf16),
            (from_x, from_y, from_cycle),
            bytes_accessed=area,
        )
        other = flip(own, "seq", 1)
        other_x = flip(from_x, "seq", 1)
        gated_shape = shaped((tokens, width // 2), f32)
        own_gated, own_squares = call(
            functools.partial(far_kernel_of_half, True),
            (gated_shape, shaped((tokens, 128), f32)),
            (turned, near, far, gain, theirs, from_x, own),
            flops=2 * dense,
            bytes_accessed=6 * area,
        )
        near_args = base, own_factor, far, other_theirs, scaled, *span_states, *span_factors
        other_near = call(
            functools.partial(other_near_kernel, spans), near_shape, (scores, turned, other_x, own_squares, *near_args), flops=dense
        )
        other_gated, sums = call(
            functools.partial(far_kernel_of_half, False),
            (gated_shape, sums_shape),
            (turned, other_near, far, gain, other_theirs, other_x, other, own_squares),
            flops=2 * dense,
            bytes_accessed=6 * area,
        )
        gated = (own_gated, other_gated)
    else:
        *gated, sums = call(
            far_kernel,
            (shaped((tokens, width), f32), sums_shape),
            (turned, near, far, gain, *far_states(shard, size)),
            flops=4 * dense,
            bytes_accessed=12 * area,
        )
    last = [sums, *around(sums, pairs)]
    return call(
        functools.partial(norm_kernel, len(last), width * parts),
        shaped((tokens, width), bf16),
        (*last, *gated),
        flops=dense,
        bytes_accessed=6 * area,
        scratch=[pltpu.VMEM((tokens, width), bf16), pltpu.SemaphoreType.DMA((NORM_CHUNKS,))],
        out_space=pl.ANY,
    )


def solution(mesh):
    return jax.shard_map(
        on_device,
        mesh=mesh,
        in_specs=(
            P("seq", "head"),
            P("seq", "head"),
            P("head", "seq"),
            P("head", "seq"),
            P("head", "seq"),
            P("head"),
            P(None, "head", "seq"),
            P("head"),
            P("head"),
        ),
        out_specs=P("seq", "head"),
        check_vma=False,
    )
```

```python
import functools

import jax
import jax.numpy as jnp
from jax import lax
from jax.experimental import pallas as pl
from jax.experimental.pallas import tpu as pltpu
from jax.sharding import PartitionSpec as P

P_SIZE = 64
GROUP = 256
DECAY_ROWS = 8
BLOCK = 256
NORM_CHUNKS = 4
FIRST_HOP = 2
LATER_SHIFTS = (2, 1, 3)
CYCLE = [(2 * chip + core, 2 * target + core) for chip, target in ((0, 3), (3, 1), (1, 2), (2, 0)) for core in (0, 1)]
VMEM_LIMIT = 40 * 1024 * 1024

f32, bf16 = jnp.float32, jnp.bfloat16
HIGHEST = lax.Precision.HIGHEST
TRANSPOSED = (((0,), (0,)), ((), ()))


def expander(heads, width, copies):
    row = lax.broadcasted_iota(jnp.int32, (copies * heads, width), 0)
    col = lax.broadcasted_iota(jnp.int32, (copies * heads, width), 1)
    return jnp.where(lax.rem(row, heads) == lax.div(col, P_SIZE), 1.0, 0.0)


def far_first_masks(size):
    return (*range(2, size), 1)


def pair_masks(size):
    return tuple(mask for mask in range(1, size) if not mask & FIRST_HOP)


def two_parts(factor):
    high = factor.astype(bf16).astype(f32)
    return jnp.concatenate([high, factor - high], axis=0).astype(bf16)


def transposed_dot(left, right):
    return lax.dot_general(left, right, TRANSPOSED, preferred_element_type=f32)


def head_row(heads, width, column):
    return jnp.sum(expander(heads, width, 1) * column, axis=0, keepdims=True)


def group_slice(group):
    return slice(group * GROUP, (group + 1) * GROUP)


def blocks_of(width):
    return [slice(at, at + BLOCK) for at in range(0, width, BLOCK)]


def local_spans(groups):
    spans = []
    for later in range(groups):
        for bit in range(groups.bit_length() - 1):
            if later >> bit & 1:
                start = later >> bit + 1 << bit + 1
                spans.append((later, bit, start, start + 2**bit))
    return spans


def column_of(row):
    size = row.shape[1]
    at = lax.broadcasted_iota(jnp.int32, (size, size), 0) == lax.broadcasted_iota(jnp.int32, (size, size), 1)
    return jnp.sum(jnp.where(at, row, 0.0), axis=1, keepdims=True)


def map_rows(maps):
    if all(rows.shape[0] % 16 == 0 for rows in maps):
        return jnp.concatenate([rows[...] for rows in maps], axis=0)
    return jnp.concatenate([rows[...].astype(f32) for rows in maps], axis=0).astype(bf16)


def out_map_rows(map_refs, parts):
    rows = map_refs[0].shape[0] // 2
    pairs = [ref if rows % 16 == 0 else ref[...].astype(f32) for ref in map_refs]
    sent = (0, *pair_masks(parts))
    picked = []
    for mask in (0, *far_first_masks(parts)):
        pair = pairs[sent.index(mask & ~FIRST_HOP)]
        at = slice(rows, 2 * rows) if mask & FIRST_HOP else slice(0, rows)
        picked.append(pair.at[at] if rows % 16 == 0 else pair[at])
    return map_rows(picked)


def fetch(sources, targets, semaphores):
    copies = [
        pltpu.make_async_copy(source, target, semaphores.at[index])
        for index, (source, target) in enumerate(zip(sources, targets))
    ]
    for copy in copies:
        copy.start()
    return copies


def prepare_kernel(*refs):
    sources, (scaled_ref, cum_ref), kept_refs = refs[:9], refs[9:11], refs[11:18]
    step_ref, rate_ref, semaphores = refs[18:]
    inputs_ref = kept_refs[0]
    copies = fetch(sources, (step_ref, rate_ref, *kept_refs), semaphores)
    heads, tokens = step_ref.shape
    width = inputs_ref.shape[1]
    row = lax.broadcasted_iota(jnp.int32, (GROUP, GROUP), 0)
    col = lax.broadcasted_iota(jnp.int32, (GROUP, GROUP), 1)
    until = jnp.where(row <= col, 1.0, 0.0)
    expand = expander(heads, width, 2).astype(bf16)
    copies[0].wait()
    copies[1].wait()
    step = step_ref[...]
    log_decay = -step * column_of(rate_ref[...])
    factors = []
    for group in range(tokens // GROUP):
        at = group_slice(group)
        cum = jnp.dot(log_decay[:, at], until, precision=HIGHEST, preferred_element_type=f32)
        cum_ref[:, at] = cum
        factors.append(two_parts(jnp.exp(-cum) * step[:, at]))
    factor = jnp.concatenate(factors, axis=1)
    copies[2].wait()
    for cols in blocks_of(width):
        scale = transposed_dot(factor, expand[:, cols])
        scaled_ref[:, cols] = (inputs_ref[:, cols].astype(f32) * scale).astype(bf16)
    for copy in copies[3:]:
        copy.wait()


def join_kernel(mine_ref, theirs_ref, _, both_ref):
    rows = mine_ref.shape[0]
    both_ref[:rows, :] = mine_ref[...]
    both_ref[rows:, :] = theirs_ref[...]


def states_kernel(parts, sides, *refs):
    map_refs, (scaled_ref, cum_ref), out_refs = refs[:parts], refs[parts : parts + 2], refs[parts + 2 :]
    shard_refs = out_refs[:sides]
    heads, tokens = cum_ref.shape
    width = scaled_ref.shape[1]
    in_map = map_rows(map_refs)
    size = in_map.shape[0]
    cum = cum_ref[...]
    states, decays = [], []
    for group in range(tokens // GROUP):
        at = group_slice(group)
        decay = head_row(heads, width, jnp.exp(cum[:, at.stop - 1 : at.stop]))
        raw = jnp.dot(in_map[:, at], scaled_ref[at, :], preferred_element_type=f32)
        states.append(raw * decay)
        decays.append(decay)
    total, decay = states[0], decays[0]
    for group in range(1, len(states)):
        total = total * decays[group] + states[group]
        decay = decay * decays[group]
    columns = width // sides
    core = lax.rem(lax.axis_index("seq"), 2)
    for ref, first in zip(shard_refs, (core == 0, core == 1)):
        at = slice(0, columns)
        ref[:size, :] = jnp.where(first, total[:, at], total[:, width - columns :]).astype(bf16)
        row = jnp.where(first, decay[:, at], decay[:, width - columns :])
        ref[size:, :] = jnp.broadcast_to(row, (DECAY_ROWS, columns)).astype(bf16)
    for index, (later, _, start, stop) in enumerate(local_spans(len(states))):
        span = states[start]
        for group in range(start + 1, later):
            span = span * decays[group]
            if group < stop:
                span = span + states[group]
        out_refs[sides][index * size : (index + 1) * size, :] = span.astype(bf16)


def merge_kernel(size, mine_ref, theirs_ref, _, pair_ref):
    core = lax.rem(lax.axis_index("seq"), 2)
    mine, theirs = mine_ref[...], theirs_ref[...]
    older = jnp.where(core == 1, theirs, mine).astype(f32)
    newer = jnp.where(core == 1, mine, theirs).astype(f32)
    decay = newer[size : size + 1]
    pair_ref[:size, :] = (older[:size] * decay + newer[:size]).astype(bf16)
    pair_ref[size:, :] = (older[size:] * decay).astype(bf16)


def factor_kernel(spans, levels, *refs):
    inputs_ref, gate_ref, mix_ref, skip_ref, cum_ref, _ = refs[:6]
    base_ref, own_ref, far_ref = refs[6:9]
    span_refs = refs[9:]
    heads, tokens = cum_ref.shape
    width = inputs_ref.shape[1]
    groups = tokens // GROUP
    first = groups.bit_length()
    expand = expander(heads, width, 2).astype(bf16)
    skip = head_row(heads, width, column_of(skip_ref[...]))
    before = jnp.zeros((heads, 1), f32)
    for group in range(groups):
        at = group_slice(group)
        cum = cum_ref[:, at]
        decay = jnp.exp(cum)
        own_mix = two_parts(mix_ref[0, :, at] * decay)
        span_mixes = [
            (index, two_parts(mix_ref[1 + bit, :, at] * decay))
            for index, (later, bit, _, _) in enumerate(spans)
            if later == group
        ]
        decay = jnp.exp(cum + before)
        before = before + cum[:, GROUP - 1 : GROUP]
        far_mixes = [two_parts(mix_ref[first + level, :, at] * decay) for level in range(levels)]
        for cols in blocks_of(width):
            gate = gate_ref[at, cols].astype(f32)
            swish = gate / (1.0 + jnp.exp(-gate))
            base_ref[at, cols] = skip[:, cols] * inputs_ref[at, cols].astype(f32) * swish
            own_ref[at, cols] = transposed_dot(own_mix, expand[:, cols]) * swish
            for level, mix in enumerate(far_mixes):
                far_ref[level, at, cols] = (transposed_dot(mix, expand[:, cols]) * swish).astype(bf16)
            for index, mix in span_mixes:
                span_refs[0][index, :, cols] = (transposed_dot(mix, expand[:, cols]) * swish).astype(bf16)


def near_body(spans, has_core, start, scores_ref, turned_ref, refs, near_ref, x_ref=None):
    base_ref, own_ref, far_ref, core_ref, scaled_ref = refs[:5]
    span_refs = refs[5:]
    tokens, size = turned_ref.shape
    for group in range(tokens // GROUP):
        at = group_slice(group)
        for cols in blocks_of(near_ref.shape[1]):
            of = pl.ds(pl.multiple_of(start + cols.start, BLOCK), BLOCK)
            own = jnp.dot(scores_ref[at, :], scaled_ref[at, of], preferred_element_type=f32)
            total = base_ref[at, of] + own_ref[at, of] * own
            for index, (later, _, _, _) in enumerate(spans):
                if later == group:
                    rows = slice(index * size, (index + 1) * size)
                    reach = jnp.dot(turned_ref[at, :], span_refs[0][rows, of], preferred_element_type=f32)
                    total = total + span_refs[1][index, :, of].astype(f32) * reach
            if has_core:
                reach = jnp.dot(turned_ref[at, :], core_ref[:size, cols], preferred_element_type=f32)
                total = total + far_ref[0, at, of].astype(f32) * reach
            if x_ref is not None:
                state = x_ref[:size, cols]
                if has_core:
                    state = (state.astype(f32) * core_ref[size:, cols].astype(f32)[:1]).astype(bf16)
                reach = jnp.dot(turned_ref[at, :], state, preferred_element_type=f32)
                total = total + far_ref[1, at, of].astype(f32) * reach
            near_ref[at, cols] = total


def near_of_core(spans, scores_ref, turned_ref, refs, near_ref, x_ref=None):
    rank = lax.axis_index("seq")
    core = lax.rem(rank, 2)
    along_x = lax.rem(lax.div(rank, 2), 2)
    for has_core in (0, 1):
        for has_x in (0,) if x_ref is None else (0, 1):

            @pl.when((core == has_core) if x_ref is None else (core == has_core) & (along_x == has_x))
            def _():
                start = (has_core if x_ref is None else 1 - has_core) * near_ref.shape[1]
                x_state = x_ref if has_x else None
                near_body(spans, has_core, start, scores_ref, turned_ref, refs, near_ref, x_state)


def near_kernel(parts, spans, paired, *refs):
    count = parts + parts // 2
    in_refs, out_refs, rest = refs[:parts], refs[parts:count], refs[count:-3]
    near_ref, turned_ref, scores_ref = refs[-3:]
    in_map = map_rows(in_refs)
    turned = jnp.transpose(out_map_rows(out_refs, parts))
    turned_ref[...] = turned
    row = lax.broadcasted_iota(jnp.int32, (GROUP, GROUP), 0)
    col = lax.broadcasted_iota(jnp.int32, (GROUP, GROUP), 1)
    for group in range(turned.shape[0] // GROUP):
        at = group_slice(group)
        scores = jnp.dot(turned[at], in_map[:, at], preferred_element_type=f32)
        scores_ref[at, :] = jnp.where(row >= col, scores, 0.0).astype(bf16)
    if paired:
        near_of_core(spans, scores_ref, turned_ref, rest, near_ref)
    else:
        near_body(spans, False, 0, scores_ref, turned_ref, rest, near_ref)


def other_near_kernel(spans, scores_ref, turned_ref, x_ref, _, *refs):
    near_of_core(spans, scores_ref, turned_ref, refs[:-1], refs[-1], x_ref)


def far_body(turned_ref, near_ref, far_ref, gain_ref, start, columns, levels, state_of, gated_ref):
    tokens = far_ref.shape[1]
    squares = jnp.zeros((tokens, 128), f32)
    for cols in blocks_of(columns):
        at = pl.ds(pl.multiple_of(start + cols.start, BLOCK), BLOCK)
        total = near_ref[:, cols]
        for level in levels:
            state = state_of(level, cols, at).astype(bf16)
            reach = jnp.dot(turned_ref[...], state, preferred_element_type=f32)
            total = total + far_ref[level, :, at].astype(f32) * reach
        gated_ref[:, cols] = total * gain_ref[:, at]
        total = total * total
        for part in range(0, BLOCK, 128):
            squares = squares + total[:, part : part + 128]
    return squares


def row_sums(squares):
    high = squares.astype(bf16)
    low = (squares - high.astype(f32)).astype(bf16)
    parts = jnp.concatenate([high, low], axis=1)
    ones = jnp.ones((16, parts.shape[1]), bf16)
    return lax.dot_general(ones, parts, (((1,), (1,)), ((), ())), preferred_element_type=f32)[:1]


def far_kernel(turned_ref, near_ref, far_ref, gain_ref, *refs):
    state_refs = refs[:-2]
    gated_ref, sums_ref = refs[-2:]

    def state_of(level, cols, _):
        return state_refs[level][:, cols]

    width = near_ref.shape[1]
    levels = range(far_ref.shape[0])
    squares = far_body(turned_ref, near_ref, far_ref, gain_ref, 0, width, levels, state_of, gated_ref)
    sums_ref[...] = row_sums(squares)


def combine_kernel(size, x_ref, y_ref, diagonal_ref, spans_ref):
    rank = lax.axis_index("seq")
    along_x = lax.rem(lax.div(rank, 2), 2)
    along_y = lax.div(rank, 4)

    def parts_of(ref):
        return ref[:size, :].astype(f32), ref[size:, :].astype(f32)[:1]

    _, x_decay = parts_of(x_ref)
    y_state, y_decay = parts_of(y_ref)
    d_state, d_decay = parts_of(diagonal_ref)
    newer = jnp.where(along_x == 1, y_state, d_state)
    newer_decay = jnp.where(along_x == 1, y_decay, d_decay)
    older = jnp.where(along_x == 1, d_state, y_state)
    running = jnp.where(along_x == 1, x_decay, 1.0)
    running = jnp.where(along_y == 1, running, 0.0)
    spans_ref[...] = ((older * newer_decay + newer) * running).astype(bf16)


def far_kernel_of_half(own, *refs):
    turned_ref, near_ref, far_ref, gain_ref, core_ref, x_ref, span_ref = refs[:7]
    gated_ref, sums_ref = refs[-2:]
    size = turned_ref.shape[1]
    rank = lax.axis_index("seq")
    core = lax.rem(rank, 2)
    along_x = lax.rem(lax.div(rank, 2), 2)
    along_y = lax.div(rank, 4)
    half = span_ref.shape[1]
    start = (core if own else 1 - core) * half

    def state_of(level, cols, at):
        core_decay = core_ref[size:, cols].astype(f32)[:1]
        running = jnp.where(core == 1, core_decay, 1.0)
        if level == 1:
            return x_ref[:size, cols].astype(f32) * running
        return span_ref[:, cols].astype(f32) * running

    for has_x, has_y in ((0, 0), (0, 1), (1, 0), (1, 1)):

        @pl.when((along_x == has_x) & (along_y == has_y))
        def _():
            levels = ((1,) * has_x if own else ()) + (2,) * has_y
            squares = far_body(turned_ref, near_ref, far_ref, gain_ref, start, half, levels, state_of, gated_ref)
            sums_ref[...] = squares if own else row_sums(squares + refs[7][...])


def norm_kernel(parts, columns, *refs):
    gated_refs, (out_hbm, out_ref, semaphores) = refs[parts:-3], refs[-3:]
    total = refs[0][...]
    for ref in refs[1:parts]:
        total = total + ref[...]
    scale = lax.rsqrt(total / columns + 1e-05)
    tokens = scale.shape[1]
    scale = jnp.broadcast_to(scale, (8, tokens))
    width = gated_refs[0].shape[1]
    core = lax.rem(lax.axis_index("seq"), 2)
    sides = (core, 1 - core) if len(gated_refs) == 2 else (0,)
    chunk = tokens // NORM_CHUNKS
    copies = []
    for index in range(NORM_CHUNKS):
        rows = slice(index * chunk, (index + 1) * chunk)
        column = jnp.transpose(scale[:, rows])[:, :1]
        for ref, side in zip(gated_refs, sides):
            at = pl.ds(pl.multiple_of(side * width, width), width)
            out_ref[rows, at] = (ref[rows, :] * column).astype(bf16)
        copies.append(pltpu.make_async_copy(out_ref.at[rows], out_hbm.at[rows], semaphores.at[index]))
        copies[-1].start()
    for copy in copies:
        copy.wait()


def call(kernel, out_shape, args, flops=0, bytes_accessed=0, hbm=0, scratch=None, out_space=pltpu.VMEM):
    specs = [pl.BlockSpec(memory_space=pl.ANY)] * hbm + [pl.BlockSpec(memory_space=pltpu.VMEM)] * (len(args) - hbm)
    args = [pltpu.with_memory_space_constraint(arg, pltpu.HBM) for arg in args[:hbm]] + list(args[hbm:])
    if scratch is None:
        scratch = [pltpu.VMEM(arg.shape, arg.dtype) for arg in args[:hbm]]
        scratch += [pltpu.SemaphoreType.DMA((hbm,))] if hbm else []
    return pl.pallas_call(
        kernel,
        out_shape=out_shape,
        in_specs=specs,
        out_specs=jax.tree.map(lambda _: pl.BlockSpec(memory_space=out_space), out_shape),
        scratch_shapes=scratch,
        compiler_params=pltpu.CompilerParams(vmem_limit_bytes=VMEM_LIMIT),
        cost_estimate=pl.CostEstimate(flops=flops, bytes_accessed=bytes_accessed, transcendentals=0),
    )(*args)


def shaped(shape, dtype):
    return jax.ShapeDtypeStruct(shape, dtype)


def flip(array, axis, mask):
    return lax.ppermute(array, axis, [(i, i ^ mask) for i in range(lax.axis_size(axis))])


def from_each(array, axis, masks):
    return [flip(array, axis, mask) for mask in masks]


def around(array, paired):
    shards, size = lax.axis_size("seq"), lax.axis_size("head")
    received = []
    for step in range(1, size):
        pairs = []
        for shard in range(shards):
            shift = LATER_SHIFTS[step - 1] if paired and shard >= shards // 2 else step
            pairs += [(shard * size + i, shard * size + (i + shift) % size) for i in range(size)]
        received.append(lax.ppermute(array, ("seq", "head"), pairs))
    return received


def merged(older, newer, size):
    older, newer = older.astype(f32), newer.astype(f32)
    decay = newer[size : size + 1]
    return jnp.concatenate([older[:size] * decay + newer[:size], older[size:] * decay], axis=0).astype(bf16)


def far_states(shard, size):
    rank = lax.axis_index("seq")
    levels = lax.axis_size("seq").bit_length() - 1
    states = []
    running = jnp.ones((1, shard.shape[1]), f32)
    for level in range(levels):
        theirs = flip(shard, "seq", 1 << level)
        upper = jnp.right_shift(rank, level) % 2 == 1
        states.append(jnp.where(upper, theirs[:size].astype(f32) * running, 0.0).astype(bf16))
        running = jnp.where(upper, running * theirs[size : size + 1].astype(f32), running)
        shard = merged(jnp.where(upper, theirs, shard), jnp.where(upper, shard, theirs), size)
    return states


def on_device(inputs, gate, input_map, output_map, step, decay_rate, level_mix, skip, norm_gain):
    tokens, width = inputs.shape
    heads = step.shape[0]
    parts = lax.axis_size("head")
    levels = lax.axis_size("seq").bit_length() - 1
    size = input_map.shape[0] * parts
    groups = tokens // GROUP
    spans = local_spans(groups)
    dense = 2 * tokens * GROUP * width
    area = tokens * width
    others = from_each(input_map, "head", far_first_masks(parts))
    kept = inputs, gate, level_mix, skip[None, :], input_map, output_map, norm_gain[None, :]
    beside = flip(output_map, "head", FIRST_HOP)
    scaled, cum, *kept = call(
        prepare_kernel,
        (
            *(shaped((tokens, width), bf16), shaped((heads, tokens), f32)),
            *(shaped(array.shape, array.dtype) for array in kept),
        ),
        (step, decay_rate[None, :], *kept),
        flops=16 * dense,
        bytes_accessed=4 * area,
        hbm=9,
        scratch=[pltpu.VMEM(step.shape, f32), pltpu.VMEM((1, heads), f32), pltpu.SemaphoreType.DMA((9,))],
    )
    inputs, gate, level_mix, skip, input_map, output_map, gain = kept
    in_maps = [input_map, *others]
    pairs = lax.axis_size("seq") == 8 and parts == 4
    sides = 2 if pairs else 1
    shard_shape = shaped((size + DECAY_ROWS, width // sides), bf16)
    span_shape = [shaped((len(spans) * size, width), bf16)] if spans else []
    shard, *rest = call(
        functools.partial(states_kernel, parts, sides),
        (*[shard_shape] * sides, *span_shape),
        (*in_maps, scaled, cum),
        flops=dense,
    )
    span_states = rest[sides - 1 :]
    rows = output_map.shape[0]
    if rows % 16 == 0:
        both = call(
            join_kernel,
            shaped((2 * rows, tokens), bf16),
            (output_map, beside, shard),
            flops=8 * dense,
        )
    else:
        both = jnp.concatenate([output_map, beside], axis=0)
    if pairs:
        theirs = flip(rest[0], "seq", 1)
        message = call(
            functools.partial(merge_kernel, size), shard_shape, (shard, theirs, both), flops=0
        )
        other_theirs = flip(lax.optimization_barrier((shard, message))[0], "seq", 1)
    else:
        other_theirs = theirs = message = shard
    out_maps = [both, *from_each(both, "head", pair_masks(parts))]
    factor_shape = [shaped((len(spans), GROUP, width), bf16)] if spans else []
    base, own_factor, far, *span_factors = call(
        functools.partial(factor_kernel, spans, levels),
        (
            *(shaped((tokens, width), f32), shaped((tokens, width), f32)),
            *(shaped((levels, tokens, width), bf16), *factor_shape),
        ),
        (inputs, gate, level_mix, skip, cum, message),
        flops=5 * dense,
        bytes_accessed=0,
    )
    near_args = base, own_factor, far, theirs, scaled, *span_states, *span_factors
    near_shape = shaped((tokens, width // 2 if pairs else width), f32)
    near, turned, scores = call(
        functools.partial(near_kernel, parts, spans, pairs),
        (near_shape, shaped((tokens, size), bf16), shaped((tokens, GROUP), bf16)),
        (*in_maps, *out_maps, *near_args),
    )
    sums_shape = shaped((1, tokens), f32)
    if pairs:
        received = [flip(message, "seq", 4), flip(message, "seq", 2), lax.ppermute(message, "seq", CYCLE)]
        from_y, from_x, from_cycle = received
        from_y, from_x, near, far = lax.optimization_barrier((from_y, from_x, near, far))
        from_cycle, near = lax.optimization_barrier((from_cycle, near))
        from_cycle, other_theirs = lax.optimization_barrier((from_cycle, other_theirs))
        own = call(
            functools.partial(combine_kernel, size),
            shaped((size, width // 2), bf16),
            (from_x, from_y, from_cycle),
            bytes_accessed=area,
        )
        other = flip(own, "seq", 1)
        other_x = flip(from_x, "seq", 1)
        gated_shape = shaped((tokens, width // 2), f32)
        own_gated, own_squares = call(
            functools.partial(far_kernel_of_half, True),
            (gated_shape, shaped((tokens, 128), f32)),
            (turned, near, far, gain, theirs, from_x, own),
            flops=2 * dense,
            bytes_accessed=6 * area,
        )
        near_args = base, own_factor, far, other_theirs, scaled, *span_states, *span_factors
        other_near = call(
            functools.partial(other_near_kernel, spans), near_shape, (scores, turned, other_x, own_squares, *near_args), flops=0
        )
        other_gated, sums = call(
            functools.partial(far_kernel_of_half, False),
            (gated_shape, sums_shape),
            (turned, other_near, far, gain, other_theirs, other_x, other, own_squares),
            flops=2 * dense,
            bytes_accessed=6 * area,
        )
        gated = (own_gated, other_gated)
    else:
        *gated, sums = call(
            far_kernel,
            (shaped((tokens, width), f32), sums_shape),
            (turned, near, far, gain, *far_states(shard, size)),
            flops=4 * dense,
            bytes_accessed=12 * area,
        )
    last = [sums, *around(sums, pairs)]
    return call(
        functools.partial(norm_kernel, len(last), width * parts),
        shaped((tokens, width), bf16),
        (*last, *gated),
        flops=dense,
        bytes_accessed=6 * area,
        scratch=[pltpu.VMEM((tokens, width), bf16), pltpu.SemaphoreType.DMA((NORM_CHUNKS,))],
        out_space=pl.ANY,
    )


def solution(mesh):
    return jax.shard_map(
        on_device,
        mesh=mesh,
        in_specs=(
            P("seq", "head"),
            P("seq", "head"),
            P("head", "seq"),
            P("head", "seq"),
            P("head", "seq"),
            P("head"),
            P(None, "head", "seq"),
            P("head"),
            P("head"),
        ),
        out_specs=P("seq", "head"),
        check_vma=False,
    )
```

```python
import functools

import jax
import jax.numpy as jnp
from jax import lax
from jax.experimental import pallas as pl
from jax.experimental.pallas import tpu as pltpu
from jax.sharding import PartitionSpec as P

P_SIZE = 64
GROUP = 256
DECAY_ROWS = 8
BLOCK = 256
NORM_CHUNKS = 8
FIRST_HOP = 2
LATER_SHIFTS = (2, 1, 3)
CYCLE = [(2 * chip + core, 2 * target + core) for chip, target in ((0, 3), (3, 1), (1, 2), (2, 0)) for core in (0, 1)]
VMEM_LIMIT = 40 * 1024 * 1024

f32, bf16 = jnp.float32, jnp.bfloat16
HIGHEST = lax.Precision.HIGHEST
TRANSPOSED = (((0,), (0,)), ((), ()))


def expander(heads, width, copies):
    row = lax.broadcasted_iota(jnp.int32, (copies * heads, width), 0)
    col = lax.broadcasted_iota(jnp.int32, (copies * heads, width), 1)
    return jnp.where(lax.rem(row, heads) == lax.div(col, P_SIZE), 1.0, 0.0)


def far_first_masks(size):
    return (*range(2, size), 1)


def pair_masks(size):
    return tuple(mask for mask in range(1, size) if not mask & FIRST_HOP)


def two_parts(factor):
    high = factor.astype(bf16).astype(f32)
    return jnp.concatenate([high, factor - high], axis=0).astype(bf16)


def transposed_dot(left, right):
    return lax.dot_general(left, right, TRANSPOSED, preferred_element_type=f32)


def head_row(heads, width, column):
    return jnp.sum(expander(heads, width, 1) * column, axis=0, keepdims=True)


def group_slice(group):
    return slice(group * GROUP, (group + 1) * GROUP)


def blocks_of(width):
    return [slice(at, at + BLOCK) for at in range(0, width, BLOCK)]


def local_spans(groups):
    spans = []
    for later in range(groups):
        for bit in range(groups.bit_length() - 1):
            if later >> bit & 1:
                start = later >> bit + 1 << bit + 1
                spans.append((later, bit, start, start + 2**bit))
    return spans


def column_of(row):
    size = row.shape[1]
    at = lax.broadcasted_iota(jnp.int32, (size, size), 0) == lax.broadcasted_iota(jnp.int32, (size, size), 1)
    return jnp.sum(jnp.where(at, row, 0.0), axis=1, keepdims=True)


def map_rows(maps):
    if all(rows.shape[0] % 16 == 0 for rows in maps):
        return jnp.concatenate([rows[...] for rows in maps], axis=0)
    return jnp.concatenate([rows[...].astype(f32) for rows in maps], axis=0).astype(bf16)


def out_map_rows(map_refs, parts):
    rows = map_refs[0].shape[0] // 2
    pairs = [ref if rows % 16 == 0 else ref[...].astype(f32) for ref in map_refs]
    sent = (0, *pair_masks(parts))
    picked = []
    for mask in (0, *far_first_masks(parts)):
        pair = pairs[sent.index(mask & ~FIRST_HOP)]
        at = slice(rows, 2 * rows) if mask & FIRST_HOP else slice(0, rows)
        picked.append(pair.at[at] if rows % 16 == 0 else pair[at])
    return map_rows(picked)


def fetch(sources, targets, semaphores):
    copies = [
        pltpu.make_async_copy(source, target, semaphores.at[index])
        for index, (source, target) in enumerate(zip(sources, targets))
    ]
    for copy in copies:
        copy.start()
    return copies


def prepare_kernel(*refs):
    sources, (scaled_ref, cum_ref), kept_refs = refs[:9], refs[9:11], refs[11:18]
    step_ref, rate_ref, semaphores = refs[18:]
    inputs_ref = kept_refs[0]
    copies = fetch(sources, (step_ref, rate_ref, *kept_refs), semaphores)
    heads, tokens = step_ref.shape
    width = inputs_ref.shape[1]
    row = lax.broadcasted_iota(jnp.int32, (GROUP, GROUP), 0)
    col = lax.broadcasted_iota(jnp.int32, (GROUP, GROUP), 1)
    until = jnp.where(row <= col, 1.0, 0.0)
    expand = expander(heads, width, 2).astype(bf16)
    copies[0].wait()
    copies[1].wait()
    step = step_ref[...]
    log_decay = -step * column_of(rate_ref[...])
    factors = []
    for group in range(tokens // GROUP):
        at = group_slice(group)
        cum = jnp.dot(log_decay[:, at], until, precision=HIGHEST, preferred_element_type=f32)
        cum_ref[:, at] = cum
        factors.append(two_parts(jnp.exp(-cum) * step[:, at]))
    factor = jnp.concatenate(factors, axis=1)
    copies[2].wait()
    for cols in blocks_of(width):
        scale = transposed_dot(factor, expand[:, cols])
        scaled_ref[:, cols] = (inputs_ref[:, cols].astype(f32) * scale).astype(bf16)
    for copy in copies[3:]:
        copy.wait()


def join_kernel(mine_ref, theirs_ref, _, both_ref):
    rows = mine_ref.shape[0]
    both_ref[:rows, :] = mine_ref[...]
    both_ref[rows:, :] = theirs_ref[...]


def states_kernel(parts, sides, *refs):
    map_refs, (scaled_ref, cum_ref), out_refs = refs[:parts], refs[parts : parts + 2], refs[parts + 2 :]
    shard_refs = out_refs[:sides]
    heads, tokens = cum_ref.shape
    width = scaled_ref.shape[1]
    in_map = map_rows(map_refs)
    size = in_map.shape[0]
    cum = cum_ref[...]
    states, decays = [], []
    for group in range(tokens // GROUP):
        at = group_slice(group)
        decay = head_row(heads, width, jnp.exp(cum[:, at.stop - 1 : at.stop]))
        raw = jnp.dot(in_map[:, at], scaled_ref[at, :], preferred_element_type=f32)
        states.append(raw * decay)
        decays.append(decay)
    total, decay = states[0], decays[0]
    for group in range(1, len(states)):
        total = total * decays[group] + states[group]
        decay = decay * decays[group]
    columns = width // sides
    core = lax.rem(lax.axis_index("seq"), 2)
    for ref, first in zip(shard_refs, (core == 0, core == 1)):
        at = slice(0, columns)
        ref[:size, :] = jnp.where(first, total[:, at], total[:, width - columns :]).astype(bf16)
        row = jnp.where(first, decay[:, at], decay[:, width - columns :])
        ref[size:, :] = jnp.broadcast_to(row, (DECAY_ROWS, columns)).astype(bf16)
    for index, (later, _, start, stop) in enumerate(local_spans(len(states))):
        span = states[start]
        for group in range(start + 1, later):
            span = span * decays[group]
            if group < stop:
                span = span + states[group]
        out_refs[sides][index * size : (index + 1) * size, :] = span.astype(bf16)


def merge_kernel(size, mine_ref, theirs_ref, _, pair_ref):
    core = lax.rem(lax.axis_index("seq"), 2)
    mine, theirs = mine_ref[...], theirs_ref[...]
    older = jnp.where(core == 1, theirs, mine).astype(f32)
    newer = jnp.where(core == 1, mine, theirs).astype(f32)
    decay = newer[size : size + 1]
    pair_ref[:size, :] = (older[:size] * decay + newer[:size]).astype(bf16)
    pair_ref[size:, :] = (older[size:] * decay).astype(bf16)


def factor_kernel(spans, levels, *refs):
    inputs_ref, gate_ref, mix_ref, skip_ref, cum_ref, _ = refs[:6]
    base_ref, own_ref, far_ref = refs[6:9]
    span_refs = refs[9:]
    heads, tokens = cum_ref.shape
    width = inputs_ref.shape[1]
    groups = tokens // GROUP
    first = groups.bit_length()
    expand = expander(heads, width, 2).astype(bf16)
    skip = head_row(heads, width, column_of(skip_ref[...]))
    before = jnp.zeros((heads, 1), f32)
    for group in range(groups):
        at = group_slice(group)
        cum = cum_ref[:, at]
        decay = jnp.exp(cum)
        own_mix = two_parts(mix_ref[0, :, at] * decay)
        span_mixes = [
            (index, two_parts(mix_ref[1 + bit, :, at] * decay))
            for index, (later, bit, _, _) in enumerate(spans)
            if later == group
        ]
        decay = jnp.exp(cum + before)
        before = before + cum[:, GROUP - 1 : GROUP]
        far_mixes = [two_parts(mix_ref[first + level, :, at] * decay) for level in range(levels)]
        for cols in blocks_of(width):
            gate = gate_ref[at, cols].astype(f32)
            swish = gate / (1.0 + jnp.exp(-gate))
            base_ref[at, cols] = skip[:, cols] * inputs_ref[at, cols].astype(f32) * swish
            own_ref[at, cols] = transposed_dot(own_mix, expand[:, cols]) * swish
            for level, mix in enumerate(far_mixes):
                far_ref[level, at, cols] = (transposed_dot(mix, expand[:, cols]) * swish).astype(bf16)
            for index, mix in span_mixes:
                span_refs[0][index, :, cols] = (transposed_dot(mix, expand[:, cols]) * swish).astype(bf16)


def near_body(spans, has_core, start, scores_ref, turned_ref, refs, near_ref, x_ref=None):
    base_ref, own_ref, far_ref, core_ref, scaled_ref = refs[:5]
    span_refs = refs[5:]
    tokens, size = turned_ref.shape
    for group in range(tokens // GROUP):
        at = group_slice(group)
        for cols in blocks_of(near_ref.shape[1]):
            of = pl.ds(pl.multiple_of(start + cols.start, BLOCK), BLOCK)
            own = jnp.dot(scores_ref[at, :], scaled_ref[at, of], preferred_element_type=f32)
            total = base_ref[at, of] + own_ref[at, of] * own
            for index, (later, _, _, _) in enumerate(spans):
                if later == group:
                    rows = slice(index * size, (index + 1) * size)
                    reach = jnp.dot(turned_ref[at, :], span_refs[0][rows, of], preferred_element_type=f32)
                    total = total + span_refs[1][index, :, of].astype(f32) * reach
            if has_core:
                reach = jnp.dot(turned_ref[at, :], core_ref[:size, cols], preferred_element_type=f32)
                total = total + far_ref[0, at, of].astype(f32) * reach
            if x_ref is not None:
                state = x_ref[:size, cols]
                if has_core:
                    state = (state.astype(f32) * core_ref[size:, cols].astype(f32)[:1]).astype(bf16)
                reach = jnp.dot(turned_ref[at, :], state, preferred_element_type=f32)
                total = total + far_ref[1, at, of].astype(f32) * reach
            near_ref[at, cols] = total


def near_of_core(spans, scores_ref, turned_ref, refs, near_ref, x_ref=None):
    rank = lax.axis_index("seq")
    core = lax.rem(rank, 2)
    along_x = lax.rem(lax.div(rank, 2), 2)
    for has_core in (0, 1):
        for has_x in (0,) if x_ref is None else (0, 1):

            @pl.when((core == has_core) if x_ref is None else (core == has_core) & (along_x == has_x))
            def _():
                start = (has_core if x_ref is None else 1 - has_core) * near_ref.shape[1]
                x_state = x_ref if has_x else None
                near_body(spans, has_core, start, scores_ref, turned_ref, refs, near_ref, x_state)


def near_kernel(parts, spans, paired, *refs):
    count = parts + parts // 2
    in_refs, out_refs, rest = refs[:parts], refs[parts:count], refs[count:-3]
    near_ref, turned_ref, scores_ref = refs[-3:]
    in_map = map_rows(in_refs)
    turned = jnp.transpose(out_map_rows(out_refs, parts))
    turned_ref[...] = turned
    row = lax.broadcasted_iota(jnp.int32, (GROUP, GROUP), 0)
    col = lax.broadcasted_iota(jnp.int32, (GROUP, GROUP), 1)
    for group in range(turned.shape[0] // GROUP):
        at = group_slice(group)
        scores = jnp.dot(turned[at], in_map[:, at], preferred_element_type=f32)
        scores_ref[at, :] = jnp.where(row >= col, scores, 0.0).astype(bf16)
    if paired:
        near_of_core(spans, scores_ref, turned_ref, rest, near_ref)
    else:
        near_body(spans, False, 0, scores_ref, turned_ref, rest, near_ref)


def other_near_kernel(spans, scores_ref, turned_ref, x_ref, _, *refs):
    near_of_core(spans, scores_ref, turned_ref, refs[:-1], refs[-1], x_ref)


def far_body(turned_ref, near_ref, far_ref, gain_ref, start, columns, levels, state_of, gated_ref):
    tokens = far_ref.shape[1]
    squares = jnp.zeros((tokens, 128), f32)
    for cols in blocks_of(columns):
        at = pl.ds(pl.multiple_of(start + cols.start, BLOCK), BLOCK)
        total = near_ref[:, cols]
        for level in levels:
            state = state_of(level, cols, at).astype(bf16)
            reach = jnp.dot(turned_ref[...], state, preferred_element_type=f32)
            total = total + far_ref[level, :, at].astype(f32) * reach
        gated_ref[:, cols] = total * gain_ref[:, at]
        total = total * total
        for part in range(0, BLOCK, 128):
            squares = squares + total[:, part : part + 128]
    return squares


def row_sums(squares):
    high = squares.astype(bf16)
    low = (squares - high.astype(f32)).astype(bf16)
    parts = jnp.concatenate([high, low], axis=1)
    ones = jnp.ones((16, parts.shape[1]), bf16)
    return lax.dot_general(ones, parts, (((1,), (1,)), ((), ())), preferred_element_type=f32)[:1]


def far_kernel(turned_ref, near_ref, far_ref, gain_ref, *refs):
    state_refs = refs[:-2]
    gated_ref, sums_ref = refs[-2:]

    def state_of(level, cols, _):
        return state_refs[level][:, cols]

    width = near_ref.shape[1]
    levels = range(far_ref.shape[0])
    squares = far_body(turned_ref, near_ref, far_ref, gain_ref, 0, width, levels, state_of, gated_ref)
    sums_ref[...] = row_sums(squares)


def combine_kernel(size, x_ref, y_ref, diagonal_ref, spans_ref):
    rank = lax.axis_index("seq")
    along_x = lax.rem(lax.div(rank, 2), 2)
    along_y = lax.div(rank, 4)

    def parts_of(ref):
        return ref[:size, :].astype(f32), ref[size:, :].astype(f32)[:1]

    _, x_decay = parts_of(x_ref)
    y_state, y_decay = parts_of(y_ref)
    d_state, d_decay = parts_of(diagonal_ref)
    newer = jnp.where(along_x == 1, y_state, d_state)
    newer_decay = jnp.where(along_x == 1, y_decay, d_decay)
    older = jnp.where(along_x == 1, d_state, y_state)
    running = jnp.where(along_x == 1, x_decay, 1.0)
    running = jnp.where(along_y == 1, running, 0.0)
    spans_ref[...] = ((older * newer_decay + newer) * running).astype(bf16)


def far_kernel_of_half(own, *refs):
    turned_ref, near_ref, far_ref, gain_ref, core_ref, x_ref, span_ref = refs[:7]
    gated_ref, sums_ref = refs[-2:]
    size = turned_ref.shape[1]
    rank = lax.axis_index("seq")
    core = lax.rem(rank, 2)
    along_x = lax.rem(lax.div(rank, 2), 2)
    along_y = lax.div(rank, 4)
    half = span_ref.shape[1]
    start = (core if own else 1 - core) * half

    def state_of(level, cols, at):
        core_decay = core_ref[size:, cols].astype(f32)[:1]
        running = jnp.where(core == 1, core_decay, 1.0)
        if level == 1:
            return x_ref[:size, cols].astype(f32) * running
        return span_ref[:, cols].astype(f32) * running

    for has_x, has_y in ((0, 0), (0, 1), (1, 0), (1, 1)):

        @pl.when((along_x == has_x) & (along_y == has_y))
        def _():
            levels = ((1,) * has_x if own else ()) + (2,) * has_y
            squares = far_body(turned_ref, near_ref, far_ref, gain_ref, start, half, levels, state_of, gated_ref)
            sums_ref[...] = squares if own else row_sums(squares + refs[7][...])


def norm_kernel(parts, columns, *refs):
    gated_refs, (out_hbm, out_ref, semaphores) = refs[parts:-3], refs[-3:]
    total = refs[0][...]
    for ref in refs[1:parts]:
        total = total + ref[...]
    scale = lax.rsqrt(total / columns + 1e-05)
    tokens = scale.shape[1]
    scale = jnp.broadcast_to(scale, (8, tokens))
    width = gated_refs[0].shape[1]
    core = lax.rem(lax.axis_index("seq"), 2)
    sides = (core, 1 - core) if len(gated_refs) == 2 else (0,)
    chunk = tokens // NORM_CHUNKS
    copies = []
    for index in range(NORM_CHUNKS):
        rows = slice(index * chunk, (index + 1) * chunk)
        column = jnp.transpose(scale[:, rows])[:, :1]
        for ref, side in zip(gated_refs, sides):
            at = pl.ds(pl.multiple_of(side * width, width), width)
            out_ref[rows, at] = (ref[rows, :] * column).astype(bf16)
        copies.append(pltpu.make_async_copy(out_ref.at[rows], out_hbm.at[rows], semaphores.at[index]))
        copies[-1].start()
    for copy in copies:
        copy.wait()


def call(kernel, out_shape, args, flops=0, bytes_accessed=0, hbm=0, scratch=None, out_space=pltpu.VMEM):
    specs = [pl.BlockSpec(memory_space=pl.ANY)] * hbm + [pl.BlockSpec(memory_space=pltpu.VMEM)] * (len(args) - hbm)
    args = [pltpu.with_memory_space_constraint(arg, pltpu.HBM) for arg in args[:hbm]] + list(args[hbm:])
    if scratch is None:
        scratch = [pltpu.VMEM(arg.shape, arg.dtype) for arg in args[:hbm]]
        scratch += [pltpu.SemaphoreType.DMA((hbm,))] if hbm else []
    return pl.pallas_call(
        kernel,
        out_shape=out_shape,
        in_specs=specs,
        out_specs=jax.tree.map(lambda _: pl.BlockSpec(memory_space=out_space), out_shape),
        scratch_shapes=scratch,
        compiler_params=pltpu.CompilerParams(vmem_limit_bytes=VMEM_LIMIT),
        cost_estimate=pl.CostEstimate(flops=flops, bytes_accessed=bytes_accessed, transcendentals=0),
    )(*args)


def shaped(shape, dtype):
    return jax.ShapeDtypeStruct(shape, dtype)


def flip(array, axis, mask):
    return lax.ppermute(array, axis, [(i, i ^ mask) for i in range(lax.axis_size(axis))])


def from_each(array, axis, masks):
    return [flip(array, axis, mask) for mask in masks]


def around(array, paired):
    shards, size = lax.axis_size("seq"), lax.axis_size("head")
    received = []
    for step in range(1, size):
        pairs = []
        for shard in range(shards):
            shift = LATER_SHIFTS[step - 1] if paired and shard >= shards // 2 else step
            pairs += [(shard * size + i, shard * size + (i + shift) % size) for i in range(size)]
        received.append(lax.ppermute(array, ("seq", "head"), pairs))
    return received


def merged(older, newer, size):
    older, newer = older.astype(f32), newer.astype(f32)
    decay = newer[size : size + 1]
    return jnp.concatenate([older[:size] * decay + newer[:size], older[size:] * decay], axis=0).astype(bf16)


def far_states(shard, size):
    rank = lax.axis_index("seq")
    levels = lax.axis_size("seq").bit_length() - 1
    states = []
    running = jnp.ones((1, shard.shape[1]), f32)
    for level in range(levels):
        theirs = flip(shard, "seq", 1 << level)
        upper = jnp.right_shift(rank, level) % 2 == 1
        states.append(jnp.where(upper, theirs[:size].astype(f32) * running, 0.0).astype(bf16))
        running = jnp.where(upper, running * theirs[size : size + 1].astype(f32), running)
        shard = merged(jnp.where(upper, theirs, shard), jnp.where(upper, shard, theirs), size)
    return states


def on_device(inputs, gate, input_map, output_map, step, decay_rate, level_mix, skip, norm_gain):
    tokens, width = inputs.shape
    heads = step.shape[0]
    parts = lax.axis_size("head")
    levels = lax.axis_size("seq").bit_length() - 1
    size = input_map.shape[0] * parts
    groups = tokens // GROUP
    spans = local_spans(groups)
    dense = 2 * tokens * GROUP * width
    area = tokens * width
    others = from_each(input_map, "head", far_first_masks(parts))
    kept = inputs, gate, level_mix, skip[None, :], input_map, output_map, norm_gain[None, :]
    beside = flip(output_map, "head", FIRST_HOP)
    scaled, cum, *kept = call(
        prepare_kernel,
        (
            *(shaped((tokens, width), bf16), shaped((heads, tokens), f32)),
            *(shaped(array.shape, array.dtype) for array in kept),
        ),
        (step, decay_rate[None, :], *kept),
        flops=16 * dense,
        bytes_accessed=4 * area,
        hbm=9,
        scratch=[pltpu.VMEM(step.shape, f32), pltpu.VMEM((1, heads), f32), pltpu.SemaphoreType.DMA((9,))],
    )
    inputs, gate, level_mix, skip, input_map, output_map, gain = kept
    in_maps = [input_map, *others]
    pairs = lax.axis_size("seq") == 8 and parts == 4
    sides = 2 if pairs else 1
    shard_shape = shaped((size + DECAY_ROWS, width // sides), bf16)
    span_shape = [shaped((len(spans) * size, width), bf16)] if spans else []
    shard, *rest = call(
        functools.partial(states_kernel, parts, sides),
        (*[shard_shape] * sides, *span_shape),
        (*in_maps, scaled, cum),
        flops=dense,
    )
    span_states = rest[sides - 1 :]
    rows = output_map.shape[0]
    if rows % 16 == 0:
        both = call(
            join_kernel,
            shaped((2 * rows, tokens), bf16),
            (output_map, beside, shard),
            flops=8 * dense,
        )
    else:
        both = jnp.concatenate([output_map, beside], axis=0)
    if pairs:
        theirs = flip(rest[0], "seq", 1)
        message = call(
            functools.partial(merge_kernel, size), shard_shape, (shard, theirs, both), flops=0
        )
        other_theirs = flip(lax.optimization_barrier((shard, message))[0], "seq", 1)
    else:
        other_theirs = theirs = message = shard
    out_maps = [both, *from_each(both, "head", pair_masks(parts))]
    factor_shape = [shaped((len(spans), GROUP, width), bf16)] if spans else []
    base, own_factor, far, *span_factors = call(
        functools.partial(factor_kernel, spans, levels),
        (
            *(shaped((tokens, width), f32), shaped((tokens, width), f32)),
            *(shaped((levels, tokens, width), bf16), *factor_shape),
        ),
        (inputs, gate, level_mix, skip, cum, message),
        flops=5 * dense,
        bytes_accessed=0,
    )
    near_args = base, own_factor, far, theirs, scaled, *span_states, *span_factors
    near_shape = shaped((tokens, width // 2 if pairs else width), f32)
    near, turned, scores = call(
        functools.partial(near_kernel, parts, spans, pairs),
        (near_shape, shaped((tokens, size), bf16), shaped((tokens, GROUP), bf16)),
        (*in_maps, *out_maps, *near_args),
    )
    sums_shape = shaped((1, tokens), f32)
    if pairs:
        received = [flip(message, "seq", 4), flip(message, "seq", 2), lax.ppermute(message, "seq", CYCLE)]
        from_y, from_x, from_cycle = received
        from_y, from_x, near, far = lax.optimization_barrier((from_y, from_x, near, far))
        from_cycle, near = lax.optimization_barrier((from_cycle, near))
        from_cycle, other_theirs = lax.optimization_barrier((from_cycle, other_theirs))
        own = call(
            functools.partial(combine_kernel, size),
            shaped((size, width // 2), bf16),
            (from_x, from_y, from_cycle),
            bytes_accessed=area,
        )
        other = flip(own, "seq", 1)
        other_x = flip(from_x, "seq", 1)
        gated_shape = shaped((tokens, width // 2), f32)
        own_gated, own_squares = call(
            functools.partial(far_kernel_of_half, True),
            (gated_shape, shaped((tokens, 128), f32)),
            (turned, near, far, gain, theirs, from_x, own),
            flops=2 * dense,
            bytes_accessed=6 * area,
        )
        near_args = base, own_factor, far, other_theirs, scaled, *span_states, *span_factors
        other_near = call(
            functools.partial(other_near_kernel, spans), near_shape, (scores, turned, other_x, own_squares, *near_args), flops=0
        )
        other_gated, sums = call(
            functools.partial(far_kernel_of_half, False),
            (gated_shape, sums_shape),
            (turned, other_near, far, gain, other_theirs, other_x, other, own_squares),
            flops=2 * dense,
            bytes_accessed=6 * area,
        )
        gated = (own_gated, other_gated)
    else:
        *gated, sums = call(
            far_kernel,
            (shaped((tokens, width), f32), sums_shape),
            (turned, near, far, gain, *far_states(shard, size)),
            flops=4 * dense,
            bytes_accessed=12 * area,
        )
    last = [sums, *around(sums, pairs)]
    return call(
        functools.partial(norm_kernel, len(last), width * parts),
        shaped((tokens, width), bf16),
        (*last, *gated),
        flops=dense,
        bytes_accessed=6 * area,
        scratch=[pltpu.VMEM((tokens, width), bf16), pltpu.SemaphoreType.DMA((NORM_CHUNKS,))],
        out_space=pl.ANY,
    )


def solution(mesh):
    return jax.shard_map(
        on_device,
        mesh=mesh,
        in_specs=(
            P("seq", "head"),
            P("seq", "head"),
            P("head", "seq"),
            P("head", "seq"),
            P("head", "seq"),
            P("head"),
            P(None, "head", "seq"),
            P("head"),
            P("head"),
        ),
        out_specs=P("seq", "head"),
        check_vma=False,
    )
```

```python
import functools

import jax
import jax.numpy as jnp
from jax import lax
from jax.experimental import pallas as pl
from jax.experimental.pallas import tpu as pltpu
from jax.sharding import PartitionSpec as P

P_SIZE = 64
GROUP = 256
DECAY_ROWS = 8
BLOCK = 128
NORM_CHUNKS = 4
FIRST_HOP = 2
LATER_SHIFTS = (2, 1, 3)
CYCLE = [(2 * chip + core, 2 * target + core) for chip, target in ((0, 3), (3, 1), (1, 2), (2, 0)) for core in (0, 1)]
VMEM_LIMIT = 40 * 1024 * 1024

f32, bf16 = jnp.float32, jnp.bfloat16
HIGHEST = lax.Precision.HIGHEST
TRANSPOSED = (((0,), (0,)), ((), ()))


def expander(heads, width, copies):
    row = lax.broadcasted_iota(jnp.int32, (copies * heads, width), 0)
    col = lax.broadcasted_iota(jnp.int32, (copies * heads, width), 1)
    return jnp.where(lax.rem(row, heads) == lax.div(col, P_SIZE), 1.0, 0.0)


def far_first_masks(size):
    return (*range(2, size), 1)


def pair_masks(size):
    return tuple(mask for mask in range(1, size) if not mask & FIRST_HOP)


def two_parts(factor):
    high = factor.astype(bf16).astype(f32)
    return jnp.concatenate([high, factor - high], axis=0).astype(bf16)


def transposed_dot(left, right):
    return lax.dot_general(left, right, TRANSPOSED, preferred_element_type=f32)


def head_row(heads, width, column):
    return jnp.sum(expander(heads, width, 1) * column, axis=0, keepdims=True)


def group_slice(group):
    return slice(group * GROUP, (group + 1) * GROUP)


def blocks_of(width):
    return [slice(at, at + BLOCK) for at in range(0, width, BLOCK)]


def local_spans(groups):
    spans = []
    for later in range(groups):
        for bit in range(groups.bit_length() - 1):
            if later >> bit & 1:
                start = later >> bit + 1 << bit + 1
                spans.append((later, bit, start, start + 2**bit))
    return spans


def column_of(row):
    size = row.shape[1]
    at = lax.broadcasted_iota(jnp.int32, (size, size), 0) == lax.broadcasted_iota(jnp.int32, (size, size), 1)
    return jnp.sum(jnp.where(at, row, 0.0), axis=1, keepdims=True)


def map_rows(maps):
    if all(rows.shape[0] % 16 == 0 for rows in maps):
        return jnp.concatenate([rows[...] for rows in maps], axis=0)
    return jnp.concatenate([rows[...].astype(f32) for rows in maps], axis=0).astype(bf16)


def out_map_rows(map_refs, parts):
    rows = map_refs[0].shape[0] // 2
    pairs = [ref if rows % 16 == 0 else ref[...].astype(f32) for ref in map_refs]
    sent = (0, *pair_masks(parts))
    picked = []
    for mask in (0, *far_first_masks(parts)):
        pair = pairs[sent.index(mask & ~FIRST_HOP)]
        at = slice(rows, 2 * rows) if mask & FIRST_HOP else slice(0, rows)
        picked.append(pair.at[at] if rows % 16 == 0 else pair[at])
    return map_rows(picked)


def fetch(sources, targets, semaphores):
    copies = [
        pltpu.make_async_copy(source, target, semaphores.at[index])
        for index, (source, target) in enumerate(zip(sources, targets))
    ]
    for copy in copies:
        copy.start()
    return copies


def prepare_kernel(*refs):
    sources, (scaled_ref, cum_ref), kept_refs = refs[:9], refs[9:11], refs[11:18]
    step_ref, rate_ref, semaphores = refs[18:]
    inputs_ref = kept_refs[0]
    copies = fetch(sources, (step_ref, rate_ref, *kept_refs), semaphores)
    heads, tokens = step_ref.shape
    width = inputs_ref.shape[1]
    row = lax.broadcasted_iota(jnp.int32, (GROUP, GROUP), 0)
    col = lax.broadcasted_iota(jnp.int32, (GROUP, GROUP), 1)
    until = jnp.where(row <= col, 1.0, 0.0)
    expand = expander(heads, width, 2).astype(bf16)
    copies[0].wait()
    copies[1].wait()
    step = step_ref[...]
    log_decay = -step * column_of(rate_ref[...])
    factors = []
    for group in range(tokens // GROUP):
        at = group_slice(group)
        cum = jnp.dot(log_decay[:, at], until, precision=HIGHEST, preferred_element_type=f32)
        cum_ref[:, at] = cum
        factors.append(two_parts(jnp.exp(-cum) * step[:, at]))
    factor = jnp.concatenate(factors, axis=1)
    copies[2].wait()
    for cols in blocks_of(width):
        scale = transposed_dot(factor, expand[:, cols])
        scaled_ref[:, cols] = (inputs_ref[:, cols].astype(f32) * scale).astype(bf16)
    for copy in copies[3:]:
        copy.wait()


def join_kernel(mine_ref, theirs_ref, _, both_ref):
    rows = mine_ref.shape[0]
    both_ref[:rows, :] = mine_ref[...]
    both_ref[rows:, :] = theirs_ref[...]


def states_kernel(parts, sides, *refs):
    map_refs, (scaled_ref, cum_ref), out_refs = refs[:parts], refs[parts : parts + 2], refs[parts + 2 :]
    shard_refs = out_refs[:sides]
    heads, tokens = cum_ref.shape
    width = scaled_ref.shape[1]
    in_map = map_rows(map_refs)
    size = in_map.shape[0]
    cum = cum_ref[...]
    states, decays = [], []
    for group in range(tokens // GROUP):
        at = group_slice(group)
        decay = head_row(heads, width, jnp.exp(cum[:, at.stop - 1 : at.stop]))
        raw = jnp.dot(in_map[:, at], scaled_ref[at, :], preferred_element_type=f32)
        states.append(raw * decay)
        decays.append(decay)
    total, decay = states[0], decays[0]
    for group in range(1, len(states)):
        total = total * decays[group] + states[group]
        decay = decay * decays[group]
    columns = width // sides
    core = lax.rem(lax.axis_index("seq"), 2)
    for ref, first in zip(shard_refs, (core == 0, core == 1)):
        at = slice(0, columns)
        ref[:size, :] = jnp.where(first, total[:, at], total[:, width - columns :]).astype(bf16)
        row = jnp.where(first, decay[:, at], decay[:, width - columns :])
        ref[size:, :] = jnp.broadcast_to(row, (DECAY_ROWS, columns)).astype(bf16)
    for index, (later, _, start, stop) in enumerate(local_spans(len(states))):
        span = states[start]
        for group in range(start + 1, later):
            span = span * decays[group]
            if group < stop:
                span = span + states[group]
        out_refs[sides][index * size : (index + 1) * size, :] = span.astype(bf16)


def merge_kernel(size, mine_ref, theirs_ref, _, pair_ref):
    core = lax.rem(lax.axis_index("seq"), 2)
    mine, theirs = mine_ref[...], theirs_ref[...]
    older = jnp.where(core == 1, theirs, mine).astype(f32)
    newer = jnp.where(core == 1, mine, theirs).astype(f32)
    decay = newer[size : size + 1]
    pair_ref[:size, :] = (older[:size] * decay + newer[:size]).astype(bf16)
    pair_ref[size:, :] = (older[size:] * decay).astype(bf16)


def factor_kernel(spans, levels, *refs):
    inputs_ref, gate_ref, mix_ref, skip_ref, cum_ref, _ = refs[:6]
    base_ref, own_ref, far_ref = refs[6:9]
    span_refs = refs[9:]
    heads, tokens = cum_ref.shape
    width = inputs_ref.shape[1]
    groups = tokens // GROUP
    first = groups.bit_length()
    expand = expander(heads, width, 2).astype(bf16)
    skip = head_row(heads, width, column_of(skip_ref[...]))
    before = jnp.zeros((heads, 1), f32)
    for group in range(groups):
        at = group_slice(group)
        cum = cum_ref[:, at]
        decay = jnp.exp(cum)
        own_mix = two_parts(mix_ref[0, :, at] * decay)
        span_mixes = [
            (index, two_parts(mix_ref[1 + bit, :, at] * decay))
            for index, (later, bit, _, _) in enumerate(spans)
            if later == group
        ]
        decay = jnp.exp(cum + before)
        before = before + cum[:, GROUP - 1 : GROUP]
        far_mixes = [two_parts(mix_ref[first + level, :, at] * decay) for level in range(levels)]
        for cols in blocks_of(width):
            gate = gate_ref[at, cols].astype(f32)
            swish = gate / (1.0 + jnp.exp(-gate))
            base_ref[at, cols] = skip[:, cols] * inputs_ref[at, cols].astype(f32) * swish
            own_ref[at, cols] = transposed_dot(own_mix, expand[:, cols]) * swish
            for level, mix in enumerate(far_mixes):
                far_ref[level, at, cols] = (transposed_dot(mix, expand[:, cols]) * swish).astype(bf16)
            for index, mix in span_mixes:
                span_refs[0][index, :, cols] = (transposed_dot(mix, expand[:, cols]) * swish).astype(bf16)


def near_body(spans, has_core, start, scores_ref, turned_ref, refs, near_ref, x_ref=None):
    base_ref, own_ref, far_ref, core_ref, scaled_ref = refs[:5]
    span_refs = refs[5:]
    tokens, size = turned_ref.shape
    for group in range(tokens // GROUP):
        at = group_slice(group)
        for cols in blocks_of(near_ref.shape[1]):
            of = pl.ds(pl.multiple_of(start + cols.start, BLOCK), BLOCK)
            own = jnp.dot(scores_ref[at, :], scaled_ref[at, of], preferred_element_type=f32)
            total = base_ref[at, of] + own_ref[at, of] * own
            for index, (later, _, _, _) in enumerate(spans):
                if later == group:
                    rows = slice(index * size, (index + 1) * size)
                    reach = jnp.dot(turned_ref[at, :], span_refs[0][rows, of], preferred_element_type=f32)
                    total = total + span_refs[1][index, :, of].astype(f32) * reach
            if has_core:
                reach = jnp.dot(turned_ref[at, :], core_ref[:size, cols], preferred_element_type=f32)
                total = total + far_ref[0, at, of].astype(f32) * reach
            if x_ref is not None:
                state = x_ref[:size, cols]
                if has_core:
                    state = (state.astype(f32) * core_ref[size:, cols].astype(f32)[:1]).astype(bf16)
                reach = jnp.dot(turned_ref[at, :], state, preferred_element_type=f32)
                total = total + far_ref[1, at, of].astype(f32) * reach
            near_ref[at, cols] = total


def near_of_core(spans, scores_ref, turned_ref, refs, near_ref, x_ref=None):
    rank = lax.axis_index("seq")
    core = lax.rem(rank, 2)
    along_x = lax.rem(lax.div(rank, 2), 2)
    for has_core in (0, 1):
        for has_x in (0,) if x_ref is None else (0, 1):

            @pl.when((core == has_core) if x_ref is None else (core == has_core) & (along_x == has_x))
            def _():
                start = (has_core if x_ref is None else 1 - has_core) * near_ref.shape[1]
                x_state = x_ref if has_x else None
                near_body(spans, has_core, start, scores_ref, turned_ref, refs, near_ref, x_state)


def near_kernel(parts, spans, paired, *refs):
    count = parts + parts // 2
    in_refs, out_refs, rest = refs[:parts], refs[parts:count], refs[count:-3]
    near_ref, turned_ref, scores_ref = refs[-3:]
    in_map = map_rows(in_refs)
    turned = jnp.transpose(out_map_rows(out_refs, parts))
    turned_ref[...] = turned
    row = lax.broadcasted_iota(jnp.int32, (GROUP, GROUP), 0)
    col = lax.broadcasted_iota(jnp.int32, (GROUP, GROUP), 1)
    for group in range(turned.shape[0] // GROUP):
        at = group_slice(group)
        scores = jnp.dot(turned[at], in_map[:, at], preferred_element_type=f32)
        scores_ref[at, :] = jnp.where(row >= col, scores, 0.0).astype(bf16)
    if paired:
        near_of_core(spans, scores_ref, turned_ref, rest, near_ref)
    else:
        near_body(spans, False, 0, scores_ref, turned_ref, rest, near_ref)


def other_near_kernel(spans, scores_ref, turned_ref, x_ref, _, *refs):
    near_of_core(spans, scores_ref, turned_ref, refs[:-1], refs[-1], x_ref)


def far_body(turned_ref, near_ref, far_ref, gain_ref, start, columns, levels, state_of, gated_ref):
    tokens = far_ref.shape[1]
    squares = jnp.zeros((tokens, 128), f32)
    for cols in blocks_of(columns):
        at = pl.ds(pl.multiple_of(start + cols.start, BLOCK), BLOCK)
        total = near_ref[:, cols]
        for level in levels:
            state = state_of(level, cols, at).astype(bf16)
            reach = jnp.dot(turned_ref[...], state, preferred_element_type=f32)
            total = total + far_ref[level, :, at].astype(f32) * reach
        gated_ref[:, cols] = total * gain_ref[:, at]
        total = total * total
        for part in range(0, BLOCK, 128):
            squares = squares + total[:, part : part + 128]
    return squares


def row_sums(squares):
    high = squares.astype(bf16)
    low = (squares - high.astype(f32)).astype(bf16)
    parts = jnp.concatenate([high, low], axis=1)
    ones = jnp.ones((16, parts.shape[1]), bf16)
    return lax.dot_general(ones, parts, (((1,), (1,)), ((), ())), preferred_element_type=f32)[:1]


def far_kernel(turned_ref, near_ref, far_ref, gain_ref, *refs):
    state_refs = refs[:-2]
    gated_ref, sums_ref = refs[-2:]

    def state_of(level, cols, _):
        return state_refs[level][:, cols]

    width = near_ref.shape[1]
    levels = range(far_ref.shape[0])
    squares = far_body(turned_ref, near_ref, far_ref, gain_ref, 0, width, levels, state_of, gated_ref)
    sums_ref[...] = row_sums(squares)


def combine_kernel(size, x_ref, y_ref, diagonal_ref, spans_ref):
    rank = lax.axis_index("seq")
    along_x = lax.rem(lax.div(rank, 2), 2)
    along_y = lax.div(rank, 4)

    def parts_of(ref):
        return ref[:size, :].astype(f32), ref[size:, :].astype(f32)[:1]

    _, x_decay = parts_of(x_ref)
    y_state, y_decay = parts_of(y_ref)
    d_state, d_decay = parts_of(diagonal_ref)
    newer = jnp.where(along_x == 1, y_state, d_state)
    newer_decay = jnp.where(along_x == 1, y_decay, d_decay)
    older = jnp.where(along_x == 1, d_state, y_state)
    running = jnp.where(along_x == 1, x_decay, 1.0)
    running = jnp.where(along_y == 1, running, 0.0)
    spans_ref[...] = ((older * newer_decay + newer) * running).astype(bf16)


def far_kernel_of_half(own, *refs):
    turned_ref, near_ref, far_ref, gain_ref, core_ref, x_ref, span_ref = refs[:7]
    gated_ref, sums_ref = refs[-2:]
    size = turned_ref.shape[1]
    rank = lax.axis_index("seq")
    core = lax.rem(rank, 2)
    along_x = lax.rem(lax.div(rank, 2), 2)
    along_y = lax.div(rank, 4)
    half = span_ref.shape[1]
    start = (core if own else 1 - core) * half

    def state_of(level, cols, at):
        core_decay = core_ref[size:, cols].astype(f32)[:1]
        running = jnp.where(core == 1, core_decay, 1.0)
        if level == 1:
            return x_ref[:size, cols].astype(f32) * running
        return span_ref[:, cols].astype(f32) * running

    for has_x, has_y in ((0, 0), (0, 1), (1, 0), (1, 1)):

        @pl.when((along_x == has_x) & (along_y == has_y))
        def _():
            levels = ((1,) * has_x if own else ()) + (2,) * has_y
            squares = far_body(turned_ref, near_ref, far_ref, gain_ref, start, half, levels, state_of, gated_ref)
            sums_ref[...] = squares if own else row_sums(squares + refs[7][...])


def norm_kernel(parts, columns, *refs):
    gated_refs, (out_hbm, out_ref, semaphores) = refs[parts:-3], refs[-3:]
    total = refs[0][...]
    for ref in refs[1:parts]:
        total = total + ref[...]
    scale = lax.rsqrt(total / columns + 1e-05)
    tokens = scale.shape[1]
    scale = jnp.broadcast_to(scale, (8, tokens))
    width = gated_refs[0].shape[1]
    core = lax.rem(lax.axis_index("seq"), 2)
    sides = (core, 1 - core) if len(gated_refs) == 2 else (0,)
    chunk = tokens // NORM_CHUNKS
    copies = []
    for index in range(NORM_CHUNKS):
        rows = slice(index * chunk, (index + 1) * chunk)
        column = jnp.transpose(scale[:, rows])[:, :1]
        for ref, side in zip(gated_refs, sides):
            at = pl.ds(pl.multiple_of(side * width, width), width)
            out_ref[rows, at] = (ref[rows, :] * column).astype(bf16)
        copies.append(pltpu.make_async_copy(out_ref.at[rows], out_hbm.at[rows], semaphores.at[index]))
        copies[-1].start()
    for copy in copies:
        copy.wait()


def call(kernel, out_shape, args, flops=0, bytes_accessed=0, hbm=0, scratch=None, out_space=pltpu.VMEM):
    specs = [pl.BlockSpec(memory_space=pl.ANY)] * hbm + [pl.BlockSpec(memory_space=pltpu.VMEM)] * (len(args) - hbm)
    args = [pltpu.with_memory_space_constraint(arg, pltpu.HBM) for arg in args[:hbm]] + list(args[hbm:])
    if scratch is None:
        scratch = [pltpu.VMEM(arg.shape, arg.dtype) for arg in args[:hbm]]
        scratch += [pltpu.SemaphoreType.DMA((hbm,))] if hbm else []
    return pl.pallas_call(
        kernel,
        out_shape=out_shape,
        in_specs=specs,
        out_specs=jax.tree.map(lambda _: pl.BlockSpec(memory_space=out_space), out_shape),
        scratch_shapes=scratch,
        compiler_params=pltpu.CompilerParams(vmem_limit_bytes=VMEM_LIMIT),
        cost_estimate=pl.CostEstimate(flops=flops, bytes_accessed=bytes_accessed, transcendentals=0),
    )(*args)


def shaped(shape, dtype):
    return jax.ShapeDtypeStruct(shape, dtype)


def flip(array, axis, mask):
    return lax.ppermute(array, axis, [(i, i ^ mask) for i in range(lax.axis_size(axis))])


def from_each(array, axis, masks):
    return [flip(array, axis, mask) for mask in masks]


def around(array, paired):
    shards, size = lax.axis_size("seq"), lax.axis_size("head")
    received = []
    for step in range(1, size):
        pairs = []
        for shard in range(shards):
            shift = LATER_SHIFTS[step - 1] if paired and shard >= shards // 2 else step
            pairs += [(shard * size + i, shard * size + (i + shift) % size) for i in range(size)]
        received.append(lax.ppermute(array, ("seq", "head"), pairs))
    return received


def merged(older, newer, size):
    older, newer = older.astype(f32), newer.astype(f32)
    decay = newer[size : size + 1]
    return jnp.concatenate([older[:size] * decay + newer[:size], older[size:] * decay], axis=0).astype(bf16)


def far_states(shard, size):
    rank = lax.axis_index("seq")
    levels = lax.axis_size("seq").bit_length() - 1
    states = []
    running = jnp.ones((1, shard.shape[1]), f32)
    for level in range(levels):
        theirs = flip(shard, "seq", 1 << level)
        upper = jnp.right_shift(rank, level) % 2 == 1
        states.append(jnp.where(upper, theirs[:size].astype(f32) * running, 0.0).astype(bf16))
        running = jnp.where(upper, running * theirs[size : size + 1].astype(f32), running)
        shard = merged(jnp.where(upper, theirs, shard), jnp.where(upper, shard, theirs), size)
    return states


def on_device(inputs, gate, input_map, output_map, step, decay_rate, level_mix, skip, norm_gain):
    tokens, width = inputs.shape
    heads = step.shape[0]
    parts = lax.axis_size("head")
    levels = lax.axis_size("seq").bit_length() - 1
    size = input_map.shape[0] * parts
    groups = tokens // GROUP
    spans = local_spans(groups)
    dense = 2 * tokens * GROUP * width
    area = tokens * width
    others = from_each(input_map, "head", far_first_masks(parts))
    kept = inputs, gate, level_mix, skip[None, :], input_map, output_map, norm_gain[None, :]
    beside = flip(output_map, "head", FIRST_HOP)
    scaled, cum, *kept = call(
        prepare_kernel,
        (
            *(shaped((tokens, width), bf16), shaped((heads, tokens), f32)),
            *(shaped(array.shape, array.dtype) for array in kept),
        ),
        (step, decay_rate[None, :], *kept),
        flops=16 * dense,
        bytes_accessed=4 * area,
        hbm=9,
        scratch=[pltpu.VMEM(step.shape, f32), pltpu.VMEM((1, heads), f32), pltpu.SemaphoreType.DMA((9,))],
    )
    inputs, gate, level_mix, skip, input_map, output_map, gain = kept
    in_maps = [input_map, *others]
    pairs = lax.axis_size("seq") == 8 and parts == 4
    sides = 2 if pairs else 1
    shard_shape = shaped((size + DECAY_ROWS, width // sides), bf16)
    span_shape = [shaped((len(spans) * size, width), bf16)] if spans else []
    shard, *rest = call(
        functools.partial(states_kernel, parts, sides),
        (*[shard_shape] * sides, *span_shape),
        (*in_maps, scaled, cum),
        flops=dense,
    )
    span_states = rest[sides - 1 :]
    rows = output_map.shape[0]
    if rows % 16 == 0:
        both = call(
            join_kernel,
            shaped((2 * rows, tokens), bf16),
            (output_map, beside, shard),
            flops=8 * dense,
        )
    else:
        both = jnp.concatenate([output_map, beside], axis=0)
    if pairs:
        theirs = flip(rest[0], "seq", 1)
        message = call(
            functools.partial(merge_kernel, size), shard_shape, (shard, theirs, both), flops=0
        )
        other_theirs = flip(lax.optimization_barrier((shard, message))[0], "seq", 1)
    else:
        other_theirs = theirs = message = shard
    out_maps = [both, *from_each(both, "head", pair_masks(parts))]
    factor_shape = [shaped((len(spans), GROUP, width), bf16)] if spans else []
    base, own_factor, far, *span_factors = call(
        functools.partial(factor_kernel, spans, levels),
        (
            *(shaped((tokens, width), f32), shaped((tokens, width), f32)),
            *(shaped((levels, tokens, width), bf16), *factor_shape),
        ),
        (inputs, gate, level_mix, skip, cum, message),
        flops=5 * dense,
        bytes_accessed=0,
    )
    near_args = base, own_factor, far, theirs, scaled, *span_states, *span_factors
    near_shape = shaped((tokens, width // 2 if pairs else width), f32)
    near, turned, scores = call(
        functools.partial(near_kernel, parts, spans, pairs),
        (near_shape, shaped((tokens, size), bf16), shaped((tokens, GROUP), bf16)),
        (*in_maps, *out_maps, *near_args),
    )
    sums_shape = shaped((1, tokens), f32)
    if pairs:
        received = [flip(message, "seq", 4), flip(message, "seq", 2), lax.ppermute(message, "seq", CYCLE)]
        from_y, from_x, from_cycle = received
        from_y, from_x, near, far = lax.optimization_barrier((from_y, from_x, near, far))
        from_cycle, near = lax.optimization_barrier((from_cycle, near))
        from_cycle, other_theirs = lax.optimization_barrier((from_cycle, other_theirs))
        own = call(
            functools.partial(combine_kernel, size),
            shaped((size, width // 2), bf16),
            (from_x, from_y, from_cycle),
            bytes_accessed=area,
        )
        other = flip(own, "seq", 1)
        other_x = flip(from_x, "seq", 1)
        gated_shape = shaped((tokens, width // 2), f32)
        own_gated, own_squares = call(
            functools.partial(far_kernel_of_half, True),
            (gated_shape, shaped((tokens, 128), f32)),
            (turned, near, far, gain, theirs, from_x, own),
            flops=2 * dense,
            bytes_accessed=6 * area,
        )
        near_args = base, own_factor, far, other_theirs, scaled, *span_states, *span_factors
        other_near = call(
            functools.partial(other_near_kernel, spans), near_shape, (scores, turned, other_x, own_squares, *near_args), flops=0
        )
        other_gated, sums = call(
            functools.partial(far_kernel_of_half, False),
            (gated_shape, sums_shape),
            (turned, other_near, far, gain, other_theirs, other_x, other, own_squares),
            flops=2 * dense,
            bytes_accessed=6 * area,
        )
        gated = (own_gated, other_gated)
    else:
        *gated, sums = call(
            far_kernel,
            (shaped((tokens, width), f32), sums_shape),
            (turned, near, far, gain, *far_states(shard, size)),
            flops=4 * dense,
            bytes_accessed=12 * area,
        )
    last = [sums, *around(sums, pairs)]
    return call(
        functools.partial(norm_kernel, len(last), width * parts),
        shaped((tokens, width), bf16),
        (*last, *gated),
        flops=dense,
        bytes_accessed=6 * area,
        scratch=[pltpu.VMEM((tokens, width), bf16), pltpu.SemaphoreType.DMA((NORM_CHUNKS,))],
        out_space=pl.ANY,
    )


def solution(mesh):
    return jax.shard_map(
        on_device,
        mesh=mesh,
        in_specs=(
            P("seq", "head"),
            P("seq", "head"),
            P("head", "seq"),
            P("head", "seq"),
            P("head", "seq"),
            P("head"),
            P(None, "head", "seq"),
            P("head"),
            P("head"),
        ),
        out_specs=P("seq", "head"),
        check_vma=False,
    )
```
